32 devices in a mesh: dp: 8 (over z, x), mp: 4 (over y, core).
Axes of the slice: x: 2, y: 2, z: 4, core: 2. Of those that a mesh axis runs over, the one named last changes fastest.
Arguments:
- tokens: bfloat16 [8192, 512], P('dp'), may hold values from -6 to 6
- ln1_gain: float32 [512], replicated, may hold values from 0.5 to 1.5
- ln1_bias: float32 [512], replicated, may hold values from -4 to 4
- w_qkv: bfloat16 [3, 512, 512], P(None, None, 'mp'), may hold values from -0.25 to 0.25
- w_out: bfloat16 [512, 512], P('mp'), may hold values from -2 to 2
- b_out: float32 [512], replicated, may hold values from -4 to 4
- ln2_gain: float32 [512], replicated, may hold values from 0.5 to 1.5
- ln2_bias: float32 [512], replicated, may hold values from -4 to 4
- w_up: bfloat16 [512, 2048], P(None, 'mp'), may hold values from -0.25 to 0.25
- b_up: float32 [2048], P('mp'), may hold values from -6 to 6
- w_down: bfloat16 [2048, 512], P('mp'), may hold values from -0.25 to 0.25
- b_down: float32 [512], replicated, may hold values from -4 to 4
- cotangent: bfloat16 [8192, 512], P('dp'), may hold values from -6 to 6
Outputs:
- output: bfloat16 [8192, 512], P('dp')
- grad_tokens: bfloat16 [8192, 512], P('dp')
- grad_ln1_gain: float32 [512], replicated
- grad_ln1_bias: float32 [512], replicated
- grad_w_qkv: float32 [3, 512, 512], P(None, None, 'mp')
- grad_w_out: float32 [512, 512], P('mp')
- grad_b_out: float32 [512], replicated
- grad_ln2_gain: float32 [512], replicated
- grad_ln2_bias: float32 [512], replicated
- grad_w_up: float32 [512, 2048], P(None, 'mp')
- grad_b_up: float32 [2048], P('mp')
- grad_w_down: float32 [2048, 512], P('mp')
- grad_b_down: float32 [512], replicated
The draws below stay inside these ranges and needn't reach their ends.
All inputs are finite; a program needn't handle non-finite values.
Results may differ from the reference program's by a relative error of at most 0.012.
Values may be sent and summed in bfloat16 or wider, within the bound.
No kernel may reach another device: no remote copies, remote signals or barrier semaphores. Data moves between devices by JAX's collectives and lax.ppermute only.
A program may use at most 64 MiB of HBM per device.

```python
import math
import jax
import jax.numpy as jnp
from jax import lax

D = 512
HEADS = 8
HEAD_DIM = 64
FF = 2048
SPAN = 128
LENGTH = 4096
TOKENS = 8192


def steps_of(rng, dims, cuts, low, top_value):
    factor_of = 1.0
    for position, blocks in cuts:
        steps = jax.random.uniform(jax.random.fold_in(jax.random.fold_in(rng, 6), position), (blocks,), jnp.float32, low / len(cuts), top_value / len(cuts))
        factor_of = factor_of * jnp.repeat(jnp.exp(steps), dims[position] // blocks).reshape((-1,) + (1,) * (len(dims) - 1 - position))
    return factor_of


def gaussian(own_key, extent, width, reach, shards=(), held_as=jnp.bfloat16):
    values = width * jax.random.normal(own_key, extent, jnp.float32)
    if shards:
        values = values * steps_of(own_key, extent, shards, -0.22, 0.18)
    return jnp.clip(values, -reach, reach).astype(held_as)


def setup_inputs(seed: int = 0) -> dict:
    key_of = jax.random.split(jax.random.key(seed), 14)
    return {
        "tokens": gaussian(key_of[0], (TOKENS, D), 1.0, 6.0, ((0, 8),)),
        "ln1_gain": jnp.clip(1.0 + 0.1 * jax.random.normal(key_of[1], (D,), jnp.float32), 0.5, 1.5),
        "ln1_bias": gaussian(key_of[2], (D,), 0.3, 4.0, (), jnp.float32),
        "w_qkv": gaussian(key_of[3], (3, D, D), D ** -0.5, 0.25, ((2, 4),)),
        "w_out": gaussian(key_of[4], (D, D), (D // 64) ** -0.5, 2.0, ((0, 4),)),
        "b_out": gaussian(key_of[5], (D,), 0.3, 4.0, (), jnp.float32),
        "ln2_gain": jnp.clip(1.0 + 0.1 * jax.random.normal(key_of[6], (D,), jnp.float32), 0.5, 1.5),
        "ln2_bias": gaussian(key_of[7], (D,), 0.3, 4.0, (), jnp.float32),
        "w_up": gaussian(key_of[8], (D, FF), D ** -0.5, 0.25, ((1, 4),)),
        "b_up": gaussian(key_of[9], (FF,), 0.5, 6.0, ((0, 4),), jnp.float32),
        "w_down": gaussian(key_of[10], (FF, D), (FF // 4) ** -0.5, 0.25, ((0, 4),)),
        "b_down": gaussian(key_of[11], (D,), 0.3, 4.0, (), jnp.float32),
        "cotangent": gaussian(key_of[12], (TOKENS, D), 1.0, 6.0, ((0, 8),)),
    }


EPSILON = 1e-05
HIGHEST = lax.Precision.HIGHEST

@jax.custom_vjp
def low(v):
    return lax.optimization_barrier(v.astype(jnp.bfloat16)).astype(jnp.float32)

@jax.custom_vjp
def low_back(v):
    return v

def low_keep(v):
    return (low(v), None)

def low_pass(kept, grad):
    return (grad,)

def back_keep(v):
    return (v, None)

def back_low(kept, grad):
    return (low(grad),)
low.defvjp(low_keep, low_pass)
low_back.defvjp(back_keep, back_low)

def matmul(left, right):
    return jnp.dot(left, right, precision=HIGHEST)

def layer_norm(values, gain, offset):
    center = values - lax.optimization_barrier(jnp.mean(values, axis=-1, keepdims=True))
    spread = lax.optimization_barrier(jnp.mean(center * center, axis=-1, keepdims=True))
    return center * lax.rsqrt(spread + EPSILON) * gain + offset

def attend(inputs):
    query, keys, values = inputs
    blocks = LENGTH // SPAN
    scale = HEAD_DIM ** (-0.5)

    def heads_first(array):
        return array.reshape(blocks, SPAN, HEADS, HEAD_DIM).transpose(2, 0, 1, 3)
    query_heads, key_heads, value_heads = (heads_first(query), heads_first(keys), heads_first(values))
    key_summary = low(lax.optimization_barrier(jnp.mean(key_heads, axis=2)))
    value_summary = low(lax.optimization_barrier(jnp.mean(value_heads, axis=2)))
    local = jnp.einsum('hbqd,hbkd->hbqk', query_heads, key_heads, precision=HIGHEST) * scale
    causal = jnp.arange(SPAN)[:, None] >= jnp.arange(SPAN)[None, :]
    local = jnp.where(causal[None, None], local, -1e+30)
    summary = jnp.einsum('hbqd,hrd->hbqr', query_heads, key_summary, precision=HIGHEST) * scale + math.log(SPAN)
    earlier = jnp.arange(blocks)[None, :] < jnp.arange(blocks)[:, None]
    summary = jnp.where(earlier[None, :, None, :], summary, -1e+30)
    scores = low_back(jnp.concatenate([local, summary], axis=-1))
    highest = lax.optimization_barrier(jnp.max(scores, axis=-1, keepdims=True))
    weights = jnp.exp(scores - highest)
    probs = low(weights / lax.optimization_barrier(jnp.sum(weights, axis=-1, keepdims=True)))
    attended = jnp.einsum('hbqk,hbkd->hbqd', probs[..., :SPAN], value_heads, precision=HIGHEST)
    attended = attended + jnp.einsum('hbqr,hrd->hbqd', probs[..., SPAN:], value_summary, precision=HIGHEST)
    return attended.transpose(1, 2, 0, 3).reshape(LENGTH, D)

def forward(inputs, ln1_gain, ln1_bias, w_qkv, w_out, b_out, ln2_gain, ln2_bias, w_up, b_up, w_down, b_down):
    first = low(layer_norm(inputs, ln1_gain, ln1_bias))
    query = low(low_back(matmul(first, w_qkv[0])))
    keys = low(low_back(matmul(first, w_qkv[1])))
    values = low(low_back(matmul(first, w_qkv[2])))
    sequences = TOKENS // LENGTH
    shaped = (query.reshape(sequences, LENGTH, D), keys.reshape(sequences, LENGTH, D), values.reshape(sequences, LENGTH, D))
    attended = lax.map(jax.checkpoint(attend), shaped).reshape(TOKENS, D)
    attended = low(low_back(attended))
    mid = inputs + low_back(matmul(attended, w_out)) + b_out
    second = low(layer_norm(mid, ln2_gain, ln2_bias))
    upper = low_back(matmul(second, w_up) + b_up)
    active = low(jax.nn.gelu(upper))
    return mid + low_back(matmul(active, w_down)) + b_down

def reference(tokens, ln1_gain, ln1_bias, w_qkv, w_out, b_out, ln2_gain, ln2_bias, w_up, b_up, w_down, b_down, cotangent):
    params = (tokens.astype(jnp.float32), ln1_gain, ln1_bias, w_qkv.astype(jnp.float32), w_out.astype(jnp.float32), b_out, ln2_gain, ln2_bias, w_up.astype(jnp.float32), b_up, w_down.astype(jnp.float32), b_down)
    result, pullback = jax.vjp(forward, *params)
    grads = pullback(cotangent.astype(jnp.float32))
    return (result.astype(jnp.bfloat16), grads[0].astype(jnp.bfloat16), grads[1], grads[2], grads[3], grads[4], grads[5], grads[6], grads[7], grads[8], grads[9], grads[10], grads[11])
```

```python
import math

import jax
import jax.numpy as jnp
from jax import lax
from jax.sharding import PartitionSpec as P

HEAD_DIM = 64
SPAN = 128
LENGTH = 4096
EPSILON = 1e-05

f32 = jnp.float32
bf16 = jnp.bfloat16


def layer_norm(values, gain, offset):
    center = values - jnp.mean(values, axis=-1, keepdims=True)
    spread = jnp.mean(center * center, axis=-1, keepdims=True)
    return center * lax.rsqrt(spread + EPSILON) * gain + offset


def masks_of(count):
    return [1 << i for i in range(count.bit_length() - 1)]


def build(n_dp, n_mp):
    def swap(x, axis, mask):
        n = n_dp if axis == "dp" else n_mp
        return lax.ppermute(x, axis, [(i, i ^ mask) for i in range(n)])

    def gather_slots(x, axis, masks):
        slots = {0: x}
        for m in masks:
            slots.update({j ^ m: swap(s, axis, m) for j, s in list(slots.items())})
        return slots

    def pick(x, index, rows):
        return lax.dynamic_slice_in_dim(x, index * rows, rows, 0)

    def join(own, other, bit):
        return jnp.where(
            bit == 0, jnp.concatenate([own, other]), jnp.concatenate([other, own])
        )

    core_masks = masks_of(n_mp)[:1]
    far_masks = masks_of(n_mp)[1:]
    dp_masks = masks_of(n_dp)

    def reduce_half(x):
        c = lax.axis_index("mp") & 1
        half = x.shape[0] // 2
        got = swap(pick(x, 1 - c, half).astype(bf16), "mp", 1)
        x = pick(x, c, half) + got.astype(f32)
        for m in far_masks:
            low = x.astype(bf16)
            x = low.astype(f32) + swap(low, "mp", m).astype(f32)
        return x

    def both_halves(x):
        c = lax.axis_index("mp") & 1
        return join(x, swap(x, "mp", 1), c)

    def reduce_dp(x, masks):
        d = lax.axis_index("dp")
        for m in masks:
            bit = jnp.where((d & m) == 0, 0, 1)
            half = x.shape[0] // 2
            got = swap(pick(x, 1 - bit, half), "dp", m)
            x = (pick(x, bit, half).astype(f32) + got.astype(f32)).astype(bf16)
        for m in reversed(masks):
            bit = jnp.where((d & m) == 0, 0, 1)
            x = join(x, swap(x, "dp", m), bit)
        return x.astype(f32)

    def per_device(
        tokens,
        ln1_gain,
        ln1_bias,
        w_qkv,
        w_out,
        b_out,
        ln2_gain,
        ln2_bias,
        w_up,
        b_up,
        w_down,
        b_down,
        cotangent,
    ):
        inputs = tokens.astype(f32)
        rows = inputs.shape[0]
        width = w_qkv.shape[2]
        heads = width // HEAD_DIM
        blocks = rows // SPAN
        scale = HEAD_DIM ** (-0.5)
        group = LENGTH // rows
        seq_masks = masks_of(group)
        place = lax.axis_index("dp") % group
        core = lax.axis_index("mp") & 1

        def heads_first(array):
            return array.reshape(blocks, SPAN, heads, HEAD_DIM).transpose(2, 0, 1, 3)

        def heads_last(array):
            return array.transpose(1, 2, 0, 3).reshape(rows, width)

        out_slots = gather_slots(w_out, "mp", far_masks + core_masks)

        first_full, first_pull = jax.vjp(layer_norm, inputs, ln1_gain, ln1_bias)
        first = first_full.astype(bf16)
        projected = jnp.einsum("td,sde->ste", first, w_qkv, preferred_element_type=f32).astype(bf16)
        query_heads = heads_first(projected[0])
        key_heads = heads_first(projected[1])
        value_heads = heads_first(projected[2])
        own_summary = jnp.mean(
            jnp.stack([key_heads, value_heads]).astype(f32), axis=3
        ).astype(bf16)
        summary = own_summary[None]
        for m in seq_masks:
            summary = jnp.concatenate([summary, swap(summary, "dp", m)])
        all_keys = summary[:, 0].transpose(1, 0, 2, 3).reshape(heads, group * blocks, HEAD_DIM)
        all_values = summary[:, 1].transpose(1, 0, 2, 3).reshape(heads, group * blocks, HEAD_DIM)
        slot_place = place ^ jnp.arange(group)
        summary_block = (slot_place[:, None] * blocks + jnp.arange(blocks)[None, :]).reshape(-1)
        query_block = place * blocks + jnp.arange(blocks)
        allowed = summary_block[None, :] < query_block[:, None]
        causal = jnp.arange(SPAN)[:, None] >= jnp.arange(SPAN)[None, :]
        local = (
            jnp.einsum("hbqd,hbkd->hbqk", query_heads, key_heads, preferred_element_type=f32)
            * scale
        )
        local = jnp.where(causal[None, None], local, -1e30)
        remote = jnp.einsum(
            "hbqd,hgd->hbqg", query_heads, all_keys, preferred_element_type=f32
        ) * scale + math.log(SPAN)
        remote = jnp.where(allowed[None, :, None, :], remote, -1e30)
        scores = jnp.concatenate([local, remote], axis=-1)
        highest = jnp.max(scores, axis=-1, keepdims=True)
        weights = jnp.exp(scores - highest)
        probs = weights / jnp.sum(weights, axis=-1, keepdims=True)
        probs_low = probs.astype(bf16)
        attended = jnp.einsum(
            "hbqk,hbkd->hbqd", probs_low[..., :SPAN], value_heads, preferred_element_type=f32
        )
        attended = attended + jnp.einsum(
            "hbqg,hgd->hbqd", probs_low[..., SPAN:], all_values, preferred_element_type=f32
        )
        attended = heads_last(attended.astype(bf16))
        att_slots = gather_slots(attended, "mp", far_masks + core_masks)
        me = lax.axis_index("mp")
        terms = jnp.stack(
            [jnp.dot(att_slots[j], out_slots[j], preferred_element_type=f32) for j in range(n_mp)]
        )
        mid = inputs + b_out
        for i in range(n_mp):
            mid = mid + lax.dynamic_index_in_dim(terms, me ^ i, 0, keepdims=False)
        second_full, second_pull = jax.vjp(layer_norm, mid, ln2_gain, ln2_bias)
        second = second_full.astype(bf16)
        upper = jnp.dot(second, w_up, preferred_element_type=f32) + b_up
        active_full, gelu_pull = jax.vjp(jax.nn.gelu, upper)
        active = active_full.astype(bf16)
        grad_active = jnp.einsum("td,fd->tf", cotangent, w_down, preferred_element_type=f32)
        grad_upper = gelu_pull(grad_active)[0].astype(bf16)
        grad_second = both_halves(
            reduce_half(
                jnp.einsum("tf,df->td", grad_upper, w_up, preferred_element_type=f32)
            ).astype(bf16)
        ).astype(f32)

        feedforward = reduce_half(jnp.dot(active, w_down, preferred_element_type=f32))
        output = both_halves((pick(mid, core, rows // 2) + feedforward + b_down).astype(bf16))

        grad_out = cotangent.astype(f32)
        grad_w_down = jnp.einsum("tf,td->fd", active, cotangent, preferred_element_type=f32)
        grad_b_down = jnp.sum(grad_out, axis=0)
        grad_w_up = jnp.einsum("td,tf->df", second, grad_upper, preferred_element_type=f32)
        grad_b_up = jnp.sum(grad_upper.astype(f32), axis=0)

        grad_mid_norm, grad_ln2_gain, grad_ln2_bias = second_pull(grad_second)
        grad_mid = grad_out + grad_mid_norm
        grad_attention = grad_mid.astype(bf16)
        grad_w_out = jnp.einsum("tc,td->cd", attended, grad_attention, preferred_element_type=f32)
        grad_b_out = jnp.sum(grad_mid, axis=0)
        grad_attended = heads_first(
            jnp.einsum("td,cd->tc", grad_attention, w_out, preferred_element_type=f32).astype(bf16)
        )
        grad_probs = jnp.concatenate(
            [
                jnp.einsum(
                    "hbqd,hbkd->hbqk", grad_attended, value_heads, preferred_element_type=f32
                ),
                jnp.einsum("hbqd,hgd->hbqg", grad_attended, all_values, preferred_element_type=f32),
            ],
            axis=-1,
        )
        centered = jnp.sum(probs * grad_probs, axis=-1, keepdims=True)
        grad_scores = (probs * (grad_probs - centered)).astype(bf16)
        grad_local = grad_scores[..., :SPAN]
        grad_remote = grad_scores[..., SPAN:]
        grad_query = (
            jnp.einsum("hbqk,hbkd->hbqd", grad_local, key_heads, preferred_element_type=f32)
            + jnp.einsum("hbqg,hgd->hbqd", grad_remote, all_keys, preferred_element_type=f32)
        ) * scale
        grad_keys = (
            jnp.einsum("hbqk,hbqd->hbkd", grad_local, query_heads, preferred_element_type=f32)
            * scale
        )
        grad_values = jnp.einsum(
            "hbqk,hbqd->hbkd", probs_low[..., :SPAN], grad_attended, preferred_element_type=f32
        )
        grad_key_summary = (
            jnp.einsum("hbqg,hbqd->hgd", grad_remote, query_heads, preferred_element_type=f32)
            * scale
        )
        grad_value_summary = jnp.einsum(
            "hbqg,hbqd->hgd", probs_low[..., SPAN:], grad_attended, preferred_element_type=f32
        )
        partial = (
            jnp.stack([grad_key_summary, grad_value_summary])
            .reshape(2, heads, group, blocks, HEAD_DIM)
            .transpose(2, 0, 1, 3, 4)
        )
        for m in reversed(seq_masks):
            partial = partial[:m] + swap(partial[m:], "dp", m)
        own = partial[0] / SPAN
        grad_keys = grad_keys + own[0][:, :, None, :]
        grad_values = grad_values + own[1][:, :, None, :]
        grad_qkv = jnp.stack(
            [
                heads_last(grad_query.astype(bf16)),
                heads_last(grad_keys.astype(bf16)),
                heads_last(grad_values.astype(bf16)),
            ]
        )
        grad_w_qkv = jnp.einsum("td,ste->sde", first, grad_qkv, preferred_element_type=f32)
        grad_first_part = jnp.einsum("ste,sde->td", grad_qkv, w_qkv, preferred_element_type=f32)
        ln1_part = first_pull(grad_first_part)[1:]
        grad_first = reduce_half(grad_first_part)

        def pull_rows(x, g):
            return jax.vjp(layer_norm, x, ln1_gain, ln1_bias)[1](g)[0]

        grad_in_norm = pull_rows(pick(inputs, core, rows // 2), grad_first)
        grad_tokens = both_halves((pick(grad_mid, core, rows // 2) + grad_in_norm).astype(bf16))

        share = jnp.stack(ln1_part)
        for m in core_masks + far_masks:
            share = share + swap(share, "mp", m)
        vectors = jnp.concatenate(
            [
                jnp.stack([grad_b_out, grad_ln2_gain, grad_ln2_bias, grad_b_down]),
                jnp.pad(grad_b_up, (0, grad_b_down.shape[0] - grad_b_up.shape[0]))[None],
                share,
                jnp.zeros_like(grad_b_down)[None],
            ]
        )
        for m in dp_masks:
            vectors = vectors + swap(vectors, "dp", m)
        feed = reduce_dp(
            jnp.concatenate([grad_w_down.reshape(-1, 512), grad_w_up.reshape(-1, 512)]).astype(bf16), dp_masks
        )
        size = grad_w_down.size // 512
        grad_w_down = feed[:size].reshape(grad_w_down.shape)
        grad_w_up = feed[size:].reshape(grad_w_up.shape)
        rest = reduce_dp(
            jnp.concatenate([grad_w_qkv.reshape(-1, width), grad_w_out.reshape(-1, width)]).astype(bf16),
            dp_masks,
        )
        size = grad_w_qkv.size // width
        return (
            output,
            grad_tokens,
            vectors[5],
            vectors[6],
            rest[:size].reshape(grad_w_qkv.shape),
            rest[size:].reshape(grad_w_out.shape),
            vectors[0],
            vectors[1],
            vectors[2],
            grad_w_up,
            vectors[4, : grad_b_up.shape[0]],
            grad_w_down,
            vectors[3],
        )

    return per_device


def solution(mesh):
    return jax.shard_map(
        build(mesh.shape["dp"], mesh.shape["mp"]),
        mesh=mesh,
        in_specs=(
            P("dp", None),
            P(),
            P(),
            P(None, None, "mp"),
            P("mp", None),
            P(),
            P(),
            P(),
            P(None, "mp"),
            P("mp"),
            P("mp", None),
            P(),
            P("dp", None),
        ),
        out_specs=(
            P("dp", None),
            P("dp", None),
            P(),
            P(),
            P(None, None, "mp"),
            P("mp", None),
            P(),
            P(),
            P(),
            P(None, "mp"),
            P("mp"),
            P("mp", None),
            P(),
        ),
        check_vma=False,
    )
```

```python
import functools
import math

import jax
import jax.numpy as jnp
from jax import lax
from jax.experimental import pallas as pl
from jax.experimental.pallas import tpu as pltpu
from jax.sharding import PartitionSpec as P

HEAD_DIM = 64
SPAN = 128
LENGTH = 4096
EPSILON = 1e-05
SCALE = HEAD_DIM ** (-0.5)
LOW = -1e30

f32 = jnp.float32
bf16 = jnp.bfloat16
i32 = jnp.int32
VMEM = pl.BlockSpec(memory_space=pltpu.VMEM)
SMEM = pl.BlockSpec(memory_space=pltpu.SMEM)


def masks_of(count):
    return [1 << i for i in range(count.bit_length() - 1)]


def params(mib=60):
    return pltpu.CompilerParams(vmem_limit_bytes=mib * 1024 * 1024)


def cost():
    return pl.CostEstimate(flops=115_000_000_000, bytes_accessed=1, transcendentals=0)


def nt(a, b):
    return lax.dot_general(a, b, (((1,), (1,)), ((), ())), preferred_element_type=f32)


def tn(a, b):
    return lax.dot_general(a, b, (((0,), (0,)), ((), ())), preferred_element_type=f32)


def nn(a, b):
    return jnp.dot(a, b, preferred_element_type=f32)


def normed(x):
    c = x - jnp.mean(x, axis=-1, keepdims=True)
    r = lax.rsqrt(jnp.mean(c * c, axis=-1, keepdims=True) + EPSILON)
    return c * r, r


def norm_back(e, n, r, gain):
    k = e * gain
    return r * (
        k - jnp.mean(k, axis=-1, keepdims=True) - n * jnp.mean(k * n, axis=-1, keepdims=True)
    )


def fold(x):
    return jnp.sum(x.reshape(-1, 8, x.shape[-1]), axis=0)


def head_mask(shape, h, dtype):
    lane = lax.broadcasted_iota(i32, shape, len(shape) - 1)
    return jnp.where(lane // HEAD_DIM == h, 1.0, 0.0).astype(dtype)


def spread(x, factor):
    heads = x.shape[1] // HEAD_DIM
    return jnp.concatenate(
        [x * (head_mask((1, x.shape[1]), h, f32) * factor).astype(x.dtype) for h in range(heads)]
    )


def collect(x, factor):
    width = x.shape[1]
    heads = width // HEAD_DIM
    rows = x.shape[0] // heads
    total = x[:rows] * (head_mask((1, width), 0, f32) * factor)
    for h in range(1, heads):
        total = total + x[h * rows : (h + 1) * rows] * (head_mask((1, width), h, f32) * factor)
    return total


def to_low(v, cols):
    v = jnp.concatenate([v[:, i : i + cols] for i in range(0, v.shape[1], cols)])
    high = v.astype(bf16)
    return jnp.concatenate([high, (v - high.astype(f32)).astype(bf16)])


def from_low(x, dim):
    half = x.shape[0] // 2
    v = x[:half].astype(f32) + x[half:].astype(f32)
    count = dim // x.shape[1]
    return jnp.concatenate([v[i * 8 : (i + 1) * 8] for i in range(count)], axis=1)


def columns_of(sums_ref, start, count):
    slots, _, blocks, width = sums_ref.shape
    parts = [sums_ref[:, start + j].reshape(slots * blocks, width) for j in range(count)]
    return jnp.concatenate(parts, axis=1)


def project_kernel(tile, tok_ref, gain_ref, bias_ref, w_ref, first_ref, qkv_ref, sum_ref, wcat):
    width = w_ref.shape[2]
    for s in range(3):
        wcat[:, s * width : (s + 1) * width] = w_ref[s]
    per = tile // SPAN
    for i in range(tok_ref.shape[0] // tile):
        at = slice(i * tile, (i + 1) * tile)
        n, _ = normed(tok_ref[at].astype(f32))
        first = (n * gain_ref[...] + bias_ref[...]).astype(bf16)
        first_ref[at] = first
        both = nn(first, wcat[...]).astype(bf16)
        for s in range(3):
            part = both[:, s * width : (s + 1) * width]
            qkv_ref[s, at] = part
            if s:
                mean = jnp.mean(part.astype(f32).reshape(per, SPAN, width), axis=1)
                sum_ref[s - 1, i * per : (i + 1) * per] = mean.astype(bf16).astype(f32)
        sums = [jnp.sum(x.reshape(per, SPAN, -1), axis=1) for x in (first.astype(f32), n)]
        total = jnp.concatenate(sums, axis=1)
        for j in range(sum_ref.shape[0] - 2):
            sum_ref[2 + j, i * per : (i + 1) * per] = total[:, j * width : (j + 1) * width]


def local_kernel(qkv_ref, exp_ref, stat_ref):
    blocks = exp_ref.shape[0]
    lanes = exp_ref.shape[2]
    key = lax.broadcasted_iota(i32, (SPAN, lanes), 0)
    query = lax.broadcasted_iota(i32, (SPAN, lanes), 1) % SPAN
    keep = key <= query
    for b in range(blocks):
        at = slice(b * SPAN, (b + 1) * SPAN)
        s = nt(qkv_ref[1, at], spread(qkv_ref[0, at], SCALE))
        s = jnp.where(keep, s, LOW)
        top = jnp.max(s, axis=0, keepdims=True)
        e = jnp.exp(s - top)
        exp_ref[b] = e
        stat_ref[b, 0:1] = top
        stat_ref[b, 1:2] = jnp.sum(e, axis=0, keepdims=True)


def attend_kernel(place_ref, qkv_ref, exp_ref, stat_ref, sums_ref, prob_ref, att_ref):
    blocks = exp_ref.shape[0]
    lanes = exp_ref.shape[2]
    slots = sums_ref.shape[0]
    place = place_ref[0]
    keys = sums_ref[:, 0].reshape(slots * blocks, -1).astype(bf16)
    values = sums_ref[:, 1].reshape(slots * blocks, -1).astype(bf16)
    row = lax.broadcasted_iota(i32, (slots * blocks, lanes), 0)
    at_block = ((row // blocks) ^ place) * blocks + row % blocks
    for b in range(blocks):
        at = slice(b * SPAN, (b + 1) * SPAN)
        s = nt(keys, spread(qkv_ref[0, at], SCALE)) + math.log(SPAN)
        s = jnp.where(at_block < place * blocks + b, s, LOW)
        mine = stat_ref[b, 0:1]
        top = jnp.maximum(mine, jnp.max(s, axis=0, keepdims=True))
        e = jnp.exp(s - top)
        shrink = jnp.exp(mine - top)
        scale = 1.0 / (stat_ref[b, 1:2] * shrink + jnp.sum(e, axis=0, keepdims=True))
        p = jnp.concatenate([exp_ref[b] * (shrink * scale), e * scale])
        prob_ref[b] = p
        a = tn(p.astype(bf16), jnp.concatenate([qkv_ref[2, at], values]))
        att_ref[at] = collect(a, 1.0).astype(bf16)


def feed_kernel(
    count, pos_ref, tok_ref, *refs
):
    att = refs[:count]
    wo = refs[count : 2 * count]
    (
        b_out_ref,
        gain_ref,
        bias_ref,
        up_ref,
        b_up_ref,
        down_ref,
        cot_ref,
        mid_ref,
        second_ref,
        active_ref,
        grad_ref,
        theirs_ref,
        mine_ref,
        vec_ref,
        wcat,
    ) = refs[2 * count :]
    step = pl.program_id(0)
    me = pos_ref[0]
    width = wo[0].shape[0]

    def in_order(arrays):
        arrays = list(arrays)
        for m in masks_of(count):
            flip = (me & m) != 0
            arrays = [jnp.where(flip, arrays[j ^ m], arrays[j]) for j in range(count)]
        return arrays

    @pl.when(step == 0)
    def _():
        for j in range(count):
            wcat[pl.ds(pl.multiple_of((me ^ j) * width, width), width)] = wo[j][...]
        vec_ref[...] = jnp.zeros_like(vec_ref)

    attended = jnp.concatenate(in_order([a[...] for a in att]), axis=1)
    mid = tok_ref[...].astype(f32) + nn(attended, wcat[...]) + b_out_ref[...]
    mid_ref[...] = mid
    n, _ = normed(mid)
    second = (n * gain_ref[...] + bias_ref[...]).astype(bf16)
    second_ref[...] = second
    u = nn(second, up_ref[...]) + b_up_ref[...]
    root = math.sqrt(2.0 / math.pi)
    square = u * u
    t = jnp.tanh(u * (root + root * 0.044715 * square))
    half = 0.5 + 0.5 * t
    active_ref[...] = (u * half).astype(bf16)
    slope = half + (0.5 * u) * (1.0 - t * t) * (root + (3.0 * root * 0.044715) * square)
    grad = nt(cot_ref[...], down_ref[...]) * slope
    low = grad.astype(bf16)
    grad_ref[...] = low
    out = nt(low, up_ref[...]).astype(bf16)
    steps = pl.num_programs(0)

    @pl.when(step < steps // 2)
    def _():
        theirs_ref[...] = out

    @pl.when(step >= steps // 2)
    def _():
        mine_ref[...] = out

    vec_ref[0:8] += fold(low.astype(f32))


def weights_kernel(
    pos_ref,
    active_ref,
    second_ref,
    grad_ref,
    cot_ref,
    down_ref,
    out_theirs_ref,
    out_mine_ref,
    theirs_ref,
    mine_ref,
    down_acc,
    up_acc,
):
    step = pl.program_id(0)
    terms = nn(active_ref[...], down_ref[...]).astype(bf16)
    down = tn(active_ref[...], cot_ref[...])
    up = tn(second_ref[...], grad_ref[...])

    @pl.when(step == 0)
    def _():
        out_theirs_ref[...] = terms
        down_acc[...] = down
        up_acc[...] = up

    @pl.when(step == 1)
    def _():
        out_mine_ref[...] = terms
        first = (down_acc[...] + down).astype(bf16)
        then = (up_acc[...] + up).astype(bf16).reshape(first.shape)
        low = pos_ref[3] == 0
        theirs_ref[...] = jnp.where(low, then, first)
        mine_ref[...] = jnp.where(low, first, then)


def rest_kernel(
    bit_ref, first_ref, gqkv_ref, low_ref, att_ref, slot_ref, sums_ref, theirs_ref, mine_ref
):
    slots, _, blocks, width = slot_ref.shape
    dim = first_ref.shape[1]
    size = dim // 2
    rows = [slot_ref[:, s].reshape(slots * blocks, width) for s in range(2)]
    far_rows = (jnp.concatenate(rows, axis=1) * (1.0 / SPAN)).astype(bf16)
    far_first = columns_of(sums_ref, 2, dim // width).astype(bf16)
    out = []
    for h in range(2):
        at = slice(h * size, (h + 1) * size)
        main = tn(first_ref[:, at], gqkv_ref[...])
        far = tn(far_first[:, at], far_rows)
        last = tn(low_ref[:, at], att_ref[...])
        out.append(
            jnp.concatenate([main[:, :width], main[:, width:] + far, last], axis=1).astype(bf16)
        )
    low = bit_ref[0] == 0
    theirs_ref[...] = jnp.where(low, out[1], out[0])
    mine_ref[...] = jnp.where(low, out[0], out[1])


def split_kernel(bit_ref, a_ref, b_ref, theirs_ref, mine_ref):
    total = (a_ref[...].astype(f32) + b_ref[...].astype(f32)).astype(bf16)
    size = total.shape[0] // 2
    low = bit_ref[0] == 0
    theirs_ref[...] = jnp.where(low, total[size:], total[:size])
    mine_ref[...] = jnp.where(low, total[:size], total[size:])


def two_halves(refs, half, core):
    own, far, other, other_far = refs
    mine = half == core
    a = jnp.where(mine, own[...], other[...])
    b = jnp.where(mine, far[...], other_far[...])
    return a.astype(f32) + b.astype(f32)


def back_kernel(
    pos_ref,
    own_ref,
    far_ref,
    other_ref,
    other_far_ref,
    mid_ref,
    cot_ref,
    gain_ref,
    wo_ref,
    qkv_ref,
    prob_ref,
    sums_ref,
    low_ref,
    gqkv_ref,
    slot_ref,
    vec_ref,
):
    step = pl.program_id(0)
    slots = sums_ref.shape[0]
    width = wo_ref.shape[0]

    @pl.when(step == 0)
    def _():
        slot_ref[...] = jnp.zeros_like(slot_ref)
        vec_ref[...] = jnp.zeros_like(vec_ref)

    e = two_halves((own_ref, far_ref, other_ref, other_far_ref), step, pos_ref[1])
    n, r = normed(mid_ref[...])
    cot = cot_ref[...].astype(f32)
    grad_mid = cot + norm_back(e, n, r, gain_ref[...])
    low = grad_mid.astype(bf16)
    low_ref[...] = low
    vec_ref[0:8] += fold(grad_mid)
    vec_ref[8:16] += fold(e * n)
    vec_ref[16:24] += fold(e)
    vec_ref[24:32] += fold(cot)

    grad_att = nt(low, wo_ref[...]).astype(bf16)
    far_keys = sums_ref[:, 0].reshape(-1, width).astype(bf16)
    far_values = sums_ref[:, 1].reshape(-1, width).astype(bf16)
    far_gk = jnp.zeros(far_keys.shape, f32)
    far_gv = jnp.zeros(far_keys.shape, f32)
    for b in range(prob_ref.shape[0]):
        at = slice(b * SPAN, (b + 1) * SPAN)
        da = spread(grad_att[at], 1.0)
        query = spread(qkv_ref[0, at], SCALE)
        keys = jnp.concatenate([qkv_ref[1, at], far_keys])
        values = jnp.concatenate([qkv_ref[2, at], far_values])
        p = prob_ref[b]
        dp = nt(values, da)
        ds = (p * (dp - jnp.sum(p * dp, axis=0, keepdims=True))).astype(bf16)
        gq = collect(tn(ds, keys), SCALE)
        gk = nn(ds, query)
        gv = nn(p.astype(bf16), da)
        gqkv_ref[at, :width] = gq.astype(bf16)
        gqkv_ref[at, width : 2 * width] = gk[:SPAN].astype(bf16)
        gqkv_ref[at, 2 * width :] = gv[:SPAN].astype(bf16)
        far_gk = far_gk + gk[SPAN:]
        far_gv = far_gv + gv[SPAN:]
    slot_ref[:, 0] += far_gk.reshape(slots, -1, width)
    slot_ref[:, 1] += far_gv.reshape(slots, -1, width)


def first_kernel(
    pos_ref, gqkv_ref, slot_ref, sums_ref, w_ref, tok_ref, theirs_ref, mine_ref, wcat, vec
):
    step = pl.program_id(0)
    steps = pl.num_programs(0)
    dim, width = w_ref.shape[1:]
    tile = gqkv_ref.shape[0]
    half = tile * (steps // 2)

    @pl.when(step == 0)
    def _():
        vec[...] = jnp.zeros_like(vec)
        for s in range(3):
            wcat[:, s * width : (s + 1) * width] = w_ref[s]

    e = nt(gqkv_ref[...], wcat[...])
    n, _ = normed(tok_ref[...].astype(f32))
    vec[0:8] += fold(e * n)
    vec[8:16] += fold(e)
    out = e.astype(bf16)
    at = pl.ds(pl.multiple_of((step % (steps // 2)) * tile, tile), tile)

    @pl.when(step < steps // 2)
    def _():
        theirs_ref[at] = out

    @pl.when(step >= steps // 2)
    def _():
        mine_ref[at] = out

    @pl.when(step == steps - 1)
    def _():
        rows = [
            (slot_ref[:, s].reshape(-1, width) * (1.0 / SPAN)).astype(bf16) for s in range(2)
        ]
        far = nt(rows[0], w_ref[1]) + nt(rows[1], w_ref[2])
        normal = columns_of(sums_ref, 2 + dim // width, dim // width)
        gain = jnp.sum(vec[0:8], axis=0, keepdims=True) + jnp.sum(
            far * normal, axis=0, keepdims=True
        )
        offset = jnp.sum(vec[8:16], axis=0, keepdims=True) + SPAN * jnp.sum(
            far, axis=0, keepdims=True
        )
        low = to_low(jnp.concatenate([gain, offset, jnp.zeros((6, dim), f32)]), dim)
        theirs_ref[half:] = low
        mine_ref[half:] = low


def pair_kernel(a_ref, b_ref, out_ref):
    dim = a_ref.shape[1]
    rows = a_ref.shape[0] - 16
    out_ref[:rows] = (a_ref[:rows].astype(f32) + b_ref[:rows].astype(f32)).astype(bf16)
    out_ref[rows:] = to_low(from_low(a_ref[rows:], dim) + from_low(b_ref[rows:], dim), dim)


def extra_kernel(a_ref, b_ref, w_ref, out_ref):
    own = ((a_ref[0] + b_ref[0]) * (1.0 / SPAN)).astype(bf16)
    out_ref[...] = nt(own[0], w_ref[1]) + nt(own[1], w_ref[2])


def piece_kernel(mine_ref, got_ref, near_ref, far_ref, back_ref, up_ref, out_ref):
    dim = near_ref.shape[1]
    hidden = up_ref.shape[1]
    rows, cols = mine_ref.shape
    out_ref[:rows] = (mine_ref[...].astype(f32) + got_ref[...].astype(f32)).astype(bf16)
    last = near_ref.shape[0] - 16
    first = (from_low(near_ref[last:], dim) + from_low(far_ref[last:], dim))[:2]
    vectors = [first]
    for k in range(4):
        vectors.append(jnp.sum(back_ref[8 * k : 8 * k + 8], axis=0, keepdims=True))
    up = jnp.sum(up_ref[...], axis=0, keepdims=True)
    if hidden < dim:
        up = jnp.concatenate([up, jnp.zeros((1, dim - hidden), f32)], axis=1)
    vectors += [up, jnp.zeros((1, dim), f32)]
    out_ref[rows:] = to_low(jnp.concatenate(vectors), cols)


def merge_kernel(dim, a_ref, b_ref, out_ref):
    cols = a_ref.shape[1]
    rows = a_ref.shape[0] - 16 * (dim // cols)
    out_ref[:rows] = a_ref[:rows]
    out_ref[rows : 2 * rows] = b_ref[:rows]
    out_ref[2 * rows :] = to_low(from_low(a_ref[rows:], dim) + from_low(b_ref[rows:], dim), cols)


def last_kernel(
    pos_ref,
    own_ref,
    far_ref,
    other_ref,
    other_far_ref,
    extra_ref,
    tok_ref,
    low_ref,
    gain_ref,
    out_ref,
):
    step = pl.program_id(0)
    half = step // (pl.num_programs(0) // 2)
    e = two_halves((own_ref, far_ref, other_ref, other_far_ref), half, pos_ref[1])
    per = e.shape[0] // SPAN
    pieces = []
    for i in range(per):
        pieces.append(e[i * SPAN : (i + 1) * SPAN] + extra_ref[pl.ds(step * per + i, 1)])
    e = jnp.concatenate(pieces)
    n, r = normed(tok_ref[...].astype(f32))
    out_ref[...] = (low_ref[...].astype(f32) + norm_back(e, n, r, gain_ref[...])).astype(bf16)


def add_kernel(parts, a_ref, b_ref, *out_refs):
    size = a_ref.shape[0] // parts
    for k in range(parts):
        at = slice(k * size, (k + 1) * size)
        out_refs[k][...] = (a_ref[at].astype(f32) + b_ref[at].astype(f32)).astype(bf16)


def slot_kernel(a_ref, b_ref, out_ref):
    out_ref[...] = a_ref[: out_ref.shape[0]] + b_ref[...]


def spacer_kernel(x_ref, out_ref):
    out_ref[...] = x_ref[...] * 0.5


def concat_kernel(a_ref, b_ref, out_ref):
    rows = a_ref.shape[0]
    out_ref[:rows] = a_ref[...]
    out_ref[rows:] = b_ref[...]


def output_kernel(
    pos_ref, own_ref, far_ref, other_ref, other_far_ref, mid_ref, b_ref, out_ref
):
    half = pl.program_id(0) // (pl.num_programs(0) // 2)
    e = two_halves((own_ref, far_ref, other_ref, other_far_ref), half, pos_ref[1])
    out_ref[...] = (mid_ref[...] + e + b_ref[...]).astype(bf16)


def feed_unpack_kernel(count, at_ref, near_ref, far_ref, down_ref, up_ref):
    rows = 2 * near_ref.shape[0] // count
    part = count // 2
    top = at_ref[0] // part
    low = at_ref[0] % part
    for step, out_ref in enumerate((down_ref, up_ref)):

        @pl.when(pl.program_id(0) == step)
        def _():
            for k in range(part):
                at = pl.ds(pl.multiple_of((k ^ low) * rows, rows), rows)
                x = jnp.where(top == step, near_ref[at], far_ref[at])
                out_ref[k * rows : (k + 1) * rows] = x.astype(f32)


def rest_unpack_kernel(
    count, dim, at_ref, near_ref, far_ref, spare_ref, qkv_ref, out_ref, vec_ref, scratch
):
    cols = near_ref.shape[1]
    last = near_ref.shape[0] - 16 * (dim // cols)
    rows = 2 * last // count
    width = qkv_ref.shape[2]
    part = count // 2
    top = at_ref[0] // part
    low = at_ref[0] % part
    for k in range(count):
        start = pl.multiple_of(((k % part) ^ low) * rows, rows)
        is_near = top == k // part
        x = jnp.where(is_near, near_ref[pl.ds(start, rows)], far_ref[pl.ds(start, rows)])
        x = x.astype(f32)
        for s in range(3):
            qkv_ref[s, k * rows : (k + 1) * rows] = x[:, s * width : (s + 1) * width]
        scratch[k * rows : (k + 1) * rows] = x[:, 3 * width :]
    out_ref[...] = scratch[...].T
    vec_ref[...] = from_low(near_ref[last:], dim) + from_low(far_ref[last:], dim)


def build(n_dp, n_mp):
    def swap(x, axis, mask, label):
        n = n_dp if axis == "dp" else n_mp
        with jax.named_scope(label):
            return lax.ppermute(x, axis, [(i, i ^ mask) for i in range(n)])

    def pick(x, index, rows):
        return lax.dynamic_slice_in_dim(x, index * rows, rows, 0)

    def halves(x, mask, axis):
        bit = jnp.where((lax.axis_index(axis) & mask) == 0, 0, 1)
        size = x.shape[0] // 2
        return pick(x, 1 - bit, size), pick(x, bit, size)

    def after(x, *others):
        return lax.optimization_barrier((x, others))[0]

    far_masks = masks_of(n_mp)[1:]
    dp_masks = masks_of(n_dp)
    feed_masks = [dp_masks[1], dp_masks[0]] + dp_masks[2:]

    class Line:
        def __init__(self):
            self.last = ()

        def __call__(self, work, *inputs):
            if self.last:
                inputs = after(inputs, *self.last)
            result = work(*inputs)
            first = result[-1] if isinstance(result, (tuple, list)) else result
            self.last = (first,)
            return result

        def space(self, x=None):
            if x is not None:
                self.spare = x
            self.spare = self(spacer, self.spare)

    def add_parts(parts, a, b):
        part = jax.ShapeDtypeStruct((a.shape[0] // parts, *a.shape[1:]), bf16)
        return pl.pallas_call(
            functools.partial(add_kernel, parts),
            out_shape=(part,) * parts,
            in_specs=[VMEM, VMEM],
            out_specs=(VMEM,) * parts,
            compiler_params=params(16),
            cost_estimate=cost(),
            name="add",
        )(a, b)

    def add_low(a, b):
        return add_parts(1, a, b)[0]

    def spacer(x):
        return pl.pallas_call(
            spacer_kernel,
            out_shape=jax.ShapeDtypeStruct(x.shape, x.dtype),
            in_specs=[VMEM],
            out_specs=VMEM,
            compiler_params=params(16),
            cost_estimate=cost(),
            name="spacer",
        )(x)

    def split_sum(bit, mine, got):
        size = mine.shape[0] // 2
        half = jax.ShapeDtypeStruct((size, mine.shape[1]), bf16)
        return pl.pallas_call(
            split_kernel,
            out_shape=(half, half),
            in_specs=[SMEM, VMEM, VMEM],
            out_specs=(VMEM, VMEM),
            compiler_params=params(16),
            cost_estimate=cost(),
            name="split",
        )(bit, mine, got)

    def bit_of(mask):
        return jnp.where((lax.axis_index("dp") & mask) == 0, 0, 1).astype(i32)[None]

    class Scatter:
        def __init__(self, line, theirs, mine, masks, label):
            self.line, self.label = line, label
            self.rest = list(masks)
            self.mine = mine
            self.got = swap(theirs, "dp", self.rest.pop(0), label)

        def step(self):
            mask = self.rest.pop(0)
            theirs, self.mine = self.line(split_sum, bit_of(mask), self.mine, self.got)
            self.got = swap(theirs, "dp", mask, self.label)

    def per_device(
        tokens,
        ln1_gain,
        ln1_bias,
        w_qkv,
        w_out,
        b_out,
        ln2_gain,
        ln2_bias,
        w_up,
        b_up,
        w_down,
        b_down,
        cotangent,
    ):
        rows, dim = tokens.shape
        width = w_qkv.shape[2]
        hidden = w_up.shape[1]
        heads = width // HEAD_DIM
        blocks = rows // SPAN
        lanes = heads * SPAN
        group = LENGTH // rows
        entries = SPAN + group * blocks
        seq_masks = masks_of(group)
        me = lax.axis_index("mp")
        place = lax.axis_index("dp") % group
        first_bit = bit_of(dp_masks[0])
        pos = jnp.concatenate(
            [jnp.stack([me, me & 1, place]).astype(i32), bit_of(feed_masks[0])]
        )
        half = rows // 2
        tile = half // 2
        tiles = 4
        sds = jax.ShapeDtypeStruct

        def rolled(i, pos):
            return ((i + (1 - pos[1]) * (tiles // 2)) % tiles, 0)

        def theirs_row(i, pos):
            return (jnp.minimum(i, tiles // 2 - 1), 0)

        def mine_row(i, pos):
            return (jnp.maximum(i - tiles // 2, 0), 0)

        def half_rolled(i, pos):
            return (jnp.where(i == 0, 1 - pos[1], pos[1]), 0)

        def whole(*_):
            return (0, 0)

        def by_row(i, *_):
            return (i, 0)

        def zeros(n):
            return lambda *_: (0,) * n

        def block(shape, index):
            return pl.BlockSpec(shape, index)

        def plain(kernel, name, in_specs, out_shape, scratch=()):
            return pl.pallas_call(
                kernel,
                out_shape=out_shape,
                in_specs=in_specs,
                out_specs=tuple(VMEM for _ in out_shape),
                scratch_shapes=list(scratch),
                compiler_params=params(24),
                cost_estimate=cost(),
                name=name,
            )

        def gridded(
            kernel, name, grid, in_specs, out_specs, out_shape, scratch=(), mib=60, aliases=None
        ):
            return pl.pallas_call(
                kernel,
                grid_spec=pltpu.PrefetchScalarGridSpec(
                    num_scalar_prefetch=1,
                    grid=(grid,),
                    in_specs=in_specs,
                    out_specs=out_specs,
                    scratch_shapes=list(scratch),
                ),
                out_shape=out_shape,
                input_output_aliases=aliases or {},
                compiler_params=params(mib),
                cost_estimate=cost(),
                name=name,
            )

        row_block = block((tile, dim), rolled)
        row_vector = block((1, dim), whole)
        tile_block = block((tile, dim), by_row)
        one_tile = block((tile, dim), whole)

        project = plain(
            functools.partial(project_kernel, tile),
            "project",
            [VMEM] * 4,
            (
                sds((rows, dim), bf16),
                sds((3, rows, width), bf16),
                sds((2 + 2 * (dim // width), blocks, width), f32),
            ),
            [pltpu.VMEM((dim, 3 * width), bf16)],
        )
        local = plain(
            local_kernel,
            "local",
            [VMEM],
            (sds((blocks, SPAN, lanes), f32), sds((blocks, 2, lanes), f32)),
        )
        attend = plain(
            attend_kernel,
            "attend",
            [SMEM] + [VMEM] * 4,
            (sds((blocks, entries, lanes), f32), sds((rows, width), bf16)),
        )
        feed = gridded(
            functools.partial(feed_kernel, n_mp),
            "feed",
            tiles,
            [row_block]
            + [block((tile, width), rolled)] * n_mp
            + [block((width, dim), whole)] * n_mp
            + [row_vector] * 3
            + [
                block((dim, hidden), whole),
                block((1, hidden), whole),
                block((hidden, dim), whole),
                row_block,
            ],
            [
                row_block,
                row_block,
                block((tile, hidden), rolled),
                block((tile, hidden), rolled),
                block((tile, dim), theirs_row),
                block((tile, dim), mine_row),
                block((8, hidden), whole),
            ],
            (
                sds((rows, dim), f32),
                sds((rows, dim), bf16),
                sds((rows, hidden), bf16),
                sds((rows, hidden), bf16),
                sds((half, dim), bf16),
                sds((half, dim), bf16),
                sds((8, hidden), f32),
            ),
            [pltpu.VMEM((dim, dim), bf16)],
        )
        half_rows = block((half, dim), half_rolled)
        half_hidden = block((half, hidden), half_rolled)
        weights = gridded(
            weights_kernel,
            "weights",
            2,
            [half_hidden, half_rows, half_hidden, half_rows, block((hidden, dim), whole)],
            [block((half, dim), whole)] * 2 + [block((hidden, dim), whole)] * 2,
            (
                sds((half, dim), bf16),
                sds((half, dim), bf16),
                sds((hidden, dim), bf16),
                sds((hidden, dim), bf16),
            ),
            [pltpu.VMEM((hidden, dim), f32), pltpu.VMEM((dim, hidden), f32)],
        )
        rest_weights = plain(
            rest_kernel,
            "rest_weights",
            [SMEM] + [VMEM] * 6,
            (sds((dim // 2, 4 * width), bf16), sds((dim // 2, 4 * width), bf16)),
        )
        slot_shape = (group, 2, blocks, width)
        sums_shape = (group, 2 + 2 * (dim // width), blocks, width)
        back = gridded(
            back_kernel,
            "back",
            2,
            [block((half, dim), whole)] * 4
            + [
                block((half, dim), by_row),
                block((half, dim), by_row),
                row_vector,
                block((width, dim), whole),
                block((3, half, width), lambda i, pos: (0, i, 0)),
                block((blocks // 2, entries, lanes), lambda i, pos: (i, 0, 0)),
                block(sums_shape, zeros(4)),
            ],
            [
                block((half, dim), by_row),
                block((half, 3 * width), by_row),
                block(slot_shape, zeros(4)),
                block((32, dim), whole),
            ],
            (
                sds((rows, dim), bf16),
                sds((rows, 3 * width), bf16),
                sds(slot_shape, f32),
                sds((32, dim), f32),
            ),
        )
        first_block = block((half + 16, dim), whole)
        first_grad = gridded(
            first_kernel,
            "first",
            tiles,
            [
                block((tile, 3 * width), rolled),
                block(slot_shape, zeros(4)),
                block(sums_shape, zeros(4)),
                block((3, dim, width), zeros(3)),
                row_block,
            ],
            [first_block, first_block],
            (sds((half + 16, dim), bf16), sds((half + 16, dim), bf16)),
            [pltpu.VMEM((dim, 3 * width), bf16), pltpu.VMEM((16, dim), f32)],
        )
        def own_tile(i, pos):
            return (jnp.clip(i - pos[1] * (tiles // 2), 0, tiles // 2 - 1), 0)

        def other_tile(i, pos):
            return (jnp.clip(i - (1 - pos[1]) * (tiles // 2), 0, tiles // 2 - 1), 0)

        terms_specs = [block((tile, dim), own_tile)] * 2 + [block((tile, dim), other_tile)] * 2
        last = gridded(
            last_kernel,
            "last",
            tiles,
            terms_specs + [block((blocks, dim), whole), tile_block, tile_block, row_vector],
            tile_block,
            sds((rows, dim), bf16),
        )
        output_sum = gridded(
            output_kernel,
            "output",
            tiles,
            terms_specs + [tile_block, row_vector],
            tile_block,
            sds((rows, dim), bf16),
        )
        feed_unpack = gridded(
            functools.partial(feed_unpack_kernel, n_dp),
            "feed_unpack",
            2,
            [block((hidden, dim), whole)] * 2,
            [block((hidden, dim), whole)] * 2,
            (sds((hidden, dim), f32), sds((hidden, dim), f32)),
        )
        rest_unpack = plain(
            functools.partial(rest_unpack_kernel, n_dp, dim),
            "rest_unpack",
            [SMEM, VMEM, VMEM, VMEM],
            (sds((3, dim, width), f32), sds((width, dim), f32), sds((8, dim), f32)),
            [pltpu.VMEM((dim, width), f32)],
        )

        def like(kernel, name, shape, dtype, *operands):
            specs = [VMEM] * len(operands)
            return plain(kernel, name, specs, (sds(shape, dtype),))(*operands)[0]

        def pair(a, b):
            return like(pair_kernel, "pair", a.shape, bf16, a, b)

        def slot_add(a, b):
            return like(slot_kernel, "slots", b.shape, f32, a, b)

        def extra_of(a, b, w):
            return like(extra_kernel, "extra", (blocks, dim), f32, a, b, w)

        def concat(a, b):
            return like(concat_kernel, "concat", (2 * a.shape[0], a.shape[1]), bf16, a, b)

        def pl_add(a, b):
            return like(slot_kernel, "plus", a.shape, f32, a, b)

        vec_rows = 16 * (dim // (4 * width))

        def piece_of(mine, *operands):
            shape = (mine.shape[0] + vec_rows, 4 * width)
            return like(piece_kernel, "piece", shape, bf16, mine, *operands)

        def merge(a, b):
            shape = (2 * a.shape[0] - vec_rows, 4 * width)
            return like(functools.partial(merge_kernel, dim), "merge", shape, bf16, a, b)

        def place_of(masks):
            at = jnp.zeros((1,), i32)
            for m in masks:
                at = at * 2 + bit_of(m)
            return at


        def wait(*arrived):
            return line(lambda *x: x, *arrived)

        def near_sum(total, label):
            for m in far_masks[:-1]:
                total = line(add_low, total, swap(total, "mp", m, label))
            return total

        last_far = far_masks[-1]

        line = Line()

        out_slots = {0: w_out}
        for m in far_masks:
            out_slots.update(
                {j ^ m: swap(x, "mp", m, "gather_w_out") for j, x in list(out_slots.items())}
            )
        line.spare = ln1_gain[None]
        first, qkv, summary = line(project, tokens, ln1_gain[None], ln1_bias[None], w_qkv)
        out_list = list(out_slots.items())
        sums = after(summary, *[x for _, x in out_list])[None]
        for i, m in enumerate(seq_masks):
            got = swap(sums, "dp", m, "summaries")
            if i == 0:
                exps, stats = line(local, qkv)
                for j, x in out_list:
                    out_slots[j ^ 1] = swap(after(x, stats), "mp", 1, "gather_w_out")
            sums = line(lambda a, b: jnp.concatenate([a, b]), sums, got)
        probs, attended = line(attend, place[None].astype(i32), qkv, exps, stats, sums)

        att_slots = {0: attended}
        for m in far_masks:
            att_slots.update(
                {j ^ m: swap(x, "mp", m, "gather_attended") for j, x in list(att_slots.items())}
            )
        for j, x in list(att_slots.items()):
            att_slots[j ^ 1] = swap(x, "mp", 1, "gather_attended")
        mid, second, active, grad_upper, theirs, mine, up_vec = line(
            feed,
            pos,
            tokens,
            *[att_slots[j] for j in range(n_mp)],
            *[out_slots[j] for j in range(n_mp)],
            b_out[None],
            ln2_gain[None],
            ln2_bias[None],
            w_up,
            b_up[None],
            w_down,
            cotangent,
        )

        total = near_sum(line(add_low, mine, swap(theirs, "mp", 1, "sum_second")), "sum_second")
        far = swap(total, "mp", last_far, "sum_second")
        other = swap(total, "mp", 1, "sum_second")
        out_theirs, out_mine, theirs, mine = line(
            weights, pos, active, second, grad_upper, cotangent, w_down
        )
        feed_sum = Scatter(line, theirs, mine, feed_masks, "feed_weights")
        out_got = swap(out_theirs, "mp", 1, "sum_output")
        (far,) = wait(far)
        other_far = swap(far, "mp", 1, "sum_second")
        out_total = near_sum(line(add_low, out_mine, out_got), "sum_output")
        out_far = swap(out_total, "mp", last_far, "sum_output")
        out_other = swap(out_total, "mp", 1, "sum_output")
        grad_low, gqkv, back_vec, slot_grad = line(
            lambda *a: (lambda r: (r[0], r[1], r[3], r[2]))(back(*a)),
            pos,
            total,
            far,
            other,
            other_far,
            mid,
            cotangent,
            ln2_gain[None],
            w_out,
            qkv,
            probs,
            sums,
        )

        following = list(reversed(seq_masks))
        slot_part = slot_grad
        slot_got = swap(slot_part[following[0] :], "dp", following[0], "sum_slots")
        (out_other,) = wait(out_other)
        theirs, mine = line(
            rest_weights, first_bit, first, gqkv, grad_low, attended, slot_grad, sums
        )
        rest_sum = Scatter(line, theirs, mine, dp_masks, "rest_weights")
        feed_sum.step()
        for low in following[1:]:
            slot_part = line(slot_add, slot_part, slot_got)
            slot_got = swap(slot_part[low:], "dp", low, "sum_slots")
        (out_far,) = wait(out_far)
        out_other_far = swap(out_far, "mp", 1, "sum_output")
        theirs, mine = line(first_grad, pos, gqkv, slot_grad, sums, w_qkv, tokens)
        got = swap(theirs, "mp", 1, "sum_first")
        (out_other_far,) = wait(out_other_far)
        extra = line(extra_of, slot_part, slot_got, w_qkv)
        extra_got = swap(extra, "mp", 1, "sum_extra")
        total = line(pair, mine, got)
        for m in far_masks[:-1]:
            total = line(pair, total, swap(total, "mp", m, "sum_first"))
        far = swap(total, "mp", last_far, "sum_first")
        rest_sum.step()
        for m in far_masks:
            extra = line(pl_add, extra, extra_got)
            extra_got = swap(extra, "mp", m, "sum_extra")
        feed_sum.step()
        output = line(
            output_sum, pos, out_total, out_far, out_other, out_other_far, mid, b_down[None]
        )
        for m in dp_masks[2:]:
            rest_sum.step()
        line.space()
        for m in feed_masks[3:]:
            feed_sum.step()
        feed_all = line(add_low, feed_sum.mine, feed_sum.got)
        feed_got = swap(feed_all, "dp", feed_masks[-1], "feed_weights")
        (far,) = wait(far)
        other = swap(after(total, far), "mp", 1, "sum_first")
        other_far = swap(far, "mp", 1, "sum_first")
        rest_all = line(
            piece_of, rest_sum.mine, rest_sum.got, total, far, back_vec, up_vec
        )
        rest_got = swap(rest_all, "dp", dp_masks[-1], "rest_weights")
        extra = line(pl_add, extra, extra_got)
        grad_tokens = line(
            last, pos, total, far, other, other_far, extra, tokens, grad_low, ln1_gain[None]
        )
        feed_next = list(reversed(feed_masks))[1:]
        rest_next = list(reversed(dp_masks))[1:]
        for feed_mask, rest_mask in zip(feed_next, rest_next):
            feed_all = line(concat, feed_all, feed_got)
            feed_got = swap(feed_all, "dp", feed_mask, "feed_weights")
            rest_all = line(merge, rest_all, rest_got)
            rest_got = swap(rest_all, "dp", rest_mask, "rest_weights")
            line.space()
        grad_w_qkv, grad_w_out, vectors = line(
            rest_unpack, place_of(dp_masks), rest_all, rest_got, line.spare
        )
        grad_w_down, grad_w_up = line(feed_unpack, place_of(feed_masks), feed_all, feed_got)
        return (
            output,
            grad_tokens,
            vectors[0],
            vectors[1],
            grad_w_qkv,
            grad_w_out,
            vectors[2],
            vectors[3],
            vectors[4],
            grad_w_up.reshape(dim, hidden),
            vectors[6, :hidden],
            grad_w_down,
            vectors[5],
        )

    return per_device


def solution(mesh):
    return jax.shard_map(
        build(mesh.shape["dp"], mesh.shape["mp"]),
        mesh=mesh,
        in_specs=(
            P("dp", None),
            P(),
            P(),
            P(None, None, "mp"),
            P("mp", None),
            P(),
            P(),
            P(),
            P(None, "mp"),
            P("mp"),
            P("mp", None),
            P(),
            P("dp", None),
        ),
        out_specs=(
            P("dp", None),
            P("dp", None),
            P(),
            P(),
            P(None, None, "mp"),
            P("mp", None),
            P(),
            P(),
            P(),
            P(None, "mp"),
            P("mp"),
            P("mp", None),
            P(),
        ),
        check_vma=False,
    )
```

```python
import functools
import math

import jax
import jax.numpy as jnp
from jax import lax
from jax.experimental import pallas as pl
from jax.experimental.pallas import tpu as pltpu
from jax.sharding import PartitionSpec as P

HEAD_DIM = 64
SPAN = 128
LENGTH = 4096
EPSILON = 1e-05
SCALE = HEAD_DIM ** (-0.5)
LOW = -1e30

f32 = jnp.float32
bf16 = jnp.bfloat16
i32 = jnp.int32
VMEM = pl.BlockSpec(memory_space=pltpu.VMEM)
SMEM = pl.BlockSpec(memory_space=pltpu.SMEM)


def masks_of(count):
    return [1 << i for i in range(count.bit_length() - 1)]


def params(mib=60):
    return pltpu.CompilerParams(vmem_limit_bytes=mib * 1024 * 1024)


def cost():
    return pl.CostEstimate(flops=115_000_000_000, bytes_accessed=1, transcendentals=0)


def nt(a, b):
    return lax.dot_general(a, b, (((1,), (1,)), ((), ())), preferred_element_type=f32)


def tn(a, b):
    return lax.dot_general(a, b, (((0,), (0,)), ((), ())), preferred_element_type=f32)


def nn(a, b):
    return jnp.dot(a, b, preferred_element_type=f32)


def normed(x):
    c = x - jnp.mean(x, axis=-1, keepdims=True)
    r = lax.rsqrt(jnp.mean(c * c, axis=-1, keepdims=True) + EPSILON)
    return c * r, r


def norm_back(e, n, r, gain):
    k = e * gain
    return r * (
        k - jnp.mean(k, axis=-1, keepdims=True) - n * jnp.mean(k * n, axis=-1, keepdims=True)
    )


def fold(x):
    return jnp.sum(x.reshape(-1, 8, x.shape[-1]), axis=0)


def head_mask(shape, h, dtype):
    lane = lax.broadcasted_iota(i32, shape, len(shape) - 1)
    return jnp.where(lane // HEAD_DIM == h, 1.0, 0.0).astype(dtype)


def spread(x, factor):
    heads = x.shape[1] // HEAD_DIM
    return jnp.concatenate(
        [x * (head_mask((1, x.shape[1]), h, f32) * factor).astype(x.dtype) for h in range(heads)]
    )


def collect(x, factor):
    width = x.shape[1]
    heads = width // HEAD_DIM
    rows = x.shape[0] // heads
    total = x[:rows] * (head_mask((1, width), 0, f32) * factor)
    for h in range(1, heads):
        total = total + x[h * rows : (h + 1) * rows] * (head_mask((1, width), h, f32) * factor)
    return total


def to_low(v, cols):
    v = jnp.concatenate([v[:, i : i + cols] for i in range(0, v.shape[1], cols)])
    high = v.astype(bf16)
    return jnp.concatenate([high, (v - high.astype(f32)).astype(bf16)])


def from_low(x, dim):
    half = x.shape[0] // 2
    v = x[:half].astype(f32) + x[half:].astype(f32)
    count = dim // x.shape[1]
    return jnp.concatenate([v[i * 8 : (i + 1) * 8] for i in range(count)], axis=1)


def columns_of(sums_ref, start, count):
    slots, _, blocks, width = sums_ref.shape
    parts = [sums_ref[:, start + j].reshape(slots * blocks, width) for j in range(count)]
    return jnp.concatenate(parts, axis=1)


def project_kernel(tile, tok_ref, gain_ref, bias_ref, w_ref, first_ref, qkv_ref, sum_ref, wcat):
    width = w_ref.shape[2]
    for s in range(3):
        wcat[:, s * width : (s + 1) * width] = w_ref[s]
    per = tile // SPAN
    for i in range(tok_ref.shape[0] // tile):
        at = slice(i * tile, (i + 1) * tile)
        n, _ = normed(tok_ref[at].astype(f32))
        first = (n * gain_ref[...] + bias_ref[...]).astype(bf16)
        first_ref[at] = first
        both = nn(first, wcat[...]).astype(bf16)
        for s in range(3):
            part = both[:, s * width : (s + 1) * width]
            qkv_ref[s, at] = part
            if s:
                mean = jnp.mean(part.astype(f32).reshape(per, SPAN, width), axis=1)
                sum_ref[s - 1, i * per : (i + 1) * per] = mean.astype(bf16).astype(f32)
        sums = [jnp.sum(x.reshape(per, SPAN, -1), axis=1) for x in (first.astype(f32), n)]
        total = jnp.concatenate(sums, axis=1)
        for j in range(sum_ref.shape[0] - 2):
            sum_ref[2 + j, i * per : (i + 1) * per] = total[:, j * width : (j + 1) * width]


def local_kernel(qkv_ref, exp_ref, stat_ref):
    blocks = exp_ref.shape[0]
    lanes = exp_ref.shape[2]
    key = lax.broadcasted_iota(i32, (SPAN, lanes), 0)
    query = lax.broadcasted_iota(i32, (SPAN, lanes), 1) % SPAN
    keep = key <= query
    for b in range(blocks):
        at = slice(b * SPAN, (b + 1) * SPAN)
        s = nt(qkv_ref[1, at], spread(qkv_ref[0, at], SCALE))
        s = jnp.where(keep, s, LOW)
        top = jnp.max(s, axis=0, keepdims=True)
        e = jnp.exp(s - top)
        exp_ref[b] = e
        stat_ref[b, 0:1] = top
        stat_ref[b, 1:2] = jnp.sum(e, axis=0, keepdims=True)


def attend_kernel(place_ref, qkv_ref, exp_ref, stat_ref, sums_ref, prob_ref, att_ref):
    blocks = exp_ref.shape[0]
    lanes = exp_ref.shape[2]
    slots = sums_ref.shape[0]
    place = place_ref[0]
    keys = sums_ref[:, 0].reshape(slots * blocks, -1).astype(bf16)
    values = sums_ref[:, 1].reshape(slots * blocks, -1).astype(bf16)
    row = lax.broadcasted_iota(i32, (slots * blocks, lanes), 0)
    at_block = ((row // blocks) ^ place) * blocks + row % blocks
    for b in range(blocks):
        at = slice(b * SPAN, (b + 1) * SPAN)
        s = nt(keys, spread(qkv_ref[0, at], SCALE)) + math.log(SPAN)
        s = jnp.where(at_block < place * blocks + b, s, LOW)
        mine = stat_ref[b, 0:1]
        top = jnp.maximum(mine, jnp.max(s, axis=0, keepdims=True))
        e = jnp.exp(s - top)
        shrink = jnp.exp(mine - top)
        scale = 1.0 / (stat_ref[b, 1:2] * shrink + jnp.sum(e, axis=0, keepdims=True))
        p = jnp.concatenate([exp_ref[b] * (shrink * scale), e * scale])
        prob_ref[b] = p
        a = tn(p.astype(bf16), jnp.concatenate([qkv_ref[2, at], values]))
        att_ref[at] = collect(a, 1.0).astype(bf16)


def feed_kernel(
    count, pos_ref, tok_ref, *refs
):
    att = refs[:count]
    wo = refs[count : 2 * count]
    (
        b_out_ref,
        gain_ref,
        bias_ref,
        up_ref,
        b_up_ref,
        down_ref,
        cot_ref,
        mid_ref,
        second_ref,
        active_ref,
        grad_ref,
        theirs_ref,
        mine_ref,
        vec_ref,
        wcat,
    ) = refs[2 * count :]
    step = pl.program_id(0)
    me = pos_ref[0]
    width = wo[0].shape[0]

    def in_order(arrays):
        arrays = list(arrays)
        for m in masks_of(count):
            flip = (me & m) != 0
            arrays = [jnp.where(flip, arrays[j ^ m], arrays[j]) for j in range(count)]
        return arrays

    @pl.when(step == 0)
    def _():
        for j in range(count):
            wcat[pl.ds(pl.multiple_of((me ^ j) * width, width), width)] = wo[j][...]
        vec_ref[...] = jnp.zeros_like(vec_ref)

    attended = jnp.concatenate(in_order([a[...] for a in att]), axis=1)
    mid = tok_ref[...].astype(f32) + nn(attended, wcat[...]) + b_out_ref[...]
    mid_ref[...] = mid
    n, _ = normed(mid)
    second = (n * gain_ref[...] + bias_ref[...]).astype(bf16)
    second_ref[...] = second
    u = nn(second, up_ref[...]) + b_up_ref[...]
    root = math.sqrt(2.0 / math.pi)
    square = u * u
    t = jnp.tanh(u * (root + root * 0.044715 * square))
    half = 0.5 + 0.5 * t
    active_ref[...] = (u * half).astype(bf16)
    slope = half + (0.5 * u) * (1.0 - t * t) * (root + (3.0 * root * 0.044715) * square)
    grad = nt(cot_ref[...], down_ref[...]) * slope
    low = grad.astype(bf16)
    grad_ref[...] = low
    out = nt(low, up_ref[...]).astype(bf16)
    steps = pl.num_programs(0)

    @pl.when(step < steps // 2)
    def _():
        theirs_ref[...] = out

    @pl.when(step >= steps // 2)
    def _():
        mine_ref[...] = out

    vec_ref[0:8] += fold(low.astype(f32))


def weights_kernel(
    pos_ref,
    active_ref,
    second_ref,
    grad_ref,
    cot_ref,
    down_ref,
    out_theirs_ref,
    out_mine_ref,
    theirs_ref,
    mine_ref,
    down_acc,
    up_acc,
):
    step = pl.program_id(0)
    terms = nn(active_ref[...], down_ref[...]).astype(bf16)
    down = tn(active_ref[...], cot_ref[...])
    up = tn(second_ref[...], grad_ref[...])

    @pl.when(step == 0)
    def _():
        out_theirs_ref[...] = terms
        down_acc[...] = down
        up_acc[...] = up

    @pl.when(step == 1)
    def _():
        out_mine_ref[...] = terms
        first = (down_acc[...] + down).astype(bf16)
        then = (up_acc[...] + up).astype(bf16).reshape(first.shape)
        low = pos_ref[3] == 0
        theirs_ref[...] = jnp.where(low, then, first)
        mine_ref[...] = jnp.where(low, first, then)


def rest_kernel(
    bit_ref, first_ref, gqkv_ref, low_ref, att_ref, slot_ref, sums_ref, theirs_ref, mine_ref
):
    slots, _, blocks, width = slot_ref.shape
    dim = first_ref.shape[1]
    size = dim // 2
    rows = [slot_ref[:, s].reshape(slots * blocks, width) for s in range(2)]
    far_rows = (jnp.concatenate(rows, axis=1) * (1.0 / SPAN)).astype(bf16)
    far_first = columns_of(sums_ref, 2, dim // width).astype(bf16)
    out = []
    for h in range(2):
        at = slice(h * size, (h + 1) * size)
        main = tn(first_ref[:, at], gqkv_ref[...])
        far = tn(far_first[:, at], far_rows)
        last = tn(low_ref[:, at], att_ref[...])
        out.append(
            jnp.concatenate([main[:, :width], main[:, width:] + far, last], axis=1).astype(bf16)
        )
    low = bit_ref[0] == 0
    theirs_ref[...] = jnp.where(low, out[1], out[0])
    mine_ref[...] = jnp.where(low, out[0], out[1])


def split_kernel(bit_ref, a_ref, b_ref, theirs_ref, mine_ref):
    total = (a_ref[...].astype(f32) + b_ref[...].astype(f32)).astype(bf16)
    size = total.shape[0] // 2
    low = bit_ref[0] == 0
    theirs_ref[...] = jnp.where(low, total[size:], total[:size])
    mine_ref[...] = jnp.where(low, total[:size], total[size:])


def two_halves(refs, half, core):
    own, far, other, other_far = refs
    mine = half == core
    a = jnp.where(mine, own[...], other[...])
    b = jnp.where(mine, far[...], other_far[...])
    return a.astype(f32) + b.astype(f32)


def back_kernel(
    pos_ref,
    own_ref,
    far_ref,
    other_ref,
    other_far_ref,
    mid_ref,
    cot_ref,
    gain_ref,
    wo_ref,
    qkv_ref,
    prob_ref,
    sums_ref,
    low_ref,
    gqkv_ref,
    slot_ref,
    vec_ref,
):
    step = pl.program_id(0)
    slots = sums_ref.shape[0]
    width = wo_ref.shape[0]

    @pl.when(step == 0)
    def _():
        slot_ref[...] = jnp.zeros_like(slot_ref)
        vec_ref[...] = jnp.zeros_like(vec_ref)

    e = two_halves((own_ref, far_ref, other_ref, other_far_ref), step, pos_ref[1])
    n, r = normed(mid_ref[...])
    cot = cot_ref[...].astype(f32)
    grad_mid = cot + norm_back(e, n, r, gain_ref[...])
    low = grad_mid.astype(bf16)
    low_ref[...] = low
    vec_ref[0:8] += fold(grad_mid)
    vec_ref[8:16] += fold(e * n)
    vec_ref[16:24] += fold(e)
    vec_ref[24:32] += fold(cot)

    grad_att = nt(low, wo_ref[...]).astype(bf16)
    far_keys = sums_ref[:, 0].reshape(-1, width).astype(bf16)
    far_values = sums_ref[:, 1].reshape(-1, width).astype(bf16)
    far_gk = jnp.zeros(far_keys.shape, f32)
    far_gv = jnp.zeros(far_keys.shape, f32)
    for b in range(prob_ref.shape[0]):
        at = slice(b * SPAN, (b + 1) * SPAN)
        da = spread(grad_att[at], 1.0)
        query = spread(qkv_ref[0, at], SCALE)
        keys = jnp.concatenate([qkv_ref[1, at], far_keys])
        values = jnp.concatenate([qkv_ref[2, at], far_values])
        p = prob_ref[b]
        dp = nt(values, da)
        ds = (p * (dp - jnp.sum(p * dp, axis=0, keepdims=True))).astype(bf16)
        gq = collect(tn(ds, keys), SCALE)
        gk = nn(ds, query)
        gv = nn(p.astype(bf16), da)
        gqkv_ref[at, :width] = gq.astype(bf16)
        gqkv_ref[at, width : 2 * width] = gk[:SPAN].astype(bf16)
        gqkv_ref[at, 2 * width :] = gv[:SPAN].astype(bf16)
        far_gk = far_gk + gk[SPAN:]
        far_gv = far_gv + gv[SPAN:]
    slot_ref[:, 0] += far_gk.reshape(slots, -1, width)
    slot_ref[:, 1] += far_gv.reshape(slots, -1, width)


def first_kernel(
    pos_ref, gqkv_ref, slot_ref, sums_ref, w_ref, tok_ref, theirs_ref, mine_ref, wcat, vec
):
    step = pl.program_id(0)
    steps = pl.num_programs(0)
    dim, width = w_ref.shape[1:]
    tile = gqkv_ref.shape[0]
    half = tile * (steps // 2)

    @pl.when(step == 0)
    def _():
        vec[...] = jnp.zeros_like(vec)
        for s in range(3):
            wcat[:, s * width : (s + 1) * width] = w_ref[s]

    e = nt(gqkv_ref[...], wcat[...])
    n, _ = normed(tok_ref[...].astype(f32))
    vec[0:8] += fold(e * n)
    vec[8:16] += fold(e)
    out = e.astype(bf16)
    at = pl.ds(pl.multiple_of((step % (steps // 2)) * tile, tile), tile)

    @pl.when(step < steps // 2)
    def _():
        theirs_ref[at] = out

    @pl.when(step >= steps // 2)
    def _():
        mine_ref[at] = out

    @pl.when(step == steps - 1)
    def _():
        rows = [
            (slot_ref[:, s].reshape(-1, width) * (1.0 / SPAN)).astype(bf16) for s in range(2)
        ]
        far = nt(rows[0], w_ref[1]) + nt(rows[1], w_ref[2])
        normal = columns_of(sums_ref, 2 + dim // width, dim // width)
        gain = jnp.sum(vec[0:8], axis=0, keepdims=True) + jnp.sum(
            far * normal, axis=0, keepdims=True
        )
        offset = jnp.sum(vec[8:16], axis=0, keepdims=True) + SPAN * jnp.sum(
            far, axis=0, keepdims=True
        )
        low = to_low(jnp.concatenate([gain, offset, jnp.zeros((6, dim), f32)]), dim)
        theirs_ref[half:] = low
        mine_ref[half:] = low


def pair_kernel(a_ref, b_ref, out_ref):
    dim = a_ref.shape[1]
    rows = a_ref.shape[0] - 16
    out_ref[:rows] = (a_ref[:rows].astype(f32) + b_ref[:rows].astype(f32)).astype(bf16)
    out_ref[rows:] = to_low(from_low(a_ref[rows:], dim) + from_low(b_ref[rows:], dim), dim)


def extra_kernel(a_ref, b_ref, w_ref, out_ref):
    own = ((a_ref[0] + b_ref[0]) * (1.0 / SPAN)).astype(bf16)
    out_ref[...] = nt(own[0], w_ref[1]) + nt(own[1], w_ref[2])


def piece_kernel(mine_ref, got_ref, near_ref, far_ref, back_ref, up_ref, out_ref):
    dim = near_ref.shape[1]
    hidden = up_ref.shape[1]
    rows, cols = mine_ref.shape
    out_ref[:rows] = (mine_ref[...].astype(f32) + got_ref[...].astype(f32)).astype(bf16)
    last = near_ref.shape[0] - 16
    first = (from_low(near_ref[last:], dim) + from_low(far_ref[last:], dim))[:2]
    vectors = [first]
    for k in range(4):
        vectors.append(jnp.sum(back_ref[8 * k : 8 * k + 8], axis=0, keepdims=True))
    up = jnp.sum(up_ref[...], axis=0, keepdims=True)
    if hidden < dim:
        up = jnp.concatenate([up, jnp.zeros((1, dim - hidden), f32)], axis=1)
    vectors += [up, jnp.zeros((1, dim), f32)]
    out_ref[rows:] = to_low(jnp.concatenate(vectors), cols)


def merge_kernel(dim, a_ref, b_ref, out_ref):
    cols = a_ref.shape[1]
    rows = a_ref.shape[0] - 16 * (dim // cols)
    out_ref[:rows] = a_ref[:rows]
    out_ref[rows : 2 * rows] = b_ref[:rows]
    out_ref[2 * rows :] = to_low(from_low(a_ref[rows:], dim) + from_low(b_ref[rows:], dim), cols)


def last_kernel(
    pos_ref,
    own_ref,
    far_ref,
    other_ref,
    other_far_ref,
    extra_ref,
    tok_ref,
    low_ref,
    gain_ref,
    out_ref,
):
    step = pl.program_id(0)
    half = step // (pl.num_programs(0) // 2)
    e = two_halves((own_ref, far_ref, other_ref, other_far_ref), half, pos_ref[1])
    per = e.shape[0] // SPAN
    pieces = []
    for i in range(per):
        pieces.append(e[i * SPAN : (i + 1) * SPAN] + extra_ref[pl.ds(step * per + i, 1)])
    e = jnp.concatenate(pieces)
    n, r = normed(tok_ref[...].astype(f32))
    out_ref[...] = (low_ref[...].astype(f32) + norm_back(e, n, r, gain_ref[...])).astype(bf16)


def add_kernel(parts, a_ref, b_ref, *out_refs):
    size = a_ref.shape[0] // parts
    for k in range(parts):
        at = slice(k * size, (k + 1) * size)
        out_refs[k][...] = (a_ref[at].astype(f32) + b_ref[at].astype(f32)).astype(bf16)


def slot_kernel(a_ref, b_ref, out_ref):
    out_ref[...] = a_ref[: out_ref.shape[0]] + b_ref[...]


def spacer_kernel(x_ref, out_ref):
    out_ref[...] = x_ref[...] * 0.5


def concat_kernel(a_ref, b_ref, out_ref):
    rows = a_ref.shape[0]
    out_ref[:rows] = a_ref[...]
    out_ref[rows:] = b_ref[...]


def output_kernel(
    pos_ref, own_ref, far_ref, other_ref, other_far_ref, mid_ref, b_ref, out_ref
):
    half = pl.program_id(0) // (pl.num_programs(0) // 2)
    e = two_halves((own_ref, far_ref, other_ref, other_far_ref), half, pos_ref[1])
    out_ref[...] = (mid_ref[...] + e + b_ref[...]).astype(bf16)


def feed_unpack_kernel(count, at_ref, near_ref, far_ref, down_ref, up_ref):
    rows = 2 * near_ref.shape[0] // count
    part = count // 2
    top = at_ref[0] // part
    low = at_ref[0] % part
    for step, out_ref in enumerate((down_ref, up_ref)):

        @pl.when(pl.program_id(0) == step)
        def _():
            for k in range(part):
                at = pl.ds(pl.multiple_of((k ^ low) * rows, rows), rows)
                x = jnp.where(top == step, near_ref[at], far_ref[at])
                out_ref[k * rows : (k + 1) * rows] = x.astype(f32)


def rest_unpack_kernel(
    count, dim, at_ref, near_ref, far_ref, spare_ref, qkv_ref, out_ref, vec_ref, scratch
):
    cols = near_ref.shape[1]
    last = near_ref.shape[0] - 16 * (dim // cols)
    rows = 2 * last // count
    width = qkv_ref.shape[2]
    part = count // 2
    top = at_ref[0] // part
    low = at_ref[0] % part
    for k in range(count):
        start = pl.multiple_of(((k % part) ^ low) * rows, rows)
        is_near = top == k // part
        x = jnp.where(is_near, near_ref[pl.ds(start, rows)], far_ref[pl.ds(start, rows)])
        x = x.astype(f32)
        for s in range(3):
            qkv_ref[s, k * rows : (k + 1) * rows] = x[:, s * width : (s + 1) * width]
        scratch[k * rows : (k + 1) * rows] = x[:, 3 * width :]
    out_ref[...] = scratch[...].T
    vec_ref[...] = from_low(near_ref[last:], dim) + from_low(far_ref[last:], dim)


def build(n_dp, n_mp):
    def swap(x, axis, mask, label):
        n = n_dp if axis == "dp" else n_mp
        with jax.named_scope(label):
            return lax.ppermute(x, axis, [(i, i ^ mask) for i in range(n)])

    def pick(x, index, rows):
        return lax.dynamic_slice_in_dim(x, index * rows, rows, 0)

    def halves(x, mask, axis):
        bit = jnp.where((lax.axis_index(axis) & mask) == 0, 0, 1)
        size = x.shape[0] // 2
        return pick(x, 1 - bit, size), pick(x, bit, size)

    def after(x, *others):
        return lax.optimization_barrier((x, others))[0]

    far_masks = masks_of(n_mp)[1:]
    dp_masks = masks_of(n_dp)
    feed_masks = [dp_masks[1], dp_masks[0]] + dp_masks[2:]

    class Line:
        def __init__(self):
            self.last = ()

        def __call__(self, work, *inputs):
            if self.last:
                inputs = after(inputs, *self.last)
            result = work(*inputs)
            first = result[-1] if isinstance(result, (tuple, list)) else result
            self.last = (first,)
            return result

        def space(self, x=None):
            if x is not None:
                self.spare = x
            self.spare = self(spacer, self.spare)

    def add_parts(parts, a, b):
        part = jax.ShapeDtypeStruct((a.shape[0] // parts, *a.shape[1:]), bf16)
        return pl.pallas_call(
            functools.partial(add_kernel, parts),
            out_shape=(part,) * parts,
            in_specs=[VMEM, VMEM],
            out_specs=(VMEM,) * parts,
            compiler_params=params(60),
            cost_estimate=cost(),
            name="add",
        )(a, b)

    def add_low(a, b):
        return add_parts(1, a, b)[0]

    def spacer(x):
        return pl.pallas_call(
            spacer_kernel,
            out_shape=jax.ShapeDtypeStruct(x.shape, x.dtype),
            in_specs=[VMEM],
            out_specs=VMEM,
            compiler_params=params(16),
            cost_estimate=cost(),
            name="spacer",
        )(x)

    def split_sum(bit, mine, got):
        size = mine.shape[0] // 2
        half = jax.ShapeDtypeStruct((size, mine.shape[1]), bf16)
        return pl.pallas_call(
            split_kernel,
            out_shape=(half, half),
            in_specs=[SMEM, VMEM, VMEM],
            out_specs=(VMEM, VMEM),
            compiler_params=params(16),
            cost_estimate=cost(),
            name="split",
        )(bit, mine, got)

    def bit_of(mask):
        return jnp.where((lax.axis_index("dp") & mask) == 0, 0, 1).astype(i32)[None]

    class Scatter:
        def __init__(self, line, theirs, mine, masks, label):
            self.line, self.label = line, label
            self.rest = list(masks)
            self.mine = mine
            self.got = swap(theirs, "dp", self.rest.pop(0), label)

        def step(self):
            mask = self.rest.pop(0)
            theirs, self.mine = self.line(split_sum, bit_of(mask), self.mine, self.got)
            self.got = swap(theirs, "dp", mask, self.label)

    def per_device(
        tokens,
        ln1_gain,
        ln1_bias,
        w_qkv,
        w_out,
        b_out,
        ln2_gain,
        ln2_bias,
        w_up,
        b_up,
        w_down,
        b_down,
        cotangent,
    ):
        rows, dim = tokens.shape
        width = w_qkv.shape[2]
        hidden = w_up.shape[1]
        heads = width // HEAD_DIM
        blocks = rows // SPAN
        lanes = heads * SPAN
        group = LENGTH // rows
        entries = SPAN + group * blocks
        seq_masks = masks_of(group)
        me = lax.axis_index("mp")
        place = lax.axis_index("dp") % group
        first_bit = bit_of(dp_masks[0])
        pos = jnp.concatenate(
            [jnp.stack([me, me & 1, place]).astype(i32), bit_of(feed_masks[0])]
        )
        half = rows // 2
        tile = half // 2
        tiles = 4
        sds = jax.ShapeDtypeStruct

        def rolled(i, pos):
            return ((i + (1 - pos[1]) * (tiles // 2)) % tiles, 0)

        def theirs_row(i, pos):
            return (jnp.minimum(i, tiles // 2 - 1), 0)

        def mine_row(i, pos):
            return (jnp.maximum(i - tiles // 2, 0), 0)

        def half_rolled(i, pos):
            return (jnp.where(i == 0, 1 - pos[1], pos[1]), 0)

        def whole(*_):
            return (0, 0)

        def by_row(i, *_):
            return (i, 0)

        def zeros(n):
            return lambda *_: (0,) * n

        def block(shape, index):
            return pl.BlockSpec(shape, index)

        def plain(kernel, name, in_specs, out_shape, scratch=(), mib=24):
            return pl.pallas_call(
                kernel,
                out_shape=out_shape,
                in_specs=in_specs,
                out_specs=tuple(VMEM for _ in out_shape),
                scratch_shapes=list(scratch),
                compiler_params=params(mib),
                cost_estimate=cost(),
                name=name,
            )

        def gridded(
            kernel, name, grid, in_specs, out_specs, out_shape, scratch=(), mib=60, aliases=None
        ):
            return pl.pallas_call(
                kernel,
                grid_spec=pltpu.PrefetchScalarGridSpec(
                    num_scalar_prefetch=1,
                    grid=(grid,),
                    in_specs=in_specs,
                    out_specs=out_specs,
                    scratch_shapes=list(scratch),
                ),
                out_shape=out_shape,
                input_output_aliases=aliases or {},
                compiler_params=params(60 if name in ('feed',) else 30 if name in ('back', 'weights') else 20),
                cost_estimate=cost(),
                name=name,
            )

        row_block = block((tile, dim), rolled)
        row_vector = block((1, dim), whole)
        tile_block = block((tile, dim), by_row)
        one_tile = block((tile, dim), whole)

        project = plain(
            functools.partial(project_kernel, tile),
            "project",
            [VMEM] * 4,
            (
                sds((rows, dim), bf16),
                sds((3, rows, width), bf16),
                sds((2 + 2 * (dim // width), blocks, width), f32),
            ),
            [pltpu.VMEM((dim, 3 * width), bf16)],
            60,
        )
        local = plain(
            local_kernel,
            "local",
            [VMEM],
            (sds((blocks, SPAN, lanes), f32), sds((blocks, 2, lanes), f32)),
        )
        attend = plain(
            attend_kernel,
            "attend",
            [SMEM] + [VMEM] * 4,
            (sds((blocks, entries, lanes), f32), sds((rows, width), bf16)),
        )
        feed = gridded(
            functools.partial(feed_kernel, n_mp),
            "feed",
            tiles,
            [row_block]
            + [block((tile, width), rolled)] * n_mp
            + [block((width, dim), whole)] * n_mp
            + [row_vector] * 3
            + [
                block((dim, hidden), whole),
                block((1, hidden), whole),
                block((hidden, dim), whole),
                row_block,
            ],
            [
                row_block,
                row_block,
                block((tile, hidden), rolled),
                block((tile, hidden), rolled),
                block((tile, dim), theirs_row),
                block((tile, dim), mine_row),
                block((8, hidden), whole),
            ],
            (
                sds((rows, dim), f32),
                sds((rows, dim), bf16),
                sds((rows, hidden), bf16),
                sds((rows, hidden), bf16),
                sds((half, dim), bf16),
                sds((half, dim), bf16),
                sds((8, hidden), f32),
            ),
            [pltpu.VMEM((dim, dim), bf16)],
        )
        half_rows = block((half, dim), half_rolled)
        half_hidden = block((half, hidden), half_rolled)
        weights = gridded(
            weights_kernel,
            "weights",
            2,
            [half_hidden, half_rows, half_hidden, half_rows, block((hidden, dim), whole)],
            [block((half, dim), whole)] * 2 + [block((hidden, dim), whole)] * 2,
            (
                sds((half, dim), bf16),
                sds((half, dim), bf16),
                sds((hidden, dim), bf16),
                sds((hidden, dim), bf16),
            ),
            [pltpu.VMEM((hidden, dim), f32), pltpu.VMEM((dim, hidden), f32)],
        )
        rest_weights = plain(
            rest_kernel,
            "rest_weights",
            [SMEM] + [VMEM] * 6,
            (sds((dim // 2, 4 * width), bf16), sds((dim // 2, 4 * width), bf16)),
            mib=60,
        )
        slot_shape = (group, 2, blocks, width)
        sums_shape = (group, 2 + 2 * (dim // width), blocks, width)
        back = gridded(
            back_kernel,
            "back",
            2,
            [block((half, dim), whole)] * 4
            + [
                block((half, dim), by_row),
                block((half, dim), by_row),
                row_vector,
                block((width, dim), whole),
                block((3, half, width), lambda i, pos: (0, i, 0)),
                block((blocks // 2, entries, lanes), lambda i, pos: (i, 0, 0)),
                block(sums_shape, zeros(4)),
            ],
            [
                block((half, dim), by_row),
                block((half, 3 * width), by_row),
                block(slot_shape, zeros(4)),
                block((32, dim), whole),
            ],
            (
                sds((rows, dim), bf16),
                sds((rows, 3 * width), bf16),
                sds(slot_shape, f32),
                sds((32, dim), f32),
            ),
        )
        first_block = block((half + 16, dim), whole)
        first_grad = gridded(
            first_kernel,
            "first",
            2,
            [
                block((half, 3 * width), half_rolled),
                block(slot_shape, zeros(4)),
                block(sums_shape, zeros(4)),
                block((3, dim, width), zeros(3)),
                half_rows,
            ],
            [first_block, first_block],
            (sds((half + 16, dim), bf16), sds((half + 16, dim), bf16)),
            [pltpu.VMEM((dim, 3 * width), bf16), pltpu.VMEM((16, dim), f32)],
        )
        def own_tile(i, pos):
            return (jnp.clip(i - pos[1] * (tiles // 2), 0, tiles // 2 - 1), 0)

        def other_tile(i, pos):
            return (jnp.clip(i - (1 - pos[1]) * (tiles // 2), 0, tiles // 2 - 1), 0)

        terms_specs = [block((half, dim), whole)] * 4
        tile_block = block((half, dim), by_row)
        last = gridded(
            last_kernel,
            "last",
            2,
            terms_specs + [block((blocks, dim), whole), tile_block, tile_block, row_vector],
            tile_block,
            sds((rows, dim), bf16),
        )
        output_sum = gridded(
            output_kernel,
            "output",
            2,
            terms_specs + [tile_block, row_vector],
            tile_block,
            sds((rows, dim), bf16),
        )
        feed_unpack = gridded(
            functools.partial(feed_unpack_kernel, n_dp),
            "feed_unpack",
            2,
            [block((hidden, dim), whole)] * 2,
            [block((hidden, dim), whole)] * 2,
            (sds((hidden, dim), f32), sds((hidden, dim), f32)),
        )
        rest_unpack = plain(
            functools.partial(rest_unpack_kernel, n_dp, dim),
            "rest_unpack",
            [SMEM, VMEM, VMEM, VMEM],
            (sds((3, dim, width), f32), sds((width, dim), f32), sds((8, dim), f32)),
            [pltpu.VMEM((dim, width), f32)],
        )

        def like(kernel, name, shape, dtype, *operands):
            specs = [VMEM] * len(operands)
            return plain(kernel, name, specs, (sds(shape, dtype),))(*operands)[0]

        def pair(a, b):
            return like(pair_kernel, "pair", a.shape, bf16, a, b)

        def slot_add(a, b):
            return like(slot_kernel, "slots", b.shape, f32, a, b)

        def extra_of(a, b, w):
            return like(extra_kernel, "extra", (blocks, dim), f32, a, b, w)

        def concat(a, b):
            return like(concat_kernel, "concat", (2 * a.shape[0], a.shape[1]), bf16, a, b)

        def pl_add(a, b):
            return like(slot_kernel, "plus", a.shape, f32, a, b)

        vec_rows = 16 * (dim // (4 * width))

        def piece_of(mine, *operands):
            shape = (mine.shape[0] + vec_rows, 4 * width)
            return like(piece_kernel, "piece", shape, bf16, mine, *operands)

        def merge(a, b):
            shape = (2 * a.shape[0] - vec_rows, 4 * width)
            return like(functools.partial(merge_kernel, dim), "merge", shape, bf16, a, b)

        def place_of(masks):
            at = jnp.zeros((1,), i32)
            for m in masks:
                at = at * 2 + bit_of(m)
            return at


        def wait(*arrived):
            return line(lambda *x: x, *arrived)

        def near_sum(total, label):
            for m in far_masks[:-1]:
                total = line(add_low, total, swap(total, "mp", m, label))
            return total

        last_far = far_masks[-1]

        line = Line()

        out_slots = {0: w_out}
        for m in far_masks:
            out_slots.update(
                {j ^ m: swap(x, "mp", m, "gather_w_out") for j, x in list(out_slots.items())}
            )
        line.spare = ln1_gain[None]
        pos, place = wait(pos, place[None].astype(i32))
        first, qkv, summary = line(project, tokens, ln1_gain[None], ln1_bias[None], w_qkv)
        out_list = list(out_slots.items())
        sums = after(summary, *[x for _, x in out_list])[None]
        for i, m in enumerate(seq_masks):
            got = swap(sums, "dp", m, "summaries")
            if i == 0:
                exps, stats = line(local, qkv)
                for j, x in out_list:
                    out_slots[j ^ 1] = swap(after(x, stats), "mp", 1, "gather_w_out")
            sums = line(lambda a, b: jnp.concatenate([a, b]), sums, got)
        probs, attended = line(attend, place, qkv, exps, stats, sums)

        att_slots = {0: attended}
        for m in far_masks:
            att_slots.update(
                {j ^ m: swap(x, "mp", m, "gather_attended") for j, x in list(att_slots.items())}
            )
        for j, x in list(att_slots.items()):
            att_slots[j ^ 1] = swap(x, "mp", 1, "gather_attended")
        mid, second, active, grad_upper, theirs, mine, up_vec = line(
            feed,
            pos,
            tokens,
            *[att_slots[j] for j in range(n_mp)],
            *[out_slots[j] for j in range(n_mp)],
            b_out[None],
            ln2_gain[None],
            ln2_bias[None],
            w_up,
            b_up[None],
            w_down,
            cotangent,
        )

        total = near_sum(line(add_low, mine, swap(theirs, "mp", 1, "sum_second")), "sum_second")
        far = swap(total, "mp", last_far, "sum_second")
        other = swap(total, "mp", 1, "sum_second")
        out_theirs, out_mine, theirs, mine = line(
            weights, pos, active, second, grad_upper, cotangent, w_down
        )
        feed_sum = Scatter(line, theirs, mine, feed_masks, "feed_weights")
        out_got = swap(out_theirs, "mp", 1, "sum_output")
        line.space()
        out_total = near_sum(line(add_low, out_mine, out_got), "sum_output")
        (far,) = wait(far)
        other_far = swap(far, "mp", 1, "sum_second")
        out_send = after(out_total, far)
        out_far = swap(out_send, "mp", last_far, "sum_output")
        out_other = swap(out_send, "mp", 1, "sum_output")
        line.space()
        grad_low, gqkv, back_vec, slot_grad = line(
            lambda *a: (lambda r: (r[0], r[1], r[3], r[2]))(back(*a)),
            pos,
            total,
            far,
            other,
            other_far,
            mid,
            cotangent,
            ln2_gain[None],
            w_out,
            qkv,
            probs,
            sums,
        )

        following = list(reversed(seq_masks))
        slot_part = slot_grad
        slot_got = swap(slot_part[following[0] :], "dp", following[0], "sum_slots")
        feed_sum.step()
        (out_other,) = wait(out_other)
        theirs, mine = line(first_grad, pos, gqkv, slot_grad, sums, w_qkv, tokens)
        got = swap(theirs, "mp", 1, "sum_first")
        theirs_w, mine_w = line(
            rest_weights, first_bit, first, gqkv, grad_low, attended, slot_grad, sums
        )
        total = line(pair, mine, got)
        for m in far_masks[:-1]:
            total = line(pair, total, swap(total, "mp", m, "sum_first"))
        far = swap(total, "mp", last_far, "sum_first")
        rest_sum = Scatter(line, theirs_w, mine_w, dp_masks, "rest_weights")
        for low in following[1:]:
            slot_part = line(slot_add, slot_part, slot_got)
            slot_got = swap(slot_part[low:], "dp", low, "sum_slots")
        (out_far,) = wait(out_far)
        out_other_far = swap(out_far, "mp", 1, "sum_output")
        feed_sum.step()
        extra = line(extra_of, slot_part, slot_got, w_qkv)
        extra_got = swap(extra, "mp", 1, "sum_extra")
        rest_sum.step()
        output = line(
            output_sum, pos, out_total, out_far, out_other, out_other_far, mid, b_down[None]
        )
        for m in far_masks:
            extra = line(pl_add, extra, extra_got)
            extra_got = swap(extra, "mp", m, "sum_extra")
        for m in feed_masks[3:]:
            feed_sum.step()
        (far,) = wait(far)
        other = swap(after(total, far), "mp", 1, "sum_first")
        other_far = swap(far, "mp", 1, "sum_first")
        feed_all = line(add_low, feed_sum.mine, feed_sum.got)
        feed_got = swap(feed_all, "dp", feed_masks[-1], "feed_weights")
        for m in dp_masks[2:]:
            rest_sum.step()
        extra = line(pl_add, extra, extra_got)
        grad_tokens = line(
            last, pos, total, far, other, other_far, extra, tokens, grad_low, ln1_gain[None]
        )
        feed_next = list(reversed(feed_masks))[1:]
        rest_next = list(reversed(dp_masks))[1:]
        feed_all = line(concat, feed_all, feed_got)
        feed_got = swap(feed_all, "dp", feed_next[0], "feed_weights")
        rest_all = line(
            piece_of, rest_sum.mine, rest_sum.got, total, far, back_vec, up_vec
        )
        rest_got = swap(rest_all, "dp", dp_masks[-1], "rest_weights")
        line.space()
        rest_all = line(merge, rest_all, rest_got)
        rest_got = swap(rest_all, "dp", rest_next[0], "rest_weights")
        for feed_mask, rest_mask in zip(feed_next[1:], rest_next[1:]):
            feed_all = line(concat, feed_all, feed_got)
            feed_got = swap(feed_all, "dp", feed_mask, "feed_weights")
            rest_all = line(merge, rest_all, rest_got)
            rest_got = swap(rest_all, "dp", rest_mask, "rest_weights")
            line.space()
        grad_w_qkv, grad_w_out, vectors = line(
            rest_unpack, place_of(dp_masks), rest_all, rest_got, line.spare
        )
        grad_w_down, grad_w_up = line(feed_unpack, place_of(feed_masks), feed_all, feed_got)
        return (
            output,
            grad_tokens,
            vectors[0],
            vectors[1],
            grad_w_qkv,
            grad_w_out,
            vectors[2],
            vectors[3],
            vectors[4],
            grad_w_up.reshape(dim, hidden),
            vectors[6, :hidden],
            grad_w_down,
            vectors[5],
        )

    return per_device


def solution(mesh):
    return jax.shard_map(
        build(mesh.shape["dp"], mesh.shape["mp"]),
        mesh=mesh,
        in_specs=(
            P("dp", None),
            P(),
            P(),
            P(None, None, "mp"),
            P("mp", None),
            P(),
            P(),
            P(),
            P(None, "mp"),
            P("mp"),
            P("mp", None),
            P(),
            P("dp", None),
        ),
        out_specs=(
            P("dp", None),
            P("dp", None),
            P(),
            P(),
            P(None, None, "mp"),
            P("mp", None),
            P(),
            P(),
            P(),
            P(None, "mp"),
            P("mp"),
            P("mp", None),
            P(),
        ),
        check_vma=False,
    )
```

```python
import functools
import math

import jax
import jax.numpy as jnp
from jax import lax
from jax.experimental import pallas as pl
from jax.experimental.pallas import tpu as pltpu
from jax.sharding import PartitionSpec as P

HEAD_DIM = 64
SPAN = 128
LENGTH = 4096
EPSILON = 1e-05
SCALE = HEAD_DIM ** (-0.5)
LOW = -1e30

f32 = jnp.float32
bf16 = jnp.bfloat16
i32 = jnp.int32
VMEM = pl.BlockSpec(memory_space=pltpu.VMEM)
SMEM = pl.BlockSpec(memory_space=pltpu.SMEM)


def masks_of(count):
    return [1 << i for i in range(count.bit_length() - 1)]


def params(mib=60):
    return pltpu.CompilerParams(vmem_limit_bytes=mib * 1024 * 1024)


def cost():
    return pl.CostEstimate(flops=115_000_000_000, bytes_accessed=1, transcendentals=0)


def nt(a, b):
    return lax.dot_general(a, b, (((1,), (1,)), ((), ())), preferred_element_type=f32)


def tn(a, b):
    return lax.dot_general(a, b, (((0,), (0,)), ((), ())), preferred_element_type=f32)


def nn(a, b):
    return jnp.dot(a, b, preferred_element_type=f32)


def normed(x):
    c = x - jnp.mean(x, axis=-1, keepdims=True)
    r = lax.rsqrt(jnp.mean(c * c, axis=-1, keepdims=True) + EPSILON)
    return c * r, r


def norm_back(e, n, r, gain):
    k = e * gain
    return r * (
        k - jnp.mean(k, axis=-1, keepdims=True) - n * jnp.mean(k * n, axis=-1, keepdims=True)
    )


def fold(x):
    return jnp.sum(x.reshape(-1, 8, x.shape[-1]), axis=0)


def head_mask(shape, h, dtype):
    lane = lax.broadcasted_iota(i32, shape, len(shape) - 1)
    return jnp.where(lane // HEAD_DIM == h, 1.0, 0.0).astype(dtype)


def spread(x, factor):
    heads = x.shape[1] // HEAD_DIM
    return jnp.concatenate(
        [x * (head_mask((1, x.shape[1]), h, f32) * factor).astype(x.dtype) for h in range(heads)]
    )


def collect(x, factor):
    width = x.shape[1]
    heads = width // HEAD_DIM
    rows = x.shape[0] // heads
    total = x[:rows] * (head_mask((1, width), 0, f32) * factor)
    for h in range(1, heads):
        total = total + x[h * rows : (h + 1) * rows] * (head_mask((1, width), h, f32) * factor)
    return total


def to_low(v, cols):
    v = jnp.concatenate([v[:, i : i + cols] for i in range(0, v.shape[1], cols)])
    high = v.astype(bf16)
    return jnp.concatenate([high, (v - high.astype(f32)).astype(bf16)])


def from_low(x, dim):
    half = x.shape[0] // 2
    v = x[:half].astype(f32) + x[half:].astype(f32)
    count = dim // x.shape[1]
    return jnp.concatenate([v[i * 8 : (i + 1) * 8] for i in range(count)], axis=1)


def columns_of(sums_ref, start, count):
    slots, _, blocks, width = sums_ref.shape
    parts = [sums_ref[:, start + j].reshape(slots * blocks, width) for j in range(count)]
    return jnp.concatenate(parts, axis=1)


def project_kernel(tile, tok_ref, gain_ref, bias_ref, w_ref, first_ref, qkv_ref, sum_ref, wcat):
    width = w_ref.shape[2]
    for s in range(3):
        wcat[:, s * width : (s + 1) * width] = w_ref[s]
    per = tile // SPAN
    for i in range(tok_ref.shape[0] // tile):
        at = slice(i * tile, (i + 1) * tile)
        n, _ = normed(tok_ref[at].astype(f32))
        first = (n * gain_ref[...] + bias_ref[...]).astype(bf16)
        first_ref[at] = first
        both = nn(first, wcat[...]).astype(bf16)
        for s in range(3):
            part = both[:, s * width : (s + 1) * width]
            qkv_ref[s, at] = part
            if s:
                mean = jnp.mean(part.astype(f32).reshape(per, SPAN, width), axis=1)
                sum_ref[s - 1, i * per : (i + 1) * per] = mean.astype(bf16).astype(f32)
        sums = [jnp.sum(x.reshape(per, SPAN, -1), axis=1) for x in (first.astype(f32), n)]
        total = jnp.concatenate(sums, axis=1)
        for j in range(sum_ref.shape[0] - 2):
            sum_ref[2 + j, i * per : (i + 1) * per] = total[:, j * width : (j + 1) * width]


def local_kernel(qkv_ref, exp_ref, stat_ref):
    blocks = exp_ref.shape[0]
    lanes = exp_ref.shape[2]
    key = lax.broadcasted_iota(i32, (SPAN, lanes), 0)
    query = lax.broadcasted_iota(i32, (SPAN, lanes), 1) % SPAN
    keep = key <= query
    for b in range(blocks):
        at = slice(b * SPAN, (b + 1) * SPAN)
        s = nt(qkv_ref[1, at], spread(qkv_ref[0, at], SCALE))
        s = jnp.where(keep, s, LOW)
        top = jnp.max(s, axis=0, keepdims=True)
        e = jnp.exp(s - top)
        exp_ref[b] = e
        stat_ref[b, 0:1] = top
        stat_ref[b, 1:2] = jnp.sum(e, axis=0, keepdims=True)


def attend_kernel(place_ref, qkv_ref, exp_ref, stat_ref, sums_ref, prob_ref, att_ref):
    blocks = exp_ref.shape[0]
    lanes = exp_ref.shape[2]
    slots = sums_ref.shape[0]
    place = place_ref[0]
    keys = sums_ref[:, 0].reshape(slots * blocks, -1).astype(bf16)
    values = sums_ref[:, 1].reshape(slots * blocks, -1).astype(bf16)
    row = lax.broadcasted_iota(i32, (slots * blocks, lanes), 0)
    at_block = ((row // blocks) ^ place) * blocks + row % blocks
    for b in range(blocks):
        at = slice(b * SPAN, (b + 1) * SPAN)
        s = nt(keys, spread(qkv_ref[0, at], SCALE)) + math.log(SPAN)
        s = jnp.where(at_block < place * blocks + b, s, LOW)
        mine = stat_ref[b, 0:1]
        top = jnp.maximum(mine, jnp.max(s, axis=0, keepdims=True))
        e = jnp.exp(s - top)
        shrink = jnp.exp(mine - top)
        scale = 1.0 / (stat_ref[b, 1:2] * shrink + jnp.sum(e, axis=0, keepdims=True))
        p = jnp.concatenate([exp_ref[b] * (shrink * scale), e * scale]).astype(bf16)
        prob_ref[b] = p
        a = tn(p, jnp.concatenate([qkv_ref[2, at], values]))
        att_ref[at] = collect(a, 1.0).astype(bf16)


def feed_kernel(
    count, pos_ref, tok_ref, *refs
):
    att = refs[:count]
    wo = refs[count : 2 * count]
    (
        b_out_ref,
        gain_ref,
        bias_ref,
        up_ref,
        b_up_ref,
        down_ref,
        cot_ref,
        mid_ref,
        second_ref,
        active_ref,
        grad_ref,
        theirs_ref,
        mine_ref,
        vec_ref,
        wcat,
    ) = refs[2 * count :]
    step = pl.program_id(0)
    me = pos_ref[0]
    width = wo[0].shape[0]

    def in_order(arrays):
        arrays = list(arrays)
        for m in masks_of(count):
            flip = (me & m) != 0
            arrays = [jnp.where(flip, arrays[j ^ m], arrays[j]) for j in range(count)]
        return arrays

    @pl.when(step == 0)
    def _():
        for j in range(count):
            wcat[pl.ds(pl.multiple_of((me ^ j) * width, width), width)] = wo[j][...]
        vec_ref[...] = jnp.zeros_like(vec_ref)

    attended = jnp.concatenate(in_order([a[...] for a in att]), axis=1)
    mid = tok_ref[...].astype(f32) + nn(attended, wcat[...]) + b_out_ref[...]
    mid_ref[...] = mid
    n, _ = normed(mid)
    second = (n * gain_ref[...] + bias_ref[...]).astype(bf16)
    second_ref[...] = second
    u = nn(second, up_ref[...]) + b_up_ref[...]
    root = math.sqrt(2.0 / math.pi)
    square = u * u
    t = jnp.tanh(u * (root + root * 0.044715 * square))
    half = 0.5 + 0.5 * t
    active_ref[...] = (u * half).astype(bf16)
    slope = half + (0.5 * u) * (1.0 - t * t) * (root + (3.0 * root * 0.044715) * square)
    grad = nt(cot_ref[...], down_ref[...]) * slope
    low = grad.astype(bf16)
    grad_ref[...] = low
    out = nt(low, up_ref[...]).astype(bf16)
    steps = pl.num_programs(0)

    @pl.when(step < steps // 2)
    def _():
        theirs_ref[...] = out

    @pl.when(step >= steps // 2)
    def _():
        mine_ref[...] = out

    vec_ref[0:8] += fold(low.astype(f32))


def weights_kernel(
    pos_ref,
    active_ref,
    second_ref,
    grad_ref,
    cot_ref,
    down_ref,
    out_theirs_ref,
    out_mine_ref,
    theirs_ref,
    mine_ref,
    down_acc,
    up_acc,
):
    step = pl.program_id(0)
    terms = nn(active_ref[...], down_ref[...]).astype(bf16)
    down = tn(active_ref[...], cot_ref[...])
    up = tn(second_ref[...], grad_ref[...])

    @pl.when(step == 0)
    def _():
        out_theirs_ref[...] = terms
        down_acc[...] = down
        up_acc[...] = up

    @pl.when(step == 1)
    def _():
        out_mine_ref[...] = terms
        first = (down_acc[...] + down).astype(bf16)
        then = (up_acc[...] + up).astype(bf16).reshape(first.shape)
        low = pos_ref[3] == 0
        theirs_ref[...] = jnp.where(low, then, first)
        mine_ref[...] = jnp.where(low, first, then)


def rest_kernel(
    bit_ref, first_ref, gqkv_ref, low_ref, att_ref, slot_ref, sums_ref, theirs_ref, mine_ref
):
    slots, _, blocks, width = slot_ref.shape
    dim = first_ref.shape[1]
    size = dim // 2
    rows = [slot_ref[:, s].reshape(slots * blocks, width) for s in range(2)]
    far_rows = (jnp.concatenate(rows, axis=1) * (1.0 / SPAN)).astype(bf16)
    far_first = columns_of(sums_ref, 2, dim // width).astype(bf16)
    out = []
    for h in range(2):
        at = slice(h * size, (h + 1) * size)
        main = tn(first_ref[:, at], gqkv_ref[...])
        far = tn(far_first[:, at], far_rows)
        last = tn(low_ref[:, at], att_ref[...])
        out.append(
            jnp.concatenate([main[:, :width], main[:, width:] + far, last], axis=1).astype(bf16)
        )
    low = bit_ref[0] == 0
    theirs_ref[...] = jnp.where(low, out[1], out[0])
    mine_ref[...] = jnp.where(low, out[0], out[1])


def split_kernel(bit_ref, a_ref, b_ref, theirs_ref, mine_ref):
    total = (a_ref[...].astype(f32) + b_ref[...].astype(f32)).astype(bf16)
    size = total.shape[0] // 2
    low = bit_ref[0] == 0
    theirs_ref[...] = jnp.where(low, total[size:], total[:size])
    mine_ref[...] = jnp.where(low, total[:size], total[size:])


def two_halves(refs, half, core):
    own, far, other, other_far = refs
    mine = half == core
    a = jnp.where(mine, own[...], other[...])
    b = jnp.where(mine, far[...], other_far[...])
    return a.astype(f32) + b.astype(f32)


def back_kernel(
    pos_ref,
    own_ref,
    far_ref,
    other_ref,
    other_far_ref,
    mid_ref,
    cot_ref,
    gain_ref,
    wo_ref,
    qkv_ref,
    prob_ref,
    sums_ref,
    low_ref,
    gqkv_ref,
    slot_ref,
    vec_ref,
):
    step = pl.program_id(0)
    slots = sums_ref.shape[0]
    width = wo_ref.shape[0]

    @pl.when(step == 0)
    def _():
        slot_ref[...] = jnp.zeros_like(slot_ref)
        vec_ref[...] = jnp.zeros_like(vec_ref)

    e = two_halves((own_ref, far_ref, other_ref, other_far_ref), step, pos_ref[1])
    n, r = normed(mid_ref[...])
    cot = cot_ref[...].astype(f32)
    grad_mid = cot + norm_back(e, n, r, gain_ref[...])
    low = grad_mid.astype(bf16)
    low_ref[...] = low
    vec_ref[0:8] += fold(grad_mid)
    vec_ref[8:16] += fold(e * n)
    vec_ref[16:24] += fold(e)
    vec_ref[24:32] += fold(cot)

    grad_att = nt(low, wo_ref[...]).astype(bf16)
    far_keys = sums_ref[:, 0].reshape(-1, width).astype(bf16)
    far_values = sums_ref[:, 1].reshape(-1, width).astype(bf16)
    far_gk = jnp.zeros(far_keys.shape, f32)
    far_gv = jnp.zeros(far_keys.shape, f32)
    for b in range(prob_ref.shape[0]):
        at = slice(b * SPAN, (b + 1) * SPAN)
        da = spread(grad_att[at], 1.0)
        query = spread(qkv_ref[0, at], SCALE)
        keys = jnp.concatenate([qkv_ref[1, at], far_keys])
        values = jnp.concatenate([qkv_ref[2, at], far_values])
        p_low = prob_ref[b]
        p = p_low.astype(f32)
        dp = nt(values, da)
        ds = (p * (dp - jnp.sum(p * dp, axis=0, keepdims=True))).astype(bf16)
        gq = collect(tn(ds, keys), SCALE)
        gk = nn(ds, query)
        gv = nn(p_low, da)
        gqkv_ref[at, :width] = gq.astype(bf16)
        gqkv_ref[at, width : 2 * width] = gk[:SPAN].astype(bf16)
        gqkv_ref[at, 2 * width :] = gv[:SPAN].astype(bf16)
        far_gk = far_gk + gk[SPAN:]
        far_gv = far_gv + gv[SPAN:]
    slot_ref[:, 0] += far_gk.reshape(slots, -1, width)
    slot_ref[:, 1] += far_gv.reshape(slots, -1, width)


def first_kernel(
    pos_ref, gqkv_ref, slot_ref, sums_ref, w_ref, tok_ref, theirs_ref, mine_ref, wcat, vec
):
    step = pl.program_id(0)
    steps = pl.num_programs(0)
    dim, width = w_ref.shape[1:]
    tile = gqkv_ref.shape[0]
    half = tile * (steps // 2)

    @pl.when(step == 0)
    def _():
        vec[...] = jnp.zeros_like(vec)
        for s in range(3):
            wcat[:, s * width : (s + 1) * width] = w_ref[s]

    e = nt(gqkv_ref[...], wcat[...])
    n, _ = normed(tok_ref[...].astype(f32))
    vec[0:8] += fold(e * n)
    vec[8:16] += fold(e)
    out = e.astype(bf16)
    at = pl.ds(pl.multiple_of((step % (steps // 2)) * tile, tile), tile)

    @pl.when(step < steps // 2)
    def _():
        theirs_ref[at] = out

    @pl.when(step >= steps // 2)
    def _():
        mine_ref[at] = out

    @pl.when(step == steps - 1)
    def _():
        rows = [
            (slot_ref[:, s].reshape(-1, width) * (1.0 / SPAN)).astype(bf16) for s in range(2)
        ]
        far = nt(rows[0], w_ref[1]) + nt(rows[1], w_ref[2])
        normal = columns_of(sums_ref, 2 + dim // width, dim // width)
        gain = jnp.sum(vec[0:8], axis=0, keepdims=True) + jnp.sum(
            far * normal, axis=0, keepdims=True
        )
        offset = jnp.sum(vec[8:16], axis=0, keepdims=True) + SPAN * jnp.sum(
            far, axis=0, keepdims=True
        )
        low = to_low(jnp.concatenate([gain, offset, jnp.zeros((6, dim), f32)]), dim)
        theirs_ref[half:] = low
        mine_ref[half:] = low


def pair_kernel(a_ref, b_ref, out_ref):
    dim = a_ref.shape[1]
    rows = a_ref.shape[0] - 16
    out_ref[:rows] = (a_ref[:rows].astype(f32) + b_ref[:rows].astype(f32)).astype(bf16)
    out_ref[rows:] = to_low(from_low(a_ref[rows:], dim) + from_low(b_ref[rows:], dim), dim)


def extra_kernel(a_ref, b_ref, w_ref, out_ref):
    own = ((a_ref[0] + b_ref[0]) * (1.0 / SPAN)).astype(bf16)
    out_ref[...] = nt(own[0], w_ref[1]) + nt(own[1], w_ref[2])


def piece_kernel(mine_ref, got_ref, near_ref, far_ref, back_ref, up_ref, out_ref):
    dim = near_ref.shape[1]
    hidden = up_ref.shape[1]
    rows, cols = mine_ref.shape
    out_ref[:rows] = (mine_ref[...].astype(f32) + got_ref[...].astype(f32)).astype(bf16)
    last = near_ref.shape[0] - 16
    first = (from_low(near_ref[last:], dim) + from_low(far_ref[last:], dim))[:2]
    vectors = [first]
    for k in range(4):
        vectors.append(jnp.sum(back_ref[8 * k : 8 * k + 8], axis=0, keepdims=True))
    up = jnp.sum(up_ref[...], axis=0, keepdims=True)
    if hidden < dim:
        up = jnp.concatenate([up, jnp.zeros((1, dim - hidden), f32)], axis=1)
    vectors += [up, jnp.zeros((1, dim), f32)]
    out_ref[rows:] = to_low(jnp.concatenate(vectors), cols)


def merge_kernel(dim, a_ref, b_ref, out_ref):
    cols = a_ref.shape[1]
    rows = a_ref.shape[0] - 16 * (dim // cols)
    out_ref[:rows] = a_ref[:rows]
    out_ref[rows : 2 * rows] = b_ref[:rows]
    out_ref[2 * rows :] = to_low(from_low(a_ref[rows:], dim) + from_low(b_ref[rows:], dim), cols)


def last_kernel(
    pos_ref,
    own_ref,
    far_ref,
    other_ref,
    other_far_ref,
    extra_ref,
    extra_far_ref,
    tok_ref,
    low_ref,
    gain_ref,
    out_ref,
):
    step = pl.program_id(0)
    half = step // (pl.num_programs(0) // 2)
    e = two_halves((own_ref, far_ref, other_ref, other_far_ref), half, pos_ref[1])
    per = e.shape[0] // SPAN
    pieces = []
    for i in range(per):
        at = pl.ds(step * per + i, 1)
        pieces.append(e[i * SPAN : (i + 1) * SPAN] + (extra_ref[at] + extra_far_ref[at]))
    e = jnp.concatenate(pieces)
    n, r = normed(tok_ref[...].astype(f32))
    out_ref[...] = (low_ref[...].astype(f32) + norm_back(e, n, r, gain_ref[...])).astype(bf16)


def add_kernel(parts, a_ref, b_ref, *out_refs):
    size = a_ref.shape[0] // parts
    for k in range(parts):
        at = slice(k * size, (k + 1) * size)
        out_refs[k][...] = (a_ref[at].astype(f32) + b_ref[at].astype(f32)).astype(bf16)


def slot_kernel(a_ref, b_ref, out_ref):
    out_ref[...] = a_ref[: out_ref.shape[0]] + b_ref[...]


def spacer_kernel(x_ref, out_ref):
    out_ref[...] = x_ref[...] * 0.5


def concat_kernel(a_ref, b_ref, out_ref):
    rows = a_ref.shape[0]
    out_ref[:rows] = a_ref[...]
    out_ref[rows:] = b_ref[...]


def output_kernel(
    pos_ref, own_ref, far_ref, other_ref, other_far_ref, mid_ref, b_ref, out_ref
):
    half = pl.program_id(0) // (pl.num_programs(0) // 2)
    e = two_halves((own_ref, far_ref, other_ref, other_far_ref), half, pos_ref[1])
    out_ref[...] = (mid_ref[...] + e + b_ref[...]).astype(bf16)


def feed_unpack_kernel(
    count, at_ref, own_ref, one_ref, two_ref, both_ref, down_ref, up_ref
):
    part = count // 4
    rows = own_ref.shape[0] // part
    top = at_ref[0] // part
    low = at_ref[0] % part
    for step, out_ref in enumerate((down_ref, up_ref)):

        @pl.when(pl.program_id(0) == step)
        def _():
            for k in range(2 * part):
                slot = top ^ (2 * step + k // part)
                at = pl.ds(pl.multiple_of(((k % part) ^ low) * rows, rows), rows)
                x = jnp.where(slot == 0, own_ref[at], one_ref[at])
                far = jnp.where(slot == 2, two_ref[at], both_ref[at])
                x = jnp.where(slot < 2, x, far)
                out_ref[k * rows : (k + 1) * rows] = x.astype(f32)


def rest_unpack_kernel(
    count, dim, at_ref, near_ref, far_ref, spare_ref, qkv_ref, out_ref, vec_ref, scratch
):
    cols = near_ref.shape[1]
    last = near_ref.shape[0] - 16 * (dim // cols)
    rows = 2 * last // count
    width = qkv_ref.shape[2]
    part = count // 2
    top = at_ref[0] // part
    low = at_ref[0] % part
    for k in range(count):
        start = pl.multiple_of(((k % part) ^ low) * rows, rows)
        is_near = top == k // part
        x = jnp.where(is_near, near_ref[pl.ds(start, rows)], far_ref[pl.ds(start, rows)])
        x = x.astype(f32)
        for s in range(3):
            qkv_ref[s, k * rows : (k + 1) * rows] = x[:, s * width : (s + 1) * width]
        scratch[k * rows : (k + 1) * rows] = x[:, 3 * width :]
    out_ref[...] = scratch[...].T
    vec_ref[...] = from_low(near_ref[last:], dim) + from_low(far_ref[last:], dim)


def build(n_dp, n_mp):
    def swap(x, axis, mask, label):
        n = n_dp if axis == "dp" else n_mp
        with jax.named_scope(label):
            return lax.ppermute(x, axis, [(i, i ^ mask) for i in range(n)])

    def pick(x, index, rows):
        return lax.dynamic_slice_in_dim(x, index * rows, rows, 0)

    def halves(x, mask, axis):
        bit = jnp.where((lax.axis_index(axis) & mask) == 0, 0, 1)
        size = x.shape[0] // 2
        return pick(x, 1 - bit, size), pick(x, bit, size)

    def after(x, *others):
        return lax.optimization_barrier((x, others))[0]

    far_masks = masks_of(n_mp)[1:]
    dp_masks = masks_of(n_dp)
    feed_masks = [dp_masks[1], dp_masks[0]] + dp_masks[2:]

    class Line:
        def __init__(self):
            self.last = ()

        def __call__(self, work, *inputs):
            if self.last:
                inputs = after(inputs, *self.last)
            result = work(*inputs)
            first = result[-1] if isinstance(result, (tuple, list)) else result
            self.last = (first,)
            return result

        def space(self, x=None):
            if x is not None:
                self.spare = x
            self.spare = self(spacer, self.spare)

    def add_parts(parts, a, b):
        part = jax.ShapeDtypeStruct((a.shape[0] // parts, *a.shape[1:]), bf16)
        return pl.pallas_call(
            functools.partial(add_kernel, parts),
            out_shape=(part,) * parts,
            in_specs=[VMEM, VMEM],
            out_specs=(VMEM,) * parts,
            compiler_params=params(16),
            cost_estimate=cost(),
            name="add",
        )(a, b)

    def add_low(a, b):
        return add_parts(1, a, b)[0]

    def spacer(x):
        return pl.pallas_call(
            spacer_kernel,
            out_shape=jax.ShapeDtypeStruct(x.shape, x.dtype),
            in_specs=[VMEM],
            out_specs=VMEM,
            compiler_params=params(16),
            cost_estimate=cost(),
            name="spacer",
        )(x)

    def split_sum(bit, mine, got):
        size = mine.shape[0] // 2
        half = jax.ShapeDtypeStruct((size, mine.shape[1]), bf16)
        return pl.pallas_call(
            split_kernel,
            out_shape=(half, half),
            in_specs=[SMEM, VMEM, VMEM],
            out_specs=(VMEM, VMEM),
            compiler_params=params(16),
            cost_estimate=cost(),
            name="split",
        )(bit, mine, got)

    def bit_of(mask):
        return jnp.where((lax.axis_index("dp") & mask) == 0, 0, 1).astype(i32)[None]

    class Scatter:
        def __init__(self, line, theirs, mine, masks, label):
            self.line, self.label = line, label
            self.rest = list(masks)
            self.mine = mine
            self.got = swap(theirs, "dp", self.rest.pop(0), label)

        def step(self):
            mask = self.rest.pop(0)
            theirs, self.mine = self.line(split_sum, bit_of(mask), self.mine, self.got)
            self.got = swap(theirs, "dp", mask, self.label)

    def per_device(
        tokens,
        ln1_gain,
        ln1_bias,
        w_qkv,
        w_out,
        b_out,
        ln2_gain,
        ln2_bias,
        w_up,
        b_up,
        w_down,
        b_down,
        cotangent,
    ):
        rows, dim = tokens.shape
        width = w_qkv.shape[2]
        hidden = w_up.shape[1]
        heads = width // HEAD_DIM
        blocks = rows // SPAN
        lanes = heads * SPAN
        group = LENGTH // rows
        entries = SPAN + group * blocks
        seq_masks = masks_of(group)
        me = lax.axis_index("mp")
        place = lax.axis_index("dp") % group
        first_bit = bit_of(dp_masks[0])
        pos = jnp.concatenate(
            [jnp.stack([me, me & 1, place]).astype(i32), bit_of(feed_masks[0])]
        )
        half = rows // 2
        tile = half // 2
        tiles = 4
        sds = jax.ShapeDtypeStruct

        def rolled(i, pos):
            return ((i + (1 - pos[1]) * (tiles // 2)) % tiles, 0)

        def theirs_row(i, pos):
            return (jnp.minimum(i, tiles // 2 - 1), 0)

        def mine_row(i, pos):
            return (jnp.maximum(i - tiles // 2, 0), 0)

        def half_rolled(i, pos):
            return (jnp.where(i == 0, 1 - pos[1], pos[1]), 0)

        def whole(*_):
            return (0, 0)

        def by_row(i, *_):
            return (i, 0)

        def zeros(n):
            return lambda *_: (0,) * n

        def block(shape, index):
            return pl.BlockSpec(shape, index)

        def plain(kernel, name, in_specs, out_shape, scratch=(), mib=24):
            return pl.pallas_call(
                kernel,
                out_shape=out_shape,
                in_specs=in_specs,
                out_specs=tuple(VMEM for _ in out_shape),
                scratch_shapes=list(scratch),
                compiler_params=params(mib),
                cost_estimate=cost(),
                name=name,
            )

        def gridded(
            kernel, name, grid, in_specs, out_specs, out_shape, scratch=(), mib=60, aliases=None
        ):
            return pl.pallas_call(
                kernel,
                grid_spec=pltpu.PrefetchScalarGridSpec(
                    num_scalar_prefetch=1,
                    grid=(grid,),
                    in_specs=in_specs,
                    out_specs=out_specs,
                    scratch_shapes=list(scratch),
                ),
                out_shape=out_shape,
                input_output_aliases=aliases or {},
                compiler_params=params(60 if name in ('feed',) else 30 if name in ('back', 'weights') else 20),
                cost_estimate=cost(),
                name=name,
            )

        row_block = block((tile, dim), rolled)
        row_vector = block((1, dim), whole)
        tile_block = block((tile, dim), by_row)
        one_tile = block((tile, dim), whole)

        project = plain(
            functools.partial(project_kernel, tile),
            "project",
            [VMEM] * 4,
            (
                sds((rows, dim), bf16),
                sds((3, rows, width), bf16),
                sds((2 + 2 * (dim // width), blocks, width), f32),
            ),
            [pltpu.VMEM((dim, 3 * width), bf16)],
            60,
        )
        local = plain(
            local_kernel,
            "local",
            [VMEM],
            (sds((blocks, SPAN, lanes), f32), sds((blocks, 2, lanes), f32)),
        )
        attend = plain(
            attend_kernel,
            "attend",
            [SMEM] + [VMEM] * 4,
            (sds((blocks, entries, lanes), bf16), sds((rows, width), bf16)),
        )
        half_rows = block((half, dim), half_rolled)
        half_hidden = block((half, hidden), half_rolled)
        feed = gridded(
            functools.partial(feed_kernel, n_mp),
            "feed",
            2,
            [half_rows]
            + [block((half, width), half_rolled)] * n_mp
            + [block((width, dim), whole)] * n_mp
            + [row_vector] * 3
            + [
                block((dim, hidden), whole),
                block((1, hidden), whole),
                block((hidden, dim), whole),
                half_rows,
            ],
            [
                half_rows,
                half_rows,
                half_hidden,
                half_hidden,
                block((half, dim), whole),
                block((half, dim), whole),
                block((8, hidden), whole),
            ],
            (
                sds((rows, dim), f32),
                sds((rows, dim), bf16),
                sds((rows, hidden), bf16),
                sds((rows, hidden), bf16),
                sds((half, dim), bf16),
                sds((half, dim), bf16),
                sds((8, hidden), f32),
            ),
            [pltpu.VMEM((dim, dim), bf16)],
        )
        weights = gridded(
            weights_kernel,
            "weights",
            2,
            [half_hidden, half_rows, half_hidden, half_rows, block((hidden, dim), whole)],
            [block((half, dim), whole)] * 2 + [block((hidden, dim), whole)] * 2,
            (
                sds((half, dim), bf16),
                sds((half, dim), bf16),
                sds((hidden, dim), bf16),
                sds((hidden, dim), bf16),
            ),
            [pltpu.VMEM((hidden, dim), f32), pltpu.VMEM((dim, hidden), f32)],
        )
        rest_weights = plain(
            rest_kernel,
            "rest_weights",
            [SMEM] + [VMEM] * 6,
            (sds((dim // 2, 4 * width), bf16), sds((dim // 2, 4 * width), bf16)),
            mib=60,
        )
        slot_shape = (group, 2, blocks, width)
        sums_shape = (group, 2 + 2 * (dim // width), blocks, width)
        back = gridded(
            back_kernel,
            "back",
            2,
            [block((half, dim), whole)] * 4
            + [
                block((half, dim), by_row),
                block((half, dim), by_row),
                row_vector,
                block((width, dim), whole),
                block((3, half, width), lambda i, pos: (0, i, 0)),
                block((blocks // 2, entries, lanes), lambda i, pos: (i, 0, 0)),
                block(sums_shape, zeros(4)),
            ],
            [
                block((half, dim), by_row),
                block((half, 3 * width), by_row),
                block(slot_shape, zeros(4)),
                block((32, dim), whole),
            ],
            (
                sds((rows, dim), bf16),
                sds((rows, 3 * width), bf16),
                sds(slot_shape, f32),
                sds((32, dim), f32),
            ),
        )
        first_block = block((half + 16, dim), whole)
        first_grad = gridded(
            first_kernel,
            "first",
            2,
            [
                block((half, 3 * width), half_rolled),
                block(slot_shape, zeros(4)),
                block(sums_shape, zeros(4)),
                block((3, dim, width), zeros(3)),
                half_rows,
            ],
            [first_block, first_block],
            (sds((half + 16, dim), bf16), sds((half + 16, dim), bf16)),
            [pltpu.VMEM((dim, 3 * width), bf16), pltpu.VMEM((16, dim), f32)],
        )
        def own_tile(i, pos):
            return (jnp.clip(i - pos[1] * (tiles // 2), 0, tiles // 2 - 1), 0)

        def other_tile(i, pos):
            return (jnp.clip(i - (1 - pos[1]) * (tiles // 2), 0, tiles // 2 - 1), 0)

        terms_specs = [block((half, dim), whole)] * 4
        tile_block = block((half, dim), by_row)
        last = gridded(
            last_kernel,
            "last",
            2,
            terms_specs + [block((blocks, dim), whole)] * 2 + [tile_block, tile_block, row_vector],
            tile_block,
            sds((rows, dim), bf16),
        )
        output_sum = gridded(
            output_kernel,
            "output",
            2,
            terms_specs + [tile_block, row_vector],
            tile_block,
            sds((rows, dim), bf16),
        )
        feed_unpack = gridded(
            functools.partial(feed_unpack_kernel, n_dp),
            "feed_unpack",
            2,
            [block((hidden // 2, dim), whole)] * 4,
            [block((hidden, dim), whole)] * 2,
            (sds((hidden, dim), f32), sds((hidden, dim), f32)),
        )
        rest_unpack = plain(
            functools.partial(rest_unpack_kernel, n_dp, dim),
            "rest_unpack",
            [SMEM, VMEM, VMEM, VMEM],
            (sds((3, dim, width), f32), sds((width, dim), f32), sds((8, dim), f32)),
            [pltpu.VMEM((dim, width), f32)],
        )

        def like(kernel, name, shape, dtype, *operands):
            specs = [VMEM] * len(operands)
            return plain(kernel, name, specs, (sds(shape, dtype),))(*operands)[0]

        def pair(a, b):
            return like(pair_kernel, "pair", a.shape, bf16, a, b)

        def slot_add(a, b):
            return like(slot_kernel, "slots", b.shape, f32, a, b)

        def extra_of(a, b, w):
            return like(extra_kernel, "extra", (blocks, dim), f32, a, b, w)

        def concat(a, b):
            return like(concat_kernel, "concat", (2 * a.shape[0], a.shape[1]), bf16, a, b)

        def pl_add(a, b):
            return like(slot_kernel, "plus", a.shape, f32, a, b)

        vec_rows = 16 * (dim // (4 * width))

        def piece_of(mine, *operands):
            shape = (mine.shape[0] + vec_rows, 4 * width)
            return like(piece_kernel, "piece", shape, bf16, mine, *operands)

        def merge(a, b):
            shape = (2 * a.shape[0] - vec_rows, 4 * width)
            return like(functools.partial(merge_kernel, dim), "merge", shape, bf16, a, b)

        def place_of(masks):
            at = jnp.zeros((1,), i32)
            for m in masks:
                at = at * 2 + bit_of(m)
            return at


        def wait(*arrived):
            return line(lambda *x: x, *arrived)

        def near_sum(total, label):
            for m in far_masks[:-1]:
                total = line(add_low, total, swap(total, "mp", m, label))
            return total

        last_far = far_masks[-1]

        line = Line()

        out_slots = {0: w_out}
        for m in far_masks:
            out_slots.update(
                {j ^ m: swap(x, "mp", m, "gather_w_out") for j, x in list(out_slots.items())}
            )
        line.spare = ln1_gain[None]
        pos, place = wait(pos, place[None].astype(i32))
        first, qkv, summary = line(project, tokens, ln1_gain[None], ln1_bias[None], w_qkv)
        out_list = list(out_slots.items())
        sums = after(summary, *[x for _, x in out_list])[None]
        for i, m in enumerate(seq_masks):
            got = swap(sums, "dp", m, "summaries")
            if i == 0:
                exps, stats = line(local, qkv)
                for j, x in out_list:
                    out_slots[j ^ 1] = swap(after(x, stats), "mp", 1, "gather_w_out")
            sums = line(lambda a, b: jnp.concatenate([a, b]), sums, got)
        cores = wait(*[out_slots[j ^ 1] for j, _ in out_list])
        for (j, _), x in zip(out_list, cores):
            out_slots[j ^ 1] = x
        probs, attended = line(attend, place, qkv, exps, stats, sums)

        att_slots = {0: attended}
        for m in far_masks:
            att_slots.update(
                {j ^ m: swap(x, "mp", m, "gather_attended") for j, x in list(att_slots.items())}
            )
        for j, x in list(att_slots.items()):
            att_slots[j ^ 1] = swap(x, "mp", 1, "gather_attended")
        mid, second, active, grad_upper, theirs, mine, up_vec = line(
            feed,
            pos,
            tokens,
            *[att_slots[j] for j in range(n_mp)],
            *[out_slots[j] for j in range(n_mp)],
            b_out[None],
            ln2_gain[None],
            ln2_bias[None],
            w_up,
            b_up[None],
            w_down,
            cotangent,
        )

        total = near_sum(line(add_low, mine, swap(theirs, "mp", 1, "sum_second")), "sum_second")
        far = swap(total, "mp", last_far, "sum_second")
        other = swap(total, "mp", 1, "sum_second")
        out_theirs, out_mine, theirs, mine = line(
            weights, pos, active, second, grad_upper, cotangent, w_down
        )
        feed_sum = Scatter(line, theirs, mine, feed_masks, "feed_weights")
        out_got = swap(out_theirs, "mp", 1, "sum_output")
        line.space()
        out_total = near_sum(line(add_low, out_mine, out_got), "sum_output")
        (far,) = wait(far)
        other_far = swap(far, "mp", 1, "sum_second")
        out_send = after(out_total, far)
        out_far = swap(out_send, "mp", last_far, "sum_output")
        out_other = swap(out_send, "mp", 1, "sum_output")
        line.space()
        grad_low, gqkv, back_vec, slot_grad = line(
            lambda *a: (lambda r: (r[0], r[1], r[3], r[2]))(back(*a)),
            pos,
            total,
            far,
            other,
            other_far,
            mid,
            cotangent,
            ln2_gain[None],
            w_out,
            qkv,
            probs,
            sums,
        )

        following = list(reversed(seq_masks))
        slot_part = slot_grad
        slot_got = swap(slot_part[following[0] :], "dp", following[0], "sum_slots")
        feed_sum.step()
        (out_other,) = wait(out_other)
        theirs, mine = line(first_grad, pos, gqkv, slot_grad, sums, w_qkv, tokens)
        got = swap(theirs, "mp", 1, "sum_first")
        theirs_w, mine_w = line(
            rest_weights, first_bit, first, gqkv, grad_low, attended, slot_grad, sums
        )
        total = line(pair, mine, got)
        for m in far_masks[:-1]:
            total = line(pair, total, swap(total, "mp", m, "sum_first"))
        far = swap(total, "mp", last_far, "sum_first")
        rest_sum = Scatter(line, theirs_w, mine_w, dp_masks, "rest_weights")
        for low in following[1:]:
            slot_part = line(slot_add, slot_part, slot_got)
            slot_got = swap(slot_part[low:], "dp", low, "sum_slots")
        (out_far,) = wait(out_far)
        out_other_far = swap(out_far, "mp", 1, "sum_output")
        feed_sum.step()
        extra = line(extra_of, slot_part, slot_got, w_qkv)
        extra_got = swap(extra, "mp", 1, "sum_extra")
        rest_sum.step()
        output = line(
            output_sum, pos, out_total, out_far, out_other, out_other_far, mid, b_down[None]
        )
        for m in far_masks:
            extra = line(pl_add, extra, extra_got)
            extra_got = swap(extra, "mp", m, "sum_extra")
        for m in dp_masks[2:]:
            rest_sum.step()
        for m in feed_masks[3:]:
            feed_sum.step()
        (far,) = wait(far)
        other = swap(after(total, far), "mp", 1, "sum_first")
        other_far = swap(far, "mp", 1, "sum_first")
        feed_all = line(add_low, feed_sum.mine, feed_sum.got)
        feed_got = swap(feed_all, "dp", feed_masks[-1], "feed_weights")
        grad_tokens = line(
            last,
            pos,
            total,
            far,
            other,
            other_far,
            extra,
            extra_got,
            tokens,
            grad_low,
            ln1_gain[None],
        )
        rest_all = line(
            piece_of, rest_sum.mine, rest_sum.got, total, far, back_vec, up_vec
        )
        rest_got = swap(rest_all, "dp", dp_masks[-1], "rest_weights")
        feed_next = list(reversed(feed_masks))[1:]
        rest_next = list(reversed(dp_masks))[1:]
        for m in feed_next[:-2]:
            feed_all = line(concat, feed_all, feed_got)
            feed_got = swap(feed_all, "dp", m, "feed_weights")
        feed_all = line(concat, feed_all, feed_got)
        two = swap(feed_all, "dp", feed_masks[0], "feed_weights")
        one = swap(feed_all, "dp", feed_masks[1], "feed_weights")
        line.space()
        rest_all = line(merge, rest_all, rest_got)
        rest_got = swap(rest_all, "dp", rest_next[0], "rest_weights")
        (two,) = wait(two)
        both = swap(two, "dp", feed_masks[1], "feed_weights")
        for m in rest_next[1:]:
            line.space()
            rest_all = line(merge, rest_all, rest_got)
            rest_got = swap(rest_all, "dp", m, "rest_weights")
        line.space()
        grad_w_down, grad_w_up = line(
            feed_unpack, place_of(feed_masks), feed_all, one, two, both
        )
        grad_w_qkv, grad_w_out, vectors = line(
            rest_unpack, place_of(dp_masks), rest_all, rest_got, line.spare
        )
        return (
            output,
            grad_tokens,
            vectors[0],
            vectors[1],
            grad_w_qkv,
            grad_w_out,
            vectors[2],
            vectors[3],
            vectors[4],
            grad_w_up.reshape(dim, hidden),
            vectors[6, :hidden],
            grad_w_down,
            vectors[5],
        )

    return per_device


def solution(mesh):
    return jax.shard_map(
        build(mesh.shape["dp"], mesh.shape["mp"]),
        mesh=mesh,
        in_specs=(
            P("dp", None),
            P(),
            P(),
            P(None, None, "mp"),
            P("mp", None),
            P(),
            P(),
            P(),
            P(None, "mp"),
            P("mp"),
            P("mp", None),
            P(),
            P("dp", None),
        ),
        out_specs=(
            P("dp", None),
            P("dp", None),
            P(),
            P(),
            P(None, None, "mp"),
            P("mp", None),
            P(),
            P(),
            P(),
            P(None, "mp"),
            P("mp"),
            P("mp", None),
            P(),
        ),
        check_vma=False,
    )
```

```python
import functools
import math

import jax
import jax.numpy as jnp
from jax import lax
from jax.experimental import pallas as pl
from jax.experimental.pallas import tpu as pltpu
from jax.sharding import PartitionSpec as P

HEAD_DIM = 64
SPAN = 128
LENGTH = 4096
EPSILON = 1e-05
SCALE = HEAD_DIM ** (-0.5)
LOW = -1e30

f32 = jnp.float32
bf16 = jnp.bfloat16
i32 = jnp.int32
VMEM = pl.BlockSpec(memory_space=pltpu.VMEM)
SMEM = pl.BlockSpec(memory_space=pltpu.SMEM)


def masks_of(count):
    return [1 << i for i in range(count.bit_length() - 1)]


def params(mib=60):
    return pltpu.CompilerParams(vmem_limit_bytes=mib * 1024 * 1024)


def cost():
    return pl.CostEstimate(flops=115_000_000_000, bytes_accessed=1, transcendentals=0)


def nt(a, b):
    return lax.dot_general(a, b, (((1,), (1,)), ((), ())), preferred_element_type=f32)


def tn(a, b):
    return lax.dot_general(a, b, (((0,), (0,)), ((), ())), preferred_element_type=f32)


def nn(a, b):
    return jnp.dot(a, b, preferred_element_type=f32)


def normed(x):
    c = x - jnp.mean(x, axis=-1, keepdims=True)
    r = lax.rsqrt(jnp.mean(c * c, axis=-1, keepdims=True) + EPSILON)
    return c * r, r


def norm_back(e, n, r, gain):
    k = e * gain
    return r * (
        k - jnp.mean(k, axis=-1, keepdims=True) - n * jnp.mean(k * n, axis=-1, keepdims=True)
    )


def fold(x):
    return jnp.sum(x.reshape(-1, 8, x.shape[-1]), axis=0)


def head_mask(shape, h, dtype):
    lane = lax.broadcasted_iota(i32, shape, len(shape) - 1)
    return jnp.where(lane // HEAD_DIM == h, 1.0, 0.0).astype(dtype)


def spread(x, factor):
    heads = x.shape[1] // HEAD_DIM
    return jnp.concatenate(
        [x * (head_mask((1, x.shape[1]), h, f32) * factor).astype(x.dtype) for h in range(heads)]
    )


def collect(x, factor):
    width = x.shape[1]
    heads = width // HEAD_DIM
    rows = x.shape[0] // heads
    total = x[:rows] * (head_mask((1, width), 0, f32) * factor)
    for h in range(1, heads):
        total = total + x[h * rows : (h + 1) * rows] * (head_mask((1, width), h, f32) * factor)
    return total


def to_low(v, cols):
    v = jnp.concatenate([v[:, i : i + cols] for i in range(0, v.shape[1], cols)])
    high = v.astype(bf16)
    return jnp.concatenate([high, (v - high.astype(f32)).astype(bf16)])


def from_low(x, dim):
    half = x.shape[0] // 2
    v = x[:half].astype(f32) + x[half:].astype(f32)
    count = dim // x.shape[1]
    return jnp.concatenate([v[i * 8 : (i + 1) * 8] for i in range(count)], axis=1)


def columns_of(sums_ref, start, count):
    slots, _, blocks, width = sums_ref.shape
    parts = [sums_ref[:, start + j].reshape(slots * blocks, width) for j in range(count)]
    return jnp.concatenate(parts, axis=1)


def project_kernel(tile, tok_ref, gain_ref, bias_ref, w_ref, first_ref, qkv_ref, sum_ref, wcat):
    width = w_ref.shape[2]
    for s in range(3):
        wcat[:, s * width : (s + 1) * width] = w_ref[s]
    per = tile // SPAN
    for i in range(tok_ref.shape[0] // tile):
        at = slice(i * tile, (i + 1) * tile)
        n, _ = normed(tok_ref[at].astype(f32))
        first = (n * gain_ref[...] + bias_ref[...]).astype(bf16)
        first_ref[at] = first
        both = nn(first, wcat[...]).astype(bf16)
        for s in range(3):
            part = both[:, s * width : (s + 1) * width]
            qkv_ref[s, at] = part
            if s:
                mean = jnp.mean(part.astype(f32).reshape(per, SPAN, width), axis=1)
                sum_ref[s - 1, i * per : (i + 1) * per] = mean.astype(bf16).astype(f32)
        sums = [jnp.sum(x.reshape(per, SPAN, -1), axis=1) for x in (first.astype(f32), n)]
        total = jnp.concatenate(sums, axis=1)
        for j in range(sum_ref.shape[0] - 2):
            sum_ref[2 + j, i * per : (i + 1) * per] = total[:, j * width : (j + 1) * width]


def local_kernel(qkv_ref, exp_ref, stat_ref):
    blocks = exp_ref.shape[0]
    lanes = exp_ref.shape[2]
    key = lax.broadcasted_iota(i32, (SPAN, lanes), 0)
    query = lax.broadcasted_iota(i32, (SPAN, lanes), 1) % SPAN
    keep = key <= query
    for b in range(blocks):
        at = slice(b * SPAN, (b + 1) * SPAN)
        s = nt(qkv_ref[1, at], spread(qkv_ref[0, at], SCALE))
        s = jnp.where(keep, s, LOW)
        top = jnp.max(s, axis=0, keepdims=True)
        e = jnp.exp(s - top)
        exp_ref[b] = e
        stat_ref[b, 0:1] = top
        stat_ref[b, 1:2] = jnp.sum(e, axis=0, keepdims=True)


def attend_kernel(place_ref, qkv_ref, exp_ref, stat_ref, sums_ref, prob_ref, att_ref):
    blocks = exp_ref.shape[0]
    lanes = exp_ref.shape[2]
    slots = sums_ref.shape[0]
    place = place_ref[0]
    keys = sums_ref[:, 0].reshape(slots * blocks, -1).astype(bf16)
    values = sums_ref[:, 1].reshape(slots * blocks, -1).astype(bf16)
    row = lax.broadcasted_iota(i32, (slots * blocks, lanes), 0)
    at_block = ((row // blocks) ^ place) * blocks + row % blocks
    for b in range(blocks):
        at = slice(b * SPAN, (b + 1) * SPAN)
        s = nt(keys, spread(qkv_ref[0, at], SCALE)) + math.log(SPAN)
        s = jnp.where(at_block < place * blocks + b, s, LOW)
        mine = stat_ref[b, 0:1]
        top = jnp.maximum(mine, jnp.max(s, axis=0, keepdims=True))
        e = jnp.exp(s - top)
        shrink = jnp.exp(mine - top)
        scale = 1.0 / (stat_ref[b, 1:2] * shrink + jnp.sum(e, axis=0, keepdims=True))
        p = jnp.concatenate([exp_ref[b] * (shrink * scale), e * scale]).astype(bf16)
        prob_ref[b] = p
        a = tn(p, jnp.concatenate([qkv_ref[2, at], values]))
        att_ref[at] = collect(a, 1.0).astype(bf16)


def feed_kernel(
    count, pos_ref, tok_ref, *refs
):
    att = refs[:count]
    wo = refs[count : 2 * count]
    (
        b_out_ref,
        gain_ref,
        bias_ref,
        up_ref,
        b_up_ref,
        down_ref,
        cot_ref,
        mid_ref,
        second_ref,
        active_ref,
        grad_ref,
        theirs_ref,
        mine_ref,
        vec_ref,
        wcat,
    ) = refs[2 * count :]
    step = pl.program_id(0)
    me = pos_ref[0]
    width = wo[0].shape[0]

    def in_order(arrays):
        arrays = list(arrays)
        for m in masks_of(count):
            flip = (me & m) != 0
            arrays = [jnp.where(flip, arrays[j ^ m], arrays[j]) for j in range(count)]
        return arrays

    @pl.when(step == 0)
    def _():
        for j in range(count):
            wcat[pl.ds(pl.multiple_of((me ^ j) * width, width), width)] = wo[j][...]
        vec_ref[...] = jnp.zeros_like(vec_ref)

    attended = jnp.concatenate(in_order([a[...] for a in att]), axis=1)
    mid = tok_ref[...].astype(f32) + nn(attended, wcat[...]) + b_out_ref[...]
    mid_ref[...] = mid
    n, _ = normed(mid)
    second = (n * gain_ref[...] + bias_ref[...]).astype(bf16)
    second_ref[...] = second
    u = nn(second, up_ref[...]) + b_up_ref[...]
    root = math.sqrt(2.0 / math.pi)
    square = u * u
    t = jnp.tanh(u * (root + root * 0.044715 * square))
    half = 0.5 + 0.5 * t
    active_ref[...] = (u * half).astype(bf16)
    slope = half + (0.5 * u) * (1.0 - t * t) * (root + (3.0 * root * 0.044715) * square)
    grad = nt(cot_ref[...], down_ref[...]) * slope
    low = grad.astype(bf16)
    grad_ref[...] = low
    out = nt(low, up_ref[...]).astype(bf16)
    steps = pl.num_programs(0)

    @pl.when(step < steps // 2)
    def _():
        theirs_ref[...] = out

    @pl.when(step >= steps // 2)
    def _():
        mine_ref[...] = out

    vec_ref[0:8] += fold(low.astype(f32))


def weights_kernel(
    pos_ref,
    active_ref,
    second_ref,
    grad_ref,
    cot_ref,
    down_ref,
    out_theirs_ref,
    out_mine_ref,
    theirs_ref,
    mine_ref,
    down_acc,
    up_acc,
):
    step = pl.program_id(0)
    terms = nn(active_ref[...], down_ref[...]).astype(bf16)
    down = tn(active_ref[...], cot_ref[...])
    up = tn(second_ref[...], grad_ref[...])

    @pl.when(step == 0)
    def _():
        out_theirs_ref[...] = terms
        down_acc[...] = down
        up_acc[...] = up

    @pl.when(step == 1)
    def _():
        out_mine_ref[...] = terms
        first = (down_acc[...] + down).astype(bf16)
        then = (up_acc[...] + up).astype(bf16).reshape(first.shape)
        low = pos_ref[3] == 0
        theirs_ref[...] = jnp.where(low, then, first)
        mine_ref[...] = jnp.where(low, first, then)


def rest_kernel(
    bit_ref, first_ref, gqkv_ref, low_ref, att_ref, slot_ref, sums_ref, theirs_ref, mine_ref
):
    slots, _, blocks, width = slot_ref.shape
    dim = first_ref.shape[1]
    size = dim // 2
    rows = [slot_ref[:, s].reshape(slots * blocks, width) for s in range(2)]
    far_rows = (jnp.concatenate(rows, axis=1) * (1.0 / SPAN)).astype(bf16)
    far_first = columns_of(sums_ref, 2, dim // width).astype(bf16)
    out = []
    for h in range(2):
        at = slice(h * size, (h + 1) * size)
        main = tn(first_ref[:, at], gqkv_ref[...])
        far = tn(far_first[:, at], far_rows)
        last = tn(low_ref[:, at], att_ref[...])
        out.append(
            jnp.concatenate([main[:, :width], main[:, width:] + far, last], axis=1).astype(bf16)
        )
    low = bit_ref[0] == 0
    theirs_ref[:size] = jnp.where(low, out[1], out[0])
    mine_ref[:size] = jnp.where(low, out[0], out[1])
    for ref, slot in ((theirs_ref, 2), (mine_ref, 0)):
        parts = [slot_ref[j, s] for j in (slot, slot + 1) for s in range(2)]
        ref[size:] = to_low(jnp.concatenate(parts, axis=1), 4 * width)


def split_first_kernel(bit_ref, a_ref, b_ref, theirs_ref, mine_ref):
    rows = a_ref.shape[0] - 16
    cols = a_ref.shape[1]
    size = rows // 2
    total = (a_ref[:rows].astype(f32) + b_ref[:rows].astype(f32)).astype(bf16)
    low = bit_ref[0] == 0
    theirs_ref[:size] = jnp.where(low, total[size:], total[:size])
    mine_ref[:size] = jnp.where(low, total[:size], total[size:])
    slots = from_low(a_ref[rows:], cols) + from_low(b_ref[rows:], cols)
    none = jnp.zeros((8, cols // 2), f32)
    for ref, at in ((theirs_ref, slice(cols // 2, cols)), (mine_ref, slice(0, cols // 2))):
        ref[size:] = to_low(jnp.concatenate([slots[:, at], none], axis=1), cols)


def split_second_kernel(bit_ref, a_ref, b_ref, w_ref, theirs_ref, mine_ref, extra_ref):
    rows = a_ref.shape[0] - 16
    cols = a_ref.shape[1]
    width = w_ref.shape[2]
    size = rows // 2
    total = (a_ref[:rows].astype(f32) + b_ref[:rows].astype(f32)).astype(bf16)
    low = bit_ref[0] == 0
    theirs_ref[...] = jnp.where(low, total[size:], total[:size])
    mine_ref[...] = jnp.where(low, total[:size], total[size:])
    own = from_low(a_ref[rows:], cols) + from_low(b_ref[rows:], cols)
    own = (own * (1.0 / SPAN)).astype(bf16)
    extra_ref[...] = nt(own[:, :width], w_ref[1]) + nt(own[:, width : 2 * width], w_ref[2])


def split_kernel(bit_ref, a_ref, b_ref, theirs_ref, mine_ref):
    total = (a_ref[...].astype(f32) + b_ref[...].astype(f32)).astype(bf16)
    size = total.shape[0] // 2
    low = bit_ref[0] == 0
    theirs_ref[...] = jnp.where(low, total[size:], total[:size])
    mine_ref[...] = jnp.where(low, total[:size], total[size:])


def two_halves(refs, half, core):
    own, far, other, other_far = refs
    mine = half == core
    a = jnp.where(mine, own[...], other[...])
    b = jnp.where(mine, far[...], other_far[...])
    return a.astype(f32) + b.astype(f32)


def back_kernel(
    pos_ref,
    own_ref,
    far_ref,
    other_ref,
    other_far_ref,
    mid_ref,
    cot_ref,
    gain_ref,
    wo_ref,
    qkv_ref,
    prob_ref,
    sums_ref,
    low_ref,
    gqkv_ref,
    slot_ref,
    vec_ref,
):
    step = pl.program_id(0)
    slots = sums_ref.shape[0]
    width = wo_ref.shape[0]

    @pl.when(step == 0)
    def _():
        slot_ref[...] = jnp.zeros_like(slot_ref)
        vec_ref[...] = jnp.zeros_like(vec_ref)

    e = two_halves((own_ref, far_ref, other_ref, other_far_ref), step, pos_ref[1])
    n, r = normed(mid_ref[...])
    cot = cot_ref[...].astype(f32)
    grad_mid = cot + norm_back(e, n, r, gain_ref[...])
    low = grad_mid.astype(bf16)
    low_ref[...] = low
    vec_ref[0:8] += fold(grad_mid)
    vec_ref[8:16] += fold(e * n)
    vec_ref[16:24] += fold(e)
    vec_ref[24:32] += fold(cot)

    grad_att = nt(low, wo_ref[...]).astype(bf16)
    far_keys = sums_ref[:, 0].reshape(-1, width).astype(bf16)
    far_values = sums_ref[:, 1].reshape(-1, width).astype(bf16)
    far_gk = jnp.zeros(far_keys.shape, f32)
    far_gv = jnp.zeros(far_keys.shape, f32)
    for b in range(prob_ref.shape[0]):
        at = slice(b * SPAN, (b + 1) * SPAN)
        da = spread(grad_att[at], 1.0)
        query = spread(qkv_ref[0, at], SCALE)
        keys = jnp.concatenate([qkv_ref[1, at], far_keys])
        values = jnp.concatenate([qkv_ref[2, at], far_values])
        p_low = prob_ref[b]
        p = p_low.astype(f32)
        dp = nt(values, da)
        ds = (p * (dp - jnp.sum(p * dp, axis=0, keepdims=True))).astype(bf16)
        gq = collect(tn(ds, keys), SCALE)
        gk = nn(ds, query)
        gv = nn(p_low, da)
        gqkv_ref[at, :width] = gq.astype(bf16)
        gqkv_ref[at, width : 2 * width] = gk[:SPAN].astype(bf16)
        gqkv_ref[at, 2 * width :] = gv[:SPAN].astype(bf16)
        far_gk = far_gk + gk[SPAN:]
        far_gv = far_gv + gv[SPAN:]
    slot_ref[:, 0] += far_gk.reshape(slots, -1, width)
    slot_ref[:, 1] += far_gv.reshape(slots, -1, width)


def first_kernel(
    pos_ref, gqkv_ref, slot_ref, sums_ref, w_ref, tok_ref, theirs_ref, mine_ref, wcat, vec
):
    step = pl.program_id(0)
    steps = pl.num_programs(0)
    dim, width = w_ref.shape[1:]
    tile = gqkv_ref.shape[0]
    half = tile * (steps // 2)

    @pl.when(step == 0)
    def _():
        vec[...] = jnp.zeros_like(vec)
        for s in range(3):
            wcat[:, s * width : (s + 1) * width] = w_ref[s]

    e = nt(gqkv_ref[...], wcat[...])
    n, _ = normed(tok_ref[...].astype(f32))
    vec[0:8] += fold(e * n)
    vec[8:16] += fold(e)
    out = e.astype(bf16)
    at = pl.ds(pl.multiple_of((step % (steps // 2)) * tile, tile), tile)

    @pl.when(step < steps // 2)
    def _():
        theirs_ref[at] = out

    @pl.when(step >= steps // 2)
    def _():
        mine_ref[at] = out

    @pl.when(step == steps - 1)
    def _():
        rows = [
            (slot_ref[:, s].reshape(-1, width) * (1.0 / SPAN)).astype(bf16) for s in range(2)
        ]
        far = nt(rows[0], w_ref[1]) + nt(rows[1], w_ref[2])
        normal = columns_of(sums_ref, 2 + dim // width, dim // width)
        gain = jnp.sum(vec[0:8], axis=0, keepdims=True) + jnp.sum(
            far * normal, axis=0, keepdims=True
        )
        offset = jnp.sum(vec[8:16], axis=0, keepdims=True) + SPAN * jnp.sum(
            far, axis=0, keepdims=True
        )
        low = to_low(jnp.concatenate([gain, offset, jnp.zeros((6, dim), f32)]), dim)
        theirs_ref[half:] = low
        mine_ref[half:] = low


def pair_kernel(a_ref, b_ref, out_ref):
    dim = a_ref.shape[1]
    rows = a_ref.shape[0] - 16
    out_ref[:rows] = (a_ref[:rows].astype(f32) + b_ref[:rows].astype(f32)).astype(bf16)
    out_ref[rows:] = to_low(from_low(a_ref[rows:], dim) + from_low(b_ref[rows:], dim), dim)


def piece_kernel(mine_ref, got_ref, near_ref, far_ref, back_ref, up_ref, out_ref):
    dim = near_ref.shape[1]
    hidden = up_ref.shape[1]
    rows, cols = mine_ref.shape
    out_ref[:rows] = (mine_ref[...].astype(f32) + got_ref[...].astype(f32)).astype(bf16)
    last = near_ref.shape[0] - 16
    first = (from_low(near_ref[last:], dim) + from_low(far_ref[last:], dim))[:2]
    vectors = [first]
    for k in range(4):
        vectors.append(jnp.sum(back_ref[8 * k : 8 * k + 8], axis=0, keepdims=True))
    up = jnp.sum(up_ref[...], axis=0, keepdims=True)
    if hidden < dim:
        up = jnp.concatenate([up, jnp.zeros((1, dim - hidden), f32)], axis=1)
    vectors += [up, jnp.zeros((1, dim), f32)]
    out_ref[rows:] = to_low(jnp.concatenate(vectors), cols)


def merge_kernel(dim, a_ref, b_ref, out_ref):
    cols = a_ref.shape[1]
    rows = a_ref.shape[0] - 16 * (dim // cols)
    out_ref[:rows] = a_ref[:rows]
    out_ref[rows : 2 * rows] = b_ref[:rows]
    out_ref[2 * rows :] = to_low(from_low(a_ref[rows:], dim) + from_low(b_ref[rows:], dim), cols)


def last_kernel(
    pos_ref,
    own_ref,
    far_ref,
    other_ref,
    other_far_ref,
    extra_ref,
    extra_far_ref,
    tok_ref,
    low_ref,
    gain_ref,
    out_ref,
):
    step = pl.program_id(0)
    half = step // (pl.num_programs(0) // 2)
    e = two_halves((own_ref, far_ref, other_ref, other_far_ref), half, pos_ref[1])
    per = e.shape[0] // SPAN
    pieces = []
    for i in range(per):
        at = pl.ds(step * per + i, 1)
        pieces.append(e[i * SPAN : (i + 1) * SPAN] + (extra_ref[at] + extra_far_ref[at]))
    e = jnp.concatenate(pieces)
    n, r = normed(tok_ref[...].astype(f32))
    out_ref[...] = (low_ref[...].astype(f32) + norm_back(e, n, r, gain_ref[...])).astype(bf16)


def add_kernel(parts, a_ref, b_ref, *out_refs):
    size = a_ref.shape[0] // parts
    for k in range(parts):
        at = slice(k * size, (k + 1) * size)
        out_refs[k][...] = (a_ref[at].astype(f32) + b_ref[at].astype(f32)).astype(bf16)


def slot_kernel(a_ref, b_ref, out_ref):
    out_ref[...] = a_ref[: out_ref.shape[0]] + b_ref[...]


def spacer_kernel(x_ref, out_ref):
    out_ref[...] = x_ref[...] * 0.5


def concat_kernel(a_ref, b_ref, out_ref):
    rows = a_ref.shape[0]
    out_ref[:rows] = a_ref[...]
    out_ref[rows:] = b_ref[...]


def output_kernel(
    pos_ref, own_ref, far_ref, other_ref, other_far_ref, mid_ref, b_ref, out_ref
):
    half = pl.program_id(0) // (pl.num_programs(0) // 2)
    e = two_halves((own_ref, far_ref, other_ref, other_far_ref), half, pos_ref[1])
    out_ref[...] = (mid_ref[...] + e + b_ref[...]).astype(bf16)


def feed_unpack_kernel(
    count, at_ref, own_ref, one_ref, two_ref, both_ref, down_ref, up_ref
):
    part = count // 4
    rows = own_ref.shape[0] // part
    top = at_ref[0] // part
    low = at_ref[0] % part
    for step, out_ref in enumerate((down_ref, up_ref)):

        @pl.when(pl.program_id(0) == step)
        def _():
            for k in range(2 * part):
                slot = top ^ (2 * step + k // part)
                at = pl.ds(pl.multiple_of(((k % part) ^ low) * rows, rows), rows)
                x = jnp.where(slot == 0, own_ref[at], one_ref[at])
                far = jnp.where(slot == 2, two_ref[at], both_ref[at])
                x = jnp.where(slot < 2, x, far)
                out_ref[k * rows : (k + 1) * rows] = x.astype(f32)


def rest_unpack_kernel(
    count, dim, at_ref, near_ref, far_ref, spare_ref, qkv_ref, out_ref, *refs
):
    vec_refs, scratch = refs[:-1], refs[-1]
    cols = near_ref.shape[1]
    last = near_ref.shape[0] - 16 * (dim // cols)
    rows = 2 * last // count
    width = qkv_ref.shape[2]
    part = count // 2
    top = at_ref[0] // part
    low = at_ref[0] % part
    for k in range(count):
        start = pl.multiple_of(((k % part) ^ low) * rows, rows)
        is_near = top == k // part
        x = jnp.where(is_near, near_ref[pl.ds(start, rows)], far_ref[pl.ds(start, rows)])
        x = x.astype(f32)
        for s in range(3):
            qkv_ref[s, k * rows : (k + 1) * rows] = x[:, s * width : (s + 1) * width]
        scratch[k * rows : (k + 1) * rows] = x[:, 3 * width :]
    out_ref[...] = scratch[...].T
    vectors = from_low(near_ref[last:], dim) + from_low(far_ref[last:], dim)
    for k, ref in enumerate(vec_refs):
        ref[...] = vectors[k : k + 1, : ref.shape[1]]


def build(n_dp, n_mp):
    def swap(x, axis, mask, label):
        n = n_dp if axis == "dp" else n_mp
        with jax.named_scope(label):
            return lax.ppermute(x, axis, [(i, i ^ mask) for i in range(n)])

    def pick(x, index, rows):
        return lax.dynamic_slice_in_dim(x, index * rows, rows, 0)

    def halves(x, mask, axis):
        bit = jnp.where((lax.axis_index(axis) & mask) == 0, 0, 1)
        size = x.shape[0] // 2
        return pick(x, 1 - bit, size), pick(x, bit, size)

    def after(x, *others):
        return lax.optimization_barrier((x, others))[0]

    far_masks = masks_of(n_mp)[1:]
    dp_masks = masks_of(n_dp)
    feed_masks = [dp_masks[1], dp_masks[0]] + dp_masks[2:]

    class Line:
        def __init__(self):
            self.last = ()

        def __call__(self, work, *inputs):
            if self.last:
                inputs = after(inputs, *self.last)
            result = work(*inputs)
            first = result[-1] if isinstance(result, (tuple, list)) else result
            self.last = (first,)
            return result

        def space(self, x=None):
            if x is not None:
                self.spare = x
            self.spare = self(spacer, self.spare)

    def add_parts(parts, a, b):
        part = jax.ShapeDtypeStruct((a.shape[0] // parts, *a.shape[1:]), bf16)
        return pl.pallas_call(
            functools.partial(add_kernel, parts),
            out_shape=(part,) * parts,
            in_specs=[VMEM, VMEM],
            out_specs=(VMEM,) * parts,
            compiler_params=params(16),
            cost_estimate=cost(),
            name="add",
        )(a, b)

    def add_low(a, b):
        return add_parts(1, a, b)[0]

    def spacer(x):
        return pl.pallas_call(
            spacer_kernel,
            out_shape=jax.ShapeDtypeStruct(x.shape, x.dtype),
            in_specs=[VMEM],
            out_specs=VMEM,
            compiler_params=params(16),
            cost_estimate=cost(),
            name="spacer",
        )(x)

    def split_sum(bit, mine, got):
        size = mine.shape[0] // 2
        half = jax.ShapeDtypeStruct((size, mine.shape[1]), bf16)
        return pl.pallas_call(
            split_kernel,
            out_shape=(half, half),
            in_specs=[SMEM, VMEM, VMEM],
            out_specs=(VMEM, VMEM),
            compiler_params=params(16),
            cost_estimate=cost(),
            name="split",
        )(bit, mine, got)

    def bit_of(mask):
        return jnp.where((lax.axis_index("dp") & mask) == 0, 0, 1).astype(i32)[None]

    class Scatter:
        def __init__(self, line, theirs, mine, masks, label):
            self.line, self.label = line, label
            self.rest = list(masks)
            self.mine = mine
            self.got = swap(theirs, "dp", self.rest.pop(0), label)

        def step(self):
            mask = self.rest.pop(0)
            theirs, self.mine = self.line(split_sum, bit_of(mask), self.mine, self.got)
            self.got = swap(theirs, "dp", mask, self.label)

    def per_device(
        tokens,
        ln1_gain,
        ln1_bias,
        w_qkv,
        w_out,
        b_out,
        ln2_gain,
        ln2_bias,
        w_up,
        b_up,
        w_down,
        b_down,
        cotangent,
    ):
        rows, dim = tokens.shape
        width = w_qkv.shape[2]
        hidden = w_up.shape[1]
        heads = width // HEAD_DIM
        blocks = rows // SPAN
        lanes = heads * SPAN
        group = LENGTH // rows
        entries = SPAN + group * blocks
        seq_masks = masks_of(group)
        me = lax.axis_index("mp")
        place = lax.axis_index("dp") % group
        first_bit = bit_of(feed_masks[0])
        pos = jnp.concatenate(
            [jnp.stack([me, me & 1, place]).astype(i32), bit_of(feed_masks[0])]
        )
        half = rows // 2
        tile = half // 2
        tiles = 4
        sds = jax.ShapeDtypeStruct

        def rolled(i, pos):
            return ((i + (1 - pos[1]) * (tiles // 2)) % tiles, 0)

        def theirs_row(i, pos):
            return (jnp.minimum(i, tiles // 2 - 1), 0)

        def mine_row(i, pos):
            return (jnp.maximum(i - tiles // 2, 0), 0)

        def half_rolled(i, pos):
            return (jnp.where(i == 0, 1 - pos[1], pos[1]), 0)

        def whole(*_):
            return (0, 0)

        def by_row(i, *_):
            return (i, 0)

        def zeros(n):
            return lambda *_: (0,) * n

        def block(shape, index):
            return pl.BlockSpec(shape, index)

        def plain(kernel, name, in_specs, out_shape, scratch=(), mib=24):
            return pl.pallas_call(
                kernel,
                out_shape=out_shape,
                in_specs=in_specs,
                out_specs=tuple(VMEM for _ in out_shape),
                scratch_shapes=list(scratch),
                compiler_params=params(mib),
                cost_estimate=cost(),
                name=name,
            )

        def gridded(
            kernel, name, grid, in_specs, out_specs, out_shape, scratch=(), mib=60, aliases=None
        ):
            return pl.pallas_call(
                kernel,
                grid_spec=pltpu.PrefetchScalarGridSpec(
                    num_scalar_prefetch=1,
                    grid=(grid,),
                    in_specs=in_specs,
                    out_specs=out_specs,
                    scratch_shapes=list(scratch),
                ),
                out_shape=out_shape,
                input_output_aliases=aliases or {},
                compiler_params=params(60 if name in ('feed',) else 30 if name in ('back', 'weights') else 20),
                cost_estimate=cost(),
                name=name,
            )

        row_block = block((tile, dim), rolled)
        row_vector = block((1, dim), whole)
        tile_block = block((tile, dim), by_row)
        one_tile = block((tile, dim), whole)

        project = plain(
            functools.partial(project_kernel, tile),
            "project",
            [VMEM] * 4,
            (
                sds((rows, dim), bf16),
                sds((3, rows, width), bf16),
                sds((2 + 2 * (dim // width), blocks, width), f32),
            ),
            [pltpu.VMEM((dim, 3 * width), bf16)],
            60,
        )
        local = plain(
            local_kernel,
            "local",
            [VMEM],
            (sds((blocks, SPAN, lanes), f32), sds((blocks, 2, lanes), f32)),
        )
        attend = plain(
            attend_kernel,
            "attend",
            [SMEM] + [VMEM] * 4,
            (sds((blocks, entries, lanes), bf16), sds((rows, width), bf16)),
        )
        half_rows = block((half, dim), half_rolled)
        half_hidden = block((half, hidden), half_rolled)
        feed = gridded(
            functools.partial(feed_kernel, n_mp),
            "feed",
            2,
            [half_rows]
            + [block((half, width), half_rolled)] * n_mp
            + [block((width, dim), whole)] * n_mp
            + [row_vector] * 3
            + [
                block((dim, hidden), whole),
                block((1, hidden), whole),
                block((hidden, dim), whole),
                half_rows,
            ],
            [
                half_rows,
                half_rows,
                half_hidden,
                half_hidden,
                block((half, dim), whole),
                block((half, dim), whole),
                block((8, hidden), whole),
            ],
            (
                sds((rows, dim), f32),
                sds((rows, dim), bf16),
                sds((rows, hidden), bf16),
                sds((rows, hidden), bf16),
                sds((half, dim), bf16),
                sds((half, dim), bf16),
                sds((8, hidden), f32),
            ),
            [pltpu.VMEM((dim, dim), bf16)],
        )
        weights = gridded(
            weights_kernel,
            "weights",
            2,
            [half_hidden, half_rows, half_hidden, half_rows, block((hidden, dim), whole)],
            [block((half, dim), whole)] * 2 + [block((hidden, dim), whole)] * 2,
            (
                sds((half, dim), bf16),
                sds((half, dim), bf16),
                sds((hidden, dim), bf16),
                sds((hidden, dim), bf16),
            ),
            [pltpu.VMEM((hidden, dim), f32), pltpu.VMEM((dim, hidden), f32)],
        )
        rest_weights = plain(
            rest_kernel,
            "rest_weights",
            [SMEM] + [VMEM] * 6,
            (sds((dim // 2 + 16, 4 * width), bf16), sds((dim // 2 + 16, 4 * width), bf16)),
            mib=60,
        )
        slot_shape = (group, 2, blocks, width)
        sums_shape = (group, 2 + 2 * (dim // width), blocks, width)
        back = gridded(
            back_kernel,
            "back",
            2,
            [block((half, dim), whole)] * 4
            + [
                block((half, dim), by_row),
                block((half, dim), by_row),
                row_vector,
                block((width, dim), whole),
                block((3, half, width), lambda i, pos: (0, i, 0)),
                block((blocks // 2, entries, lanes), lambda i, pos: (i, 0, 0)),
                block(sums_shape, zeros(4)),
            ],
            [
                block((half, dim), by_row),
                block((half, 3 * width), by_row),
                block(slot_shape, zeros(4)),
                block((32, dim), whole),
            ],
            (
                sds((rows, dim), bf16),
                sds((rows, 3 * width), bf16),
                sds(slot_shape, f32),
                sds((32, dim), f32),
            ),
        )
        first_block = block((half + 16, dim), whole)
        first_grad = gridded(
            first_kernel,
            "first",
            2,
            [
                block((half, 3 * width), half_rolled),
                block(slot_shape, zeros(4)),
                block(sums_shape, zeros(4)),
                block((3, dim, width), zeros(3)),
                half_rows,
            ],
            [first_block, first_block],
            (sds((half + 16, dim), bf16), sds((half + 16, dim), bf16)),
            [pltpu.VMEM((dim, 3 * width), bf16), pltpu.VMEM((16, dim), f32)],
        )
        def own_tile(i, pos):
            return (jnp.clip(i - pos[1] * (tiles // 2), 0, tiles // 2 - 1), 0)

        def other_tile(i, pos):
            return (jnp.clip(i - (1 - pos[1]) * (tiles // 2), 0, tiles // 2 - 1), 0)

        terms_specs = [block((half, dim), whole)] * 4
        tile_block = block((half, dim), by_row)
        last = gridded(
            last_kernel,
            "last",
            2,
            terms_specs + [block((blocks, dim), whole)] * 2 + [tile_block, tile_block, row_vector],
            tile_block,
            sds((rows, dim), bf16),
        )
        output_sum = gridded(
            output_kernel,
            "output",
            2,
            terms_specs + [tile_block, row_vector],
            tile_block,
            sds((rows, dim), bf16),
        )
        feed_unpack = gridded(
            functools.partial(feed_unpack_kernel, n_dp),
            "feed_unpack",
            2,
            [block((hidden // 2, dim), whole)] * 4,
            [block((hidden, dim), whole)] * 2,
            (sds((hidden, dim), f32), sds((hidden, dim), f32)),
        )
        rest_unpack = plain(
            functools.partial(rest_unpack_kernel, n_dp, dim),
            "rest_unpack",
            [SMEM, VMEM, VMEM, VMEM],
            (sds((3, dim, width), f32), sds((width, dim), f32))
            + (sds((1, dim), f32),) * 6
            + (sds((1, hidden), f32),),
            [pltpu.VMEM((dim, width), f32)],
        )

        def like(kernel, name, shape, dtype, *operands):
            specs = [VMEM] * len(operands)
            return plain(kernel, name, specs, (sds(shape, dtype),))(*operands)[0]

        def pair(a, b):
            return like(pair_kernel, "pair", a.shape, bf16, a, b)

        def concat(a, b):
            return like(concat_kernel, "concat", (2 * a.shape[0], a.shape[1]), bf16, a, b)

        def pl_add(a, b):
            return like(slot_kernel, "plus", a.shape, f32, a, b)

        cols = 4 * width
        quarter = dim // 4
        split_first = plain(
            split_first_kernel,
            "split_first",
            [SMEM, VMEM, VMEM],
            (sds((quarter + 16, cols), bf16), sds((quarter + 16, cols), bf16)),
        )
        split_second = plain(
            split_second_kernel,
            "split_second",
            [SMEM, VMEM, VMEM, VMEM],
            (
                sds((quarter // 2, cols), bf16),
                sds((quarter // 2, cols), bf16),
                sds((blocks, dim), f32),
            ),
        )

        vec_rows = 16 * (dim // (4 * width))

        def piece_of(mine, *operands):
            shape = (mine.shape[0] + vec_rows, 4 * width)
            return like(piece_kernel, "piece", shape, bf16, mine, *operands)

        def merge(a, b):
            shape = (2 * a.shape[0] - vec_rows, 4 * width)
            return like(functools.partial(merge_kernel, dim), "merge", shape, bf16, a, b)

        def place_of(masks):
            at = jnp.zeros((1,), i32)
            for m in masks:
                at = at * 2 + bit_of(m)
            return at


        def wait(*arrived):
            return line(lambda *x: x, *arrived)

        def near_sum(total, label):
            for m in far_masks[:-1]:
                total = line(add_low, total, swap(total, "mp", m, label))
            return total

        last_far = far_masks[-1]

        line = Line()

        out_slots = {0: w_out}
        for m in far_masks:
            out_slots.update(
                {j ^ m: swap(x, "mp", m, "gather_w_out") for j, x in list(out_slots.items())}
            )
        line.spare = ln1_gain[None]
        pos, place = wait(pos, place[None].astype(i32))
        first, qkv, summary = line(project, tokens, ln1_gain[None], ln1_bias[None], w_qkv)
        out_list = list(out_slots.items())
        sums = after(summary, *[x for _, x in out_list])[None]
        for i, m in enumerate(seq_masks):
            got = swap(sums, "dp", m, "summaries")
            if i == 0:
                exps, stats = line(local, qkv)
                for j, x in out_list:
                    out_slots[j ^ 1] = swap(after(x, stats), "mp", 1, "gather_w_out")
            sums = line(lambda a, b: jnp.concatenate([a, b]), sums, got)
        cores = wait(*[out_slots[j ^ 1] for j, _ in out_list])
        for (j, _), x in zip(out_list, cores):
            out_slots[j ^ 1] = x
        probs, attended = line(attend, place, qkv, exps, stats, sums)

        att_slots = {0: attended}
        for m in far_masks:
            att_slots.update(
                {j ^ m: swap(x, "mp", m, "gather_attended") for j, x in list(att_slots.items())}
            )
        for j, x in list(att_slots.items()):
            att_slots[j ^ 1] = swap(x, "mp", 1, "gather_attended")
        mid, second, active, grad_upper, theirs, mine, up_vec = line(
            feed,
            pos,
            tokens,
            *[att_slots[j] for j in range(n_mp)],
            *[out_slots[j] for j in range(n_mp)],
            b_out[None],
            ln2_gain[None],
            ln2_bias[None],
            w_up,
            b_up[None],
            w_down,
            cotangent,
        )

        total = near_sum(line(add_low, mine, swap(theirs, "mp", 1, "sum_second")), "sum_second")
        far = swap(total, "mp", last_far, "sum_second")
        other = swap(total, "mp", 1, "sum_second")
        out_theirs, out_mine, theirs, mine = line(
            weights, pos, active, second, grad_upper, cotangent, w_down
        )
        feed_sum = Scatter(line, theirs, mine, feed_masks, "feed_weights")
        out_got = swap(out_theirs, "mp", 1, "sum_output")
        line.space()
        out_total = near_sum(line(add_low, out_mine, out_got), "sum_output")
        (far,) = wait(far)
        other_far = swap(far, "mp", 1, "sum_second")
        out_send = after(out_total, far)
        out_far = swap(out_send, "mp", last_far, "sum_output")
        out_other = swap(out_send, "mp", 1, "sum_output")
        line.space()
        grad_low, gqkv, back_vec, slot_grad = line(
            lambda *a: (lambda r: (r[0], r[1], r[3], r[2]))(back(*a)),
            pos,
            total,
            far,
            other,
            other_far,
            mid,
            cotangent,
            ln2_gain[None],
            w_out,
            qkv,
            probs,
            sums,
        )

        feed_sum.step()
        (out_other,) = wait(out_other)
        theirs, mine = line(first_grad, pos, gqkv, slot_grad, sums, w_qkv, tokens)
        got = swap(theirs, "mp", 1, "sum_first")
        theirs_w, rest = line(
            rest_weights, first_bit, first, gqkv, grad_low, attended, slot_grad, sums
        )
        rest_got = swap(theirs_w, "dp", feed_masks[0], "rest_weights")
        total = line(pair, mine, got)
        for m in far_masks[:-1]:
            total = line(pair, total, swap(total, "mp", m, "sum_first"))
        far = swap(total, "mp", last_far, "sum_first")
        (out_far,) = wait(out_far)
        out_other_far = swap(out_far, "mp", 1, "sum_output")
        feed_sum.step()
        theirs_w, rest = line(split_first, bit_of(feed_masks[1]), rest, rest_got)
        rest_got = swap(theirs_w, "dp", feed_masks[1], "rest_weights")
        output = line(
            output_sum, pos, out_total, out_far, out_other, out_other_far, mid, b_down[None]
        )
        for m in feed_masks[3:]:
            feed_sum.step()
        feed_all = line(add_low, feed_sum.mine, feed_sum.got)
        feed_got = swap(feed_all, "dp", feed_masks[-1], "feed_weights")
        theirs_w, rest, extra = line(split_second, bit_of(feed_masks[2]), rest, rest_got, w_qkv)
        rest_got = swap(theirs_w, "dp", feed_masks[2], "rest_weights")
        extra_got = swap(extra, "mp", 1, "sum_extra")
        for m in feed_masks[3:]:
            theirs_w, rest = line(split_sum, bit_of(m), rest, rest_got)
            rest_got = swap(theirs_w, "dp", m, "rest_weights")
        for m in far_masks:
            line.space()
            extra = line(pl_add, extra, extra_got)
            extra_got = swap(extra, "mp", m, "sum_extra")
        (far,) = wait(far)
        other = swap(after(total, far), "mp", 1, "sum_first")
        other_far = swap(far, "mp", 1, "sum_first")
        grad_tokens = line(
            last,
            pos,
            total,
            far,
            other,
            other_far,
            extra,
            extra_got,
            tokens,
            grad_low,
            ln1_gain[None],
        )
        feed_next = list(reversed(feed_masks))[1:]
        rest_next = list(reversed(feed_masks))[1:]
        for m in feed_next[:-2]:
            feed_all = line(concat, feed_all, feed_got)
            feed_got = swap(feed_all, "dp", m, "feed_weights")
        feed_all = line(concat, feed_all, feed_got)
        two = swap(feed_all, "dp", feed_masks[0], "feed_weights")
        one = swap(feed_all, "dp", feed_masks[1], "feed_weights")
        rest_all = line(
            piece_of, rest, rest_got, total, far, back_vec, up_vec
        )
        rest_got = swap(rest_all, "dp", feed_masks[-1], "rest_weights")
        line.space()
        rest_all = line(merge, rest_all, rest_got)
        rest_got = swap(rest_all, "dp", rest_next[0], "rest_weights")
        (two,) = wait(two)
        both = swap(two, "dp", feed_masks[1], "feed_weights")
        for m in rest_next[1:]:
            line.space()
            rest_all = line(merge, rest_all, rest_got)
            rest_got = swap(rest_all, "dp", m, "rest_weights")
        line.space()
        grad_w_down, grad_w_up = line(
            feed_unpack, place_of(feed_masks), feed_all, one, two, both
        )
        grad_w_qkv, grad_w_out, *vectors = line(
            rest_unpack, place_of(feed_masks), rest_all, rest_got, line.spare
        )
        return (
            output,
            grad_tokens,
            vectors[0][0],
            vectors[1][0],
            grad_w_qkv,
            grad_w_out,
            vectors[2][0],
            vectors[3][0],
            vectors[4][0],
            grad_w_up.reshape(dim, hidden),
            vectors[6][0],
            grad_w_down,
            vectors[5][0],
        )

    return per_device


def solution(mesh):
    return jax.shard_map(
        build(mesh.shape["dp"], mesh.shape["mp"]),
        mesh=mesh,
        in_specs=(
            P("dp", None),
            P(),
            P(),
            P(None, None, "mp"),
            P("mp", None),
            P(),
            P(),
            P(),
            P(None, "mp"),
            P("mp"),
            P("mp", None),
            P(),
            P("dp", None),
        ),
        out_specs=(
            P("dp", None),
            P("dp", None),
            P(),
            P(),
            P(None, None, "mp"),
            P("mp", None),
            P(),
            P(),
            P(),
            P(None, "mp"),
            P("mp"),
            P("mp", None),
            P(),
        ),
        check_vma=False,
    )
```

```python
import functools
import math

import jax
import jax.numpy as jnp
from jax import lax
from jax.experimental import pallas as pl
from jax.experimental.pallas import tpu as pltpu
from jax.sharding import PartitionSpec as P

HEAD_DIM = 64
SPAN = 128
LENGTH = 4096
EPSILON = 1e-05
SCALE = HEAD_DIM ** (-0.5)
LOW = -1e30

f32 = jnp.float32
bf16 = jnp.bfloat16
i32 = jnp.int32
VMEM = pl.BlockSpec(memory_space=pltpu.VMEM)
SMEM = pl.BlockSpec(memory_space=pltpu.SMEM)


def masks_of(count):
    return [1 << i for i in range(count.bit_length() - 1)]


def params(mib=60):
    return pltpu.CompilerParams(vmem_limit_bytes=mib * 1024 * 1024)


def cost():
    return pl.CostEstimate(flops=115_000_000_000, bytes_accessed=1, transcendentals=0)


def nt(a, b):
    return lax.dot_general(a, b, (((1,), (1,)), ((), ())), preferred_element_type=f32)


def tn(a, b):
    return lax.dot_general(a, b, (((0,), (0,)), ((), ())), preferred_element_type=f32)


def nn(a, b):
    return jnp.dot(a, b, preferred_element_type=f32)


def normed(x):
    c = x - jnp.mean(x, axis=-1, keepdims=True)
    r = lax.rsqrt(jnp.mean(c * c, axis=-1, keepdims=True) + EPSILON)
    return c * r, r


def norm_back(e, n, r, gain):
    k = e * gain
    return r * (
        k - jnp.mean(k, axis=-1, keepdims=True) - n * jnp.mean(k * n, axis=-1, keepdims=True)
    )


def fold(x):
    return jnp.sum(x.reshape(-1, 8, x.shape[-1]), axis=0)


def head_mask(shape, h, dtype):
    lane = lax.broadcasted_iota(i32, shape, len(shape) - 1)
    return jnp.where(lane // HEAD_DIM == h, 1.0, 0.0).astype(dtype)


def spread(x, factor):
    heads = x.shape[1] // HEAD_DIM
    return jnp.concatenate(
        [x * (head_mask((1, x.shape[1]), h, f32) * factor).astype(x.dtype) for h in range(heads)]
    )


def collect(x, factor):
    width = x.shape[1]
    heads = width // HEAD_DIM
    rows = x.shape[0] // heads
    total = x[:rows] * (head_mask((1, width), 0, f32) * factor)
    for h in range(1, heads):
        total = total + x[h * rows : (h + 1) * rows] * (head_mask((1, width), h, f32) * factor)
    return total


def to_low(v, cols):
    v = jnp.concatenate([v[:, i : i + cols] for i in range(0, v.shape[1], cols)])
    high = v.astype(bf16)
    return jnp.concatenate([high, (v - high.astype(f32)).astype(bf16)])


def from_low(x, dim):
    half = x.shape[0] // 2
    v = x[:half].astype(f32) + x[half:].astype(f32)
    count = dim // x.shape[1]
    return jnp.concatenate([v[i * 8 : (i + 1) * 8] for i in range(count)], axis=1)


def columns_of(sums_ref, start, count):
    slots, _, blocks, width = sums_ref.shape
    parts = [sums_ref[:, start + j].reshape(slots * blocks, width) for j in range(count)]
    return jnp.concatenate(parts, axis=1)


def project_kernel(tile, tok_ref, gain_ref, bias_ref, w_ref, first_ref, qkv_ref, sum_ref, wcat):
    width = w_ref.shape[2]
    for s in range(3):
        wcat[:, s * width : (s + 1) * width] = w_ref[s]
    per = tile // SPAN
    for i in range(tok_ref.shape[0] // tile):
        at = slice(i * tile, (i + 1) * tile)
        n, _ = normed(tok_ref[at].astype(f32))
        first = (n * gain_ref[...] + bias_ref[...]).astype(bf16)
        first_ref[at] = first
        both = nn(first, wcat[...]).astype(bf16)
        for s in range(3):
            part = both[:, s * width : (s + 1) * width]
            qkv_ref[s, at] = part
            if s:
                mean = jnp.mean(part.astype(f32).reshape(per, SPAN, width), axis=1)
                sum_ref[s - 1, i * per : (i + 1) * per] = mean.astype(bf16).astype(f32)
        sums = [jnp.sum(x.reshape(per, SPAN, -1), axis=1) for x in (first.astype(f32), n)]
        total = jnp.concatenate(sums, axis=1)
        for j in range(sum_ref.shape[0] - 2):
            sum_ref[2 + j, i * per : (i + 1) * per] = total[:, j * width : (j + 1) * width]


def local_kernel(qkv_ref, exp_ref, stat_ref):
    blocks = exp_ref.shape[0]
    lanes = exp_ref.shape[2]
    key = lax.broadcasted_iota(i32, (SPAN, lanes), 0)
    query = lax.broadcasted_iota(i32, (SPAN, lanes), 1) % SPAN
    keep = key <= query
    for b in range(blocks):
        at = slice(b * SPAN, (b + 1) * SPAN)
        s = nt(qkv_ref[1, at], spread(qkv_ref[0, at], SCALE))
        s = jnp.where(keep, s, LOW)
        top = jnp.max(s, axis=0, keepdims=True)
        e = jnp.exp(s - top)
        exp_ref[b] = e
        stat_ref[b, 0:1] = top
        stat_ref[b, 1:2] = jnp.sum(e, axis=0, keepdims=True)


def attend_kernel(place_ref, qkv_ref, exp_ref, stat_ref, sums_ref, prob_ref, att_ref):
    blocks = exp_ref.shape[0]
    lanes = exp_ref.shape[2]
    slots = sums_ref.shape[0]
    place = place_ref[0]
    keys = sums_ref[:, 0].reshape(slots * blocks, -1).astype(bf16)
    values = sums_ref[:, 1].reshape(slots * blocks, -1).astype(bf16)
    row = lax.broadcasted_iota(i32, (slots * blocks, lanes), 0)
    at_block = ((row // blocks) ^ place) * blocks + row % blocks
    for b in range(blocks):
        at = slice(b * SPAN, (b + 1) * SPAN)
        s = nt(keys, spread(qkv_ref[0, at], SCALE)) + math.log(SPAN)
        s = jnp.where(at_block < place * blocks + b, s, LOW)
        mine = stat_ref[b, 0:1]
        top = jnp.maximum(mine, jnp.max(s, axis=0, keepdims=True))
        e = jnp.exp(s - top)
        shrink = jnp.exp(mine - top)
        scale = 1.0 / (stat_ref[b, 1:2] * shrink + jnp.sum(e, axis=0, keepdims=True))
        p = jnp.concatenate([exp_ref[b] * (shrink * scale), e * scale]).astype(bf16)
        prob_ref[b] = p
        a = tn(p, jnp.concatenate([qkv_ref[2, at], values]))
        att_ref[at] = collect(a, 1.0).astype(bf16)


def feed_kernel(
    count, pos_ref, tok_ref, *refs
):
    att = refs[:count]
    wo = refs[count : 2 * count]
    (
        b_out_ref,
        gain_ref,
        bias_ref,
        up_ref,
        b_up_ref,
        down_ref,
        cot_ref,
        mid_ref,
        second_ref,
        active_ref,
        grad_ref,
        theirs_ref,
        mine_ref,
        vec_ref,
        wcat,
    ) = refs[2 * count :]
    step = pl.program_id(0)
    me = pos_ref[0]
    width = wo[0].shape[0]

    def in_order(arrays):
        arrays = list(arrays)
        for m in masks_of(count):
            flip = (me & m) != 0
            arrays = [jnp.where(flip, arrays[j ^ m], arrays[j]) for j in range(count)]
        return arrays

    @pl.when(step == 0)
    def _():
        for j in range(count):
            wcat[pl.ds(pl.multiple_of((me ^ j) * width, width), width)] = wo[j][...]
        vec_ref[...] = jnp.zeros_like(vec_ref)

    attended = jnp.concatenate(in_order([a[...] for a in att]), axis=1)
    mid = tok_ref[...].astype(f32) + nn(attended, wcat[...]) + b_out_ref[...]
    mid_ref[...] = mid
    n, _ = normed(mid)
    second = (n * gain_ref[...] + bias_ref[...]).astype(bf16)
    second_ref[...] = second
    u = nn(second, up_ref[...]) + b_up_ref[...]
    root = math.sqrt(2.0 / math.pi)
    square = u * u
    t = jnp.tanh(u * (root + root * 0.044715 * square))
    half = 0.5 + 0.5 * t
    active_ref[...] = (u * half).astype(bf16)
    slope = half + (0.5 * u) * (1.0 - t * t) * (root + (3.0 * root * 0.044715) * square)
    grad = nt(cot_ref[...], down_ref[...]) * slope
    low = grad.astype(bf16)
    grad_ref[...] = low
    out = nt(low, up_ref[...]).astype(bf16)
    steps = pl.num_programs(0)

    @pl.when(step < steps // 2)
    def _():
        theirs_ref[...] = out

    @pl.when(step >= steps // 2)
    def _():
        mine_ref[...] = out

    vec_ref[0:8] += fold(low.astype(f32))


def weights_kernel(
    pos_ref,
    active_ref,
    second_ref,
    grad_ref,
    cot_ref,
    down_ref,
    out_theirs_ref,
    out_mine_ref,
    theirs_ref,
    mine_ref,
    down_acc,
    up_acc,
):
    step = pl.program_id(0)
    terms = nn(active_ref[...], down_ref[...]).astype(bf16)
    down = tn(active_ref[...], cot_ref[...])
    up = tn(second_ref[...], grad_ref[...])

    @pl.when(step == 0)
    def _():
        out_theirs_ref[...] = terms
        down_acc[...] = down
        up_acc[...] = up

    @pl.when(step == 1)
    def _():
        out_mine_ref[...] = terms
        first = (down_acc[...] + down).astype(bf16)
        then = (up_acc[...] + up).astype(bf16).reshape(first.shape)
        low = pos_ref[3] == 0
        theirs_ref[...] = jnp.where(low, then, first)
        mine_ref[...] = jnp.where(low, first, then)


def rest_kernel(
    bit_ref, first_ref, gqkv_ref, low_ref, att_ref, slot_ref, sums_ref, theirs_ref, mine_ref
):
    slots, _, blocks, width = slot_ref.shape
    dim = first_ref.shape[1]
    size = dim // 2
    rows = [slot_ref[:, s].reshape(slots * blocks, width) for s in range(2)]
    far_rows = (jnp.concatenate(rows, axis=1) * (1.0 / SPAN)).astype(bf16)
    far_first = columns_of(sums_ref, 2, dim // width).astype(bf16)
    out = []
    for h in range(2):
        at = slice(h * size, (h + 1) * size)
        main = tn(first_ref[:, at], gqkv_ref[...])
        far = tn(far_first[:, at], far_rows)
        last = tn(low_ref[:, at], att_ref[...])
        out.append(
            jnp.concatenate([main[:, :width], main[:, width:] + far, last], axis=1).astype(bf16)
        )
    low = bit_ref[0] == 0
    theirs_ref[:size] = jnp.where(low, out[1], out[0])
    mine_ref[:size] = jnp.where(low, out[0], out[1])
    for ref, slot in ((theirs_ref, 2), (mine_ref, 0)):
        parts = [slot_ref[j, s] for j in (slot, slot + 1) for s in range(2)]
        ref[size:] = to_low(jnp.concatenate(parts, axis=1), 4 * width)


def split_first_kernel(bit_ref, a_ref, b_ref, theirs_ref, mine_ref):
    rows = a_ref.shape[0] - 16
    cols = a_ref.shape[1]
    size = rows // 2
    total = (a_ref[:rows].astype(f32) + b_ref[:rows].astype(f32)).astype(bf16)
    low = bit_ref[0] == 0
    theirs_ref[:size] = jnp.where(low, total[size:], total[:size])
    mine_ref[:size] = jnp.where(low, total[:size], total[size:])
    slots = from_low(a_ref[rows:], cols) + from_low(b_ref[rows:], cols)
    none = jnp.zeros((8, cols // 2), f32)
    for ref, at in ((theirs_ref, slice(cols // 2, cols)), (mine_ref, slice(0, cols // 2))):
        ref[size:] = to_low(jnp.concatenate([slots[:, at], none], axis=1), cols)


def split_second_kernel(bit_ref, a_ref, b_ref, w_ref, theirs_ref, mine_ref, extra_ref):
    rows = a_ref.shape[0] - 16
    cols = a_ref.shape[1]
    width = w_ref.shape[2]
    size = rows // 2
    total = (a_ref[:rows].astype(f32) + b_ref[:rows].astype(f32)).astype(bf16)
    low = bit_ref[0] == 0
    theirs_ref[...] = jnp.where(low, total[size:], total[:size])
    mine_ref[...] = jnp.where(low, total[:size], total[size:])
    own = from_low(a_ref[rows:], cols) + from_low(b_ref[rows:], cols)
    own = (own * (1.0 / SPAN)).astype(bf16)
    extra_ref[...] = nt(own[:, :width], w_ref[1]) + nt(own[:, width : 2 * width], w_ref[2])


def split_kernel(bit_ref, a_ref, b_ref, theirs_ref, mine_ref):
    total = (a_ref[...].astype(f32) + b_ref[...].astype(f32)).astype(bf16)
    size = total.shape[0] // 2
    low = bit_ref[0] == 0
    theirs_ref[...] = jnp.where(low, total[size:], total[:size])
    mine_ref[...] = jnp.where(low, total[:size], total[size:])


def two_halves(refs, half, core):
    own, far, other, other_far = refs
    mine = half == core
    a = jnp.where(mine, own[...], other[...])
    b = jnp.where(mine, far[...], other_far[...])
    return a.astype(f32) + b.astype(f32)


def back_kernel(
    pos_ref,
    own_ref,
    far_ref,
    other_ref,
    other_far_ref,
    mid_ref,
    cot_ref,
    gain_ref,
    wo_ref,
    qkv_ref,
    prob_ref,
    sums_ref,
    low_ref,
    gqkv_ref,
    slot_ref,
    vec_ref,
):
    step = pl.program_id(0)
    slots = sums_ref.shape[0]
    width = wo_ref.shape[0]

    @pl.when(step == 0)
    def _():
        slot_ref[...] = jnp.zeros_like(slot_ref)
        vec_ref[...] = jnp.zeros_like(vec_ref)

    e = two_halves((own_ref, far_ref, other_ref, other_far_ref), step, pos_ref[1])
    n, r = normed(mid_ref[...])
    cot = cot_ref[...].astype(f32)
    grad_mid = cot + norm_back(e, n, r, gain_ref[...])
    low = grad_mid.astype(bf16)
    low_ref[...] = low
    vec_ref[0:8] += fold(grad_mid)
    vec_ref[8:16] += fold(e * n)
    vec_ref[16:24] += fold(e)
    vec_ref[24:32] += fold(cot)

    grad_att = nt(low, wo_ref[...]).astype(bf16)
    far_keys = sums_ref[:, 0].reshape(-1, width).astype(bf16)
    far_values = sums_ref[:, 1].reshape(-1, width).astype(bf16)
    far_gk = jnp.zeros(far_keys.shape, f32)
    far_gv = jnp.zeros(far_keys.shape, f32)
    for b in range(prob_ref.shape[0]):
        at = slice(b * SPAN, (b + 1) * SPAN)
        da = spread(grad_att[at], 1.0)
        query = spread(qkv_ref[0, at], SCALE)
        keys = jnp.concatenate([qkv_ref[1, at], far_keys])
        values = jnp.concatenate([qkv_ref[2, at], far_values])
        p_low = prob_ref[b]
        p = p_low.astype(f32)
        dp = nt(values, da)
        ds = (p * (dp - jnp.sum(p * dp, axis=0, keepdims=True))).astype(bf16)
        gq = collect(tn(ds, keys), SCALE)
        gk = nn(ds, query)
        gv = nn(p_low, da)
        gqkv_ref[at, :width] = gq.astype(bf16)
        gqkv_ref[at, width : 2 * width] = gk[:SPAN].astype(bf16)
        gqkv_ref[at, 2 * width :] = gv[:SPAN].astype(bf16)
        far_gk = far_gk + gk[SPAN:]
        far_gv = far_gv + gv[SPAN:]
    slot_ref[:, 0] += far_gk.reshape(slots, -1, width)
    slot_ref[:, 1] += far_gv.reshape(slots, -1, width)


def first_kernel(
    pos_ref, gqkv_ref, slot_ref, sums_ref, w_ref, tok_ref, theirs_ref, mine_ref, wcat, vec
):
    step = pl.program_id(0)
    steps = pl.num_programs(0)
    dim, width = w_ref.shape[1:]
    tile = gqkv_ref.shape[0]
    half = tile * (steps // 2)

    @pl.when(step == 0)
    def _():
        vec[...] = jnp.zeros_like(vec)
        for s in range(3):
            wcat[:, s * width : (s + 1) * width] = w_ref[s]

    e = nt(gqkv_ref[...], wcat[...])
    n, _ = normed(tok_ref[...].astype(f32))
    vec[0:8] += fold(e * n)
    vec[8:16] += fold(e)
    out = e.astype(bf16)
    at = pl.ds(pl.multiple_of((step % (steps // 2)) * tile, tile), tile)

    @pl.when(step < steps // 2)
    def _():
        theirs_ref[at] = out

    @pl.when(step >= steps // 2)
    def _():
        mine_ref[at] = out

    @pl.when(step == steps - 1)
    def _():
        rows = [
            (slot_ref[:, s].reshape(-1, width) * (1.0 / SPAN)).astype(bf16) for s in range(2)
        ]
        far = nt(rows[0], w_ref[1]) + nt(rows[1], w_ref[2])
        normal = columns_of(sums_ref, 2 + dim // width, dim // width)
        gain = jnp.sum(vec[0:8], axis=0, keepdims=True) + jnp.sum(
            far * normal, axis=0, keepdims=True
        )
        offset = jnp.sum(vec[8:16], axis=0, keepdims=True) + SPAN * jnp.sum(
            far, axis=0, keepdims=True
        )
        low = to_low(jnp.concatenate([gain, offset, jnp.zeros((6, dim), f32)]), dim)
        theirs_ref[half:] = low
        mine_ref[half:] = low


def pair_kernel(a_ref, b_ref, out_ref):
    dim = a_ref.shape[1]
    rows = a_ref.shape[0] - 16
    out_ref[:rows] = (a_ref[:rows].astype(f32) + b_ref[:rows].astype(f32)).astype(bf16)
    out_ref[rows:] = to_low(from_low(a_ref[rows:], dim) + from_low(b_ref[rows:], dim), dim)


def piece_kernel(mine_ref, got_ref, near_ref, far_ref, back_ref, up_ref, out_ref):
    dim = near_ref.shape[1]
    hidden = up_ref.shape[1]
    rows, cols = mine_ref.shape
    out_ref[:rows] = (mine_ref[...].astype(f32) + got_ref[...].astype(f32)).astype(bf16)
    last = near_ref.shape[0] - 16
    first = (from_low(near_ref[last:], dim) + from_low(far_ref[last:], dim))[:2]
    vectors = [first]
    for k in range(4):
        vectors.append(jnp.sum(back_ref[8 * k : 8 * k + 8], axis=0, keepdims=True))
    up = jnp.sum(up_ref[...], axis=0, keepdims=True)
    if hidden < dim:
        up = jnp.concatenate([up, jnp.zeros((1, dim - hidden), f32)], axis=1)
    vectors += [up, jnp.zeros((1, dim), f32)]
    out_ref[rows:] = to_low(jnp.concatenate(vectors), cols)


def merge_kernel(dim, a_ref, b_ref, out_ref):
    cols = a_ref.shape[1]
    rows = a_ref.shape[0] - 16 * (dim // cols)
    out_ref[:rows] = a_ref[:rows]
    out_ref[rows : 2 * rows] = b_ref[:rows]
    out_ref[2 * rows :] = to_low(from_low(a_ref[rows:], dim) + from_low(b_ref[rows:], dim), cols)


def last_kernel(
    pos_ref,
    own_ref,
    far_ref,
    other_ref,
    other_far_ref,
    extra_ref,
    extra_far_ref,
    tok_ref,
    low_ref,
    gain_ref,
    out_ref,
):
    step = pl.program_id(0)
    half = step // (pl.num_programs(0) // 2)
    e = two_halves((own_ref, far_ref, other_ref, other_far_ref), half, pos_ref[1])
    per = e.shape[0] // SPAN
    pieces = []
    for i in range(per):
        at = pl.ds(step * per + i, 1)
        pieces.append(e[i * SPAN : (i + 1) * SPAN] + (extra_ref[at] + extra_far_ref[at]))
    e = jnp.concatenate(pieces)
    n, r = normed(tok_ref[...].astype(f32))
    out_ref[...] = (low_ref[...].astype(f32) + norm_back(e, n, r, gain_ref[...])).astype(bf16)


def add_kernel(parts, a_ref, b_ref, *out_refs):
    size = a_ref.shape[0] // parts
    for k in range(parts):
        at = slice(k * size, (k + 1) * size)
        out_refs[k][...] = (a_ref[at].astype(f32) + b_ref[at].astype(f32)).astype(bf16)


def slot_kernel(a_ref, b_ref, out_ref):
    out_ref[...] = a_ref[: out_ref.shape[0]] + b_ref[...]


def spacer_kernel(x_ref, out_ref):
    out_ref[...] = x_ref[...] * 0.5


def concat_kernel(a_ref, b_ref, out_ref):
    rows = a_ref.shape[0]
    out_ref[:rows] = a_ref[...]
    out_ref[rows:] = b_ref[...]


def output_kernel(
    pos_ref, own_ref, far_ref, other_ref, other_far_ref, mid_ref, b_ref, out_ref
):
    half = pl.program_id(0) // (pl.num_programs(0) // 2)
    e = two_halves((own_ref, far_ref, other_ref, other_far_ref), half, pos_ref[1])
    out_ref[...] = (mid_ref[...] + e + b_ref[...]).astype(bf16)


def feed_unpack_kernel(pieces, far, at_ref, own_ref, one_ref, *refs):
    down_ref, up_ref, scratch, sems = refs[-4:]
    rows = own_ref.shape[0]
    size = rows // pieces
    top = at_ref[0] // pieces
    low = at_ref[0] % pieces

    def copies(ref):
        return [
            pltpu.make_async_copy(
                scratch.at[pl.ds(q * rows, rows)], ref.at[pl.ds(q * rows, rows)], sems.at[q]
            )
            for q in range(2)
        ]

    def fill(ref):
        out = copies(ref)
        for q in range(2):
            for k in range(pieces):
                at = pl.ds(pl.multiple_of((k ^ low) * size, size), size)
                x = jnp.where(top % 2 == q, own_ref[at], one_ref[at])
                scratch[q * rows + k * size : q * rows + (k + 1) * size] = x.astype(f32)
            out[q].start()
        for q in range(2):
            out[q].wait()

    is_down = top // 2 == far

    @pl.when(is_down)
    def _():
        fill(down_ref)

    @pl.when(jnp.logical_not(is_down))
    def _():
        fill(up_ref)


def rest_unpack_kernel(
    count, dim, at_ref, near_ref, far_ref, spare_ref, qkv_ref, out_ref, *refs
):
    vec_refs, scratch = refs[:-1], refs[-1]
    cols = near_ref.shape[1]
    last = near_ref.shape[0] - 16 * (dim // cols)
    rows = 2 * last // count
    width = qkv_ref.shape[2]
    part = count // 2
    top = at_ref[0] // part
    low = at_ref[0] % part
    for k in range(count):
        start = pl.multiple_of(((k % part) ^ low) * rows, rows)
        is_near = top == k // part
        x = jnp.where(is_near, near_ref[pl.ds(start, rows)], far_ref[pl.ds(start, rows)])
        x = x.astype(f32)
        for s in range(3):
            qkv_ref[s, k * rows : (k + 1) * rows] = x[:, s * width : (s + 1) * width]
        scratch[k * rows : (k + 1) * rows] = x[:, 3 * width :]
    out_ref[...] = scratch[...].T
    vectors = from_low(near_ref[last:], dim) + from_low(far_ref[last:], dim)
    for k, ref in enumerate(vec_refs):
        ref[...] = vectors[k : k + 1, : ref.shape[1]]


def build(n_dp, n_mp):
    def swap(x, axis, mask, label):
        n = n_dp if axis == "dp" else n_mp
        with jax.named_scope(label):
            return lax.ppermute(x, axis, [(i, i ^ mask) for i in range(n)])

    def pick(x, index, rows):
        return lax.dynamic_slice_in_dim(x, index * rows, rows, 0)

    def halves(x, mask, axis):
        bit = jnp.where((lax.axis_index(axis) & mask) == 0, 0, 1)
        size = x.shape[0] // 2
        return pick(x, 1 - bit, size), pick(x, bit, size)

    def after(x, *others):
        return lax.optimization_barrier((x, others))[0]

    far_masks = masks_of(n_mp)[1:]
    dp_masks = masks_of(n_dp)
    feed_masks = [dp_masks[1], dp_masks[0]] + dp_masks[2:]

    class Line:
        def __init__(self):
            self.last = ()

        def __call__(self, work, *inputs):
            if self.last:
                inputs = after(inputs, *self.last)
            result = work(*inputs)
            first = result[-1] if isinstance(result, (tuple, list)) else result
            self.last = (first,)
            return result

        def space(self, x=None):
            if x is not None:
                self.spare = x
            self.spare = self(spacer, self.spare)

    def add_parts(parts, a, b):
        part = jax.ShapeDtypeStruct((a.shape[0] // parts, *a.shape[1:]), bf16)
        return pl.pallas_call(
            functools.partial(add_kernel, parts),
            out_shape=(part,) * parts,
            in_specs=[VMEM, VMEM],
            out_specs=(VMEM,) * parts,
            compiler_params=params(16),
            cost_estimate=cost(),
            name="add",
        )(a, b)

    def add_low(a, b):
        return add_parts(1, a, b)[0]

    def spacer(x):
        return pl.pallas_call(
            spacer_kernel,
            out_shape=jax.ShapeDtypeStruct(x.shape, x.dtype),
            in_specs=[VMEM],
            out_specs=VMEM,
            compiler_params=params(16),
            cost_estimate=cost(),
            name="spacer",
        )(x)

    def split_sum(bit, mine, got):
        size = mine.shape[0] // 2
        half = jax.ShapeDtypeStruct((size, mine.shape[1]), bf16)
        return pl.pallas_call(
            split_kernel,
            out_shape=(half, half),
            in_specs=[SMEM, VMEM, VMEM],
            out_specs=(VMEM, VMEM),
            compiler_params=params(16),
            cost_estimate=cost(),
            name="split",
        )(bit, mine, got)

    def bit_of(mask):
        return jnp.where((lax.axis_index("dp") & mask) == 0, 0, 1).astype(i32)[None]

    class Scatter:
        def __init__(self, line, theirs, mine, masks, label):
            self.line, self.label = line, label
            self.rest = list(masks)
            self.mine = mine
            self.got = swap(theirs, "dp", self.rest.pop(0), label)

        def step(self):
            mask = self.rest.pop(0)
            theirs, self.mine = self.line(split_sum, bit_of(mask), self.mine, self.got)
            self.got = swap(theirs, "dp", mask, self.label)

    def per_device(
        tokens,
        ln1_gain,
        ln1_bias,
        w_qkv,
        w_out,
        b_out,
        ln2_gain,
        ln2_bias,
        w_up,
        b_up,
        w_down,
        b_down,
        cotangent,
    ):
        rows, dim = tokens.shape
        width = w_qkv.shape[2]
        hidden = w_up.shape[1]
        heads = width // HEAD_DIM
        blocks = rows // SPAN
        lanes = heads * SPAN
        group = LENGTH // rows
        entries = SPAN + group * blocks
        seq_masks = masks_of(group)
        me = lax.axis_index("mp")
        place = lax.axis_index("dp") % group
        first_bit = bit_of(feed_masks[0])
        pos = jnp.concatenate(
            [jnp.stack([me, me & 1, place]).astype(i32), bit_of(feed_masks[0])]
        )
        half = rows // 2
        tile = half // 2
        tiles = 4
        sds = jax.ShapeDtypeStruct

        def rolled(i, pos):
            return ((i + (1 - pos[1]) * (tiles // 2)) % tiles, 0)

        def theirs_row(i, pos):
            return (jnp.minimum(i, tiles // 2 - 1), 0)

        def mine_row(i, pos):
            return (jnp.maximum(i - tiles // 2, 0), 0)

        def half_rolled(i, pos):
            return (jnp.where(i == 0, 1 - pos[1], pos[1]), 0)

        def whole(*_):
            return (0, 0)

        def by_row(i, *_):
            return (i, 0)

        def zeros(n):
            return lambda *_: (0,) * n

        def block(shape, index):
            return pl.BlockSpec(shape, index)

        def plain(kernel, name, in_specs, out_shape, scratch=(), mib=24):
            return pl.pallas_call(
                kernel,
                out_shape=out_shape,
                in_specs=in_specs,
                out_specs=tuple(VMEM for _ in out_shape),
                scratch_shapes=list(scratch),
                compiler_params=params(mib),
                cost_estimate=cost(),
                name=name,
            )

        def gridded(
            kernel, name, grid, in_specs, out_specs, out_shape, scratch=(), mib=60, aliases=None
        ):
            return pl.pallas_call(
                kernel,
                grid_spec=pltpu.PrefetchScalarGridSpec(
                    num_scalar_prefetch=1,
                    grid=(grid,),
                    in_specs=in_specs,
                    out_specs=out_specs,
                    scratch_shapes=list(scratch),
                ),
                out_shape=out_shape,
                input_output_aliases=aliases or {},
                compiler_params=params(60 if name in ('feed',) else 30 if name in ('back', 'weights') else 20),
                cost_estimate=cost(),
                name=name,
            )

        row_block = block((tile, dim), rolled)
        row_vector = block((1, dim), whole)
        tile_block = block((tile, dim), by_row)
        one_tile = block((tile, dim), whole)

        project = plain(
            functools.partial(project_kernel, tile),
            "project",
            [VMEM] * 4,
            (
                sds((rows, dim), bf16),
                sds((3, rows, width), bf16),
                sds((2 + 2 * (dim // width), blocks, width), f32),
            ),
            [pltpu.VMEM((dim, 3 * width), bf16)],
            60,
        )
        local = plain(
            local_kernel,
            "local",
            [VMEM],
            (sds((blocks, SPAN, lanes), f32), sds((blocks, 2, lanes), f32)),
        )
        attend = plain(
            attend_kernel,
            "attend",
            [SMEM] + [VMEM] * 4,
            (sds((blocks, entries, lanes), bf16), sds((rows, width), bf16)),
        )
        half_rows = block((half, dim), half_rolled)
        half_hidden = block((half, hidden), half_rolled)
        feed = gridded(
            functools.partial(feed_kernel, n_mp),
            "feed",
            2,
            [half_rows]
            + [block((half, width), half_rolled)] * n_mp
            + [block((width, dim), whole)] * n_mp
            + [row_vector] * 3
            + [
                block((dim, hidden), whole),
                block((1, hidden), whole),
                block((hidden, dim), whole),
                half_rows,
            ],
            [
                half_rows,
                half_rows,
                half_hidden,
                half_hidden,
                block((half, dim), whole),
                block((half, dim), whole),
                block((8, hidden), whole),
            ],
            (
                sds((rows, dim), f32),
                sds((rows, dim), bf16),
                sds((rows, hidden), bf16),
                sds((rows, hidden), bf16),
                sds((half, dim), bf16),
                sds((half, dim), bf16),
                sds((8, hidden), f32),
            ),
            [pltpu.VMEM((dim, dim), bf16)],
        )
        weights = gridded(
            weights_kernel,
            "weights",
            2,
            [half_hidden, half_rows, half_hidden, half_rows, block((hidden, dim), whole)],
            [block((half, dim), whole)] * 2 + [block((hidden, dim), whole)] * 2,
            (
                sds((half, dim), bf16),
                sds((half, dim), bf16),
                sds((hidden, dim), bf16),
                sds((hidden, dim), bf16),
            ),
            [pltpu.VMEM((hidden, dim), f32), pltpu.VMEM((dim, hidden), f32)],
        )
        rest_weights = plain(
            rest_kernel,
            "rest_weights",
            [SMEM] + [VMEM] * 6,
            (sds((dim // 2 + 16, 4 * width), bf16), sds((dim // 2 + 16, 4 * width), bf16)),
            mib=60,
        )
        slot_shape = (group, 2, blocks, width)
        sums_shape = (group, 2 + 2 * (dim // width), blocks, width)
        back = gridded(
            back_kernel,
            "back",
            2,
            [block((half, dim), whole)] * 4
            + [
                block((half, dim), by_row),
                block((half, dim), by_row),
                row_vector,
                block((width, dim), whole),
                block((3, half, width), lambda i, pos: (0, i, 0)),
                block((blocks // 2, entries, lanes), lambda i, pos: (i, 0, 0)),
                block(sums_shape, zeros(4)),
            ],
            [
                block((half, dim), by_row),
                block((half, 3 * width), by_row),
                block(slot_shape, zeros(4)),
                block((32, dim), whole),
            ],
            (
                sds((rows, dim), bf16),
                sds((rows, 3 * width), bf16),
                sds(slot_shape, f32),
                sds((32, dim), f32),
            ),
        )
        first_block = block((half + 16, dim), whole)
        first_grad = gridded(
            first_kernel,
            "first",
            2,
            [
                block((half, 3 * width), half_rolled),
                block(slot_shape, zeros(4)),
                block(sums_shape, zeros(4)),
                block((3, dim, width), zeros(3)),
                half_rows,
            ],
            [first_block, first_block],
            (sds((half + 16, dim), bf16), sds((half + 16, dim), bf16)),
            [pltpu.VMEM((dim, 3 * width), bf16), pltpu.VMEM((16, dim), f32)],
        )
        def own_tile(i, pos):
            return (jnp.clip(i - pos[1] * (tiles // 2), 0, tiles // 2 - 1), 0)

        def other_tile(i, pos):
            return (jnp.clip(i - (1 - pos[1]) * (tiles // 2), 0, tiles // 2 - 1), 0)

        terms_specs = [block((half, dim), whole)] * 4
        tile_block = block((half, dim), by_row)
        last = gridded(
            last_kernel,
            "last",
            2,
            terms_specs + [block((blocks, dim), whole)] * 2 + [tile_block, tile_block, row_vector],
            tile_block,
            sds((rows, dim), bf16),
        )
        output_sum = gridded(
            output_kernel,
            "output",
            2,
            terms_specs + [tile_block, row_vector],
            tile_block,
            sds((rows, dim), bf16),
        )
        def feed_unpack(at, own, one, *held):
            anywhere = pl.BlockSpec(memory_space=pl.ANY)
            return pl.pallas_call(
                functools.partial(feed_unpack_kernel, n_dp // 4, 1 if held else 0),
                out_shape=(sds((hidden, dim), f32), sds((hidden, dim), f32)),
                in_specs=[SMEM, VMEM, VMEM] + [anywhere] * len(held),
                out_specs=(anywhere, anywhere),
                scratch_shapes=[pltpu.VMEM((hidden, dim), f32), pltpu.SemaphoreType.DMA((2,))],
                input_output_aliases={3 + k: k for k in range(len(held))},
                compiler_params=params(20),
                cost_estimate=cost(),
                name="feed_unpack",
            )(at, own, one, *held)

        rest_unpack = plain(
            functools.partial(rest_unpack_kernel, n_dp, dim),
            "rest_unpack",
            [SMEM, VMEM, VMEM, VMEM],
            (sds((3, dim, width), f32), sds((width, dim), f32))
            + (sds((1, dim), f32),) * 6
            + (sds((1, hidden), f32),),
            [pltpu.VMEM((dim, width), f32)],
        )

        def like(kernel, name, shape, dtype, *operands):
            specs = [VMEM] * len(operands)
            return plain(kernel, name, specs, (sds(shape, dtype),))(*operands)[0]

        def pair(a, b):
            return like(pair_kernel, "pair", a.shape, bf16, a, b)

        def concat(a, b):
            return like(concat_kernel, "concat", (2 * a.shape[0], a.shape[1]), bf16, a, b)

        def pl_add(a, b):
            return like(slot_kernel, "plus", a.shape, f32, a, b)

        cols = 4 * width
        quarter = dim // 4
        split_first = plain(
            split_first_kernel,
            "split_first",
            [SMEM, VMEM, VMEM],
            (sds((quarter + 16, cols), bf16), sds((quarter + 16, cols), bf16)),
        )
        split_second = plain(
            split_second_kernel,
            "split_second",
            [SMEM, VMEM, VMEM, VMEM],
            (
                sds((quarter // 2, cols), bf16),
                sds((quarter // 2, cols), bf16),
                sds((blocks, dim), f32),
            ),
        )

        vec_rows = 16 * (dim // (4 * width))

        def piece_of(mine, *operands):
            shape = (mine.shape[0] + vec_rows, 4 * width)
            return like(piece_kernel, "piece", shape, bf16, mine, *operands)

        def merge(a, b):
            shape = (2 * a.shape[0] - vec_rows, 4 * width)
            return like(functools.partial(merge_kernel, dim), "merge", shape, bf16, a, b)

        def place_of(masks):
            at = jnp.zeros((1,), i32)
            for m in masks:
                at = at * 2 + bit_of(m)
            return at


        def wait(*arrived):
            return line(lambda *x: x, *arrived)

        def near_sum(total, label):
            for m in far_masks[:-1]:
                total = line(add_low, total, swap(total, "mp", m, label))
            return total

        last_far = far_masks[-1]

        line = Line()

        out_slots = {0: w_out}
        for m in far_masks:
            out_slots.update(
                {j ^ m: swap(x, "mp", m, "gather_w_out") for j, x in list(out_slots.items())}
            )
        line.spare = ln1_gain[None]
        pos, place = wait(pos, place[None].astype(i32))
        first, qkv, summary = line(project, tokens, ln1_gain[None], ln1_bias[None], w_qkv)
        out_list = list(out_slots.items())
        sums = after(summary, *[x for _, x in out_list])[None]
        for i, m in enumerate(seq_masks):
            got = swap(sums, "dp", m, "summaries")
            if i == 0:
                exps, stats = line(local, qkv)
                for j, x in out_list:
                    out_slots[j ^ 1] = swap(after(x, stats), "mp", 1, "gather_w_out")
            sums = line(lambda a, b: jnp.concatenate([a, b]), sums, got)
        cores = wait(*[out_slots[j ^ 1] for j, _ in out_list])
        for (j, _), x in zip(out_list, cores):
            out_slots[j ^ 1] = x
        probs, attended = line(attend, place, qkv, exps, stats, sums)

        att_slots = {0: attended}
        for m in far_masks:
            att_slots.update(
                {j ^ m: swap(x, "mp", m, "gather_attended") for j, x in list(att_slots.items())}
            )
        for j, x in list(att_slots.items()):
            att_slots[j ^ 1] = swap(x, "mp", 1, "gather_attended")
        mid, second, active, grad_upper, theirs, mine, up_vec = line(
            feed,
            pos,
            tokens,
            *[att_slots[j] for j in range(n_mp)],
            *[out_slots[j] for j in range(n_mp)],
            b_out[None],
            ln2_gain[None],
            ln2_bias[None],
            w_up,
            b_up[None],
            w_down,
            cotangent,
        )

        total = near_sum(line(add_low, mine, swap(theirs, "mp", 1, "sum_second")), "sum_second")
        far = swap(total, "mp", last_far, "sum_second")
        other = swap(total, "mp", 1, "sum_second")
        out_theirs, out_mine, theirs, mine = line(
            weights, pos, active, second, grad_upper, cotangent, w_down
        )
        feed_sum = Scatter(line, theirs, mine, feed_masks, "feed_weights")
        out_got = swap(out_theirs, "mp", 1, "sum_output")
        line.space()
        out_total = near_sum(line(add_low, out_mine, out_got), "sum_output")
        (far,) = wait(far)
        other_far = swap(far, "mp", 1, "sum_second")
        out_send = after(out_total, far)
        out_far = swap(out_send, "mp", last_far, "sum_output")
        out_other = swap(out_send, "mp", 1, "sum_output")
        line.space()
        grad_low, gqkv, back_vec, slot_grad = line(
            lambda *a: (lambda r: (r[0], r[1], r[3], r[2]))(back(*a)),
            pos,
            total,
            far,
            other,
            other_far,
            mid,
            cotangent,
            ln2_gain[None],
            w_out,
            qkv,
            probs,
            sums,
        )

        feed_sum.step()
        (out_other,) = wait(out_other)
        theirs_w, rest = line(
            rest_weights, first_bit, first, gqkv, grad_low, attended, slot_grad, sums
        )
        rest_got = swap(theirs_w, "dp", feed_masks[0], "rest_weights")
        (out_far,) = wait(out_far)
        out_other_far = swap(out_far, "mp", 1, "sum_output")
        theirs, mine = line(first_grad, pos, gqkv, slot_grad, sums, w_qkv, tokens)
        got = swap(theirs, "mp", 1, "sum_first")
        feed_sum.step()
        total = line(pair, mine, got)
        for m in far_masks[:-1]:
            total = line(pair, total, swap(total, "mp", m, "sum_first"))
        far = swap(total, "mp", last_far, "sum_first")
        theirs_w, rest = line(split_first, bit_of(feed_masks[1]), rest, rest_got)
        rest_got = swap(theirs_w, "dp", feed_masks[1], "rest_weights")
        output = line(
            output_sum, pos, out_total, out_far, out_other, out_other_far, mid, b_down[None]
        )
        theirs_w, rest, extra = line(split_second, bit_of(feed_masks[2]), rest, rest_got, w_qkv)
        rest_got = swap(theirs_w, "dp", feed_masks[2], "rest_weights")
        extra_got = swap(extra, "mp", 1, "sum_extra")
        for m in feed_masks[3:]:
            theirs_w, rest = line(split_sum, bit_of(m), rest, rest_got)
            rest_got = swap(theirs_w, "dp", m, "rest_weights")
        for m in feed_masks[3:]:
            feed_sum.step()
        feed_all = line(add_low, feed_sum.mine, feed_sum.got)
        feed_got = swap(feed_all, "dp", feed_masks[-1], "feed_weights")
        (far,) = wait(far)
        other = swap(after(total, far), "mp", 1, "sum_first")
        other_far = swap(far, "mp", 1, "sum_first")
        for m in far_masks:
            extra = line(pl_add, extra, extra_got)
            extra_got = swap(extra, "mp", m, "sum_extra")
        rest_all = line(
            piece_of, rest, rest_got, total, far, back_vec, up_vec
        )
        rest_got = swap(rest_all, "dp", feed_masks[-1], "rest_weights")
        feed_next = list(reversed(feed_masks))[1:]
        rest_next = list(reversed(feed_masks))[1:]
        for m in feed_next[:-2]:
            feed_all = line(concat, feed_all, feed_got)
            feed_got = swap(feed_all, "dp", m, "feed_weights")
        feed_all = line(concat, feed_all, feed_got)
        two = swap(feed_all, "dp", feed_masks[0], "feed_weights")
        one = swap(feed_all, "dp", feed_masks[1], "feed_weights")
        rest_all = line(merge, rest_all, rest_got)
        rest_got = swap(rest_all, "dp", rest_next[0], "rest_weights")
        grad_tokens = line(
            last,
            pos,
            total,
            far,
            other,
            other_far,
            extra,
            extra_got,
            tokens,
            grad_low,
            ln1_gain[None],
        )
        (two,) = wait(two)
        both = swap(two, "dp", feed_masks[1], "feed_weights")
        for m in rest_next[1:]:
            line.space()
            rest_all = line(merge, rest_all, rest_got)
            rest_got = swap(rest_all, "dp", m, "rest_weights")
        held = line(feed_unpack, place_of(feed_masks), feed_all, one)
        grad_w_down, grad_w_up = line(
            feed_unpack, place_of(feed_masks), two, both, *held
        )
        grad_w_qkv, grad_w_out, *vectors = line(
            rest_unpack, place_of(feed_masks), rest_all, rest_got, line.spare
        )
        return (
            output,
            grad_tokens,
            vectors[0][0],
            vectors[1][0],
            grad_w_qkv,
            grad_w_out,
            vectors[2][0],
            vectors[3][0],
            vectors[4][0],
            grad_w_up.reshape(dim, hidden),
            vectors[6][0],
            grad_w_down,
            vectors[5][0],
        )

    return per_device


def solution(mesh):
    return jax.shard_map(
        build(mesh.shape["dp"], mesh.shape["mp"]),
        mesh=mesh,
        in_specs=(
            P("dp", None),
            P(),
            P(),
            P(None, None, "mp"),
            P("mp", None),
            P(),
            P(),
            P(),
            P(None, "mp"),
            P("mp"),
            P("mp", None),
            P(),
            P("dp", None),
        ),
        out_specs=(
            P("dp", None),
            P("dp", None),
            P(),
            P(),
            P(None, None, "mp"),
            P("mp", None),
            P(),
            P(),
            P(),
            P(None, "mp"),
            P("mp"),
            P("mp", None),
            P(),
        ),
        check_vma=False,
    )
```

```python
import functools
import math

import jax
import jax.numpy as jnp
from jax import lax
from jax.experimental import pallas as pl
from jax.experimental.pallas import tpu as pltpu
from jax.sharding import PartitionSpec as P

HEAD_DIM = 64
SPAN = 128
LENGTH = 4096
EPSILON = 1e-05
SCALE = HEAD_DIM ** (-0.5)
LOW = -1e30

f32 = jnp.float32
bf16 = jnp.bfloat16
i32 = jnp.int32
VMEM = pl.BlockSpec(memory_space=pltpu.VMEM)
SMEM = pl.BlockSpec(memory_space=pltpu.SMEM)


def masks_of(count):
    return [1 << i for i in range(count.bit_length() - 1)]


def params(mib=60):
    return pltpu.CompilerParams(vmem_limit_bytes=mib * 1024 * 1024)


def cost():
    return pl.CostEstimate(flops=115_000_000_000, bytes_accessed=1, transcendentals=0)


def nt(a, b):
    return lax.dot_general(a, b, (((1,), (1,)), ((), ())), preferred_element_type=f32)


def tn(a, b):
    return lax.dot_general(a, b, (((0,), (0,)), ((), ())), preferred_element_type=f32)


def nn(a, b):
    return jnp.dot(a, b, preferred_element_type=f32)


def normed(x):
    c = x - jnp.mean(x, axis=-1, keepdims=True)
    r = lax.rsqrt(jnp.mean(c * c, axis=-1, keepdims=True) + EPSILON)
    return c * r, r


def norm_back(e, n, r, gain):
    k = e * gain
    return r * (
        k - jnp.mean(k, axis=-1, keepdims=True) - n * jnp.mean(k * n, axis=-1, keepdims=True)
    )


def fold(x):
    return jnp.sum(x.reshape(-1, 8, x.shape[-1]), axis=0)


def head_mask(shape, h, dtype):
    lane = lax.broadcasted_iota(i32, shape, len(shape) - 1)
    return jnp.where(lane // HEAD_DIM == h, 1.0, 0.0).astype(dtype)


def spread(x, factor):
    heads = x.shape[1] // HEAD_DIM
    return jnp.concatenate(
        [x * (head_mask((1, x.shape[1]), h, f32) * factor).astype(x.dtype) for h in range(heads)]
    )


def collect(x, factor):
    width = x.shape[1]
    heads = width // HEAD_DIM
    rows = x.shape[0] // heads
    total = x[:rows] * (head_mask((1, width), 0, f32) * factor)
    for h in range(1, heads):
        total = total + x[h * rows : (h + 1) * rows] * (head_mask((1, width), h, f32) * factor)
    return total


def to_low(v, cols):
    v = jnp.concatenate([v[:, i : i + cols] for i in range(0, v.shape[1], cols)])
    high = v.astype(bf16)
    return jnp.concatenate([high, (v - high.astype(f32)).astype(bf16)])


def from_low(x, dim):
    half = x.shape[0] // 2
    v = x[:half].astype(f32) + x[half:].astype(f32)
    count = dim // x.shape[1]
    return jnp.concatenate([v[i * 8 : (i + 1) * 8] for i in range(count)], axis=1)


def sums_of(sums_ref, which):
    pair = sums_ref[:, which // 2].astype(f32)
    blocks = pair.shape[1] // 2
    start = which % 2 * blocks
    return pair[:, start : start + blocks].reshape(-1, pair.shape[2])


def columns_of(sums_ref, start, count):
    return jnp.concatenate([sums_of(sums_ref, start + j) for j in range(count)], axis=1)


def project_kernel(
    tile, tok_ref, gain_ref, bias_ref, w_ref, first_ref, qkv_ref, out_ref, wcat, sum_ref
):
    width = w_ref.shape[2]
    for s in range(3):
        wcat[:, s * width : (s + 1) * width] = w_ref[s]
    per = tile // SPAN
    for i in range(tok_ref.shape[0] // tile):
        at = slice(i * tile, (i + 1) * tile)
        n, _ = normed(tok_ref[at].astype(f32))
        first = (n * gain_ref[...] + bias_ref[...]).astype(bf16)
        first_ref[at] = first
        both = nn(first, wcat[...]).astype(bf16)
        for s in range(3):
            part = both[:, s * width : (s + 1) * width]
            qkv_ref[s, at] = part
            if s:
                mean = jnp.mean(part.astype(f32).reshape(per, SPAN, width), axis=1)
                sum_ref[s - 1, i * per : (i + 1) * per] = mean
        sums = [jnp.sum(x.reshape(per, SPAN, -1), axis=1) for x in (first.astype(f32), n)]
        total = jnp.concatenate(sums, axis=1)
        for j in range(sum_ref.shape[0] - 2):
            sum_ref[2 + j, i * per : (i + 1) * per] = total[:, j * width : (j + 1) * width]
    for j in range(out_ref.shape[0]):
        out_ref[j] = jnp.concatenate([sum_ref[2 * j], sum_ref[2 * j + 1]]).astype(bf16)


def local_kernel(qkv_ref, exp_ref, stat_ref):
    blocks = exp_ref.shape[0]
    lanes = exp_ref.shape[2]
    key = lax.broadcasted_iota(i32, (SPAN, lanes), 0)
    query = lax.broadcasted_iota(i32, (SPAN, lanes), 1) % SPAN
    keep = key <= query
    for b in range(blocks):
        at = slice(b * SPAN, (b + 1) * SPAN)
        s = nt(qkv_ref[1, at], spread(qkv_ref[0, at], SCALE))
        s = jnp.where(keep, s, LOW)
        top = jnp.max(s, axis=0, keepdims=True)
        e = jnp.exp(s - top)
        exp_ref[b] = e
        stat_ref[b, 0:1] = top
        stat_ref[b, 1:2] = jnp.sum(e, axis=0, keepdims=True)


def attend_kernel(place_ref, qkv_ref, exp_ref, stat_ref, sums_ref, prob_ref, att_ref):
    blocks = exp_ref.shape[0]
    lanes = exp_ref.shape[2]
    slots = sums_ref.shape[0]
    place = place_ref[0]
    keys = sums_of(sums_ref, 0).astype(bf16)
    values = sums_of(sums_ref, 1).astype(bf16)
    row = lax.broadcasted_iota(i32, (slots * blocks, lanes), 0)
    at_block = ((row // blocks) ^ place) * blocks + row % blocks
    for b in range(blocks):
        at = slice(b * SPAN, (b + 1) * SPAN)
        s = nt(keys, spread(qkv_ref[0, at], SCALE)) + math.log(SPAN)
        s = jnp.where(at_block < place * blocks + b, s, LOW)
        mine = stat_ref[b, 0:1]
        top = jnp.maximum(mine, jnp.max(s, axis=0, keepdims=True))
        e = jnp.exp(s - top)
        shrink = jnp.exp(mine - top)
        scale = 1.0 / (stat_ref[b, 1:2] * shrink + jnp.sum(e, axis=0, keepdims=True))
        p = jnp.concatenate([exp_ref[b] * (shrink * scale), e * scale]).astype(bf16)
        prob_ref[b] = p
        a = tn(p, jnp.concatenate([qkv_ref[2, at], values]))
        att_ref[at] = collect(a, 1.0).astype(bf16)


def feed_kernel(
    count, pos_ref, tok_ref, *refs
):
    att = refs[:count]
    wo = refs[count : 2 * count]
    (
        b_out_ref,
        gain_ref,
        bias_ref,
        up_ref,
        b_up_ref,
        down_ref,
        cot_ref,
        mid_ref,
        second_ref,
        active_ref,
        grad_ref,
        theirs_ref,
        mine_ref,
        vec_ref,
        wcat,
    ) = refs[2 * count :]
    step = pl.program_id(0)
    me = pos_ref[0]
    width = wo[0].shape[0]

    def in_order(arrays):
        arrays = list(arrays)
        for m in masks_of(count):
            flip = (me & m) != 0
            arrays = [jnp.where(flip, arrays[j ^ m], arrays[j]) for j in range(count)]
        return arrays

    @pl.when(step == 0)
    def _():
        for j in range(count):
            wcat[pl.ds(pl.multiple_of((me ^ j) * width, width), width)] = wo[j][...]
        vec_ref[...] = jnp.zeros_like(vec_ref)

    attended = jnp.concatenate(in_order([a[...] for a in att]), axis=1)
    mid = tok_ref[...].astype(f32) + nn(attended, wcat[...]) + b_out_ref[...]
    mid_ref[...] = mid
    n, _ = normed(mid)
    second = (n * gain_ref[...] + bias_ref[...]).astype(bf16)
    second_ref[...] = second
    u = nn(second, up_ref[...]) + b_up_ref[...]
    root = math.sqrt(2.0 / math.pi)
    square = u * u
    t = jnp.tanh(u * (root + root * 0.044715 * square))
    half = 0.5 + 0.5 * t
    active_ref[...] = (u * half).astype(bf16)
    slope = half + (0.5 * u) * (1.0 - t * t) * (root + (3.0 * root * 0.044715) * square)
    grad = nt(cot_ref[...], down_ref[...]) * slope
    low = grad.astype(bf16)
    grad_ref[...] = low
    out = nt(low, up_ref[...]).astype(bf16)
    steps = pl.num_programs(0)

    @pl.when(step < steps // 2)
    def _():
        theirs_ref[...] = out

    @pl.when(step >= steps // 2)
    def _():
        mine_ref[...] = out

    vec_ref[0:8] += fold(low.astype(f32))


def weights_kernel(
    pos_ref,
    active_ref,
    second_ref,
    grad_ref,
    cot_ref,
    down_ref,
    out_theirs_ref,
    out_mine_ref,
    theirs_ref,
    mine_ref,
    down_acc,
    up_acc,
):
    step = pl.program_id(0)
    terms = nn(active_ref[...], down_ref[...]).astype(bf16)
    down = tn(active_ref[...], cot_ref[...])
    up = tn(second_ref[...], grad_ref[...])

    @pl.when(step == 0)
    def _():
        out_theirs_ref[...] = terms
        down_acc[...] = down
        up_acc[...] = up

    @pl.when(step == 1)
    def _():
        out_mine_ref[...] = terms
        first = (down_acc[...] + down).astype(bf16)
        then = (up_acc[...] + up).astype(bf16).reshape(first.shape)
        low = pos_ref[3] == 0
        theirs_ref[...] = jnp.where(low, then, first)
        mine_ref[...] = jnp.where(low, first, then)


def rest_kernel(
    bit_ref, first_ref, gqkv_ref, low_ref, att_ref, slot_ref, sums_ref, theirs_ref, mine_ref
):
    slots, _, blocks, width = slot_ref.shape
    dim = first_ref.shape[1]
    size = dim // 2
    rows = [slot_ref[:, s].reshape(slots * blocks, width) for s in range(2)]
    far_rows = (jnp.concatenate(rows, axis=1) * (1.0 / SPAN)).astype(bf16)
    far_first = columns_of(sums_ref, 2, dim // width).astype(bf16)
    out = []
    for h in range(2):
        at = slice(h * size, (h + 1) * size)
        main = tn(first_ref[:, at], gqkv_ref[...])
        far = tn(far_first[:, at], far_rows)
        last = tn(low_ref[:, at], att_ref[...])
        out.append(
            jnp.concatenate([main[:, :width], main[:, width:] + far, last], axis=1).astype(bf16)
        )
    low = bit_ref[0] == 0
    theirs_ref[:size] = jnp.where(low, out[1], out[0])
    mine_ref[:size] = jnp.where(low, out[0], out[1])
    for ref, slot in ((theirs_ref, 2), (mine_ref, 0)):
        parts = [slot_ref[j, s] for j in (slot, slot + 1) for s in range(2)]
        ref[size:] = to_low(jnp.concatenate(parts, axis=1), 4 * width)


def split_first_kernel(bit_ref, a_ref, b_ref, theirs_ref, mine_ref):
    rows = a_ref.shape[0] - 16
    cols = a_ref.shape[1]
    size = rows // 2
    total = (a_ref[:rows].astype(f32) + b_ref[:rows].astype(f32)).astype(bf16)
    low = bit_ref[0] == 0
    theirs_ref[:size] = jnp.where(low, total[size:], total[:size])
    mine_ref[:size] = jnp.where(low, total[:size], total[size:])
    slots = from_low(a_ref[rows:], cols) + from_low(b_ref[rows:], cols)
    none = jnp.zeros((8, cols // 2), f32)
    for ref, at in ((theirs_ref, slice(cols // 2, cols)), (mine_ref, slice(0, cols // 2))):
        ref[size:] = to_low(jnp.concatenate([slots[:, at], none], axis=1), cols)


def split_second_kernel(bit_ref, a_ref, b_ref, w_ref, theirs_ref, mine_ref, extra_ref):
    rows = a_ref.shape[0] - 16
    cols = a_ref.shape[1]
    width = w_ref.shape[2]
    size = rows // 2
    total = (a_ref[:rows].astype(f32) + b_ref[:rows].astype(f32)).astype(bf16)
    low = bit_ref[0] == 0
    theirs_ref[...] = jnp.where(low, total[size:], total[:size])
    mine_ref[...] = jnp.where(low, total[:size], total[size:])
    own = from_low(a_ref[rows:], cols) + from_low(b_ref[rows:], cols)
    own = (own * (1.0 / SPAN)).astype(bf16)
    extra_ref[...] = nt(own[:, :width], w_ref[1]) + nt(own[:, width : 2 * width], w_ref[2])


def split_kernel(bit_ref, a_ref, b_ref, theirs_ref, mine_ref):
    total = (a_ref[...].astype(f32) + b_ref[...].astype(f32)).astype(bf16)
    size = total.shape[0] // 2
    low = bit_ref[0] == 0
    theirs_ref[...] = jnp.where(low, total[size:], total[:size])
    mine_ref[...] = jnp.where(low, total[:size], total[size:])


def two_halves(refs, half, core):
    own, far, other, other_far = refs
    mine = half == core
    a = jnp.where(mine, own[...], other[...])
    b = jnp.where(mine, far[...], other_far[...])
    return a.astype(f32) + b.astype(f32)


def back_kernel(
    pos_ref,
    own_ref,
    far_ref,
    other_ref,
    other_far_ref,
    mid_ref,
    cot_ref,
    gain_ref,
    wo_ref,
    qkv_ref,
    prob_ref,
    sums_ref,
    low_ref,
    gqkv_ref,
    slot_ref,
    vec_ref,
):
    step = pl.program_id(0)
    slots = sums_ref.shape[0]
    width = wo_ref.shape[0]

    @pl.when(step == 0)
    def _():
        slot_ref[...] = jnp.zeros_like(slot_ref)
        vec_ref[...] = jnp.zeros_like(vec_ref)

    e = two_halves((own_ref, far_ref, other_ref, other_far_ref), step, pos_ref[1])
    n, r = normed(mid_ref[...])
    cot = cot_ref[...].astype(f32)
    grad_mid = cot + norm_back(e, n, r, gain_ref[...])
    low = grad_mid.astype(bf16)
    low_ref[...] = low
    vec_ref[0:8] += fold(grad_mid)
    vec_ref[8:16] += fold(e * n)
    vec_ref[16:24] += fold(e)
    vec_ref[24:32] += fold(cot)

    grad_att = nt(low, wo_ref[...]).astype(bf16)
    far_keys = sums_of(sums_ref, 0).astype(bf16)
    far_values = sums_of(sums_ref, 1).astype(bf16)
    far_gk = jnp.zeros(far_keys.shape, f32)
    far_gv = jnp.zeros(far_keys.shape, f32)
    for b in range(prob_ref.shape[0]):
        at = slice(b * SPAN, (b + 1) * SPAN)
        da = spread(grad_att[at], 1.0)
        query = spread(qkv_ref[0, at], SCALE)
        keys = jnp.concatenate([qkv_ref[1, at], far_keys])
        values = jnp.concatenate([qkv_ref[2, at], far_values])
        p_low = prob_ref[b]
        p = p_low.astype(f32)
        dp = nt(values, da)
        ds = (p * (dp - jnp.sum(p * dp, axis=0, keepdims=True))).astype(bf16)
        gq = collect(tn(ds, keys), SCALE)
        gk = nn(ds, query)
        gv = nn(p_low, da)
        gqkv_ref[at, :width] = gq.astype(bf16)
        gqkv_ref[at, width : 2 * width] = gk[:SPAN].astype(bf16)
        gqkv_ref[at, 2 * width :] = gv[:SPAN].astype(bf16)
        far_gk = far_gk + gk[SPAN:]
        far_gv = far_gv + gv[SPAN:]
    slot_ref[:, 0] += far_gk.reshape(slots, -1, width)
    slot_ref[:, 1] += far_gv.reshape(slots, -1, width)


def first_kernel(
    pos_ref, gqkv_ref, slot_ref, sums_ref, w_ref, tok_ref, theirs_ref, mine_ref, wcat, vec
):
    step = pl.program_id(0)
    steps = pl.num_programs(0)
    dim, width = w_ref.shape[1:]
    tile = gqkv_ref.shape[0]
    half = tile * (steps // 2)

    @pl.when(step == 0)
    def _():
        vec[...] = jnp.zeros_like(vec)
        for s in range(3):
            wcat[:, s * width : (s + 1) * width] = w_ref[s]

    e = nt(gqkv_ref[...], wcat[...])
    n, _ = normed(tok_ref[...].astype(f32))
    vec[0:8] += fold(e * n)
    vec[8:16] += fold(e)
    out = e.astype(bf16)
    at = pl.ds(pl.multiple_of((step % (steps // 2)) * tile, tile), tile)

    @pl.when(step < steps // 2)
    def _():
        theirs_ref[at] = out

    @pl.when(step >= steps // 2)
    def _():
        mine_ref[at] = out

    @pl.when(step == steps - 1)
    def _():
        rows = [
            (slot_ref[:, s].reshape(-1, width) * (1.0 / SPAN)).astype(bf16) for s in range(2)
        ]
        far = nt(rows[0], w_ref[1]) + nt(rows[1], w_ref[2])
        normal = columns_of(sums_ref, 2 + dim // width, dim // width)
        gain = jnp.sum(vec[0:8], axis=0, keepdims=True) + jnp.sum(
            far * normal, axis=0, keepdims=True
        )
        offset = jnp.sum(vec[8:16], axis=0, keepdims=True) + SPAN * jnp.sum(
            far, axis=0, keepdims=True
        )
        low = to_low(jnp.concatenate([gain, offset, jnp.zeros((6, dim), f32)]), dim)
        theirs_ref[half:] = low
        mine_ref[half:] = low


def pair_kernel(a_ref, b_ref, out_ref):
    dim = a_ref.shape[1]
    rows = a_ref.shape[0] - 16
    out_ref[:rows] = (a_ref[:rows].astype(f32) + b_ref[:rows].astype(f32)).astype(bf16)
    out_ref[rows:] = to_low(from_low(a_ref[rows:], dim) + from_low(b_ref[rows:], dim), dim)


def piece_kernel(mine_ref, got_ref, near_ref, far_ref, back_ref, up_ref, out_ref):
    dim = near_ref.shape[1]
    hidden = up_ref.shape[1]
    rows, cols = mine_ref.shape
    out_ref[:rows] = (mine_ref[...].astype(f32) + got_ref[...].astype(f32)).astype(bf16)
    last = near_ref.shape[0] - 16
    first = (from_low(near_ref[last:], dim) + from_low(far_ref[last:], dim))[:2]
    vectors = [first]
    for k in range(4):
        vectors.append(jnp.sum(back_ref[8 * k : 8 * k + 8], axis=0, keepdims=True))
    up = jnp.sum(up_ref[...], axis=0, keepdims=True)
    if hidden < dim:
        up = jnp.concatenate([up, jnp.zeros((1, dim - hidden), f32)], axis=1)
    vectors += [up, jnp.zeros((1, dim), f32)]
    out_ref[rows:] = to_low(jnp.concatenate(vectors), cols)


def merge_kernel(dim, a_ref, b_ref, out_ref):
    cols = a_ref.shape[1]
    rows = a_ref.shape[0] - 16 * (dim // cols)
    out_ref[:rows] = a_ref[:rows]
    out_ref[rows : 2 * rows] = b_ref[:rows]
    out_ref[2 * rows :] = to_low(from_low(a_ref[rows:], dim) + from_low(b_ref[rows:], dim), cols)


def last_kernel(
    pos_ref,
    own_ref,
    far_ref,
    other_ref,
    other_far_ref,
    extra_ref,
    extra_far_ref,
    tok_ref,
    low_ref,
    gain_ref,
    out_ref,
):
    step = pl.program_id(0)
    half = step // (pl.num_programs(0) // 2)
    e = two_halves((own_ref, far_ref, other_ref, other_far_ref), half, pos_ref[1])
    per = e.shape[0] // SPAN
    pieces = []
    for i in range(per):
        at = pl.ds(step * per + i, 1)
        pieces.append(e[i * SPAN : (i + 1) * SPAN] + (extra_ref[at] + extra_far_ref[at]))
    e = jnp.concatenate(pieces)
    n, r = normed(tok_ref[...].astype(f32))
    out_ref[...] = (low_ref[...].astype(f32) + norm_back(e, n, r, gain_ref[...])).astype(bf16)


def add_kernel(parts, a_ref, b_ref, *out_refs):
    size = a_ref.shape[0] // parts
    for k in range(parts):
        at = slice(k * size, (k + 1) * size)
        out_refs[k][...] = (a_ref[at].astype(f32) + b_ref[at].astype(f32)).astype(bf16)


def slot_kernel(a_ref, b_ref, out_ref):
    out_ref[...] = a_ref[: out_ref.shape[0]] + b_ref[...]


def spacer_kernel(x_ref, out_ref):
    out_ref[...] = x_ref[...] * 0.5


def keep_kernel(x_ref, out_ref):
    out_ref[...] = x_ref[...]


def concat_kernel(a_ref, b_ref, out_ref):
    rows = a_ref.shape[0]
    out_ref[:rows] = a_ref[...]
    out_ref[rows:] = b_ref[...]


def output_kernel(
    pos_ref, own_ref, far_ref, other_ref, other_far_ref, mid_ref, b_ref, out_ref
):
    half = pl.program_id(0) // (pl.num_programs(0) // 2)
    e = two_halves((own_ref, far_ref, other_ref, other_far_ref), half, pos_ref[1])
    out_ref[...] = (mid_ref[...] + e + b_ref[...]).astype(bf16)


def feed_unpack_kernel(pieces, far, at_ref, own_ref, one_ref, *refs):
    down_ref, up_ref, scratch, sems = refs[-4:]
    rows = own_ref.shape[0]
    size = rows // pieces
    top = at_ref[0] // pieces
    low = at_ref[0] % pieces

    def copies(ref):
        return [
            pltpu.make_async_copy(
                scratch.at[pl.ds(q * rows, rows)], ref.at[pl.ds(q * rows, rows)], sems.at[q]
            )
            for q in range(2)
        ]

    def fill(ref):
        out = copies(ref)
        for q in range(2):
            for k in range(pieces):
                at = pl.ds(pl.multiple_of((k ^ low) * size, size), size)
                x = jnp.where(top % 2 == q, own_ref[at], one_ref[at])
                scratch[q * rows + k * size : q * rows + (k + 1) * size] = x.astype(f32)
            out[q].start()
        for q in range(2):
            out[q].wait()

    is_down = top // 2 == far

    @pl.when(is_down)
    def _():
        fill(down_ref)

    @pl.when(jnp.logical_not(is_down))
    def _():
        fill(up_ref)


def rest_unpack_kernel(
    count, dim, at_ref, near_ref, far_ref, spare_ref, qkv_ref, out_ref, *refs
):
    vec_refs, scratch = refs[:-1], refs[-1]
    cols = near_ref.shape[1]
    last = near_ref.shape[0] - 16 * (dim // cols)
    rows = 2 * last // count
    width = qkv_ref.shape[2]
    part = count // 2
    top = at_ref[0] // part
    low = at_ref[0] % part
    for k in range(count):
        start = pl.multiple_of(((k % part) ^ low) * rows, rows)
        is_near = top == k // part
        x = jnp.where(is_near, near_ref[pl.ds(start, rows)], far_ref[pl.ds(start, rows)])
        x = x.astype(f32)
        for s in range(3):
            qkv_ref[s, k * rows : (k + 1) * rows] = x[:, s * width : (s + 1) * width]
        scratch[k * rows : (k + 1) * rows] = x[:, 3 * width :]
    out_ref[...] = scratch[...].T
    vectors = from_low(near_ref[last:], dim) + from_low(far_ref[last:], dim)
    for k, ref in enumerate(vec_refs):
        ref[...] = vectors[k : k + 1, : ref.shape[1]]


def build(n_dp, n_mp):
    def swap(x, axis, mask, label):
        n = n_dp if axis == "dp" else n_mp
        with jax.named_scope(label):
            return lax.ppermute(x, axis, [(i, i ^ mask) for i in range(n)])

    def pick(x, index, rows):
        return lax.dynamic_slice_in_dim(x, index * rows, rows, 0)

    def halves(x, mask, axis):
        bit = jnp.where((lax.axis_index(axis) & mask) == 0, 0, 1)
        size = x.shape[0] // 2
        return pick(x, 1 - bit, size), pick(x, bit, size)

    def after(x, *others):
        return lax.optimization_barrier((x, others))[0]

    far_masks = masks_of(n_mp)[1:]
    dp_masks = masks_of(n_dp)
    feed_masks = [dp_masks[1], dp_masks[0]] + dp_masks[2:]

    class Line:
        def __init__(self):
            self.last = ()

        def __call__(self, work, *inputs):
            if self.last:
                inputs = after(inputs, *self.last)
            result = work(*inputs)
            first = result[-1] if isinstance(result, (tuple, list)) else result
            self.last = (first,)
            return result

        def space(self, x=None):
            if x is not None:
                self.spare = x
            self.spare = self(spacer, self.spare)

    def add_parts(parts, a, b):
        part = jax.ShapeDtypeStruct((a.shape[0] // parts, *a.shape[1:]), bf16)
        return pl.pallas_call(
            functools.partial(add_kernel, parts),
            out_shape=(part,) * parts,
            in_specs=[VMEM, VMEM],
            out_specs=(VMEM,) * parts,
            compiler_params=params(16),
            cost_estimate=cost(),
            name="add",
        )(a, b)

    def add_low(a, b):
        return add_parts(1, a, b)[0]

    def spacer(x):
        return pl.pallas_call(
            spacer_kernel,
            out_shape=jax.ShapeDtypeStruct(x.shape, x.dtype),
            in_specs=[VMEM],
            out_specs=VMEM,
            compiler_params=params(16),
            cost_estimate=cost(),
            name="spacer",
        )(x)

    def split_sum(bit, mine, got):
        size = mine.shape[0] // 2
        half = jax.ShapeDtypeStruct((size, mine.shape[1]), bf16)
        return pl.pallas_call(
            split_kernel,
            out_shape=(half, half),
            in_specs=[SMEM, VMEM, VMEM],
            out_specs=(VMEM, VMEM),
            compiler_params=params(16),
            cost_estimate=cost(),
            name="split",
        )(bit, mine, got)

    def bit_of(mask):
        return jnp.where((lax.axis_index("dp") & mask) == 0, 0, 1).astype(i32)[None]

    class Scatter:
        def __init__(self, line, theirs, mine, masks, label):
            self.line, self.label = line, label
            self.rest = list(masks)
            self.mine = mine
            self.got = swap(theirs, "dp", self.rest.pop(0), label)

        def step(self):
            mask = self.rest.pop(0)
            theirs, self.mine = self.line(split_sum, bit_of(mask), self.mine, self.got)
            self.got = swap(theirs, "dp", mask, self.label)

    def per_device(
        tokens,
        ln1_gain,
        ln1_bias,
        w_qkv,
        w_out,
        b_out,
        ln2_gain,
        ln2_bias,
        w_up,
        b_up,
        w_down,
        b_down,
        cotangent,
    ):
        rows, dim = tokens.shape
        width = w_qkv.shape[2]
        hidden = w_up.shape[1]
        heads = width // HEAD_DIM
        blocks = rows // SPAN
        lanes = heads * SPAN
        group = LENGTH // rows
        entries = SPAN + group * blocks
        seq_masks = masks_of(group)
        me = lax.axis_index("mp")
        place = lax.axis_index("dp") % group
        first_bit = bit_of(feed_masks[0])
        pos = jnp.concatenate(
            [jnp.stack([me, me & 1, place]).astype(i32), bit_of(feed_masks[0])]
        )
        half = rows // 2
        tile = half // 2
        tiles = 4
        sds = jax.ShapeDtypeStruct

        def rolled(i, pos):
            return ((i + (1 - pos[1]) * (tiles // 2)) % tiles, 0)

        def theirs_row(i, pos):
            return (jnp.minimum(i, tiles // 2 - 1), 0)

        def mine_row(i, pos):
            return (jnp.maximum(i - tiles // 2, 0), 0)

        def half_rolled(i, pos):
            return (jnp.where(i == 0, 1 - pos[1], pos[1]), 0)

        def whole(*_):
            return (0, 0)

        def by_row(i, *_):
            return (i, 0)

        def zeros(n):
            return lambda *_: (0,) * n

        def block(shape, index):
            return pl.BlockSpec(shape, index)

        def plain(kernel, name, in_specs, out_shape, scratch=(), mib=24):
            return pl.pallas_call(
                kernel,
                out_shape=out_shape,
                in_specs=in_specs,
                out_specs=tuple(VMEM for _ in out_shape),
                scratch_shapes=list(scratch),
                compiler_params=params(mib),
                cost_estimate=cost(),
                name=name,
            )

        def gridded(
            kernel, name, grid, in_specs, out_specs, out_shape, scratch=(), mib=60, aliases=None
        ):
            return pl.pallas_call(
                kernel,
                grid_spec=pltpu.PrefetchScalarGridSpec(
                    num_scalar_prefetch=1,
                    grid=(grid,),
                    in_specs=in_specs,
                    out_specs=out_specs,
                    scratch_shapes=list(scratch),
                ),
                out_shape=out_shape,
                input_output_aliases=aliases or {},
                compiler_params=params(60 if name in ('feed',) else 30 if name in ('back', 'weights') else 20),
                cost_estimate=cost(),
                name=name,
            )

        row_block = block((tile, dim), rolled)
        row_vector = block((1, dim), whole)
        tile_block = block((tile, dim), by_row)
        one_tile = block((tile, dim), whole)

        project = plain(
            functools.partial(project_kernel, tile),
            "project",
            [VMEM] * 4,
            (
                sds((rows, dim), bf16),
                sds((3, rows, width), bf16),
                sds((1 + dim // width, 2 * blocks, width), bf16),
            ),
            [
                pltpu.VMEM((dim, 3 * width), bf16),
                pltpu.VMEM((2 + 2 * (dim // width), blocks, width), f32),
            ],
            60,
        )
        local = plain(
            local_kernel,
            "local",
            [VMEM],
            (sds((blocks, SPAN, lanes), f32), sds((blocks, 2, lanes), f32)),
        )
        attend = plain(
            attend_kernel,
            "attend",
            [SMEM] + [VMEM] * 4,
            (sds((blocks, entries, lanes), bf16), sds((rows, width), bf16)),
        )
        half_rows = block((half, dim), half_rolled)
        half_hidden = block((half, hidden), half_rolled)
        feed = gridded(
            functools.partial(feed_kernel, n_mp),
            "feed",
            2,
            [half_rows]
            + [block((half, width), half_rolled)] * n_mp
            + [block((width, dim), whole)] * n_mp
            + [row_vector] * 3
            + [
                block((dim, hidden), whole),
                block((1, hidden), whole),
                block((hidden, dim), whole),
                half_rows,
            ],
            [
                half_rows,
                half_rows,
                half_hidden,
                half_hidden,
                block((half, dim), whole),
                block((half, dim), whole),
                block((8, hidden), whole),
            ],
            (
                sds((rows, dim), f32),
                sds((rows, dim), bf16),
                sds((rows, hidden), bf16),
                sds((rows, hidden), bf16),
                sds((half, dim), bf16),
                sds((half, dim), bf16),
                sds((8, hidden), f32),
            ),
            [pltpu.VMEM((dim, dim), bf16)],
        )
        weights = gridded(
            weights_kernel,
            "weights",
            2,
            [half_hidden, half_rows, half_hidden, half_rows, block((hidden, dim), whole)],
            [block((half, dim), whole)] * 2 + [block((hidden, dim), whole)] * 2,
            (
                sds((half, dim), bf16),
                sds((half, dim), bf16),
                sds((hidden, dim), bf16),
                sds((hidden, dim), bf16),
            ),
            [pltpu.VMEM((hidden, dim), f32), pltpu.VMEM((dim, hidden), f32)],
        )
        rest_weights = plain(
            rest_kernel,
            "rest_weights",
            [SMEM] + [VMEM] * 6,
            (sds((dim // 2 + 16, 4 * width), bf16), sds((dim // 2 + 16, 4 * width), bf16)),
            mib=60,
        )
        slot_shape = (group, 2, blocks, width)
        sums_shape = (group, 1 + dim // width, 2 * blocks, width)
        back = gridded(
            back_kernel,
            "back",
            2,
            [block((half, dim), whole)] * 4
            + [
                block((half, dim), by_row),
                block((half, dim), by_row),
                row_vector,
                block((width, dim), whole),
                block((3, half, width), lambda i, pos: (0, i, 0)),
                block((blocks // 2, entries, lanes), lambda i, pos: (i, 0, 0)),
                block(sums_shape, zeros(4)),
            ],
            [
                block((half, dim), by_row),
                block((half, 3 * width), by_row),
                block(slot_shape, zeros(4)),
                block((32, dim), whole),
            ],
            (
                sds((rows, dim), bf16),
                sds((rows, 3 * width), bf16),
                sds(slot_shape, f32),
                sds((32, dim), f32),
            ),
        )
        first_block = block((half + 16, dim), whole)
        first_grad = gridded(
            first_kernel,
            "first",
            2,
            [
                block((half, 3 * width), half_rolled),
                block(slot_shape, zeros(4)),
                block(sums_shape, zeros(4)),
                block((3, dim, width), zeros(3)),
                half_rows,
            ],
            [first_block, first_block],
            (sds((half + 16, dim), bf16), sds((half + 16, dim), bf16)),
            [pltpu.VMEM((dim, 3 * width), bf16), pltpu.VMEM((16, dim), f32)],
        )
        def own_tile(i, pos):
            return (jnp.clip(i - pos[1] * (tiles // 2), 0, tiles // 2 - 1), 0)

        def other_tile(i, pos):
            return (jnp.clip(i - (1 - pos[1]) * (tiles // 2), 0, tiles // 2 - 1), 0)

        terms_specs = [block((half, dim), whole)] * 4
        tile_block = block((half, dim), by_row)
        last = gridded(
            last_kernel,
            "last",
            2,
            terms_specs + [block((blocks, dim), whole)] * 2 + [tile_block, tile_block, row_vector],
            tile_block,
            sds((rows, dim), bf16),
        )
        output_sum = gridded(
            output_kernel,
            "output",
            2,
            terms_specs + [tile_block, row_vector],
            tile_block,
            sds((rows, dim), bf16),
        )
        def feed_unpack(at, own, one, *held):
            anywhere = pl.BlockSpec(memory_space=pl.ANY)
            return pl.pallas_call(
                functools.partial(feed_unpack_kernel, n_dp // 4, 1 if held else 0),
                out_shape=(sds((hidden, dim), f32), sds((hidden, dim), f32)),
                in_specs=[SMEM, VMEM, VMEM] + [anywhere] * len(held),
                out_specs=(anywhere, anywhere),
                scratch_shapes=[pltpu.VMEM((hidden, dim), f32), pltpu.SemaphoreType.DMA((2,))],
                input_output_aliases={3 + k: k for k in range(len(held))},
                compiler_params=params(20),
                cost_estimate=cost(),
                name="feed_unpack",
            )(at, own, one, *held)

        rest_unpack = plain(
            functools.partial(rest_unpack_kernel, n_dp, dim),
            "rest_unpack",
            [SMEM, VMEM, VMEM, VMEM],
            (sds((3, dim, width), f32), sds((width, dim), f32))
            + (sds((1, dim), f32),) * 6
            + (sds((1, hidden), f32),),
            [pltpu.VMEM((dim, width), f32)],
        )

        def like(kernel, name, shape, dtype, *operands):
            specs = [VMEM] * len(operands)
            return plain(kernel, name, specs, (sds(shape, dtype),))(*operands)[0]

        def pair(a, b):
            return like(pair_kernel, "pair", a.shape, bf16, a, b)

        def concat(a, b):
            return like(concat_kernel, "concat", (2 * a.shape[0], a.shape[1]), bf16, a, b)

        def keep(x):
            return like(keep_kernel, "keep", x.shape, bf16, x)

        def pl_add(a, b):
            return like(slot_kernel, "plus", a.shape, f32, a, b)

        cols = 4 * width
        quarter = dim // 4
        split_first = plain(
            split_first_kernel,
            "split_first",
            [SMEM, VMEM, VMEM],
            (sds((quarter + 16, cols), bf16), sds((quarter + 16, cols), bf16)),
        )
        split_second = plain(
            split_second_kernel,
            "split_second",
            [SMEM, VMEM, VMEM, VMEM],
            (
                sds((quarter // 2, cols), bf16),
                sds((quarter // 2, cols), bf16),
                sds((blocks, dim), f32),
            ),
        )

        vec_rows = 16 * (dim // (4 * width))

        def piece_of(mine, *operands):
            shape = (mine.shape[0] + vec_rows, 4 * width)
            return like(piece_kernel, "piece", shape, bf16, mine, *operands)

        def merge(a, b):
            shape = (2 * a.shape[0] - vec_rows, 4 * width)
            return like(functools.partial(merge_kernel, dim), "merge", shape, bf16, a, b)

        def place_of(masks):
            at = jnp.zeros((1,), i32)
            for m in masks:
                at = at * 2 + bit_of(m)
            return at


        def wait(*arrived):
            return line(lambda *x: x, *arrived)

        def near_sum(total, label):
            for m in far_masks[:-1]:
                total = line(add_low, total, swap(total, "mp", m, label))
            return total

        last_far = far_masks[-1]

        line = Line()

        out_slots = {0: w_out}
        for m in far_masks:
            out_slots.update(
                {j ^ m: swap(x, "mp", m, "gather_w_out") for j, x in list(out_slots.items())}
            )
        line.spare = ln1_gain[None]
        pos, place = wait(pos, place[None].astype(i32))
        first, qkv, summary = line(project, tokens, ln1_gain[None], ln1_bias[None], w_qkv)
        out_list = list(out_slots.items())
        sums = after(summary, *[x for _, x in out_list])[None]
        for i, m in enumerate(seq_masks):
            got = swap(sums, "dp", m, "summaries")
            if i == 0:
                exps, stats = line(local, qkv)
                for j, x in out_list:
                    out_slots[j ^ 1] = swap(after(x, stats), "mp", 1, "gather_w_out")
            sums = line(lambda a, b: jnp.concatenate([a, b]), sums, got)
        cores = wait(*[out_slots[j ^ 1] for j, _ in out_list])
        for (j, _), x in zip(out_list, cores):
            out_slots[j ^ 1] = x
        probs, attended = line(attend, place, qkv, exps, stats, sums)

        att_slots = {0: attended}
        for m in far_masks:
            att_slots.update(
                {j ^ m: swap(x, "mp", m, "gather_attended") for j, x in list(att_slots.items())}
            )
        for j, x in list(att_slots.items()):
            att_slots[j ^ 1] = swap(x, "mp", 1, "gather_attended")
        mid, second, active, grad_upper, theirs, mine, up_vec = line(
            feed,
            pos,
            tokens,
            *[att_slots[j] for j in range(n_mp)],
            *[out_slots[j] for j in range(n_mp)],
            b_out[None],
            ln2_gain[None],
            ln2_bias[None],
            w_up,
            b_up[None],
            w_down,
            cotangent,
        )

        got = swap(theirs, "mp", 1, "sum_second")
        mine = line(keep, mine)
        total = near_sum(line(add_low, mine, got), "sum_second")
        far = swap(total, "mp", last_far, "sum_second")
        other = swap(total, "mp", 1, "sum_second")
        out_theirs, out_mine, theirs, mine = line(
            weights, pos, active, second, grad_upper, cotangent, w_down
        )
        feed_sum = Scatter(line, theirs, mine, feed_masks, "feed_weights")
        out_got = swap(out_theirs, "mp", 1, "sum_output")
        line.space()
        out_total = near_sum(line(add_low, out_mine, out_got), "sum_output")
        (far,) = wait(far)
        other_far = swap(far, "mp", 1, "sum_second")
        out_send = after(out_total, far)
        out_far = swap(out_send, "mp", last_far, "sum_output")
        out_other = swap(out_send, "mp", 1, "sum_output")
        line.space()
        grad_low, gqkv, back_vec, slot_grad = line(
            lambda *a: (lambda r: (r[0], r[1], r[3], r[2]))(back(*a)),
            pos,
            total,
            far,
            other,
            other_far,
            mid,
            cotangent,
            ln2_gain[None],
            w_out,
            qkv,
            probs,
            sums,
        )

        feed_sum.step()
        (out_other,) = wait(out_other)
        theirs_w, rest = line(
            rest_weights, first_bit, first, gqkv, grad_low, attended, slot_grad, sums
        )
        rest_got = swap(theirs_w, "dp", feed_masks[0], "rest_weights")
        (out_far,) = wait(out_far)
        out_other_far = swap(out_far, "mp", 1, "sum_output")
        theirs, mine = line(first_grad, pos, gqkv, slot_grad, sums, w_qkv, tokens)
        got = swap(theirs, "mp", 1, "sum_first")
        feed_sum.step()
        total = line(pair, mine, got)
        for m in far_masks[:-1]:
            total = line(pair, total, swap(total, "mp", m, "sum_first"))
        far = swap(total, "mp", last_far, "sum_first")
        theirs_w, rest = line(split_first, bit_of(feed_masks[1]), rest, rest_got)
        rest_got = swap(theirs_w, "dp", feed_masks[1], "rest_weights")
        output = line(
            output_sum, pos, out_total, out_far, out_other, out_other_far, mid, b_down[None]
        )
        theirs_w, rest, extra = line(split_second, bit_of(feed_masks[2]), rest, rest_got, w_qkv)
        rest_got = swap(theirs_w, "dp", feed_masks[2], "rest_weights")
        extra_got = swap(extra, "mp", 1, "sum_extra")
        for m in feed_masks[3:]:
            theirs_w, rest = line(split_sum, bit_of(m), rest, rest_got)
            rest_got = swap(theirs_w, "dp", m, "rest_weights")
        for m in feed_masks[3:]:
            feed_sum.step()
        feed_all = line(add_low, feed_sum.mine, feed_sum.got)
        feed_got = swap(feed_all, "dp", feed_masks[-1], "feed_weights")
        (far,) = wait(far)
        other = swap(after(total, far), "mp", 1, "sum_first")
        other_far = swap(far, "mp", 1, "sum_first")
        for m in far_masks:
            extra = line(pl_add, extra, extra_got)
            extra_got = swap(extra, "mp", m, "sum_extra")
        rest_all = line(
            piece_of, rest, rest_got, total, far, back_vec, up_vec
        )
        rest_got = swap(rest_all, "dp", feed_masks[-1], "rest_weights")
        feed_next = list(reversed(feed_masks))[1:]
        rest_next = list(reversed(feed_masks))[1:]
        for m in feed_next[:-2]:
            feed_all = line(concat, feed_all, feed_got)
            feed_got = swap(feed_all, "dp", m, "feed_weights")
        feed_all = line(concat, feed_all, feed_got)
        two = swap(feed_all, "dp", feed_masks[0], "feed_weights")
        one = swap(feed_all, "dp", feed_masks[1], "feed_weights")
        rest_all = line(merge, rest_all, rest_got)
        rest_got = swap(rest_all, "dp", rest_next[0], "rest_weights")
        grad_tokens = line(
            last,
            pos,
            total,
            far,
            other,
            other_far,
            extra,
            extra_got,
            tokens,
            grad_low,
            ln1_gain[None],
        )
        (two,) = wait(two)
        both = swap(two, "dp", feed_masks[1], "feed_weights")
        for m in rest_next[1:]:
            line.space()
            rest_all = line(merge, rest_all, rest_got)
            rest_got = swap(rest_all, "dp", m, "rest_weights")
        held = line(feed_unpack, place_of(feed_masks), feed_all, one)
        grad_w_down, grad_w_up = line(
            feed_unpack, place_of(feed_masks), two, both, *held
        )
        grad_w_qkv, grad_w_out, *vectors = line(
            rest_unpack, place_of(feed_masks), rest_all, rest_got, line.spare
        )
        return (
            output,
            grad_tokens,
            vectors[0][0],
            vectors[1][0],
            grad_w_qkv,
            grad_w_out,
            vectors[2][0],
            vectors[3][0],
            vectors[4][0],
            grad_w_up.reshape(dim, hidden),
            vectors[6][0],
            grad_w_down,
            vectors[5][0],
        )

    return per_device


def solution(mesh):
    return jax.shard_map(
        build(mesh.shape["dp"], mesh.shape["mp"]),
        mesh=mesh,
        in_specs=(
            P("dp", None),
            P(),
            P(),
            P(None, None, "mp"),
            P("mp", None),
            P(),
            P(),
            P(),
            P(None, "mp"),
            P("mp"),
            P("mp", None),
            P(),
            P("dp", None),
        ),
        out_specs=(
            P("dp", None),
            P("dp", None),
            P(),
            P(),
            P(None, None, "mp"),
            P("mp", None),
            P(),
            P(),
            P(),
            P(None, "mp"),
            P("mp"),
            P("mp", None),
            P(),
        ),
        check_vma=False,
    )
```

```python
import functools
import math

import jax
import jax.numpy as jnp
from jax import lax
from jax.experimental import pallas as pl
from jax.experimental.pallas import tpu as pltpu
from jax.sharding import PartitionSpec as P

HEAD_DIM = 64
SPAN = 128
LENGTH = 4096
EPSILON = 1e-05
SCALE = HEAD_DIM ** (-0.5)
LOW = -1e30

f32 = jnp.float32
bf16 = jnp.bfloat16
i32 = jnp.int32
VMEM = pl.BlockSpec(memory_space=pltpu.VMEM)
SMEM = pl.BlockSpec(memory_space=pltpu.SMEM)


def masks_of(count):
    return [1 << i for i in range(count.bit_length() - 1)]


def params(mib=60):
    return pltpu.CompilerParams(vmem_limit_bytes=mib * 1024 * 1024)


def cost():
    return pl.CostEstimate(flops=12_000_000_000, bytes_accessed=1, transcendentals=0)


def nt(a, b):
    return lax.dot_general(a, b, (((1,), (1,)), ((), ())), preferred_element_type=f32)


def tn(a, b):
    return lax.dot_general(a, b, (((0,), (0,)), ((), ())), preferred_element_type=f32)


def nn(a, b):
    return jnp.dot(a, b, preferred_element_type=f32)


def normed(x):
    c = x - jnp.mean(x, axis=-1, keepdims=True)
    r = lax.rsqrt(jnp.mean(c * c, axis=-1, keepdims=True) + EPSILON)
    return c * r, r


def norm_back(e, n, r, gain):
    k = e * gain
    return r * (
        k - jnp.mean(k, axis=-1, keepdims=True) - n * jnp.mean(k * n, axis=-1, keepdims=True)
    )


def fold(x):
    return jnp.sum(x.reshape(-1, 8, x.shape[-1]), axis=0)


def head_mask(shape, h, dtype):
    lane = lax.broadcasted_iota(i32, shape, len(shape) - 1)
    return jnp.where(lane // HEAD_DIM == h, 1.0, 0.0).astype(dtype)


def spread(x, factor):
    heads = x.shape[1] // HEAD_DIM
    return jnp.concatenate(
        [x * (head_mask((1, x.shape[1]), h, f32) * factor).astype(x.dtype) for h in range(heads)]
    )


def collect(x, factor):
    width = x.shape[1]
    heads = width // HEAD_DIM
    rows = x.shape[0] // heads
    total = x[:rows] * (head_mask((1, width), 0, f32) * factor)
    for h in range(1, heads):
        total = total + x[h * rows : (h + 1) * rows] * (head_mask((1, width), h, f32) * factor)
    return total


def to_low(v, cols):
    v = jnp.concatenate([v[:, i : i + cols] for i in range(0, v.shape[1], cols)])
    high = v.astype(bf16)
    return jnp.concatenate([high, (v - high.astype(f32)).astype(bf16)])


def from_low(x, dim):
    half = x.shape[0] // 2
    v = x[:half].astype(f32) + x[half:].astype(f32)
    count = dim // x.shape[1]
    return jnp.concatenate([v[i * 8 : (i + 1) * 8] for i in range(count)], axis=1)


def sums_of(sums_ref, which):
    pair = sums_ref[:, which // 2].astype(f32)
    blocks = pair.shape[1] // 2
    start = which % 2 * blocks
    return pair[:, start : start + blocks].reshape(-1, pair.shape[2])


def columns_of(sums_ref, start, count):
    return jnp.concatenate([sums_of(sums_ref, start + j) for j in range(count)], axis=1)


def project_kernel(
    tile, tok_ref, gain_ref, bias_ref, w_ref, first_ref, qkv_ref, out_ref, wcat, sum_ref
):
    width = w_ref.shape[2]
    for s in range(3):
        wcat[:, s * width : (s + 1) * width] = w_ref[s]
    per = tile // SPAN
    for i in range(tok_ref.shape[0] // tile):
        at = slice(i * tile, (i + 1) * tile)
        n, _ = normed(tok_ref[at].astype(f32))
        first = (n * gain_ref[...] + bias_ref[...]).astype(bf16)
        first_ref[at] = first
        both = nn(first, wcat[...]).astype(bf16)
        for s in range(3):
            part = both[:, s * width : (s + 1) * width]
            qkv_ref[s, at] = part
            if s:
                mean = jnp.mean(part.astype(f32).reshape(per, SPAN, width), axis=1)
                sum_ref[s - 1, i * per : (i + 1) * per] = mean
        sums = [jnp.sum(x.reshape(per, SPAN, -1), axis=1) for x in (first.astype(f32), n)]
        total = jnp.concatenate(sums, axis=1)
        for j in range(sum_ref.shape[0] - 2):
            sum_ref[2 + j, i * per : (i + 1) * per] = total[:, j * width : (j + 1) * width]
    for j in range(out_ref.shape[0]):
        out_ref[j] = jnp.concatenate([sum_ref[2 * j], sum_ref[2 * j + 1]]).astype(bf16)


def local_kernel(qkv_ref, exp_ref, stat_ref):
    blocks = exp_ref.shape[0]
    lanes = exp_ref.shape[2]
    key = lax.broadcasted_iota(i32, (SPAN, lanes), 0)
    query = lax.broadcasted_iota(i32, (SPAN, lanes), 1) % SPAN
    keep = key <= query
    for b in range(blocks):
        at = slice(b * SPAN, (b + 1) * SPAN)
        s = nt(qkv_ref[1, at], spread(qkv_ref[0, at], SCALE))
        s = jnp.where(keep, s, LOW)
        top = jnp.max(s, axis=0, keepdims=True)
        e = jnp.exp(s - top)
        exp_ref[b] = e
        stat_ref[b, 0:1] = top
        stat_ref[b, 1:2] = jnp.sum(e, axis=0, keepdims=True)


def attend_kernel(place_ref, qkv_ref, exp_ref, stat_ref, sums_ref, prob_ref, att_ref):
    blocks = exp_ref.shape[0]
    lanes = exp_ref.shape[2]
    slots = sums_ref.shape[0]
    place = place_ref[0]
    keys = sums_of(sums_ref, 0).astype(bf16)
    values = sums_of(sums_ref, 1).astype(bf16)
    row = lax.broadcasted_iota(i32, (slots * blocks, lanes), 0)
    at_block = ((row // blocks) ^ place) * blocks + row % blocks
    for b in range(blocks):
        at = slice(b * SPAN, (b + 1) * SPAN)
        s = nt(keys, spread(qkv_ref[0, at], SCALE)) + math.log(SPAN)
        s = jnp.where(at_block < place * blocks + b, s, LOW)
        mine = stat_ref[b, 0:1]
        top = jnp.maximum(mine, jnp.max(s, axis=0, keepdims=True))
        e = jnp.exp(s - top)
        shrink = jnp.exp(mine - top)
        scale = 1.0 / (stat_ref[b, 1:2] * shrink + jnp.sum(e, axis=0, keepdims=True))
        p = jnp.concatenate([exp_ref[b] * (shrink * scale), e * scale]).astype(bf16)
        prob_ref[b] = p
        a = tn(p, jnp.concatenate([qkv_ref[2, at], values]))
        att_ref[at] = collect(a, 1.0).astype(bf16)


def feed_kernel(
    count, pos_ref, tok_ref, *refs
):
    att = refs[:count]
    wo = refs[count : 2 * count]
    (
        b_out_ref,
        gain_ref,
        bias_ref,
        up_ref,
        b_up_ref,
        down_ref,
        cot_ref,
        mid_ref,
        second_ref,
        active_ref,
        grad_ref,
        theirs_ref,
        mine_ref,
        vec_ref,
        wcat,
    ) = refs[2 * count :]
    step = pl.program_id(0)
    me = pos_ref[0]
    width = wo[0].shape[0]

    def in_order(arrays):
        arrays = list(arrays)
        for m in masks_of(count):
            flip = (me & m) != 0
            arrays = [jnp.where(flip, arrays[j ^ m], arrays[j]) for j in range(count)]
        return arrays

    @pl.when(step == 0)
    def _():
        for j in range(count):
            wcat[pl.ds(pl.multiple_of((me ^ j) * width, width), width)] = wo[j][...]
        vec_ref[...] = jnp.zeros_like(vec_ref)

    attended = jnp.concatenate(in_order([a[...] for a in att]), axis=1)
    mid = tok_ref[...].astype(f32) + nn(attended, wcat[...]) + b_out_ref[...]
    mid_ref[...] = mid
    n, _ = normed(mid)
    second = (n * gain_ref[...] + bias_ref[...]).astype(bf16)
    second_ref[...] = second
    u = nn(second, up_ref[...]) + b_up_ref[...]
    root = math.sqrt(2.0 / math.pi)
    square = u * u
    t = jnp.tanh(u * (root + root * 0.044715 * square))
    half = 0.5 + 0.5 * t
    active_ref[...] = (u * half).astype(bf16)
    slope = half + (0.5 * u) * (1.0 - t * t) * (root + (3.0 * root * 0.044715) * square)
    grad = nt(cot_ref[...], down_ref[...]) * slope
    low = grad.astype(bf16)
    grad_ref[...] = low
    out = nt(low, up_ref[...]).astype(bf16)
    steps = pl.num_programs(0)

    @pl.when(step < steps // 2)
    def _():
        theirs_ref[...] = out

    @pl.when(step >= steps // 2)
    def _():
        mine_ref[...] = out

    vec_ref[0:8] += fold(low.astype(f32))


def weights_kernel(
    pos_ref,
    active_ref,
    second_ref,
    grad_ref,
    cot_ref,
    down_ref,
    out_theirs_ref,
    out_mine_ref,
    theirs_ref,
    mine_ref,
    down_acc,
    up_acc,
):
    step = pl.program_id(0)
    terms = nn(active_ref[...], down_ref[...]).astype(bf16)
    down = tn(active_ref[...], cot_ref[...])
    up = tn(second_ref[...], grad_ref[...])

    @pl.when(step == 0)
    def _():
        out_theirs_ref[...] = terms
        down_acc[...] = down
        up_acc[...] = up

    @pl.when(step == 1)
    def _():
        out_mine_ref[...] = terms
        first = (down_acc[...] + down).astype(bf16)
        then = (up_acc[...] + up).astype(bf16).reshape(first.shape)
        low = pos_ref[3] == 0
        theirs_ref[...] = jnp.where(low, then, first)
        mine_ref[...] = jnp.where(low, first, then)


def rest_kernel(
    bit_ref, first_ref, gqkv_ref, low_ref, att_ref, slot_ref, sums_ref, theirs_ref, mine_ref
):
    slots, _, blocks, width = slot_ref.shape
    dim = first_ref.shape[1]
    size = dim // 2
    rows = [slot_ref[:, s].reshape(slots * blocks, width) for s in range(2)]
    far_rows = (jnp.concatenate(rows, axis=1) * (1.0 / SPAN)).astype(bf16)
    far_first = columns_of(sums_ref, 2, dim // width).astype(bf16)
    out = []
    for h in range(2):
        at = slice(h * size, (h + 1) * size)
        main = tn(first_ref[:, at], gqkv_ref[...])
        far = tn(far_first[:, at], far_rows)
        last = tn(low_ref[:, at], att_ref[...])
        out.append(
            jnp.concatenate([main[:, :width], main[:, width:] + far, last], axis=1).astype(bf16)
        )
    low = bit_ref[0] == 0
    theirs_ref[:size] = jnp.where(low, out[1], out[0])
    mine_ref[:size] = jnp.where(low, out[0], out[1])
    for ref, slot in ((theirs_ref, 2), (mine_ref, 0)):
        parts = [slot_ref[j, s] for j in (slot, slot + 1) for s in range(2)]
        ref[size:] = to_low(jnp.concatenate(parts, axis=1), 4 * width)


def split_first_kernel(bit_ref, a_ref, b_ref, theirs_ref, mine_ref):
    rows = a_ref.shape[0] - 16
    cols = a_ref.shape[1]
    size = rows // 2
    total = (a_ref[:rows].astype(f32) + b_ref[:rows].astype(f32)).astype(bf16)
    low = bit_ref[0] == 0
    theirs_ref[:size] = jnp.where(low, total[size:], total[:size])
    mine_ref[:size] = jnp.where(low, total[:size], total[size:])
    slots = from_low(a_ref[rows:], cols) + from_low(b_ref[rows:], cols)
    none = jnp.zeros((8, cols // 2), f32)
    for ref, at in ((theirs_ref, slice(cols // 2, cols)), (mine_ref, slice(0, cols // 2))):
        ref[size:] = to_low(jnp.concatenate([slots[:, at], none], axis=1), cols)


def split_second_kernel(bit_ref, a_ref, b_ref, w_ref, theirs_ref, mine_ref, extra_ref):
    rows = a_ref.shape[0] - 16
    cols = a_ref.shape[1]
    width = w_ref.shape[2]
    size = rows // 2
    total = (a_ref[:rows].astype(f32) + b_ref[:rows].astype(f32)).astype(bf16)
    low = bit_ref[0] == 0
    theirs_ref[...] = jnp.where(low, total[size:], total[:size])
    mine_ref[...] = jnp.where(low, total[:size], total[size:])
    own = from_low(a_ref[rows:], cols) + from_low(b_ref[rows:], cols)
    own = (own * (1.0 / SPAN)).astype(bf16)
    extra_ref[...] = nt(own[:, :width], w_ref[1]) + nt(own[:, width : 2 * width], w_ref[2])


def split_kernel(bit_ref, a_ref, b_ref, theirs_ref, mine_ref):
    total = (a_ref[...].astype(f32) + b_ref[...].astype(f32)).astype(bf16)
    size = total.shape[0] // 2
    low = bit_ref[0] == 0
    theirs_ref[...] = jnp.where(low, total[size:], total[:size])
    mine_ref[...] = jnp.where(low, total[:size], total[size:])


def two_halves(refs, half, core):
    own, far, other, other_far = refs
    mine = half == core
    a = jnp.where(mine, own[...], other[...])
    b = jnp.where(mine, far[...], other_far[...])
    return a.astype(f32) + b.astype(f32)


def back_kernel(
    pos_ref,
    own_ref,
    far_ref,
    other_ref,
    other_far_ref,
    mid_ref,
    cot_ref,
    gain_ref,
    wo_ref,
    qkv_ref,
    prob_ref,
    sums_ref,
    low_ref,
    gqkv_ref,
    slot_ref,
    vec_ref,
):
    step = pl.program_id(0)
    slots = sums_ref.shape[0]
    width = wo_ref.shape[0]

    @pl.when(step == 0)
    def _():
        slot_ref[...] = jnp.zeros_like(slot_ref)
        vec_ref[...] = jnp.zeros_like(vec_ref)

    e = two_halves((own_ref, far_ref, other_ref, other_far_ref), step, pos_ref[1])
    n, r = normed(mid_ref[...])
    cot = cot_ref[...].astype(f32)
    grad_mid = cot + norm_back(e, n, r, gain_ref[...])
    low = grad_mid.astype(bf16)
    low_ref[...] = low
    vec_ref[0:8] += fold(grad_mid)
    vec_ref[8:16] += fold(e * n)
    vec_ref[16:24] += fold(e)
    vec_ref[24:32] += fold(cot)

    grad_att = nt(low, wo_ref[...]).astype(bf16)
    far_keys = sums_of(sums_ref, 0).astype(bf16)
    far_values = sums_of(sums_ref, 1).astype(bf16)
    far_gk = jnp.zeros(far_keys.shape, f32)
    far_gv = jnp.zeros(far_keys.shape, f32)
    for b in range(prob_ref.shape[0]):
        at = slice(b * SPAN, (b + 1) * SPAN)
        da = spread(grad_att[at], 1.0)
        query = spread(qkv_ref[0, at], SCALE)
        keys = jnp.concatenate([qkv_ref[1, at], far_keys])
        values = jnp.concatenate([qkv_ref[2, at], far_values])
        p_low = prob_ref[b]
        p = p_low.astype(f32)
        dp = nt(values, da)
        ds = (p * (dp - jnp.sum(p * dp, axis=0, keepdims=True))).astype(bf16)
        gq = collect(tn(ds, keys), SCALE)
        gk = nn(ds, query)
        gv = nn(p_low, da)
        gqkv_ref[at, :width] = gq.astype(bf16)
        gqkv_ref[at, width : 2 * width] = gk[:SPAN].astype(bf16)
        gqkv_ref[at, 2 * width :] = gv[:SPAN].astype(bf16)
        far_gk = far_gk + gk[SPAN:]
        far_gv = far_gv + gv[SPAN:]
    slot_ref[:, 0] += far_gk.reshape(slots, -1, width)
    slot_ref[:, 1] += far_gv.reshape(slots, -1, width)


def first_kernel(
    pos_ref, gqkv_ref, slot_ref, sums_ref, w_ref, tok_ref, theirs_ref, mine_ref, wcat, vec
):
    step = pl.program_id(0)
    steps = pl.num_programs(0)
    dim, width = w_ref.shape[1:]
    tile = gqkv_ref.shape[0]
    half = tile * (steps // 2)

    @pl.when(step == 0)
    def _():
        vec[...] = jnp.zeros_like(vec)
        for s in range(3):
            wcat[:, s * width : (s + 1) * width] = w_ref[s]

    e = nt(gqkv_ref[...], wcat[...])
    n, _ = normed(tok_ref[...].astype(f32))
    vec[0:8] += fold(e * n)
    vec[8:16] += fold(e)
    out = e.astype(bf16)
    at = pl.ds(pl.multiple_of((step % (steps // 2)) * tile, tile), tile)

    @pl.when(step < steps // 2)
    def _():
        theirs_ref[at] = out

    @pl.when(step >= steps // 2)
    def _():
        mine_ref[at] = out

    @pl.when(step == steps - 1)
    def _():
        rows = [
            (slot_ref[:, s].reshape(-1, width) * (1.0 / SPAN)).astype(bf16) for s in range(2)
        ]
        far = nt(rows[0], w_ref[1]) + nt(rows[1], w_ref[2])
        normal = columns_of(sums_ref, 2 + dim // width, dim // width)
        gain = jnp.sum(vec[0:8], axis=0, keepdims=True) + jnp.sum(
            far * normal, axis=0, keepdims=True
        )
        offset = jnp.sum(vec[8:16], axis=0, keepdims=True) + SPAN * jnp.sum(
            far, axis=0, keepdims=True
        )
        low = to_low(jnp.concatenate([gain, offset, jnp.zeros((6, dim), f32)]), dim)
        theirs_ref[half:] = low
        mine_ref[half:] = low


def pair_kernel(a_ref, b_ref, out_ref):
    dim = a_ref.shape[1]
    rows = a_ref.shape[0] - 16
    out_ref[:rows] = (a_ref[:rows].astype(f32) + b_ref[:rows].astype(f32)).astype(bf16)
    out_ref[rows:] = to_low(from_low(a_ref[rows:], dim) + from_low(b_ref[rows:], dim), dim)


def piece_kernel(mine_ref, got_ref, near_ref, far_ref, back_ref, up_ref, out_ref):
    dim = near_ref.shape[1]
    hidden = up_ref.shape[1]
    rows, cols = mine_ref.shape
    out_ref[:rows] = (mine_ref[...].astype(f32) + got_ref[...].astype(f32)).astype(bf16)
    last = near_ref.shape[0] - 16
    first = (from_low(near_ref[last:], dim) + from_low(far_ref[last:], dim))[:2]
    vectors = [first]
    for k in range(4):
        vectors.append(jnp.sum(back_ref[8 * k : 8 * k + 8], axis=0, keepdims=True))
    up = jnp.sum(up_ref[...], axis=0, keepdims=True)
    if hidden < dim:
        up = jnp.concatenate([up, jnp.zeros((1, dim - hidden), f32)], axis=1)
    vectors += [up, jnp.zeros((1, dim), f32)]
    out_ref[rows:] = to_low(jnp.concatenate(vectors), cols)


def merge_kernel(dim, a_ref, b_ref, out_ref):
    cols = a_ref.shape[1]
    rows = a_ref.shape[0] - 16 * (dim // cols)
    out_ref[:rows] = a_ref[:rows]
    out_ref[rows : 2 * rows] = b_ref[:rows]
    out_ref[2 * rows :] = to_low(from_low(a_ref[rows:], dim) + from_low(b_ref[rows:], dim), cols)


def last_kernel(
    pos_ref,
    own_ref,
    far_ref,
    other_ref,
    other_far_ref,
    extra_ref,
    extra_far_ref,
    tok_ref,
    low_ref,
    gain_ref,
    out_ref,
):
    step = pl.program_id(0)
    half = step // (pl.num_programs(0) // 2)
    e = two_halves((own_ref, far_ref, other_ref, other_far_ref), half, pos_ref[1])
    per = e.shape[0] // SPAN
    pieces = []
    for i in range(per):
        at = pl.ds(step * per + i, 1)
        pieces.append(e[i * SPAN : (i + 1) * SPAN] + (extra_ref[at] + extra_far_ref[at]))
    e = jnp.concatenate(pieces)
    n, r = normed(tok_ref[...].astype(f32))
    out_ref[...] = (low_ref[...].astype(f32) + norm_back(e, n, r, gain_ref[...])).astype(bf16)


def add_kernel(parts, a_ref, b_ref, *out_refs):
    size = a_ref.shape[0] // parts
    for k in range(parts):
        at = slice(k * size, (k + 1) * size)
        out_refs[k][...] = (a_ref[at].astype(f32) + b_ref[at].astype(f32)).astype(bf16)


def slot_kernel(a_ref, b_ref, out_ref):
    out_ref[...] = a_ref[: out_ref.shape[0]] + b_ref[...]


def spacer_kernel(x_ref, out_ref):
    out_ref[...] = x_ref[...] * 0.5


def keep_kernel(x_ref, out_ref):
    out_ref[...] = x_ref[...]


def concat_kernel(a_ref, b_ref, out_ref):
    rows = a_ref.shape[0]
    out_ref[:rows] = a_ref[...]
    out_ref[rows:] = b_ref[...]


def output_kernel(
    pos_ref, own_ref, far_ref, other_ref, other_far_ref, mid_ref, b_ref, out_ref
):
    half = pl.program_id(0) // (pl.num_programs(0) // 2)
    e = two_halves((own_ref, far_ref, other_ref, other_far_ref), half, pos_ref[1])
    out_ref[...] = (mid_ref[...] + e + b_ref[...]).astype(bf16)


def feed_unpack_kernel(pieces, far, at_ref, own_ref, one_ref, *refs):
    down_ref, up_ref, scratch, sems = refs[-4:]
    rows = own_ref.shape[0]
    size = rows // pieces
    top = at_ref[0] // pieces
    low = at_ref[0] % pieces

    def copies(ref):
        return [
            pltpu.make_async_copy(
                scratch.at[pl.ds(q * rows, rows)], ref.at[pl.ds(q * rows, rows)], sems.at[q]
            )
            for q in range(2)
        ]

    def fill(ref):
        out = copies(ref)
        for q in range(2):
            for k in range(pieces):
                at = pl.ds(pl.multiple_of((k ^ low) * size, size), size)
                x = jnp.where(top % 2 == q, own_ref[at], one_ref[at])
                scratch[q * rows + k * size : q * rows + (k + 1) * size] = x.astype(f32)
            out[q].start()
        for q in range(2):
            out[q].wait()

    is_down = top // 2 == far

    @pl.when(is_down)
    def _():
        fill(down_ref)

    @pl.when(jnp.logical_not(is_down))
    def _():
        fill(up_ref)


def rest_unpack_kernel(
    count, dim, at_ref, near_ref, far_ref, spare_ref, qkv_ref, out_ref, *refs
):
    vec_refs, scratch = refs[:-1], refs[-1]
    cols = near_ref.shape[1]
    last = near_ref.shape[0] - 16 * (dim // cols)
    rows = 2 * last // count
    width = qkv_ref.shape[2]
    part = count // 2
    top = at_ref[0] // part
    low = at_ref[0] % part
    for k in range(count):
        start = pl.multiple_of(((k % part) ^ low) * rows, rows)
        is_near = top == k // part
        x = jnp.where(is_near, near_ref[pl.ds(start, rows)], far_ref[pl.ds(start, rows)])
        x = x.astype(f32)
        for s in range(3):
            qkv_ref[s, k * rows : (k + 1) * rows] = x[:, s * width : (s + 1) * width]
        scratch[k * rows : (k + 1) * rows] = x[:, 3 * width :]
    out_ref[...] = scratch[...].T
    vectors = from_low(near_ref[last:], dim) + from_low(far_ref[last:], dim)
    for k, ref in enumerate(vec_refs):
        ref[...] = vectors[k : k + 1, : ref.shape[1]]


def build(n_dp, n_mp):
    def swap(x, axis, mask, label):
        n = n_dp if axis == "dp" else n_mp
        with jax.named_scope(label):
            return lax.ppermute(x, axis, [(i, i ^ mask) for i in range(n)])

    def pick(x, index, rows):
        return lax.dynamic_slice_in_dim(x, index * rows, rows, 0)

    def halves(x, mask, axis):
        bit = jnp.where((lax.axis_index(axis) & mask) == 0, 0, 1)
        size = x.shape[0] // 2
        return pick(x, 1 - bit, size), pick(x, bit, size)

    def after(x, *others):
        return lax.optimization_barrier((x, others))[0]

    far_masks = masks_of(n_mp)[1:]
    dp_masks = masks_of(n_dp)
    feed_masks = [dp_masks[1], dp_masks[0]] + dp_masks[2:]

    class Line:
        def __init__(self):
            self.last = ()

        def __call__(self, work, *inputs):
            if self.last:
                inputs = after(inputs, *self.last)
            result = work(*inputs)
            first = result[-1] if isinstance(result, (tuple, list)) else result
            self.last = (first,)
            return result

        def space(self, x=None):
            if x is not None:
                self.spare = x
            self.spare = self(spacer, self.spare)

    def add_parts(parts, a, b):
        part = jax.ShapeDtypeStruct((a.shape[0] // parts, *a.shape[1:]), bf16)
        return pl.pallas_call(
            functools.partial(add_kernel, parts),
            out_shape=(part,) * parts,
            in_specs=[VMEM, VMEM],
            out_specs=(VMEM,) * parts,
            compiler_params=params(16),
            cost_estimate=cost(),
            name="add",
        )(a, b)

    def add_low(a, b):
        return add_parts(1, a, b)[0]

    def spacer(x):
        return pl.pallas_call(
            spacer_kernel,
            out_shape=jax.ShapeDtypeStruct(x.shape, x.dtype),
            in_specs=[VMEM],
            out_specs=VMEM,
            compiler_params=params(16),
            cost_estimate=cost(),
            name="spacer",
        )(x)

    def split_sum(bit, mine, got):
        size = mine.shape[0] // 2
        half = jax.ShapeDtypeStruct((size, mine.shape[1]), bf16)
        return pl.pallas_call(
            split_kernel,
            out_shape=(half, half),
            in_specs=[SMEM, VMEM, VMEM],
            out_specs=(VMEM, VMEM),
            compiler_params=params(16),
            cost_estimate=cost(),
            name="split",
        )(bit, mine, got)

    def bit_of(mask):
        return jnp.where((lax.axis_index("dp") & mask) == 0, 0, 1).astype(i32)[None]

    class Scatter:
        def __init__(self, line, theirs, mine, masks, label):
            self.line, self.label = line, label
            self.rest = list(masks)
            self.mine = mine
            self.got = swap(theirs, "dp", self.rest.pop(0), label)

        def step(self):
            mask = self.rest.pop(0)
            theirs, self.mine = self.line(split_sum, bit_of(mask), self.mine, self.got)
            self.got = swap(theirs, "dp", mask, self.label)

    def per_device(
        tokens,
        ln1_gain,
        ln1_bias,
        w_qkv,
        w_out,
        b_out,
        ln2_gain,
        ln2_bias,
        w_up,
        b_up,
        w_down,
        b_down,
        cotangent,
    ):
        rows, dim = tokens.shape
        width = w_qkv.shape[2]
        hidden = w_up.shape[1]
        heads = width // HEAD_DIM
        blocks = rows // SPAN
        lanes = heads * SPAN
        group = LENGTH // rows
        entries = SPAN + group * blocks
        seq_masks = masks_of(group)
        me = lax.axis_index("mp")
        place = lax.axis_index("dp") % group
        first_bit = bit_of(feed_masks[0])
        pos = jnp.concatenate(
            [jnp.stack([me, me & 1, place]).astype(i32), bit_of(feed_masks[0])]
        )
        half = rows // 2
        tile = half // 2
        tiles = 4
        sds = jax.ShapeDtypeStruct

        def rolled(i, pos):
            return ((i + (1 - pos[1]) * (tiles // 2)) % tiles, 0)

        def theirs_row(i, pos):
            return (jnp.minimum(i, tiles // 2 - 1), 0)

        def mine_row(i, pos):
            return (jnp.maximum(i - tiles // 2, 0), 0)

        def half_rolled(i, pos):
            return (jnp.where(i == 0, 1 - pos[1], pos[1]), 0)

        def whole(*_):
            return (0, 0)

        def by_row(i, *_):
            return (i, 0)

        def zeros(n):
            return lambda *_: (0,) * n

        def block(shape, index):
            return pl.BlockSpec(shape, index)

        def plain(kernel, name, in_specs, out_shape, scratch=(), mib=24):
            return pl.pallas_call(
                kernel,
                out_shape=out_shape,
                in_specs=in_specs,
                out_specs=tuple(VMEM for _ in out_shape),
                scratch_shapes=list(scratch),
                compiler_params=params(mib),
                cost_estimate=cost(),
                name=name,
            )

        def gridded(
            kernel, name, grid, in_specs, out_specs, out_shape, scratch=(), mib=60, aliases=None
        ):
            return pl.pallas_call(
                kernel,
                grid_spec=pltpu.PrefetchScalarGridSpec(
                    num_scalar_prefetch=1,
                    grid=(grid,),
                    in_specs=in_specs,
                    out_specs=out_specs,
                    scratch_shapes=list(scratch),
                ),
                out_shape=out_shape,
                input_output_aliases=aliases or {},
                compiler_params=params(60 if name in ('feed',) else 30 if name in ('back', 'weights') else 20),
                cost_estimate=cost(),
                name=name,
            )

        row_block = block((tile, dim), rolled)
        row_vector = block((1, dim), whole)
        tile_block = block((tile, dim), by_row)
        one_tile = block((tile, dim), whole)

        project = plain(
            functools.partial(project_kernel, tile),
            "project",
            [VMEM] * 4,
            (
                sds((rows, dim), bf16),
                sds((3, rows, width), bf16),
                sds((1 + dim // width, 2 * blocks, width), bf16),
            ),
            [
                pltpu.VMEM((dim, 3 * width), bf16),
                pltpu.VMEM((2 + 2 * (dim // width), blocks, width), f32),
            ],
            60,
        )
        local = plain(
            local_kernel,
            "local",
            [VMEM],
            (sds((blocks, SPAN, lanes), f32), sds((blocks, 2, lanes), f32)),
        )
        attend = plain(
            attend_kernel,
            "attend",
            [SMEM] + [VMEM] * 4,
            (sds((blocks, entries, lanes), bf16), sds((rows, width), bf16)),
        )
        half_rows = block((half, dim), half_rolled)
        half_hidden = block((half, hidden), half_rolled)
        feed = gridded(
            functools.partial(feed_kernel, n_mp),
            "feed",
            2,
            [half_rows]
            + [block((half, width), half_rolled)] * n_mp
            + [block((width, dim), whole)] * n_mp
            + [row_vector] * 3
            + [
                block((dim, hidden), whole),
                block((1, hidden), whole),
                block((hidden, dim), whole),
                half_rows,
            ],
            [
                half_rows,
                half_rows,
                half_hidden,
                half_hidden,
                block((half, dim), whole),
                block((half, dim), whole),
                block((8, hidden), whole),
            ],
            (
                sds((rows, dim), f32),
                sds((rows, dim), bf16),
                sds((rows, hidden), bf16),
                sds((rows, hidden), bf16),
                sds((half, dim), bf16),
                sds((half, dim), bf16),
                sds((8, hidden), f32),
            ),
            [pltpu.VMEM((dim, dim), bf16)],
        )
        weights = gridded(
            weights_kernel,
            "weights",
            2,
            [half_hidden, half_rows, half_hidden, half_rows, block((hidden, dim), whole)],
            [block((half, dim), whole)] * 2 + [block((hidden, dim), whole)] * 2,
            (
                sds((half, dim), bf16),
                sds((half, dim), bf16),
                sds((hidden, dim), bf16),
                sds((hidden, dim), bf16),
            ),
            [pltpu.VMEM((hidden, dim), f32), pltpu.VMEM((dim, hidden), f32)],
        )
        rest_weights = plain(
            rest_kernel,
            "rest_weights",
            [SMEM] + [VMEM] * 6,
            (sds((dim // 2 + 16, 4 * width), bf16), sds((dim // 2 + 16, 4 * width), bf16)),
            mib=60,
        )
        slot_shape = (group, 2, blocks, width)
        sums_shape = (group, 1 + dim // width, 2 * blocks, width)
        back = gridded(
            back_kernel,
            "back",
            2,
            [block((half, dim), whole)] * 4
            + [
                block((half, dim), by_row),
                block((half, dim), by_row),
                row_vector,
                block((width, dim), whole),
                block((3, half, width), lambda i, pos: (0, i, 0)),
                block((blocks // 2, entries, lanes), lambda i, pos: (i, 0, 0)),
                block(sums_shape, zeros(4)),
            ],
            [
                block((half, dim), by_row),
                block((half, 3 * width), by_row),
                block(slot_shape, zeros(4)),
                block((32, dim), whole),
            ],
            (
                sds((rows, dim), bf16),
                sds((rows, 3 * width), bf16),
                sds(slot_shape, f32),
                sds((32, dim), f32),
            ),
        )
        first_block = block((half + 16, dim), whole)
        first_grad = gridded(
            first_kernel,
            "first",
            2,
            [
                block((half, 3 * width), half_rolled),
                block(slot_shape, zeros(4)),
                block(sums_shape, zeros(4)),
                block((3, dim, width), zeros(3)),
                half_rows,
            ],
            [first_block, first_block],
            (sds((half + 16, dim), bf16), sds((half + 16, dim), bf16)),
            [pltpu.VMEM((dim, 3 * width), bf16), pltpu.VMEM((16, dim), f32)],
        )
        def own_tile(i, pos):
            return (jnp.clip(i - pos[1] * (tiles // 2), 0, tiles // 2 - 1), 0)

        def other_tile(i, pos):
            return (jnp.clip(i - (1 - pos[1]) * (tiles // 2), 0, tiles // 2 - 1), 0)

        terms_specs = [block((half, dim), whole)] * 4
        tile_block = block((half, dim), by_row)
        last = gridded(
            last_kernel,
            "last",
            2,
            terms_specs + [block((blocks, dim), whole)] * 2 + [tile_block, tile_block, row_vector],
            tile_block,
            sds((rows, dim), bf16),
        )
        output_sum = gridded(
            output_kernel,
            "output",
            2,
            terms_specs + [tile_block, row_vector],
            tile_block,
            sds((rows, dim), bf16),
        )
        def feed_unpack(at, own, one, *held):
            anywhere = pl.BlockSpec(memory_space=pl.ANY)
            return pl.pallas_call(
                functools.partial(feed_unpack_kernel, n_dp // 4, 1 if held else 0),
                out_shape=(sds((hidden, dim), f32), sds((hidden, dim), f32)),
                in_specs=[SMEM, VMEM, VMEM] + [anywhere] * len(held),
                out_specs=(anywhere, anywhere),
                scratch_shapes=[pltpu.VMEM((hidden, dim), f32), pltpu.SemaphoreType.DMA((2,))],
                input_output_aliases={3 + k: k for k in range(len(held))},
                compiler_params=params(20),
                cost_estimate=cost(),
                name="feed_unpack",
            )(at, own, one, *held)

        rest_unpack = plain(
            functools.partial(rest_unpack_kernel, n_dp, dim),
            "rest_unpack",
            [SMEM, VMEM, VMEM, VMEM],
            (sds((3, dim, width), f32), sds((width, dim), f32))
            + (sds((1, dim), f32),) * 6
            + (sds((1, hidden), f32),),
            [pltpu.VMEM((dim, width), f32)],
        )

        def like(kernel, name, shape, dtype, *operands):
            specs = [VMEM] * len(operands)
            return plain(kernel, name, specs, (sds(shape, dtype),))(*operands)[0]

        def pair(a, b):
            return like(pair_kernel, "pair", a.shape, bf16, a, b)

        def concat(a, b):
            return like(concat_kernel, "concat", (2 * a.shape[0], a.shape[1]), bf16, a, b)

        def keep(x):
            return like(keep_kernel, "keep", x.shape, bf16, x)

        def pl_add(a, b):
            return like(slot_kernel, "plus", a.shape, f32, a, b)

        cols = 4 * width
        quarter = dim // 4
        split_first = plain(
            split_first_kernel,
            "split_first",
            [SMEM, VMEM, VMEM],
            (sds((quarter + 16, cols), bf16), sds((quarter + 16, cols), bf16)),
        )
        split_second = plain(
            split_second_kernel,
            "split_second",
            [SMEM, VMEM, VMEM, VMEM],
            (
                sds((quarter // 2, cols), bf16),
                sds((quarter // 2, cols), bf16),
                sds((blocks, dim), f32),
            ),
        )

        vec_rows = 16 * (dim // (4 * width))

        def piece_of(mine, *operands):
            shape = (mine.shape[0] + vec_rows, 4 * width)
            return like(piece_kernel, "piece", shape, bf16, mine, *operands)

        def merge(a, b):
            shape = (2 * a.shape[0] - vec_rows, 4 * width)
            return like(functools.partial(merge_kernel, dim), "merge", shape, bf16, a, b)

        def place_of(masks):
            at = jnp.zeros((1,), i32)
            for m in masks:
                at = at * 2 + bit_of(m)
            return at


        def wait(*arrived):
            return line(lambda *x: x, *arrived)

        def near_sum(total, label):
            for m in far_masks[:-1]:
                total = line(add_low, total, swap(total, "mp", m, label))
            return total

        last_far = far_masks[-1]

        line = Line()

        out_slots = {0: w_out}
        for m in far_masks:
            out_slots.update(
                {j ^ m: swap(x, "mp", m, "gather_w_out") for j, x in list(out_slots.items())}
            )
        line.spare = ln1_gain[None]
        pos, place = wait(pos, place[None].astype(i32))
        first, qkv, summary = line(project, tokens, ln1_gain[None], ln1_bias[None], w_qkv)
        out_list = list(out_slots.items())
        sums = after(summary, *[x for _, x in out_list])[None]
        for i, m in enumerate(seq_masks):
            got = swap(sums, "dp", m, "summaries")
            if i == 0:
                exps, stats = line(local, qkv)
                for j, x in out_list:
                    out_slots[j ^ 1] = swap(after(x, stats), "mp", 1, "gather_w_out")
            sums = line(lambda a, b: jnp.concatenate([a, b]), sums, got)
        cores = wait(*[out_slots[j ^ 1] for j, _ in out_list])
        for (j, _), x in zip(out_list, cores):
            out_slots[j ^ 1] = x
        probs, attended = line(attend, place, qkv, exps, stats, sums)

        att_slots = {0: attended}
        for m in far_masks:
            att_slots.update(
                {j ^ m: swap(x, "mp", m, "gather_attended") for j, x in list(att_slots.items())}
            )
        for j, x in list(att_slots.items()):
            att_slots[j ^ 1] = swap(x, "mp", 1, "gather_attended")
        mid, second, active, grad_upper, theirs, mine, up_vec = line(
            feed,
            pos,
            tokens,
            *[att_slots[j] for j in range(n_mp)],
            *[out_slots[j] for j in range(n_mp)],
            b_out[None],
            ln2_gain[None],
            ln2_bias[None],
            w_up,
            b_up[None],
            w_down,
            cotangent,
        )

        got = swap(theirs, "mp", 1, "sum_second")
        mine = line(keep, mine)
        total = near_sum(line(add_low, mine, got), "sum_second")
        far = swap(total, "mp", last_far, "sum_second")
        other = swap(total, "mp", 1, "sum_second")
        out_theirs, out_mine, theirs, mine = line(
            weights, pos, active, second, grad_upper, cotangent, w_down
        )
        feed_sum = Scatter(line, theirs, mine, feed_masks, "feed_weights")
        out_got = swap(out_theirs, "mp", 1, "sum_output")
        line.space()
        out_total = near_sum(line(add_low, out_mine, out_got), "sum_output")
        (far,) = wait(far)
        other_far = swap(far, "mp", 1, "sum_second")
        out_send = after(out_total, far)
        out_far = swap(out_send, "mp", last_far, "sum_output")
        out_other = swap(out_send, "mp", 1, "sum_output")
        line.space()
        grad_low, gqkv, back_vec, slot_grad = line(
            lambda *a: (lambda r: (r[0], r[1], r[3], r[2]))(back(*a)),
            pos,
            total,
            far,
            other,
            other_far,
            mid,
            cotangent,
            ln2_gain[None],
            w_out,
            qkv,
            probs,
            sums,
        )

        feed_sum.step()
        (out_other,) = wait(out_other)
        theirs_w, rest = line(
            rest_weights, first_bit, first, gqkv, grad_low, attended, slot_grad, sums
        )
        rest_got = swap(theirs_w, "dp", feed_masks[0], "rest_weights")
        (out_far,) = wait(out_far)
        out_other_far = swap(out_far, "mp", 1, "sum_output")
        theirs, mine = line(first_grad, pos, gqkv, slot_grad, sums, w_qkv, tokens)
        got = swap(theirs, "mp", 1, "sum_first")
        feed_sum.step()
        total = line(pair, mine, got)
        for m in far_masks[:-1]:
            total = line(pair, total, swap(total, "mp", m, "sum_first"))
        far = swap(total, "mp", last_far, "sum_first")
        theirs_w, rest = line(split_first, bit_of(feed_masks[1]), rest, rest_got)
        rest_got = swap(theirs_w, "dp", feed_masks[1], "rest_weights")
        output = line(
            output_sum, pos, out_total, out_far, out_other, out_other_far, mid, b_down[None]
        )
        theirs_w, rest, extra = line(split_second, bit_of(feed_masks[2]), rest, rest_got, w_qkv)
        rest_got = swap(theirs_w, "dp", feed_masks[2], "rest_weights")
        extra_got = swap(extra, "mp", 1, "sum_extra")
        for m in feed_masks[3:]:
            theirs_w, rest = line(split_sum, bit_of(m), rest, rest_got)
            rest_got = swap(theirs_w, "dp", m, "rest_weights")
        for m in feed_masks[3:]:
            feed_sum.step()
        feed_all = line(add_low, feed_sum.mine, feed_sum.got)
        feed_got = swap(feed_all, "dp", feed_masks[-1], "feed_weights")
        (far,) = wait(far)
        other = swap(after(total, far), "mp", 1, "sum_first")
        other_far = swap(far, "mp", 1, "sum_first")
        for m in far_masks:
            extra = line(pl_add, extra, extra_got)
            extra_got = swap(extra, "mp", m, "sum_extra")
        rest_all = line(
            piece_of, rest, rest_got, total, far, back_vec, up_vec
        )
        rest_got = swap(rest_all, "dp", feed_masks[-1], "rest_weights")
        feed_next = list(reversed(feed_masks))[1:]
        rest_next = list(reversed(feed_masks))[1:]
        for m in feed_next[:-2]:
            feed_all = line(concat, feed_all, feed_got)
            feed_got = swap(feed_all, "dp", m, "feed_weights")
        feed_all = line(concat, feed_all, feed_got)
        two = swap(feed_all, "dp", feed_masks[0], "feed_weights")
        one = swap(feed_all, "dp", feed_masks[1], "feed_weights")
        rest_all = line(merge, rest_all, rest_got)
        rest_got = swap(rest_all, "dp", rest_next[0], "rest_weights")
        grad_tokens = line(
            last,
            pos,
            total,
            far,
            other,
            other_far,
            extra,
            extra_got,
            tokens,
            grad_low,
            ln1_gain[None],
        )
        (two,) = wait(two)
        both = swap(two, "dp", feed_masks[1], "feed_weights")
        for m in rest_next[1:]:
            line.space()
            rest_all = line(merge, rest_all, rest_got)
            rest_got = swap(rest_all, "dp", m, "rest_weights")
        held = line(feed_unpack, place_of(feed_masks), feed_all, one)
        grad_w_down, grad_w_up = line(
            feed_unpack, place_of(feed_masks), two, both, *held
        )
        grad_w_qkv, grad_w_out, *vectors = line(
            rest_unpack, place_of(feed_masks), rest_all, rest_got, line.spare
        )
        return (
            output,
            grad_tokens,
            vectors[0][0],
            vectors[1][0],
            grad_w_qkv,
            grad_w_out,
            vectors[2][0],
            vectors[3][0],
            vectors[4][0],
            grad_w_up.reshape(dim, hidden),
            vectors[6][0],
            grad_w_down,
            vectors[5][0],
        )

    return per_device


def solution(mesh):
    return jax.shard_map(
        build(mesh.shape["dp"], mesh.shape["mp"]),
        mesh=mesh,
        in_specs=(
            P("dp", None),
            P(),
            P(),
            P(None, None, "mp"),
            P("mp", None),
            P(),
            P(),
            P(),
            P(None, "mp"),
            P("mp"),
            P("mp", None),
            P(),
            P("dp", None),
        ),
        out_specs=(
            P("dp", None),
            P("dp", None),
            P(),
            P(),
            P(None, None, "mp"),
            P("mp", None),
            P(),
            P(),
            P(),
            P(None, "mp"),
            P("mp"),
            P("mp", None),
            P(),
        ),
        check_vma=False,
    )
```

```python
import functools
import math

import jax
import jax.numpy as jnp
from jax import lax
from jax.experimental import pallas as pl
from jax.experimental.pallas import tpu as pltpu
from jax.sharding import PartitionSpec as P

HEAD_DIM = 64
SPAN = 128
LENGTH = 4096
EPSILON = 1e-05
SCALE = HEAD_DIM ** (-0.5)
LOW = -1e30

f32 = jnp.float32
bf16 = jnp.bfloat16
i32 = jnp.int32
VMEM = pl.BlockSpec(memory_space=pltpu.VMEM)
SMEM = pl.BlockSpec(memory_space=pltpu.SMEM)


def masks_of(count):
    return [1 << i for i in range(count.bit_length() - 1)]


def params(mib=60):
    return pltpu.CompilerParams(vmem_limit_bytes=mib * 1024 * 1024)


def cost():
    return pl.CostEstimate(flops=12_000_000_000, bytes_accessed=1, transcendentals=0)


def nt(a, b):
    return lax.dot_general(a, b, (((1,), (1,)), ((), ())), preferred_element_type=f32)


def tn(a, b):
    return lax.dot_general(a, b, (((0,), (0,)), ((), ())), preferred_element_type=f32)


def nn(a, b):
    return jnp.dot(a, b, preferred_element_type=f32)


def normed(x):
    c = x - jnp.mean(x, axis=-1, keepdims=True)
    r = lax.rsqrt(jnp.mean(c * c, axis=-1, keepdims=True) + EPSILON)
    return c * r, r


def norm_back(e, n, r, gain):
    k = e * gain
    return r * (
        k - jnp.mean(k, axis=-1, keepdims=True) - n * jnp.mean(k * n, axis=-1, keepdims=True)
    )


def fold(x):
    return jnp.sum(x.reshape(-1, 8, x.shape[-1]), axis=0)


def head_mask(shape, h, dtype):
    lane = lax.broadcasted_iota(i32, shape, len(shape) - 1)
    return jnp.where(lane // HEAD_DIM == h, 1.0, 0.0).astype(dtype)


def spread(x, factor):
    heads = x.shape[1] // HEAD_DIM
    return jnp.concatenate(
        [x * (head_mask((1, x.shape[1]), h, f32) * factor).astype(x.dtype) for h in range(heads)]
    )


def collect(x, factor):
    width = x.shape[1]
    heads = width // HEAD_DIM
    rows = x.shape[0] // heads
    total = x[:rows] * (head_mask((1, width), 0, f32) * factor)
    for h in range(1, heads):
        total = total + x[h * rows : (h + 1) * rows] * (head_mask((1, width), h, f32) * factor)
    return total


def to_low(v, cols):
    v = jnp.concatenate([v[:, i : i + cols] for i in range(0, v.shape[1], cols)])
    high = v.astype(bf16)
    return jnp.concatenate([high, (v - high.astype(f32)).astype(bf16)])


def from_low(x, dim):
    half = x.shape[0] // 2
    v = x[:half].astype(f32) + x[half:].astype(f32)
    count = dim // x.shape[1]
    return jnp.concatenate([v[i * 8 : (i + 1) * 8] for i in range(count)], axis=1)


def sums_of(sums_ref, which):
    pair = sums_ref[:, which // 2].astype(f32)
    blocks = pair.shape[1] // 2
    start = which % 2 * blocks
    return pair[:, start : start + blocks].reshape(-1, pair.shape[2])


def columns_of(sums_ref, start, count):
    return jnp.concatenate([sums_of(sums_ref, start + j) for j in range(count)], axis=1)


def project_kernel(
    tile, tok_ref, gain_ref, bias_ref, w_ref, first_ref, qkv_ref, out_ref, wcat, sum_ref
):
    width = w_ref.shape[2]
    for s in range(3):
        wcat[:, s * width : (s + 1) * width] = w_ref[s]
    per = tile // SPAN
    for i in range(tok_ref.shape[0] // tile):
        at = slice(i * tile, (i + 1) * tile)
        n, _ = normed(tok_ref[at].astype(f32))
        first = (n * gain_ref[...] + bias_ref[...]).astype(bf16)
        first_ref[at] = first
        both = nn(first, wcat[...]).astype(bf16)
        for s in range(3):
            part = both[:, s * width : (s + 1) * width]
            qkv_ref[s, at] = part
            if s:
                mean = jnp.mean(part.astype(f32).reshape(per, SPAN, width), axis=1)
                sum_ref[s - 1, i * per : (i + 1) * per] = mean
        sums = [jnp.sum(x.reshape(per, SPAN, -1), axis=1) for x in (first.astype(f32), n)]
        total = jnp.concatenate(sums, axis=1)
        for j in range(sum_ref.shape[0] - 2):
            sum_ref[2 + j, i * per : (i + 1) * per] = total[:, j * width : (j + 1) * width]
    for j in range(out_ref.shape[0]):
        out_ref[j] = jnp.concatenate([sum_ref[2 * j], sum_ref[2 * j + 1]]).astype(bf16)


def local_kernel(qkv_ref, exp_ref, stat_ref):
    blocks = exp_ref.shape[0]
    lanes = exp_ref.shape[2]
    key = lax.broadcasted_iota(i32, (SPAN, lanes), 0)
    query = lax.broadcasted_iota(i32, (SPAN, lanes), 1) % SPAN
    keep = key <= query
    for b in range(blocks):
        at = slice(b * SPAN, (b + 1) * SPAN)
        s = nt(qkv_ref[1, at], spread(qkv_ref[0, at], SCALE))
        s = jnp.where(keep, s, LOW)
        top = jnp.max(s, axis=0, keepdims=True)
        e = jnp.exp(s - top)
        exp_ref[b] = e
        stat_ref[b, 0:1] = top
        stat_ref[b, 1:2] = jnp.sum(e, axis=0, keepdims=True)


def attend_kernel(place_ref, qkv_ref, exp_ref, stat_ref, sums_ref, prob_ref, att_ref):
    blocks = exp_ref.shape[0]
    lanes = exp_ref.shape[2]
    slots = sums_ref.shape[0]
    place = place_ref[0]
    keys = sums_of(sums_ref, 0).astype(bf16)
    values = sums_of(sums_ref, 1).astype(bf16)
    row = lax.broadcasted_iota(i32, (slots * blocks, lanes), 0)
    at_block = ((row // blocks) ^ place) * blocks + row % blocks
    for b in range(blocks):
        at = slice(b * SPAN, (b + 1) * SPAN)
        s = nt(keys, spread(qkv_ref[0, at], SCALE)) + math.log(SPAN)
        s = jnp.where(at_block < place * blocks + b, s, LOW)
        mine = stat_ref[b, 0:1]
        top = jnp.maximum(mine, jnp.max(s, axis=0, keepdims=True))
        e = jnp.exp(s - top)
        shrink = jnp.exp(mine - top)
        scale = 1.0 / (stat_ref[b, 1:2] * shrink + jnp.sum(e, axis=0, keepdims=True))
        p = jnp.concatenate([exp_ref[b] * (shrink * scale), e * scale]).astype(bf16)
        prob_ref[b] = p
        a = tn(p, jnp.concatenate([qkv_ref[2, at], values]))
        att_ref[at] = collect(a, 1.0).astype(bf16)


def feed_kernel(
    count, pos_ref, tok_ref, *refs
):
    att = refs[:count]
    wo = refs[count : 2 * count]
    (
        b_out_ref,
        gain_ref,
        bias_ref,
        up_ref,
        b_up_ref,
        down_ref,
        cot_ref,
        mid_ref,
        second_ref,
        active_ref,
        grad_ref,
        theirs_ref,
        mine_ref,
        vec_ref,
        wcat,
    ) = refs[2 * count :]
    step = pl.program_id(0)
    me = pos_ref[0]
    width = wo[0].shape[0]

    def in_order(arrays):
        arrays = list(arrays)
        for m in masks_of(count):
            flip = (me & m) != 0
            arrays = [jnp.where(flip, arrays[j ^ m], arrays[j]) for j in range(count)]
        return arrays

    @pl.when(step == 0)
    def _():
        for j in range(count):
            wcat[pl.ds(pl.multiple_of((me ^ j) * width, width), width)] = wo[j][...]
        vec_ref[...] = jnp.zeros_like(vec_ref)

    attended = jnp.concatenate(in_order([a[...] for a in att]), axis=1)
    mid = tok_ref[...].astype(f32) + nn(attended, wcat[...]) + b_out_ref[...]
    mid_ref[...] = mid
    n, _ = normed(mid)
    second = (n * gain_ref[...] + bias_ref[...]).astype(bf16)
    second_ref[...] = second
    u = nn(second, up_ref[...]) + b_up_ref[...]
    root = math.sqrt(2.0 / math.pi)
    square = u * u
    t = jnp.tanh(u * (root + root * 0.044715 * square))
    half = 0.5 + 0.5 * t
    active_ref[...] = (u * half).astype(bf16)
    slope = half + (0.5 * u) * (1.0 - t * t) * (root + (3.0 * root * 0.044715) * square)
    grad = nt(cot_ref[...], down_ref[...]) * slope
    low = grad.astype(bf16)
    grad_ref[...] = low
    out = nt(low, up_ref[...]).astype(bf16)
    steps = pl.num_programs(0)

    @pl.when(step < steps // 2)
    def _():
        theirs_ref[...] = out

    @pl.when(step >= steps // 2)
    def _():
        mine_ref[...] = out

    vec_ref[0:8] += fold(low.astype(f32))


def weights_kernel(
    pos_ref,
    active_ref,
    second_ref,
    grad_ref,
    cot_ref,
    down_ref,
    out_theirs_ref,
    out_mine_ref,
    theirs_ref,
    mine_ref,
    down_acc,
    up_acc,
):
    step = pl.program_id(0)
    terms = nn(active_ref[...], down_ref[...]).astype(bf16)
    down = tn(active_ref[...], cot_ref[...])
    up = tn(second_ref[...], grad_ref[...])

    @pl.when(step == 0)
    def _():
        out_theirs_ref[...] = terms
        down_acc[...] = down
        up_acc[...] = up

    @pl.when(step == 1)
    def _():
        out_mine_ref[...] = terms
        first = (down_acc[...] + down).astype(bf16)
        then = (up_acc[...] + up).astype(bf16).reshape(first.shape)
        low = pos_ref[3] == 0
        theirs_ref[...] = jnp.where(low, then, first)
        mine_ref[...] = jnp.where(low, first, then)


def rest_kernel(
    bit_ref, first_ref, gqkv_ref, low_ref, att_ref, slot_ref, sums_ref, theirs_ref, mine_ref
):
    slots, _, blocks, width = slot_ref.shape
    dim = first_ref.shape[1]
    size = dim // 2
    rows = [slot_ref[:, s].reshape(slots * blocks, width) for s in range(2)]
    far_rows = (jnp.concatenate(rows, axis=1) * (1.0 / SPAN)).astype(bf16)
    far_first = columns_of(sums_ref, 2, dim // width).astype(bf16)
    out = []
    for h in range(2):
        at = slice(h * size, (h + 1) * size)
        main = tn(first_ref[:, at], gqkv_ref[...])
        far = tn(far_first[:, at], far_rows)
        last = tn(low_ref[:, at], att_ref[...])
        out.append(
            jnp.concatenate([main[:, :width], main[:, width:] + far, last], axis=1).astype(bf16)
        )
    low = bit_ref[0] == 0
    theirs_ref[:size] = jnp.where(low, out[1], out[0])
    mine_ref[:size] = jnp.where(low, out[0], out[1])
    for ref, slot in ((theirs_ref, 2), (mine_ref, 0)):
        parts = [slot_ref[j, s] for j in (slot, slot + 1) for s in range(2)]
        ref[size:] = to_low(jnp.concatenate(parts, axis=1), 4 * width)


def split_first_kernel(bit_ref, a_ref, b_ref, theirs_ref, mine_ref):
    rows = a_ref.shape[0] - 16
    cols = a_ref.shape[1]
    size = rows // 2
    total = (a_ref[:rows].astype(f32) + b_ref[:rows].astype(f32)).astype(bf16)
    low = bit_ref[0] == 0
    theirs_ref[:size] = jnp.where(low, total[size:], total[:size])
    mine_ref[:size] = jnp.where(low, total[:size], total[size:])
    slots = from_low(a_ref[rows:], cols) + from_low(b_ref[rows:], cols)
    none = jnp.zeros((8, cols // 2), f32)
    for ref, at in ((theirs_ref, slice(cols // 2, cols)), (mine_ref, slice(0, cols // 2))):
        ref[size:] = to_low(jnp.concatenate([slots[:, at], none], axis=1), cols)


def split_second_kernel(bit_ref, a_ref, b_ref, w_ref, theirs_ref, mine_ref, extra_ref):
    rows = a_ref.shape[0] - 16
    cols = a_ref.shape[1]
    width = w_ref.shape[2]
    size = rows // 2
    total = (a_ref[:rows].astype(f32) + b_ref[:rows].astype(f32)).astype(bf16)
    low = bit_ref[0] == 0
    theirs_ref[...] = jnp.where(low, total[size:], total[:size])
    mine_ref[...] = jnp.where(low, total[:size], total[size:])
    own = from_low(a_ref[rows:], cols) + from_low(b_ref[rows:], cols)
    own = (own * (1.0 / SPAN)).astype(bf16)
    extra_ref[...] = nt(own[:, :width], w_ref[1]) + nt(own[:, width : 2 * width], w_ref[2])


def split_kernel(bit_ref, a_ref, b_ref, theirs_ref, mine_ref):
    total = (a_ref[...].astype(f32) + b_ref[...].astype(f32)).astype(bf16)
    size = total.shape[0] // 2
    low = bit_ref[0] == 0
    theirs_ref[...] = jnp.where(low, total[size:], total[:size])
    mine_ref[...] = jnp.where(low, total[:size], total[size:])


def two_halves(refs, half, core):
    own, far, other, other_far = refs
    mine = half == core
    a = jnp.where(mine, own[...], other[...])
    b = jnp.where(mine, far[...], other_far[...])
    return a.astype(f32) + b.astype(f32)


def back_kernel(
    pos_ref,
    own_ref,
    far_ref,
    other_ref,
    other_far_ref,
    mid_ref,
    cot_ref,
    gain_ref,
    wo_ref,
    qkv_ref,
    prob_ref,
    sums_ref,
    low_ref,
    gqkv_ref,
    slot_ref,
    vec_ref,
):
    step = pl.program_id(0)
    slots = sums_ref.shape[0]
    width = wo_ref.shape[0]

    @pl.when(step == 0)
    def _():
        slot_ref[...] = jnp.zeros_like(slot_ref)
        vec_ref[...] = jnp.zeros_like(vec_ref)

    e = two_halves((own_ref, far_ref, other_ref, other_far_ref), step, pos_ref[1])
    n, r = normed(mid_ref[...])
    cot = cot_ref[...].astype(f32)
    grad_mid = cot + norm_back(e, n, r, gain_ref[...])
    low = grad_mid.astype(bf16)
    low_ref[...] = low
    vec_ref[0:8] += fold(grad_mid)
    vec_ref[8:16] += fold(e * n)
    vec_ref[16:24] += fold(e)
    vec_ref[24:32] += fold(cot)

    grad_att = nt(low, wo_ref[...]).astype(bf16)
    far_keys = sums_of(sums_ref, 0).astype(bf16)
    far_values = sums_of(sums_ref, 1).astype(bf16)
    far_gk = jnp.zeros(far_keys.shape, f32)
    far_gv = jnp.zeros(far_keys.shape, f32)
    for b in range(prob_ref.shape[0]):
        at = slice(b * SPAN, (b + 1) * SPAN)
        da = spread(grad_att[at], 1.0)
        query = spread(qkv_ref[0, at], SCALE)
        keys = jnp.concatenate([qkv_ref[1, at], far_keys])
        values = jnp.concatenate([qkv_ref[2, at], far_values])
        p_low = prob_ref[b]
        p = p_low.astype(f32)
        dp = nt(values, da)
        ds = (p * (dp - jnp.sum(p * dp, axis=0, keepdims=True))).astype(bf16)
        gq = collect(tn(ds, keys), SCALE)
        gk = nn(ds, query)
        gv = nn(p_low, da)
        gqkv_ref[at, :width] = gq.astype(bf16)
        gqkv_ref[at, width : 2 * width] = gk[:SPAN].astype(bf16)
        gqkv_ref[at, 2 * width :] = gv[:SPAN].astype(bf16)
        far_gk = far_gk + gk[SPAN:]
        far_gv = far_gv + gv[SPAN:]
    slot_ref[:, 0] += far_gk.reshape(slots, -1, width)
    slot_ref[:, 1] += far_gv.reshape(slots, -1, width)


def first_kernel(
    pos_ref, gqkv_ref, slot_ref, sums_ref, w_ref, tok_ref, theirs_ref, mine_ref, wcat, vec
):
    step = pl.program_id(0)
    steps = pl.num_programs(0)
    dim, width = w_ref.shape[1:]
    tile = gqkv_ref.shape[0]
    half = tile * (steps // 2)

    @pl.when(step == 0)
    def _():
        vec[...] = jnp.zeros_like(vec)
        for s in range(3):
            wcat[:, s * width : (s + 1) * width] = w_ref[s]

    e = nt(gqkv_ref[...], wcat[...])
    n, _ = normed(tok_ref[...].astype(f32))
    vec[0:8] += fold(e * n)
    vec[8:16] += fold(e)
    out = e.astype(bf16)
    at = pl.ds(pl.multiple_of((step % (steps // 2)) * tile, tile), tile)

    @pl.when(step < steps // 2)
    def _():
        theirs_ref[at] = out

    @pl.when(step >= steps // 2)
    def _():
        mine_ref[at] = out

    @pl.when(step == steps - 1)
    def _():
        rows = [
            (slot_ref[:, s].reshape(-1, width) * (1.0 / SPAN)).astype(bf16) for s in range(2)
        ]
        far = nt(rows[0], w_ref[1]) + nt(rows[1], w_ref[2])
        normal = columns_of(sums_ref, 2 + dim // width, dim // width)
        gain = jnp.sum(vec[0:8], axis=0, keepdims=True) + jnp.sum(
            far * normal, axis=0, keepdims=True
        )
        offset = jnp.sum(vec[8:16], axis=0, keepdims=True) + SPAN * jnp.sum(
            far, axis=0, keepdims=True
        )
        low = to_low(jnp.concatenate([gain, offset, jnp.zeros((6, dim), f32)]), dim)
        theirs_ref[half:] = low
        mine_ref[half:] = low


def pair_kernel(a_ref, b_ref, out_ref):
    dim = a_ref.shape[1]
    rows = a_ref.shape[0] - 16
    out_ref[:rows] = (a_ref[:rows].astype(f32) + b_ref[:rows].astype(f32)).astype(bf16)
    out_ref[rows:] = to_low(from_low(a_ref[rows:], dim) + from_low(b_ref[rows:], dim), dim)


def piece_kernel(mine_ref, got_ref, near_ref, far_ref, back_ref, up_ref, out_ref):
    dim = near_ref.shape[1]
    hidden = up_ref.shape[1]
    rows, cols = mine_ref.shape
    out_ref[:rows] = (mine_ref[...].astype(f32) + got_ref[...].astype(f32)).astype(bf16)
    last = near_ref.shape[0] - 16
    first = (from_low(near_ref[last:], dim) + from_low(far_ref[last:], dim))[:2]
    vectors = [first]
    for k in range(4):
        vectors.append(jnp.sum(back_ref[8 * k : 8 * k + 8], axis=0, keepdims=True))
    up = jnp.sum(up_ref[...], axis=0, keepdims=True)
    if hidden < dim:
        up = jnp.concatenate([up, jnp.zeros((1, dim - hidden), f32)], axis=1)
    vectors += [up, jnp.zeros((1, dim), f32)]
    out_ref[rows:] = to_low(jnp.concatenate(vectors), cols)


def merge_kernel(dim, a_ref, b_ref, out_ref):
    cols = a_ref.shape[1]
    rows = a_ref.shape[0] - 16 * (dim // cols)
    out_ref[:rows] = a_ref[:rows]
    out_ref[rows : 2 * rows] = b_ref[:rows]
    out_ref[2 * rows :] = to_low(from_low(a_ref[rows:], dim) + from_low(b_ref[rows:], dim), cols)


def last_kernel(
    pos_ref,
    own_ref,
    far_ref,
    other_ref,
    other_far_ref,
    extra_ref,
    extra_far_ref,
    tok_ref,
    low_ref,
    gain_ref,
    out_ref,
):
    step = pl.program_id(0)
    half = step // (pl.num_programs(0) // 2)
    e = two_halves((own_ref, far_ref, other_ref, other_far_ref), half, pos_ref[1])
    per = e.shape[0] // SPAN
    pieces = []
    for i in range(per):
        at = pl.ds(step * per + i, 1)
        pieces.append(e[i * SPAN : (i + 1) * SPAN] + (extra_ref[at] + extra_far_ref[at]))
    e = jnp.concatenate(pieces)
    n, r = normed(tok_ref[...].astype(f32))
    out_ref[...] = (low_ref[...].astype(f32) + norm_back(e, n, r, gain_ref[...])).astype(bf16)


def add_kernel(parts, a_ref, b_ref, *out_refs):
    size = a_ref.shape[0] // parts
    for k in range(parts):
        at = slice(k * size, (k + 1) * size)
        out_refs[k][...] = (a_ref[at].astype(f32) + b_ref[at].astype(f32)).astype(bf16)


def slot_kernel(a_ref, b_ref, out_ref):
    out_ref[...] = a_ref[: out_ref.shape[0]] + b_ref[...]


def spacer_kernel(x_ref, out_ref):
    out_ref[...] = x_ref[...] * 0.5


def keep_kernel(x_ref, out_ref):
    out_ref[...] = x_ref[...]


def concat_kernel(a_ref, b_ref, out_ref):
    rows = a_ref.shape[0]
    out_ref[:rows] = a_ref[...]
    out_ref[rows:] = b_ref[...]


def output_kernel(
    pos_ref, own_ref, far_ref, other_ref, other_far_ref, mid_ref, b_ref, out_ref
):
    half = pl.program_id(0) // (pl.num_programs(0) // 2)
    e = two_halves((own_ref, far_ref, other_ref, other_far_ref), half, pos_ref[1])
    out_ref[...] = (mid_ref[...] + e + b_ref[...]).astype(bf16)


def feed_unpack_kernel(pieces, far, at_ref, own_ref, one_ref, *refs):
    down_ref, up_ref, scratch, sems = refs[-4:]
    rows = own_ref.shape[0]
    size = rows // pieces
    top = at_ref[0] // pieces
    low = at_ref[0] % pieces

    def copies(ref):
        return [
            pltpu.make_async_copy(
                scratch.at[pl.ds(q * rows, rows)], ref.at[pl.ds(q * rows, rows)], sems.at[q]
            )
            for q in range(2)
        ]

    def fill(ref):
        out = copies(ref)
        for q in range(2):
            for k in range(pieces):
                at = pl.ds(pl.multiple_of((k ^ low) * size, size), size)
                x = jnp.where(top % 2 == q, own_ref[at], one_ref[at])
                scratch[q * rows + k * size : q * rows + (k + 1) * size] = x.astype(f32)
            out[q].start()
        for q in range(2):
            out[q].wait()

    is_down = top // 2 == far

    @pl.when(is_down)
    def _():
        fill(down_ref)

    @pl.when(jnp.logical_not(is_down))
    def _():
        fill(up_ref)


def rest_unpack_kernel(
    count, dim, at_ref, near_ref, far_ref, spare_ref, qkv_ref, out_ref, *refs
):
    vec_refs, scratch = refs[:-1], refs[-1]
    cols = near_ref.shape[1]
    last = near_ref.shape[0] - 16 * (dim // cols)
    rows = 2 * last // count
    width = qkv_ref.shape[2]
    part = count // 2
    top = at_ref[0] // part
    low = at_ref[0] % part
    for k in range(count):
        start = pl.multiple_of(((k % part) ^ low) * rows, rows)
        is_near = top == k // part
        x = jnp.where(is_near, near_ref[pl.ds(start, rows)], far_ref[pl.ds(start, rows)])
        x = x.astype(f32)
        for s in range(3):
            qkv_ref[s, k * rows : (k + 1) * rows] = x[:, s * width : (s + 1) * width]
        scratch[k * rows : (k + 1) * rows] = x[:, 3 * width :]
    out_ref[...] = scratch[...].T
    vectors = from_low(near_ref[last:], dim) + from_low(far_ref[last:], dim)
    for k, ref in enumerate(vec_refs):
        ref[...] = vectors[k : k + 1, : ref.shape[1]]


def build(n_dp, n_mp):
    def swap(x, axis, mask, label):
        n = n_dp if axis == "dp" else n_mp
        with jax.named_scope(label):
            return lax.ppermute(x, axis, [(i, i ^ mask) for i in range(n)])

    def pick(x, index, rows):
        return lax.dynamic_slice_in_dim(x, index * rows, rows, 0)

    def halves(x, mask, axis):
        bit = jnp.where((lax.axis_index(axis) & mask) == 0, 0, 1)
        size = x.shape[0] // 2
        return pick(x, 1 - bit, size), pick(x, bit, size)

    def after(x, *others):
        return lax.optimization_barrier((x, others))[0]

    far_masks = masks_of(n_mp)[1:]
    dp_masks = masks_of(n_dp)
    feed_masks = [dp_masks[1], dp_masks[0]] + dp_masks[2:]

    class Line:
        def __init__(self):
            self.last = ()

        def __call__(self, work, *inputs):
            if self.last:
                inputs = after(inputs, *self.last)
            result = work(*inputs)
            first = result[-1] if isinstance(result, (tuple, list)) else result
            self.last = (first,)
            return result

        def space(self, x=None):
            if x is not None:
                self.spare = x
            self.spare = self(spacer, self.spare)

    def add_parts(parts, a, b):
        part = jax.ShapeDtypeStruct((a.shape[0] // parts, *a.shape[1:]), bf16)
        return pl.pallas_call(
            functools.partial(add_kernel, parts),
            out_shape=(part,) * parts,
            in_specs=[VMEM, VMEM],
            out_specs=(VMEM,) * parts,
            compiler_params=params(16),
            cost_estimate=cost(),
            name="add",
        )(a, b)

    def add_low(a, b):
        return add_parts(1, a, b)[0]

    def spacer(x):
        return pl.pallas_call(
            spacer_kernel,
            out_shape=jax.ShapeDtypeStruct(x.shape, x.dtype),
            in_specs=[VMEM],
            out_specs=VMEM,
            compiler_params=params(16),
            cost_estimate=cost(),
            name="spacer",
        )(x)

    def split_sum(bit, mine, got):
        size = mine.shape[0] // 2
        half = jax.ShapeDtypeStruct((size, mine.shape[1]), bf16)
        return pl.pallas_call(
            split_kernel,
            out_shape=(half, half),
            in_specs=[SMEM, VMEM, VMEM],
            out_specs=(VMEM, VMEM),
            compiler_params=params(16),
            cost_estimate=cost(),
            name="split",
        )(bit, mine, got)

    def bit_of(mask):
        return jnp.where((lax.axis_index("dp") & mask) == 0, 0, 1).astype(i32)[None]

    class Scatter:
        def __init__(self, line, theirs, mine, masks, label):
            self.line, self.label = line, label
            self.rest = list(masks)
            self.mine = mine
            self.got = swap(theirs, "dp", self.rest.pop(0), label)

        def step(self):
            mask = self.rest.pop(0)
            theirs, self.mine = self.line(split_sum, bit_of(mask), self.mine, self.got)
            self.got = swap(theirs, "dp", mask, self.label)

    def per_device(
        tokens,
        ln1_gain,
        ln1_bias,
        w_qkv,
        w_out,
        b_out,
        ln2_gain,
        ln2_bias,
        w_up,
        b_up,
        w_down,
        b_down,
        cotangent,
    ):
        rows, dim = tokens.shape
        width = w_qkv.shape[2]
        hidden = w_up.shape[1]
        heads = width // HEAD_DIM
        blocks = rows // SPAN
        lanes = heads * SPAN
        group = LENGTH // rows
        entries = SPAN + group * blocks
        seq_masks = masks_of(group)
        me = lax.axis_index("mp")
        place = lax.axis_index("dp") % group
        first_bit = bit_of(feed_masks[0])
        pos = jnp.concatenate(
            [jnp.stack([me, me & 1, place]).astype(i32), bit_of(feed_masks[0])]
        )
        half = rows // 2
        tile = half // 2
        tiles = 4
        sds = jax.ShapeDtypeStruct

        def rolled(i, pos):
            return ((i + (1 - pos[1]) * (tiles // 2)) % tiles, 0)

        def theirs_row(i, pos):
            return (jnp.minimum(i, tiles // 2 - 1), 0)

        def mine_row(i, pos):
            return (jnp.maximum(i - tiles // 2, 0), 0)

        def half_rolled(i, pos):
            return (jnp.where(i == 0, 1 - pos[1], pos[1]), 0)

        def whole(*_):
            return (0, 0)

        def by_row(i, *_):
            return (i, 0)

        def zeros(n):
            return lambda *_: (0,) * n

        def block(shape, index):
            return pl.BlockSpec(shape, index)

        def plain(kernel, name, in_specs, out_shape, scratch=(), mib=24):
            return pl.pallas_call(
                kernel,
                out_shape=out_shape,
                in_specs=in_specs,
                out_specs=tuple(VMEM for _ in out_shape),
                scratch_shapes=list(scratch),
                compiler_params=params(mib),
                cost_estimate=cost(),
                name=name,
            )

        def gridded(
            kernel, name, grid, in_specs, out_specs, out_shape, scratch=(), mib=60, aliases=None
        ):
            return pl.pallas_call(
                kernel,
                grid_spec=pltpu.PrefetchScalarGridSpec(
                    num_scalar_prefetch=1,
                    grid=(grid,),
                    in_specs=in_specs,
                    out_specs=out_specs,
                    scratch_shapes=list(scratch),
                ),
                out_shape=out_shape,
                input_output_aliases=aliases or {},
                compiler_params=params(60 if name in ('feed',) else 30 if name in ('back', 'weights') else 20),
                cost_estimate=cost(),
                name=name,
            )

        row_block = block((tile, dim), rolled)
        row_vector = block((1, dim), whole)
        tile_block = block((tile, dim), by_row)
        one_tile = block((tile, dim), whole)

        project = plain(
            functools.partial(project_kernel, tile),
            "project",
            [VMEM] * 4,
            (
                sds((rows, dim), bf16),
                sds((3, rows, width), bf16),
                sds((1 + dim // width, 2 * blocks, width), bf16),
            ),
            [
                pltpu.VMEM((dim, 3 * width), bf16),
                pltpu.VMEM((2 + 2 * (dim // width), blocks, width), f32),
            ],
            60,
        )
        local = plain(
            local_kernel,
            "local",
            [VMEM],
            (sds((blocks, SPAN, lanes), f32), sds((blocks, 2, lanes), f32)),
        )
        attend = plain(
            attend_kernel,
            "attend",
            [SMEM] + [VMEM] * 4,
            (sds((blocks, entries, lanes), bf16), sds((rows, width), bf16)),
        )
        half_rows = block((half, dim), half_rolled)
        half_hidden = block((half, hidden), half_rolled)
        feed = gridded(
            functools.partial(feed_kernel, n_mp),
            "feed",
            2,
            [half_rows]
            + [block((half, width), half_rolled)] * n_mp
            + [block((width, dim), whole)] * n_mp
            + [row_vector] * 3
            + [
                block((dim, hidden), whole),
                block((1, hidden), whole),
                block((hidden, dim), whole),
                half_rows,
            ],
            [
                half_rows,
                half_rows,
                half_hidden,
                half_hidden,
                block((half, dim), whole),
                block((half, dim), whole),
                block((8, hidden), whole),
            ],
            (
                sds((rows, dim), f32),
                sds((rows, dim), bf16),
                sds((rows, hidden), bf16),
                sds((rows, hidden), bf16),
                sds((half, dim), bf16),
                sds((half, dim), bf16),
                sds((8, hidden), f32),
            ),
            [pltpu.VMEM((dim, dim), bf16)],
        )
        weights = gridded(
            weights_kernel,
            "weights",
            2,
            [half_hidden, half_rows, half_hidden, half_rows, block((hidden, dim), whole)],
            [block((half, dim), whole)] * 2 + [block((hidden, dim), whole)] * 2,
            (
                sds((half, dim), bf16),
                sds((half, dim), bf16),
                sds((hidden, dim), bf16),
                sds((hidden, dim), bf16),
            ),
            [pltpu.VMEM((hidden, dim), f32), pltpu.VMEM((dim, hidden), f32)],
        )
        rest_weights = plain(
            rest_kernel,
            "rest_weights",
            [SMEM] + [VMEM] * 6,
            (sds((dim // 2 + 16, 4 * width), bf16), sds((dim // 2 + 16, 4 * width), bf16)),
            mib=60,
        )
        slot_shape = (group, 2, blocks, width)
        sums_shape = (group, 1 + dim // width, 2 * blocks, width)
        back = gridded(
            back_kernel,
            "back",
            2,
            [block((half, dim), whole)] * 4
            + [
                block((half, dim), by_row),
                block((half, dim), by_row),
                row_vector,
                block((width, dim), whole),
                block((3, half, width), lambda i, pos: (0, i, 0)),
                block((blocks // 2, entries, lanes), lambda i, pos: (i, 0, 0)),
                block(sums_shape, zeros(4)),
            ],
            [
                block((half, dim), by_row),
                block((half, 3 * width), by_row),
                block(slot_shape, zeros(4)),
                block((32, dim), whole),
            ],
            (
                sds((rows, dim), bf16),
                sds((rows, 3 * width), bf16),
                sds(slot_shape, f32),
                sds((32, dim), f32),
            ),
        )
        first_block = block((half + 16, dim), whole)
        first_grad = gridded(
            first_kernel,
            "first",
            2,
            [
                block((half, 3 * width), half_rolled),
                block(slot_shape, zeros(4)),
                block(sums_shape, zeros(4)),
                block((3, dim, width), zeros(3)),
                half_rows,
            ],
            [first_block, first_block],
            (sds((half + 16, dim), bf16), sds((half + 16, dim), bf16)),
            [pltpu.VMEM((dim, 3 * width), bf16), pltpu.VMEM((16, dim), f32)],
        )
        def own_tile(i, pos):
            return (jnp.clip(i - pos[1] * (tiles // 2), 0, tiles // 2 - 1), 0)

        def other_tile(i, pos):
            return (jnp.clip(i - (1 - pos[1]) * (tiles // 2), 0, tiles // 2 - 1), 0)

        terms_specs = [block((half, dim), whole)] * 4
        tile_block = block((half, dim), by_row)
        last = gridded(
            last_kernel,
            "last",
            2,
            terms_specs + [block((blocks, dim), whole)] * 2 + [tile_block, tile_block, row_vector],
            tile_block,
            sds((rows, dim), bf16),
        )
        output_sum = gridded(
            output_kernel,
            "output",
            2,
            terms_specs + [tile_block, row_vector],
            tile_block,
            sds((rows, dim), bf16),
        )
        def feed_unpack(at, own, one, *held):
            anywhere = pl.BlockSpec(memory_space=pl.ANY)
            return pl.pallas_call(
                functools.partial(feed_unpack_kernel, n_dp // 4, 1 if held else 0),
                out_shape=(sds((hidden, dim), f32), sds((hidden, dim), f32)),
                in_specs=[SMEM, VMEM, VMEM] + [anywhere] * len(held),
                out_specs=(anywhere, anywhere),
                scratch_shapes=[pltpu.VMEM((hidden, dim), f32), pltpu.SemaphoreType.DMA((2,))],
                input_output_aliases={3 + k: k for k in range(len(held))},
                compiler_params=params(20),
                cost_estimate=cost(),
                name="feed_unpack",
            )(at, own, one, *held)

        rest_unpack = plain(
            functools.partial(rest_unpack_kernel, n_dp, dim),
            "rest_unpack",
            [SMEM, VMEM, VMEM, VMEM],
            (sds((3, dim, width), f32), sds((width, dim), f32))
            + (sds((1, dim), f32),) * 6
            + (sds((1, hidden), f32),),
            [pltpu.VMEM((dim, width), f32)],
        )

        def like(kernel, name, shape, dtype, *operands):
            specs = [VMEM] * len(operands)
            return plain(kernel, name, specs, (sds(shape, dtype),))(*operands)[0]

        def pair(a, b):
            return like(pair_kernel, "pair", a.shape, bf16, a, b)

        def concat(a, b):
            return like(concat_kernel, "concat", (2 * a.shape[0], a.shape[1]), bf16, a, b)

        def keep(x):
            return like(keep_kernel, "keep", x.shape, bf16, x)

        def pl_add(a, b):
            return like(slot_kernel, "plus", a.shape, f32, a, b)

        cols = 4 * width
        quarter = dim // 4
        split_first = plain(
            split_first_kernel,
            "split_first",
            [SMEM, VMEM, VMEM],
            (sds((quarter + 16, cols), bf16), sds((quarter + 16, cols), bf16)),
        )
        split_second = plain(
            split_second_kernel,
            "split_second",
            [SMEM, VMEM, VMEM, VMEM],
            (
                sds((quarter // 2, cols), bf16),
                sds((quarter // 2, cols), bf16),
                sds((blocks, dim), f32),
            ),
        )

        vec_rows = 16 * (dim // (4 * width))

        def piece_of(mine, *operands):
            shape = (mine.shape[0] + vec_rows, 4 * width)
            return like(piece_kernel, "piece", shape, bf16, mine, *operands)

        def merge(a, b):
            shape = (2 * a.shape[0] - vec_rows, 4 * width)
            return like(functools.partial(merge_kernel, dim), "merge", shape, bf16, a, b)

        def place_of(masks):
            at = jnp.zeros((1,), i32)
            for m in masks:
                at = at * 2 + bit_of(m)
            return at


        def wait(*arrived):
            return line(lambda *x: x, *arrived)

        def near_sum(total, label):
            for m in far_masks[:-1]:
                total = line(add_low, total, swap(total, "mp", m, label))
            return total

        last_far = far_masks[-1]

        line = Line()

        out_slots = {0: w_out}
        for m in far_masks:
            out_slots.update(
                {j ^ m: swap(x, "mp", m, "gather_w_out") for j, x in list(out_slots.items())}
            )
        line.spare = ln1_gain[None]
        pos, place = wait(pos, place[None].astype(i32))
        first, qkv, summary = line(project, tokens, ln1_gain[None], ln1_bias[None], w_qkv)
        out_list = list(out_slots.items())
        sums = after(summary, *[x for _, x in out_list])[None]
        for i, m in enumerate(seq_masks):
            got = swap(sums, "dp", m, "summaries")
            if i == 0:
                exps, stats = line(local, qkv)
                for j, x in out_list:
                    out_slots[j ^ 1] = swap(after(x, stats), "mp", 1, "gather_w_out")
            sums = line(lambda a, b: jnp.concatenate([a, b]), sums, got)
        cores = wait(*[out_slots[j ^ 1] for j, _ in out_list])
        for (j, _), x in zip(out_list, cores):
            out_slots[j ^ 1] = x
        probs, attended = line(attend, place, qkv, exps, stats, sums)

        att_slots = {0: attended}
        for m in far_masks:
            att_slots.update(
                {j ^ m: swap(x, "mp", m, "gather_attended") for j, x in list(att_slots.items())}
            )
        for j, x in list(att_slots.items()):
            att_slots[j ^ 1] = swap(x, "mp", 1, "gather_attended")
        mid, second, active, grad_upper, theirs, mine, up_vec = line(
            feed,
            pos,
            tokens,
            *[att_slots[j] for j in range(n_mp)],
            *[out_slots[j] for j in range(n_mp)],
            b_out[None],
            ln2_gain[None],
            ln2_bias[None],
            w_up,
            b_up[None],
            w_down,
            cotangent,
        )

        got = swap(theirs, "mp", 1, "sum_second")
        mine = line(keep, mine)
        total = near_sum(line(add_low, mine, got), "sum_second")
        far = swap(total, "mp", last_far, "sum_second")
        other = swap(total, "mp", 1, "sum_second")
        out_theirs, out_mine, theirs, mine = line(
            weights, pos, active, second, grad_upper, cotangent, w_down
        )
        feed_sum = Scatter(line, theirs, mine, feed_masks, "feed_weights")
        out_got = swap(out_theirs, "mp", 1, "sum_output")
        line.space()
        out_total = near_sum(line(add_low, out_mine, out_got), "sum_output")
        (far,) = wait(far)
        other_far = swap(far, "mp", 1, "sum_second")
        out_send = after(out_total, far)
        out_far = swap(out_send, "mp", last_far, "sum_output")
        out_other = swap(out_send, "mp", 1, "sum_output")
        line.space()
        grad_low, gqkv, back_vec, slot_grad = line(
            lambda *a: (lambda r: (r[0], r[1], r[3], r[2]))(back(*a)),
            pos,
            total,
            far,
            other,
            other_far,
            mid,
            cotangent,
            ln2_gain[None],
            w_out,
            qkv,
            probs,
            sums,
        )

        feed_sum.step()
        (out_other,) = wait(out_other)
        theirs_w, rest = line(
            rest_weights, first_bit, first, gqkv, grad_low, attended, slot_grad, sums
        )
        rest_got = swap(theirs_w, "dp", feed_masks[0], "rest_weights")
        (out_far,) = wait(out_far)
        out_other_far = swap(out_far, "mp", 1, "sum_output")
        theirs, mine = line(first_grad, pos, gqkv, slot_grad, sums, w_qkv, tokens)
        got = swap(theirs, "mp", 1, "sum_first")
        feed_sum.step()
        theirs_w, rest = line(split_first, bit_of(feed_masks[1]), rest, rest_got)
        rest_got = swap(theirs_w, "dp", feed_masks[1], "rest_weights")
        total = line(pair, mine, got)
        for m in far_masks[:-1]:
            total = line(pair, total, swap(total, "mp", m, "sum_first"))
        far = swap(total, "mp", last_far, "sum_first")
        output = line(
            output_sum, pos, out_total, out_far, out_other, out_other_far, mid, b_down[None]
        )
        theirs_w, rest, extra = line(split_second, bit_of(feed_masks[2]), rest, rest_got, w_qkv)
        rest_got = swap(theirs_w, "dp", feed_masks[2], "rest_weights")
        extra_got = swap(extra, "mp", 1, "sum_extra")
        for m in feed_masks[3:]:
            theirs_w, rest = line(split_sum, bit_of(m), rest, rest_got)
            rest_got = swap(theirs_w, "dp", m, "rest_weights")
        for m in feed_masks[3:]:
            feed_sum.step()
        feed_all = line(add_low, feed_sum.mine, feed_sum.got)
        feed_got = swap(feed_all, "dp", feed_masks[-1], "feed_weights")
        (far,) = wait(far)
        other = swap(after(total, far), "mp", 1, "sum_first")
        other_far = swap(far, "mp", 1, "sum_first")
        for m in far_masks:
            extra = line(pl_add, extra, extra_got)
            extra_got = swap(extra, "mp", m, "sum_extra")
        rest_all = line(
            piece_of, rest, rest_got, total, far, back_vec, up_vec
        )
        rest_got = swap(rest_all, "dp", feed_masks[-1], "rest_weights")
        feed_next = list(reversed(feed_masks))[1:]
        rest_next = list(reversed(feed_masks))[1:]
        for m in feed_next[:-2]:
            feed_all = line(concat, feed_all, feed_got)
            feed_got = swap(feed_all, "dp", m, "feed_weights")
        feed_all = line(concat, feed_all, feed_got)
        two = swap(feed_all, "dp", feed_masks[0], "feed_weights")
        one = swap(feed_all, "dp", feed_masks[1], "feed_weights")
        rest_all = line(merge, rest_all, rest_got)
        rest_got = swap(rest_all, "dp", rest_next[0], "rest_weights")
        grad_tokens = line(
            last,
            pos,
            total,
            far,
            other,
            other_far,
            extra,
            extra_got,
            tokens,
            grad_low,
            ln1_gain[None],
        )
        (two,) = wait(two)
        both = swap(two, "dp", feed_masks[1], "feed_weights")
        for m in rest_next[1:]:
            line.space()
            rest_all = line(merge, rest_all, rest_got)
            rest_got = swap(rest_all, "dp", m, "rest_weights")
        held = line(feed_unpack, place_of(feed_masks), feed_all, one)
        grad_w_down, grad_w_up = line(
            feed_unpack, place_of(feed_masks), two, both, *held
        )
        grad_w_qkv, grad_w_out, *vectors = line(
            rest_unpack, place_of(feed_masks), rest_all, rest_got, line.spare
        )
        return (
            output,
            grad_tokens,
            vectors[0][0],
            vectors[1][0],
            grad_w_qkv,
            grad_w_out,
            vectors[2][0],
            vectors[3][0],
            vectors[4][0],
            grad_w_up.reshape(dim, hidden),
            vectors[6][0],
            grad_w_down,
            vectors[5][0],
        )

    return per_device


def solution(mesh):
    return jax.shard_map(
        build(mesh.shape["dp"], mesh.shape["mp"]),
        mesh=mesh,
        in_specs=(
            P("dp", None),
            P(),
            P(),
            P(None, None, "mp"),
            P("mp", None),
            P(),
            P(),
            P(),
            P(None, "mp"),
            P("mp"),
            P("mp", None),
            P(),
            P("dp", None),
        ),
        out_specs=(
            P("dp", None),
            P("dp", None),
            P(),
            P(),
            P(None, None, "mp"),
            P("mp", None),
            P(),
            P(),
            P(),
            P(None, "mp"),
            P("mp"),
            P("mp", None),
            P(),
        ),
        check_vma=False,
    )
```

```python
import functools
import math

import jax
import jax.numpy as jnp
from jax import lax
from jax.experimental import pallas as pl
from jax.experimental.pallas import tpu as pltpu
from jax.sharding import PartitionSpec as P

HEAD_DIM = 64
SPAN = 128
LENGTH = 4096
EPSILON = 1e-05
SCALE = HEAD_DIM ** (-0.5)
LOW = -1e30

f32 = jnp.float32
bf16 = jnp.bfloat16
i32 = jnp.int32
VMEM = pl.BlockSpec(memory_space=pltpu.VMEM)
SMEM = pl.BlockSpec(memory_space=pltpu.SMEM)


def masks_of(count):
    return [1 << i for i in range(count.bit_length() - 1)]


def params(mib=60):
    return pltpu.CompilerParams(vmem_limit_bytes=mib * 1024 * 1024)


def cost():
    return pl.CostEstimate(flops=12_000_000_000, bytes_accessed=1, transcendentals=0)


def nt(a, b):
    return lax.dot_general(a, b, (((1,), (1,)), ((), ())), preferred_element_type=f32)


def tn(a, b):
    return lax.dot_general(a, b, (((0,), (0,)), ((), ())), preferred_element_type=f32)


def nn(a, b):
    return jnp.dot(a, b, preferred_element_type=f32)


def normed(x):
    c = x - jnp.mean(x, axis=-1, keepdims=True)
    r = lax.rsqrt(jnp.mean(c * c, axis=-1, keepdims=True) + EPSILON)
    return c * r, r


def norm_back(e, n, r, gain):
    k = e * gain
    return r * (
        k - jnp.mean(k, axis=-1, keepdims=True) - n * jnp.mean(k * n, axis=-1, keepdims=True)
    )


def fold(x):
    return jnp.sum(x.reshape(-1, 8, x.shape[-1]), axis=0)


def head_mask(shape, h, dtype):
    lane = lax.broadcasted_iota(i32, shape, len(shape) - 1)
    return jnp.where(lane // HEAD_DIM == h, 1.0, 0.0).astype(dtype)


def spread(x, factor):
    heads = x.shape[1] // HEAD_DIM
    return jnp.concatenate(
        [x * (head_mask((1, x.shape[1]), h, f32) * factor).astype(x.dtype) for h in range(heads)]
    )


def collect(x, factor):
    width = x.shape[1]
    heads = width // HEAD_DIM
    rows = x.shape[0] // heads
    total = x[:rows] * (head_mask((1, width), 0, f32) * factor)
    for h in range(1, heads):
        total = total + x[h * rows : (h + 1) * rows] * (head_mask((1, width), h, f32) * factor)
    return total


def to_low(v, cols):
    v = jnp.concatenate([v[:, i : i + cols] for i in range(0, v.shape[1], cols)])
    high = v.astype(bf16)
    return jnp.concatenate([high, (v - high.astype(f32)).astype(bf16)])


def from_low(x, dim):
    half = x.shape[0] // 2
    v = x[:half].astype(f32) + x[half:].astype(f32)
    count = dim // x.shape[1]
    return jnp.concatenate([v[i * 8 : (i + 1) * 8] for i in range(count)], axis=1)


def sums_of(sums_ref, which):
    pair = sums_ref[:, which // 2].astype(f32)
    blocks = pair.shape[1] // 2
    start = which % 2 * blocks
    return pair[:, start : start + blocks].reshape(-1, pair.shape[2])


def columns_of(sums_ref, start, count):
    return jnp.concatenate([sums_of(sums_ref, start + j) for j in range(count)], axis=1)


def project_kernel(
    tile, tok_ref, gain_ref, bias_ref, w_ref, first_ref, qkv_ref, out_ref, wcat, sum_ref
):
    width = w_ref.shape[2]
    for s in range(3):
        wcat[:, s * width : (s + 1) * width] = w_ref[s]
    per = tile // SPAN
    for i in range(tok_ref.shape[0] // tile):
        at = slice(i * tile, (i + 1) * tile)
        n, _ = normed(tok_ref[at].astype(f32))
        first = (n * gain_ref[...] + bias_ref[...]).astype(bf16)
        first_ref[at] = first
        both = nn(first, wcat[...]).astype(bf16)
        for s in range(3):
            part = both[:, s * width : (s + 1) * width]
            qkv_ref[s, at] = part
            if s:
                mean = jnp.mean(part.astype(f32).reshape(per, SPAN, width), axis=1)
                sum_ref[s - 1, i * per : (i + 1) * per] = mean
        sums = [jnp.sum(x.reshape(per, SPAN, -1), axis=1) for x in (first.astype(f32), n)]
        total = jnp.concatenate(sums, axis=1)
        for j in range(sum_ref.shape[0] - 2):
            sum_ref[2 + j, i * per : (i + 1) * per] = total[:, j * width : (j + 1) * width]
    for j in range(out_ref.shape[0]):
        out_ref[j] = jnp.concatenate([sum_ref[2 * j], sum_ref[2 * j + 1]]).astype(bf16)


def local_kernel(qkv_ref, exp_ref, stat_ref):
    blocks = exp_ref.shape[0]
    lanes = exp_ref.shape[2]
    key = lax.broadcasted_iota(i32, (SPAN, lanes), 0)
    query = lax.broadcasted_iota(i32, (SPAN, lanes), 1) % SPAN
    keep = key <= query
    for b in range(blocks):
        at = slice(b * SPAN, (b + 1) * SPAN)
        s = nt(qkv_ref[1, at], spread(qkv_ref[0, at], SCALE))
        s = jnp.where(keep, s, LOW)
        top = jnp.max(s, axis=0, keepdims=True)
        e = jnp.exp(s - top)
        exp_ref[b] = e
        stat_ref[b, 0:1] = top
        stat_ref[b, 1:2] = jnp.sum(e, axis=0, keepdims=True)


def attend_kernel(place_ref, qkv_ref, exp_ref, stat_ref, sums_ref, prob_ref, att_ref):
    blocks = exp_ref.shape[0]
    lanes = exp_ref.shape[2]
    slots = sums_ref.shape[0]
    place = place_ref[0]
    keys = sums_of(sums_ref, 0).astype(bf16)
    values = sums_of(sums_ref, 1).astype(bf16)
    row = lax.broadcasted_iota(i32, (slots * blocks, lanes), 0)
    at_block = ((row // blocks) ^ place) * blocks + row % blocks
    for b in range(blocks):
        at = slice(b * SPAN, (b + 1) * SPAN)
        s = nt(keys, spread(qkv_ref[0, at], SCALE)) + math.log(SPAN)
        s = jnp.where(at_block < place * blocks + b, s, LOW)
        mine = stat_ref[b, 0:1]
        top = jnp.maximum(mine, jnp.max(s, axis=0, keepdims=True))
        e = jnp.exp(s - top)
        shrink = jnp.exp(mine - top)
        scale = 1.0 / (stat_ref[b, 1:2] * shrink + jnp.sum(e, axis=0, keepdims=True))
        p = jnp.concatenate([exp_ref[b] * (shrink * scale), e * scale]).astype(bf16)
        prob_ref[b] = p
        a = tn(p, jnp.concatenate([qkv_ref[2, at], values]))
        att_ref[at] = collect(a, 1.0).astype(bf16)


def feed_kernel(
    count, pos_ref, tok_ref, *refs
):
    att = refs[:count]
    wo = refs[count : 2 * count]
    (
        b_out_ref,
        gain_ref,
        bias_ref,
        up_ref,
        b_up_ref,
        down_ref,
        cot_ref,
        mid_ref,
        second_ref,
        active_ref,
        grad_ref,
        theirs_ref,
        mine_ref,
        vec_ref,
        wcat,
    ) = refs[2 * count :]
    step = pl.program_id(0)
    me = pos_ref[0]
    width = wo[0].shape[0]

    def in_order(arrays):
        arrays = list(arrays)
        for m in masks_of(count):
            flip = (me & m) != 0
            arrays = [jnp.where(flip, arrays[j ^ m], arrays[j]) for j in range(count)]
        return arrays

    @pl.when(step == 0)
    def _():
        for j in range(count):
            wcat[pl.ds(pl.multiple_of((me ^ j) * width, width), width)] = wo[j][...]
        vec_ref[...] = jnp.zeros_like(vec_ref)

    attended = jnp.concatenate(in_order([a[...] for a in att]), axis=1)
    mid = tok_ref[...].astype(f32) + nn(attended, wcat[...]) + b_out_ref[...]
    mid_ref[...] = mid
    n, _ = normed(mid)
    second = (n * gain_ref[...] + bias_ref[...]).astype(bf16)
    second_ref[...] = second
    u = nn(second, up_ref[...]) + b_up_ref[...]
    root = math.sqrt(2.0 / math.pi)
    square = u * u
    t = jnp.tanh(u * (root + root * 0.044715 * square))
    half = 0.5 + 0.5 * t
    active_ref[...] = (u * half).astype(bf16)
    slope = half + (0.5 * u) * (1.0 - t * t) * (root + (3.0 * root * 0.044715) * square)
    grad = nt(cot_ref[...], down_ref[...]) * slope
    low = grad.astype(bf16)
    grad_ref[...] = low
    out = nt(low, up_ref[...]).astype(bf16)
    steps = pl.num_programs(0)

    @pl.when(step < steps // 2)
    def _():
        theirs_ref[...] = out

    @pl.when(step >= steps // 2)
    def _():
        mine_ref[...] = out

    vec_ref[0:8] += fold(low.astype(f32))


def weights_kernel(
    pos_ref,
    active_ref,
    second_ref,
    grad_ref,
    cot_ref,
    down_ref,
    out_theirs_ref,
    out_mine_ref,
    theirs_ref,
    mine_ref,
    down_acc,
    up_acc,
):
    step = pl.program_id(0)
    terms = nn(active_ref[...], down_ref[...]).astype(bf16)
    down = tn(active_ref[...], cot_ref[...])
    up = tn(second_ref[...], grad_ref[...])

    @pl.when(step == 0)
    def _():
        out_theirs_ref[...] = terms
        down_acc[...] = down
        up_acc[...] = up

    @pl.when(step == 1)
    def _():
        out_mine_ref[...] = terms
        first = (down_acc[...] + down).astype(bf16)
        then = (up_acc[...] + up).astype(bf16).reshape(first.shape)
        low = pos_ref[3] == 0
        theirs_ref[...] = jnp.where(low, then, first)
        mine_ref[...] = jnp.where(low, first, then)


def rest_kernel(
    bit_ref, first_ref, gqkv_ref, low_ref, att_ref, slot_ref, sums_ref, theirs_ref, mine_ref
):
    slots, _, blocks, width = slot_ref.shape
    dim = first_ref.shape[1]
    size = dim // 2
    rows = [slot_ref[:, s].reshape(slots * blocks, width) for s in range(2)]
    far_rows = (jnp.concatenate(rows, axis=1) * (1.0 / SPAN)).astype(bf16)
    far_first = columns_of(sums_ref, 2, dim // width).astype(bf16)
    out = []
    for h in range(2):
        at = slice(h * size, (h + 1) * size)
        main = tn(first_ref[:, at], gqkv_ref[...])
        far = tn(far_first[:, at], far_rows)
        last = tn(low_ref[:, at], att_ref[...])
        out.append(
            jnp.concatenate([main[:, :width], main[:, width:] + far, last], axis=1).astype(bf16)
        )
    low = bit_ref[0] == 0
    theirs_ref[:size] = jnp.where(low, out[1], out[0])
    mine_ref[:size] = jnp.where(low, out[0], out[1])
    for ref, slot in ((theirs_ref, 2), (mine_ref, 0)):
        parts = [slot_ref[j, s] for j in (slot, slot + 1) for s in range(2)]
        ref[size:] = to_low(jnp.concatenate(parts, axis=1), 4 * width)


def split_first_kernel(bit_ref, a_ref, b_ref, theirs_ref, mine_ref):
    rows = a_ref.shape[0] - 16
    cols = a_ref.shape[1]
    size = rows // 2
    total = (a_ref[:rows].astype(f32) + b_ref[:rows].astype(f32)).astype(bf16)
    low = bit_ref[0] == 0
    theirs_ref[:size] = jnp.where(low, total[size:], total[:size])
    mine_ref[:size] = jnp.where(low, total[:size], total[size:])
    slots = from_low(a_ref[rows:], cols) + from_low(b_ref[rows:], cols)
    none = jnp.zeros((8, cols // 2), f32)
    for ref, at in ((theirs_ref, slice(cols // 2, cols)), (mine_ref, slice(0, cols // 2))):
        ref[size:] = to_low(jnp.concatenate([slots[:, at], none], axis=1), cols)


def split_second_kernel(bit_ref, a_ref, b_ref, w_ref, theirs_ref, mine_ref, extra_ref):
    rows = a_ref.shape[0] - 16
    cols = a_ref.shape[1]
    width = w_ref.shape[2]
    size = rows // 2
    total = (a_ref[:rows].astype(f32) + b_ref[:rows].astype(f32)).astype(bf16)
    low = bit_ref[0] == 0
    theirs_ref[...] = jnp.where(low, total[size:], total[:size])
    mine_ref[...] = jnp.where(low, total[:size], total[size:])
    own = from_low(a_ref[rows:], cols) + from_low(b_ref[rows:], cols)
    own = (own * (1.0 / SPAN)).astype(bf16)
    extra_ref[...] = nt(own[:, :width], w_ref[1]) + nt(own[:, width : 2 * width], w_ref[2])


def split_kernel(bit_ref, a_ref, b_ref, theirs_ref, mine_ref):
    total = (a_ref[...].astype(f32) + b_ref[...].astype(f32)).astype(bf16)
    size = total.shape[0] // 2
    low = bit_ref[0] == 0
    theirs_ref[...] = jnp.where(low, total[size:], total[:size])
    mine_ref[...] = jnp.where(low, total[:size], total[size:])


def two_halves(refs, half, core):
    own, far, other, other_far = refs
    mine = half == core
    a = jnp.where(mine, own[...], other[...])
    b = jnp.where(mine, far[...], other_far[...])
    return a.astype(f32) + b.astype(f32)


def back_kernel(
    pos_ref,
    own_ref,
    far_ref,
    other_ref,
    other_far_ref,
    mid_ref,
    cot_ref,
    gain_ref,
    wo_ref,
    qkv_ref,
    prob_ref,
    sums_ref,
    low_ref,
    gqkv_ref,
    slot_ref,
    vec_ref,
):
    step = pl.program_id(0)
    slots = sums_ref.shape[0]
    width = wo_ref.shape[0]

    @pl.when(step == 0)
    def _():
        slot_ref[...] = jnp.zeros_like(slot_ref)
        vec_ref[...] = jnp.zeros_like(vec_ref)

    e = two_halves((own_ref, far_ref, other_ref, other_far_ref), step, pos_ref[1])
    n, r = normed(mid_ref[...])
    cot = cot_ref[...].astype(f32)
    grad_mid = cot + norm_back(e, n, r, gain_ref[...])
    low = grad_mid.astype(bf16)
    low_ref[...] = low
    vec_ref[0:8] += fold(grad_mid)
    vec_ref[8:16] += fold(e * n)
    vec_ref[16:24] += fold(e)
    vec_ref[24:32] += fold(cot)

    grad_att = nt(low, wo_ref[...]).astype(bf16)
    far_keys = sums_of(sums_ref, 0).astype(bf16)
    far_values = sums_of(sums_ref, 1).astype(bf16)
    far_gk = jnp.zeros(far_keys.shape, f32)
    far_gv = jnp.zeros(far_keys.shape, f32)
    for b in range(prob_ref.shape[0]):
        at = slice(b * SPAN, (b + 1) * SPAN)
        da = spread(grad_att[at], 1.0)
        query = spread(qkv_ref[0, at], SCALE)
        keys = jnp.concatenate([qkv_ref[1, at], far_keys])
        values = jnp.concatenate([qkv_ref[2, at], far_values])
        p_low = prob_ref[b]
        p = p_low.astype(f32)
        dp = nt(values, da)
        ds = (p * (dp - jnp.sum(p * dp, axis=0, keepdims=True))).astype(bf16)
        gq = collect(tn(ds, keys), SCALE)
        gk = nn(ds, query)
        gv = nn(p_low, da)
        gqkv_ref[at, :width] = gq.astype(bf16)
        gqkv_ref[at, width : 2 * width] = gk[:SPAN].astype(bf16)
        gqkv_ref[at, 2 * width :] = gv[:SPAN].astype(bf16)
        far_gk = far_gk + gk[SPAN:]
        far_gv = far_gv + gv[SPAN:]
    slot_ref[:, 0] += far_gk.reshape(slots, -1, width)
    slot_ref[:, 1] += far_gv.reshape(slots, -1, width)


def first_kernel(
    pos_ref, gqkv_ref, slot_ref, sums_ref, w_ref, tok_ref, theirs_ref, mine_ref, wcat, vec
):
    step = pl.program_id(0)
    steps = pl.num_programs(0)
    dim, width = w_ref.shape[1:]
    tile = gqkv_ref.shape[0]
    half = tile * (steps // 2)

    @pl.when(step == 0)
    def _():
        vec[...] = jnp.zeros_like(vec)
        for s in range(3):
            wcat[:, s * width : (s + 1) * width] = w_ref[s]

    e = nt(gqkv_ref[...], wcat[...])
    n, _ = normed(tok_ref[...].astype(f32))
    vec[0:8] += fold(e * n)
    vec[8:16] += fold(e)
    out = e.astype(bf16)
    at = pl.ds(pl.multiple_of((step % (steps // 2)) * tile, tile), tile)

    @pl.when(step < steps // 2)
    def _():
        theirs_ref[at] = out

    @pl.when(step >= steps // 2)
    def _():
        mine_ref[at] = out

    @pl.when(step == steps - 1)
    def _():
        rows = [
            (slot_ref[:, s].reshape(-1, width) * (1.0 / SPAN)).astype(bf16) for s in range(2)
        ]
        far = nt(rows[0], w_ref[1]) + nt(rows[1], w_ref[2])
        normal = columns_of(sums_ref, 2 + dim // width, dim // width)
        gain = jnp.sum(vec[0:8], axis=0, keepdims=True) + jnp.sum(
            far * normal, axis=0, keepdims=True
        )
        offset = jnp.sum(vec[8:16], axis=0, keepdims=True) + SPAN * jnp.sum(
            far, axis=0, keepdims=True
        )
        low = to_low(jnp.concatenate([gain, offset, jnp.zeros((6, dim), f32)]), dim)
        theirs_ref[half:] = low
        mine_ref[half:] = low


def pair_kernel(a_ref, b_ref, out_ref):
    dim = a_ref.shape[1]
    rows = a_ref.shape[0] - 16
    out_ref[:rows] = (a_ref[:rows].astype(f32) + b_ref[:rows].astype(f32)).astype(bf16)
    out_ref[rows:] = to_low(from_low(a_ref[rows:], dim) + from_low(b_ref[rows:], dim), dim)


def piece_kernel(mine_ref, got_ref, near_ref, far_ref, back_ref, up_ref, out_ref):
    dim = near_ref.shape[1]
    hidden = up_ref.shape[1]
    rows, cols = mine_ref.shape
    out_ref[:rows] = (mine_ref[...].astype(f32) + got_ref[...].astype(f32)).astype(bf16)
    last = near_ref.shape[0] - 16
    first = (from_low(near_ref[last:], dim) + from_low(far_ref[last:], dim))[:2]
    vectors = [first]
    for k in range(4):
        vectors.append(jnp.sum(back_ref[8 * k : 8 * k + 8], axis=0, keepdims=True))
    up = jnp.sum(up_ref[...], axis=0, keepdims=True)
    if hidden < dim:
        up = jnp.concatenate([up, jnp.zeros((1, dim - hidden), f32)], axis=1)
    vectors += [up, jnp.zeros((1, dim), f32)]
    out_ref[rows:] = to_low(jnp.concatenate(vectors), cols)


def merge_kernel(dim, a_ref, b_ref, out_ref):
    cols = a_ref.shape[1]
    rows = a_ref.shape[0] - 16 * (dim // cols)
    out_ref[:rows] = a_ref[:rows]
    out_ref[rows : 2 * rows] = b_ref[:rows]
    out_ref[2 * rows :] = to_low(from_low(a_ref[rows:], dim) + from_low(b_ref[rows:], dim), cols)


def last_kernel(
    pos_ref,
    own_ref,
    far_ref,
    other_ref,
    other_far_ref,
    extra_ref,
    extra_far_ref,
    tok_ref,
    low_ref,
    gain_ref,
    out_ref,
):
    step = pl.program_id(0)
    half = step // (pl.num_programs(0) // 2)
    e = two_halves((own_ref, far_ref, other_ref, other_far_ref), half, pos_ref[1])
    per = e.shape[0] // SPAN
    pieces = []
    for i in range(per):
        at = pl.ds(step * per + i, 1)
        pieces.append(e[i * SPAN : (i + 1) * SPAN] + (extra_ref[at] + extra_far_ref[at]))
    e = jnp.concatenate(pieces)
    n, r = normed(tok_ref[...].astype(f32))
    out_ref[...] = (low_ref[...].astype(f32) + norm_back(e, n, r, gain_ref[...])).astype(bf16)


def add_kernel(parts, a_ref, b_ref, *out_refs):
    size = a_ref.shape[0] // parts
    for k in range(parts):
        at = slice(k * size, (k + 1) * size)
        out_refs[k][...] = (a_ref[at].astype(f32) + b_ref[at].astype(f32)).astype(bf16)


def slot_kernel(a_ref, b_ref, out_ref):
    out_ref[...] = a_ref[: out_ref.shape[0]] + b_ref[...]


def spacer_kernel(x_ref, out_ref):
    out_ref[...] = x_ref[...] * 0.5


def keep_kernel(x_ref, out_ref):
    out_ref[...] = x_ref[...]


def concat_kernel(a_ref, b_ref, out_ref):
    rows = a_ref.shape[0]
    out_ref[:rows] = a_ref[...]
    out_ref[rows:] = b_ref[...]


def output_kernel(
    pos_ref, own_ref, far_ref, other_ref, other_far_ref, mid_ref, b_ref, out_ref
):
    half = pl.program_id(0) // (pl.num_programs(0) // 2)
    e = two_halves((own_ref, far_ref, other_ref, other_far_ref), half, pos_ref[1])
    out_ref[...] = (mid_ref[...] + e + b_ref[...]).astype(bf16)


def feed_unpack_kernel(pieces, far, at_ref, own_ref, one_ref, *refs):
    down_ref, up_ref, scratch, sems = refs[-4:]
    rows = own_ref.shape[0]
    size = rows // pieces
    top = at_ref[0] // pieces
    low = at_ref[0] % pieces

    def copies(ref):
        return [
            pltpu.make_async_copy(
                scratch.at[pl.ds(q * rows, rows)], ref.at[pl.ds(q * rows, rows)], sems.at[q]
            )
            for q in range(2)
        ]

    def fill(ref):
        out = copies(ref)
        for q in range(2):
            for k in range(pieces):
                at = pl.ds(pl.multiple_of((k ^ low) * size, size), size)
                x = jnp.where(top % 2 == q, own_ref[at], one_ref[at])
                scratch[q * rows + k * size : q * rows + (k + 1) * size] = x.astype(f32)
            out[q].start()
        for q in range(2):
            out[q].wait()

    is_down = top // 2 == far

    @pl.when(is_down)
    def _():
        fill(down_ref)

    @pl.when(jnp.logical_not(is_down))
    def _():
        fill(up_ref)


def rest_unpack_kernel(
    count, dim, at_ref, near_ref, far_ref, spare_ref, qkv_ref, out_ref, *refs
):
    vec_refs, scratch = refs[:-1], refs[-1]
    cols = near_ref.shape[1]
    last = near_ref.shape[0] - 16 * (dim // cols)
    rows = 2 * last // count
    width = qkv_ref.shape[2]
    part = count // 2
    top = at_ref[0] // part
    low = at_ref[0] % part
    for k in range(count):
        start = pl.multiple_of(((k % part) ^ low) * rows, rows)
        is_near = top == k // part
        x = jnp.where(is_near, near_ref[pl.ds(start, rows)], far_ref[pl.ds(start, rows)])
        x = x.astype(f32)
        for s in range(3):
            qkv_ref[s, k * rows : (k + 1) * rows] = x[:, s * width : (s + 1) * width]
        scratch[k * rows : (k + 1) * rows] = x[:, 3 * width :]
    out_ref[...] = scratch[...].T
    vectors = from_low(near_ref[last:], dim) + from_low(far_ref[last:], dim)
    for k, ref in enumerate(vec_refs):
        ref[...] = vectors[k : k + 1, : ref.shape[1]]


def build(n_dp, n_mp):
    def swap(x, axis, mask, label):
        n = n_dp if axis == "dp" else n_mp
        with jax.named_scope(label):
            return lax.ppermute(x, axis, [(i, i ^ mask) for i in range(n)])

    def pick(x, index, rows):
        return lax.dynamic_slice_in_dim(x, index * rows, rows, 0)

    def halves(x, mask, axis):
        bit = jnp.where((lax.axis_index(axis) & mask) == 0, 0, 1)
        size = x.shape[0] // 2
        return pick(x, 1 - bit, size), pick(x, bit, size)

    def after(x, *others):
        return lax.optimization_barrier((x, others))[0]

    far_masks = masks_of(n_mp)[1:]
    dp_masks = masks_of(n_dp)
    feed_masks = [dp_masks[1], dp_masks[0]] + dp_masks[2:]

    class Line:
        def __init__(self):
            self.last = ()

        def __call__(self, work, *inputs):
            if self.last:
                inputs = after(inputs, *self.last)
            result = work(*inputs)
            first = result[-1] if isinstance(result, (tuple, list)) else result
            self.last = (first,)
            return result

        def space(self, x=None):
            if x is not None:
                self.spare = x
            self.spare = self(spacer, self.spare)

    def add_parts(parts, a, b):
        part = jax.ShapeDtypeStruct((a.shape[0] // parts, *a.shape[1:]), bf16)
        return pl.pallas_call(
            functools.partial(add_kernel, parts),
            out_shape=(part,) * parts,
            in_specs=[VMEM, VMEM],
            out_specs=(VMEM,) * parts,
            compiler_params=params(16),
            cost_estimate=cost(),
            name="add",
        )(a, b)

    def add_low(a, b):
        return add_parts(1, a, b)[0]

    def spacer(x):
        return pl.pallas_call(
            spacer_kernel,
            out_shape=jax.ShapeDtypeStruct(x.shape, x.dtype),
            in_specs=[VMEM],
            out_specs=VMEM,
            compiler_params=params(16),
            cost_estimate=cost(),
            name="spacer",
        )(x)

    def split_sum(bit, mine, got):
        size = mine.shape[0] // 2
        half = jax.ShapeDtypeStruct((size, mine.shape[1]), bf16)
        return pl.pallas_call(
            split_kernel,
            out_shape=(half, half),
            in_specs=[SMEM, VMEM, VMEM],
            out_specs=(VMEM, VMEM),
            compiler_params=params(16),
            cost_estimate=cost(),
            name="split",
        )(bit, mine, got)

    def bit_of(mask):
        return jnp.where((lax.axis_index("dp") & mask) == 0, 0, 1).astype(i32)[None]

    class Scatter:
        def __init__(self, line, theirs, mine, masks, label):
            self.line, self.label = line, label
            self.rest = list(masks)
            self.mine = mine
            self.got = swap(theirs, "dp", self.rest.pop(0), label)

        def step(self):
            mask = self.rest.pop(0)
            theirs, self.mine = self.line(split_sum, bit_of(mask), self.mine, self.got)
            self.got = swap(theirs, "dp", mask, self.label)

    def per_device(
        tokens,
        ln1_gain,
        ln1_bias,
        w_qkv,
        w_out,
        b_out,
        ln2_gain,
        ln2_bias,
        w_up,
        b_up,
        w_down,
        b_down,
        cotangent,
    ):
        rows, dim = tokens.shape
        width = w_qkv.shape[2]
        hidden = w_up.shape[1]
        heads = width // HEAD_DIM
        blocks = rows // SPAN
        lanes = heads * SPAN
        group = LENGTH // rows
        entries = SPAN + group * blocks
        seq_masks = masks_of(group)
        me = lax.axis_index("mp")
        place = lax.axis_index("dp") % group
        first_bit = bit_of(feed_masks[0])
        pos = jnp.concatenate(
            [jnp.stack([me, me & 1, place]).astype(i32), bit_of(feed_masks[0])]
        )
        half = rows // 2
        tile = half // 2
        tiles = 4
        sds = jax.ShapeDtypeStruct

        def rolled(i, pos):
            return ((i + (1 - pos[1]) * (tiles // 2)) % tiles, 0)

        def theirs_row(i, pos):
            return (jnp.minimum(i, tiles // 2 - 1), 0)

        def mine_row(i, pos):
            return (jnp.maximum(i - tiles // 2, 0), 0)

        def half_rolled(i, pos):
            return (jnp.where(i == 0, 1 - pos[1], pos[1]), 0)

        def whole(*_):
            return (0, 0)

        def by_row(i, *_):
            return (i, 0)

        def zeros(n):
            return lambda *_: (0,) * n

        def block(shape, index):
            return pl.BlockSpec(shape, index)

        def plain(kernel, name, in_specs, out_shape, scratch=(), mib=24):
            return pl.pallas_call(
                kernel,
                out_shape=out_shape,
                in_specs=in_specs,
                out_specs=tuple(VMEM for _ in out_shape),
                scratch_shapes=list(scratch),
                compiler_params=params(mib),
                cost_estimate=cost(),
                name=name,
            )

        def gridded(
            kernel, name, grid, in_specs, out_specs, out_shape, scratch=(), mib=60, aliases=None
        ):
            return pl.pallas_call(
                kernel,
                grid_spec=pltpu.PrefetchScalarGridSpec(
                    num_scalar_prefetch=1,
                    grid=(grid,),
                    in_specs=in_specs,
                    out_specs=out_specs,
                    scratch_shapes=list(scratch),
                ),
                out_shape=out_shape,
                input_output_aliases=aliases or {},
                compiler_params=params(60 if name in ('feed',) else 30 if name in ('back', 'weights') else 20),
                cost_estimate=cost(),
                name=name,
            )

        row_block = block((tile, dim), rolled)
        row_vector = block((1, dim), whole)
        tile_block = block((tile, dim), by_row)
        one_tile = block((tile, dim), whole)

        project = plain(
            functools.partial(project_kernel, tile),
            "project",
            [VMEM] * 4,
            (
                sds((rows, dim), bf16),
                sds((3, rows, width), bf16),
                sds((1 + dim // width, 2 * blocks, width), bf16),
            ),
            [
                pltpu.VMEM((dim, 3 * width), bf16),
                pltpu.VMEM((2 + 2 * (dim // width), blocks, width), f32),
            ],
            60,
        )
        local = plain(
            local_kernel,
            "local",
            [VMEM],
            (sds((blocks, SPAN, lanes), f32), sds((blocks, 2, lanes), f32)),
        )
        attend = plain(
            attend_kernel,
            "attend",
            [SMEM] + [VMEM] * 4,
            (sds((blocks, entries, lanes), bf16), sds((rows, width), bf16)),
        )
        half_rows = block((half, dim), half_rolled)
        half_hidden = block((half, hidden), half_rolled)
        feed = gridded(
            functools.partial(feed_kernel, n_mp),
            "feed",
            2,
            [half_rows]
            + [block((half, width), half_rolled)] * n_mp
            + [block((width, dim), whole)] * n_mp
            + [row_vector] * 3
            + [
                block((dim, hidden), whole),
                block((1, hidden), whole),
                block((hidden, dim), whole),
                half_rows,
            ],
            [
                half_rows,
                half_rows,
                half_hidden,
                half_hidden,
                block((half, dim), whole),
                block((half, dim), whole),
                block((8, hidden), whole),
            ],
            (
                sds((rows, dim), f32),
                sds((rows, dim), bf16),
                sds((rows, hidden), bf16),
                sds((rows, hidden), bf16),
                sds((half, dim), bf16),
                sds((half, dim), bf16),
                sds((8, hidden), f32),
            ),
            [pltpu.VMEM((dim, dim), bf16)],
        )
        weights = gridded(
            weights_kernel,
            "weights",
            2,
            [half_hidden, half_rows, half_hidden, half_rows, block((hidden, dim), whole)],
            [block((half, dim), whole)] * 2 + [block((hidden, dim), whole)] * 2,
            (
                sds((half, dim), bf16),
                sds((half, dim), bf16),
                sds((hidden, dim), bf16),
                sds((hidden, dim), bf16),
            ),
            [pltpu.VMEM((hidden, dim), f32), pltpu.VMEM((dim, hidden), f32)],
        )
        rest_weights = plain(
            rest_kernel,
            "rest_weights",
            [SMEM] + [VMEM] * 6,
            (sds((dim // 2 + 16, 4 * width), bf16), sds((dim // 2 + 16, 4 * width), bf16)),
            mib=60,
        )
        slot_shape = (group, 2, blocks, width)
        sums_shape = (group, 1 + dim // width, 2 * blocks, width)
        back = gridded(
            back_kernel,
            "back",
            2,
            [block((half, dim), whole)] * 4
            + [
                block((half, dim), by_row),
                block((half, dim), by_row),
                row_vector,
                block((width, dim), whole),
                block((3, half, width), lambda i, pos: (0, i, 0)),
                block((blocks // 2, entries, lanes), lambda i, pos: (i, 0, 0)),
                block(sums_shape, zeros(4)),
            ],
            [
                block((half, dim), by_row),
                block((half, 3 * width), by_row),
                block(slot_shape, zeros(4)),
                block((32, dim), whole),
            ],
            (
                sds((rows, dim), bf16),
                sds((rows, 3 * width), bf16),
                sds(slot_shape, f32),
                sds((32, dim), f32),
            ),
        )
        first_block = block((half + 16, dim), whole)
        first_grad = gridded(
            first_kernel,
            "first",
            2,
            [
                block((half, 3 * width), half_rolled),
                block(slot_shape, zeros(4)),
                block(sums_shape, zeros(4)),
                block((3, dim, width), zeros(3)),
                half_rows,
            ],
            [first_block, first_block],
            (sds((half + 16, dim), bf16), sds((half + 16, dim), bf16)),
            [pltpu.VMEM((dim, 3 * width), bf16), pltpu.VMEM((16, dim), f32)],
        )
        def own_tile(i, pos):
            return (jnp.clip(i - pos[1] * (tiles // 2), 0, tiles // 2 - 1), 0)

        def other_tile(i, pos):
            return (jnp.clip(i - (1 - pos[1]) * (tiles // 2), 0, tiles // 2 - 1), 0)

        terms_specs = [block((half, dim), whole)] * 4
        tile_block = block((half, dim), by_row)
        last = gridded(
            last_kernel,
            "last",
            2,
            terms_specs + [block((blocks, dim), whole)] * 2 + [tile_block, tile_block, row_vector],
            tile_block,
            sds((rows, dim), bf16),
        )
        output_sum = gridded(
            output_kernel,
            "output",
            2,
            terms_specs + [tile_block, row_vector],
            tile_block,
            sds((rows, dim), bf16),
        )
        def feed_unpack(at, own, one, *held):
            anywhere = pl.BlockSpec(memory_space=pl.ANY)
            return pl.pallas_call(
                functools.partial(feed_unpack_kernel, n_dp // 4, 1 if held else 0),
                out_shape=(sds((hidden, dim), f32), sds((hidden, dim), f32)),
                in_specs=[SMEM, VMEM, VMEM] + [anywhere] * len(held),
                out_specs=(anywhere, anywhere),
                scratch_shapes=[pltpu.VMEM((hidden, dim), f32), pltpu.SemaphoreType.DMA((2,))],
                input_output_aliases={3 + k: k for k in range(len(held))},
                compiler_params=params(20),
                cost_estimate=cost(),
                name="feed_unpack",
            )(at, own, one, *held)

        rest_unpack = plain(
            functools.partial(rest_unpack_kernel, n_dp, dim),
            "rest_unpack",
            [SMEM, VMEM, VMEM, VMEM],
            (sds((3, dim, width), f32), sds((width, dim), f32))
            + (sds((1, dim), f32),) * 6
            + (sds((1, hidden), f32),),
            [pltpu.VMEM((dim, width), f32)],
        )

        def like(kernel, name, shape, dtype, *operands):
            specs = [VMEM] * len(operands)
            return plain(kernel, name, specs, (sds(shape, dtype),))(*operands)[0]

        def pair(a, b):
            return like(pair_kernel, "pair", a.shape, bf16, a, b)

        def concat(a, b):
            return like(concat_kernel, "concat", (2 * a.shape[0], a.shape[1]), bf16, a, b)

        def keep(x):
            return like(keep_kernel, "keep", x.shape, bf16, x)

        def pl_add(a, b):
            return like(slot_kernel, "plus", a.shape, f32, a, b)

        cols = 4 * width
        quarter = dim // 4
        split_first = plain(
            split_first_kernel,
            "split_first",
            [SMEM, VMEM, VMEM],
            (sds((quarter + 16, cols), bf16), sds((quarter + 16, cols), bf16)),
        )
        split_second = plain(
            split_second_kernel,
            "split_second",
            [SMEM, VMEM, VMEM, VMEM],
            (
                sds((quarter // 2, cols), bf16),
                sds((quarter // 2, cols), bf16),
                sds((blocks, dim), f32),
            ),
        )

        vec_rows = 16 * (dim // (4 * width))

        def piece_of(mine, *operands):
            shape = (mine.shape[0] + vec_rows, 4 * width)
            return like(piece_kernel, "piece", shape, bf16, mine, *operands)

        def merge(a, b):
            shape = (2 * a.shape[0] - vec_rows, 4 * width)
            return like(functools.partial(merge_kernel, dim), "merge", shape, bf16, a, b)

        def place_of(masks):
            at = jnp.zeros((1,), i32)
            for m in masks:
                at = at * 2 + bit_of(m)
            return at


        def wait(*arrived):
            return line(lambda *x: x, *arrived)

        def near_sum(total, label):
            for m in far_masks[:-1]:
                total = line(add_low, total, swap(total, "mp", m, label))
            return total

        last_far = far_masks[-1]

        line = Line()

        out_slots = {0: w_out}
        for m in far_masks:
            out_slots.update(
                {j ^ m: swap(x, "mp", m, "gather_w_out") for j, x in list(out_slots.items())}
            )
        line.spare = ln1_gain[None]
        pos, place = wait(pos, place[None].astype(i32))
        first, qkv, summary = line(project, tokens, ln1_gain[None], ln1_bias[None], w_qkv)
        out_list = list(out_slots.items())
        sums = after(summary, *[x for _, x in out_list])[None]
        for i, m in enumerate(seq_masks):
            got = swap(sums, "dp", m, "summaries")
            if i == 0:
                exps, stats = line(local, qkv)
                for j, x in out_list:
                    out_slots[j ^ 1] = swap(after(x, stats), "mp", 1, "gather_w_out")
            sums = line(lambda a, b: jnp.concatenate([a, b]), sums, got)
        cores = wait(*[out_slots[j ^ 1] for j, _ in out_list])
        for (j, _), x in zip(out_list, cores):
            out_slots[j ^ 1] = x
        probs, attended = line(attend, place, qkv, exps, stats, sums)

        att_slots = {0: attended}
        for m in far_masks:
            att_slots.update(
                {j ^ m: swap(x, "mp", m, "gather_attended") for j, x in list(att_slots.items())}
            )
        for j, x in list(att_slots.items()):
            att_slots[j ^ 1] = swap(x, "mp", 1, "gather_attended")
        mid, second, active, grad_upper, theirs, mine, up_vec = line(
            feed,
            pos,
            tokens,
            *[att_slots[j] for j in range(n_mp)],
            *[out_slots[j] for j in range(n_mp)],
            b_out[None],
            ln2_gain[None],
            ln2_bias[None],
            w_up,
            b_up[None],
            w_down,
            cotangent,
        )

        got = swap(theirs, "mp", 1, "sum_second")
        mine = line(keep, mine)
        total = near_sum(line(add_low, mine, got), "sum_second")
        far = swap(total, "mp", last_far, "sum_second")
        other = swap(total, "mp", 1, "sum_second")
        out_theirs, out_mine, theirs, mine = line(
            weights, pos, active, second, grad_upper, cotangent, w_down
        )
        feed_sum = Scatter(line, theirs, mine, feed_masks, "feed_weights")
        out_got = swap(out_theirs, "mp", 1, "sum_output")
        line.space()
        out_total = near_sum(line(add_low, out_mine, out_got), "sum_output")
        (far,) = wait(far)
        other_far = swap(far, "mp", 1, "sum_second")
        out_send = after(out_total, far)
        out_far = swap(out_send, "mp", last_far, "sum_output")
        out_other = swap(out_send, "mp", 1, "sum_output")
        line.space()
        grad_low, gqkv, back_vec, slot_grad = line(
            lambda *a: (lambda r: (r[0], r[1], r[3], r[2]))(back(*a)),
            pos,
            total,
            far,
            other,
            other_far,
            mid,
            cotangent,
            ln2_gain[None],
            w_out,
            qkv,
            probs,
            sums,
        )

        theirs_w, rest = line(
            rest_weights, first_bit, first, gqkv, grad_low, attended, slot_grad, sums
        )
        rest_got = swap(theirs_w, "dp", feed_masks[0], "rest_weights")
        feed_sum.step()
        (out_other,) = wait(out_other)
        (out_far,) = wait(out_far)
        out_other_far = swap(out_far, "mp", 1, "sum_output")
        theirs, mine = line(first_grad, pos, gqkv, slot_grad, sums, w_qkv, tokens)
        got = swap(theirs, "mp", 1, "sum_first")
        theirs_w, rest = line(split_first, bit_of(feed_masks[1]), rest, rest_got)
        rest_got = swap(theirs_w, "dp", feed_masks[1], "rest_weights")
        feed_sum.step()
        total = line(pair, mine, got)
        for m in far_masks[:-1]:
            total = line(pair, total, swap(total, "mp", m, "sum_first"))
        far = swap(total, "mp", last_far, "sum_first")
        output = line(
            output_sum, pos, out_total, out_far, out_other, out_other_far, mid, b_down[None]
        )
        theirs_w, rest, extra = line(split_second, bit_of(feed_masks[2]), rest, rest_got, w_qkv)
        rest_got = swap(theirs_w, "dp", feed_masks[2], "rest_weights")
        extra_got = swap(extra, "mp", 1, "sum_extra")
        for m in feed_masks[3:]:
            theirs_w, rest = line(split_sum, bit_of(m), rest, rest_got)
            rest_got = swap(theirs_w, "dp", m, "rest_weights")
        for m in feed_masks[3:]:
            feed_sum.step()
        feed_all = line(add_low, feed_sum.mine, feed_sum.got)
        feed_got = swap(feed_all, "dp", feed_masks[-1], "feed_weights")
        (far,) = wait(far)
        other = swap(after(total, far), "mp", 1, "sum_first")
        other_far = swap(far, "mp", 1, "sum_first")
        for m in far_masks:
            extra = line(pl_add, extra, extra_got)
            extra_got = swap(extra, "mp", m, "sum_extra")
        rest_all = line(
            piece_of, rest, rest_got, total, far, back_vec, up_vec
        )
        rest_got = swap(rest_all, "dp", feed_masks[-1], "rest_weights")
        feed_next = list(reversed(feed_masks))[1:]
        rest_next = list(reversed(feed_masks))[1:]
        for m in feed_next[:-2]:
            feed_all = line(concat, feed_all, feed_got)
            feed_got = swap(feed_all, "dp", m, "feed_weights")
        feed_all = line(concat, feed_all, feed_got)
        two = swap(feed_all, "dp", feed_masks[0], "feed_weights")
        one = swap(feed_all, "dp", feed_masks[1], "feed_weights")
        rest_all = line(merge, rest_all, rest_got)
        rest_got = swap(rest_all, "dp", rest_next[0], "rest_weights")
        grad_tokens = line(
            last,
            pos,
            total,
            far,
            other,
            other_far,
            extra,
            extra_got,
            tokens,
            grad_low,
            ln1_gain[None],
        )
        (two,) = wait(two)
        both = swap(two, "dp", feed_masks[1], "feed_weights")
        for m in rest_next[1:]:
            line.space()
            rest_all = line(merge, rest_all, rest_got)
            rest_got = swap(rest_all, "dp", m, "rest_weights")
        held = line(feed_unpack, place_of(feed_masks), feed_all, one)
        grad_w_down, grad_w_up = line(
            feed_unpack, place_of(feed_masks), two, both, *held
        )
        grad_w_qkv, grad_w_out, *vectors = line(
            rest_unpack, place_of(feed_masks), rest_all, rest_got, line.spare
        )
        return (
            output,
            grad_tokens,
            vectors[0][0],
            vectors[1][0],
            grad_w_qkv,
            grad_w_out,
            vectors[2][0],
            vectors[3][0],
            vectors[4][0],
            grad_w_up.reshape(dim, hidden),
            vectors[6][0],
            grad_w_down,
            vectors[5][0],
        )

    return per_device


def solution(mesh):
    return jax.shard_map(
        build(mesh.shape["dp"], mesh.shape["mp"]),
        mesh=mesh,
        in_specs=(
            P("dp", None),
            P(),
            P(),
            P(None, None, "mp"),
            P("mp", None),
            P(),
            P(),
            P(),
            P(None, "mp"),
            P("mp"),
            P("mp", None),
            P(),
            P("dp", None),
        ),
        out_specs=(
            P("dp", None),
            P("dp", None),
            P(),
            P(),
            P(None, None, "mp"),
            P("mp", None),
            P(),
            P(),
            P(),
            P(None, "mp"),
            P("mp"),
            P("mp", None),
            P(),
        ),
        check_vma=False,
    )
```
